128 devices in a mesh: dp: 8 (over y, x_lo), ctx: 4 (over x_hi, core), opt: 4 (over z).
Axes of the slice: x: 4 (x_hi: 2, x_lo: 2; x = x_hi * 2 + x_lo), y: 4, z: 4, core: 2. Of those that a mesh axis runs over, the one named last changes fastest.
Arguments:
- hidden_in: bfloat16 [16384, 1024], P(('dp', 'ctx', 'opt')), may hold values from -6 to 6
- segment_ids: int32 [8, 2048], P('dp'), may hold values from 0 to 5, as said below
- out_cotangent: bfloat16 [16384, 1024], P(('dp', 'ctx', 'opt')), may hold values from -6 to 6
- qkv_weight: float32 [1024, 4096], P(('ctx', 'opt')), may hold values from -0.1875 to 0.1875
- qkv_moment: float32 [1024, 4096], P(('ctx', 'opt')), may hold values from -64 to 64
- qkv_square: float32 [1024, 4096], P(('ctx', 'opt')), may hold values from 655.36 to 4096
- proj_weight: float32 [2048, 1024], P(('ctx', 'opt')), may hold values from -0.125 to 0.125
- proj_moment: float32 [2048, 1024], P(('ctx', 'opt')), may hold values from -64 to 64
- proj_square: float32 [2048, 1024], P(('ctx', 'opt')), may hold values from 655.36 to 4096
- gate_up_weight: float32 [1024, 6144], P(('ctx', 'opt')), may hold values from -0.1875 to 0.1875
- gate_up_moment: float32 [1024, 6144], P(('ctx', 'opt')), may hold values from -64 to 64
- gate_up_square: float32 [1024, 6144], P(('ctx', 'opt')), may hold values from 655.36 to 4096
- down_weight: float32 [3072, 1024], P(('ctx', 'opt')), may hold values from -0.109375 to 0.109375
- down_moment: float32 [3072, 1024], P(('ctx', 'opt')), may hold values from -64 to 64
- down_square: float32 [3072, 1024], P(('ctx', 'opt')), may hold values from 655.36 to 4096
- gains: float32 [5120], P(('ctx', 'opt')), may hold values from 0.5 to 1.5
- gain_moment: float32 [5120], P(('ctx', 'opt')), may hold values from -64 to 64
- gain_square: float32 [5120], P(('ctx', 'opt')), may hold values from 655.36 to 4096
Outputs:
- block_out: bfloat16 [16384, 1024], P(('dp', 'ctx', 'opt'))
- input_grad: float32 [16384, 1024], P(('dp', 'ctx', 'opt'))
- qkv_weight_new: float32 [1024, 4096], P(('ctx', 'opt'))
- qkv_moment_new: float32 [1024, 4096], P(('ctx', 'opt'))
- qkv_square_new: float32 [1024, 4096], P(('ctx', 'opt'))
- proj_weight_new: float32 [2048, 1024], P(('ctx', 'opt'))
- proj_moment_new: float32 [2048, 1024], P(('ctx', 'opt'))
- proj_square_new: float32 [2048, 1024], P(('ctx', 'opt'))
- gate_up_weight_new: float32 [1024, 6144], P(('ctx', 'opt'))
- gate_up_moment_new: float32 [1024, 6144], P(('ctx', 'opt'))
- gate_up_square_new: float32 [1024, 6144], P(('ctx', 'opt'))
- down_weight_new: float32 [3072, 1024], P(('ctx', 'opt'))
- down_moment_new: float32 [3072, 1024], P(('ctx', 'opt'))
- down_square_new: float32 [3072, 1024], P(('ctx', 'opt'))
- gains_new: float32 [5120], P(('ctx', 'opt'))
- gain_moment_new: float32 [5120], P(('ctx', 'opt'))
- gain_square_new: float32 [5120], P(('ctx', 'opt'))
The draws below stay inside these ranges and needn't reach their ends.
Inputs may be any that keep to these rules, and one draw needn't show every extreme that they name: `segment_ids`: document ids start at 0 in each row and rise by one at each new document. In one row, chosen by the seed, there are three documents, the first and the last of 32 to 96 positions each. Every other row holds six documents; each one but the last has 204 to 341 positions, and the last takes what remains of the row.
All inputs are finite; a program needn't handle non-finite values.
Results may differ from the reference program's by a relative error of at most 0.025.
Values may be sent and summed in bfloat16 or wider, within the bound.
A program may use at most 256 MiB of HBM per device.

```python
import math
import jax
import jax.numpy as jnp
from jax import lax

D = 1024
FF = 3072
HEADS = 16
KV_HEADS = 8
HEAD = 128
TOK_DEV = 128
STEP = 10
QD = 2048
KD = 1024
GAINS = 5120
LEN = 2048
SEQS = 8
TOKENS = 16384


def draw_segment_ids(key, part):
    key = jax.random.fold_in(key, 7)
    length_key, head_key, tail_key, pick_key = jax.random.split(key, 4)
    short_end = max(1, LEN // 10)
    long_end = max(short_end + 1, LEN // 6 + 1)
    doc_lengths = jax.random.randint(length_key, (SEQS, 5), short_end, long_end, dtype=jnp.int32)
    boundaries = jnp.cumsum(doc_lengths, axis=1).astype(jnp.int32)
    row_index = jnp.arange(LEN, dtype=jnp.int32)[None, :]
    packed = jnp.sum((row_index[:, :, None] >= boundaries[:, None, :]).astype(jnp.int32), axis=2).astype(jnp.int32)
    lower_end = max(1, TOK_DEV // 4)
    upper_end = 3 * TOK_DEV // 4 + 1
    head_length = jax.random.randint(head_key, (SEQS, 1), lower_end, upper_end, dtype=jnp.int32)
    tail_length = jax.random.randint(tail_key, (SEQS, 1), lower_end, upper_end, dtype=jnp.int32)
    spanning = (row_index >= head_length).astype(jnp.int32) + (row_index >= LEN - tail_length).astype(jnp.int32)
    picked = jax.random.randint(pick_key, (), 0, SEQS, dtype=jnp.int32)
    is_picked = (jnp.arange(SEQS, dtype=jnp.int32) == picked)[:, None]
    return jnp.where(is_picked, spanning, packed).astype(jnp.int32)


def levels(stream_key, extent, shards, low, top_value):
    def one(dim, parts):
        heights = jax.random.uniform(jax.random.fold_in(jax.random.fold_in(stream_key, 6), dim), (parts,), jnp.float32, low / len(shards), top_value / len(shards))
        return jnp.repeat(jnp.exp(heights), extent[dim] // parts).reshape((-1,) + (1,) * (len(extent) - dim - 1))

    factor_of = one(*shards[0])
    for cut in shards[1:]:
        factor_of = factor_of * one(*cut)
    return factor_of


def gaussian(own_key, extent, spread, most, cuts=(), kind=jnp.bfloat16):
    entries = spread * jax.random.normal(own_key, extent, jnp.float32)
    if cuts:
        entries = entries * levels(own_key, extent, cuts, -0.22, 0.18)
    return jnp.clip(entries, -most, most).astype(kind)


def setup_inputs(seed: int = 0) -> dict:
    keys = jax.random.split(jax.random.key(seed), 19)
    return {
        "hidden_in": gaussian(keys[0], (TOKENS, D), 1.0, 6.0, ((0, 128),)),
        "segment_ids": draw_segment_ids(jax.random.fold_in(keys[18], 71), 0),
        "out_cotangent": gaussian(keys[2], (TOKENS, D), 1.0, 6.0, ((0, 128),)),
        "qkv_weight": gaussian(keys[3], (D, QD + 2 * KD), D ** -0.5, 0.1875, ((0, 16),), jnp.float32),
        "qkv_moment": gaussian(keys[4], (D, QD + 2 * KD), (0.11 * TOKENS ** 0.5), 64.0, ((0, 16),), jnp.float32),
        "qkv_square": jnp.clip(jnp.exp(math.log(4096.0) - 1.8325815 * jax.random.uniform(keys[5], (D, QD + 2 * KD), jnp.float32) ** levels(keys[5], (D, QD + 2 * KD), ((0, 16),), -0.2, 0.2)), 655.36, 4096.0),
        "proj_weight": gaussian(keys[6], (QD, D), QD ** -0.5, 0.125, ((0, 16),), jnp.float32),
        "proj_moment": gaussian(keys[7], (QD, D), (0.11 * TOKENS ** 0.5), 64.0, ((0, 16),), jnp.float32),
        "proj_square": jnp.clip(jnp.exp(math.log(4096.0) - 1.8325815 * jax.random.uniform(keys[8], (QD, D), jnp.float32) ** levels(keys[8], (QD, D), ((0, 16),), -0.2, 0.2)), 655.36, 4096.0),
        "gate_up_weight": gaussian(keys[9], (D, 2 * FF), D ** -0.5, 0.1875, ((0, 16),), jnp.float32),
        "gate_up_moment": gaussian(keys[10], (D, 2 * FF), (0.11 * TOKENS ** 0.5), 64.0, ((0, 16),), jnp.float32),
        "gate_up_square": jnp.clip(jnp.exp(math.log(4096.0) - 1.8325815 * jax.random.uniform(keys[11], (D, 2 * FF), jnp.float32) ** levels(keys[11], (D, 2 * FF), ((0, 16),), -0.2, 0.2)), 655.36, 4096.0),
        "down_weight": gaussian(keys[12], (FF, D), FF ** -0.5, 0.109375, ((0, 16),), jnp.float32),
        "down_moment": gaussian(keys[13], (FF, D), (0.11 * TOKENS ** 0.5), 64.0, ((0, 16),), jnp.float32),
        "down_square": jnp.clip(jnp.exp(math.log(4096.0) - 1.8325815 * jax.random.uniform(keys[14], (FF, D), jnp.float32) ** levels(keys[14], (FF, D), ((0, 16),), -0.2, 0.2)), 655.36, 4096.0),
        "gains": jnp.clip(1.0 + 0.1 * jax.random.normal(keys[15], (GAINS,), jnp.float32), 0.5, 1.5),
        "gain_moment": gaussian(keys[16], (GAINS,), (0.11 * TOKENS ** 0.5), 64.0, ((0, 16),), jnp.float32),
        "gain_square": jnp.clip(jnp.exp(math.log(4096.0) - 1.8325815 * jax.random.uniform(keys[17], (GAINS,), jnp.float32) ** levels(keys[17], (GAINS,), ((0, 16),), -0.2, 0.2)), 655.36, 4096.0),
    }


@jax.custom_vjp
def low(v):
    return lax.optimization_barrier(v.astype(jnp.bfloat16)).astype(jnp.float32)

@jax.custom_vjp
def low_back(v):
    return v

def low_keep(v):
    return (low(v), None)

def low_pass(kept, grad):
    return (grad,)

def back_keep(v):
    return (v, None)

def back_low(kept, grad):
    return (low(grad),)
low.defvjp(low_keep, low_pass)
low_back.defvjp(back_keep, back_low)
NORM_EPS = 1e-06
THETA = 500000.0
MASKED = -1e+30
HIGHEST = lax.Precision.HIGHEST
BETA_ONE = 0.9
BETA_TWO = 0.95
ADAM_EPS = 1e-08
RATE_MATRIX = 0.06
RATE_GAIN = 1.0
DECAY = 0.1

def rms_scale(values):
    return lax.rsqrt(lax.optimization_barrier(jnp.mean(values * values, axis=-1, keepdims=True)) + NORM_EPS)

def doc_positions(seq_segments):
    row_index = jnp.arange(seq_segments.shape[0], dtype=jnp.int32)
    new_doc = jnp.concatenate([jnp.ones((1,), dtype=bool), seq_segments[1:] != seq_segments[:-1]])
    starts = lax.cummax(jnp.where(new_doc, row_index, 0).astype(jnp.int32), axis=0)
    return row_index - starts

def rotary_tables(positions, half_width):
    frequency = jnp.exp(jnp.arange(half_width, dtype=jnp.float32) * (-math.log(THETA) / half_width))
    angles = positions.astype(jnp.float32)[:, None] * frequency[None, :]
    return (jnp.cos(angles), jnp.sin(angles))

def rotate(heads, cosine_table, sine_table):
    half_width = heads.shape[-1] // 2
    first_half = heads[..., :half_width]
    second_half = heads[..., half_width:]
    cosine = cosine_table[:, None, :]
    sine_rows = sine_table[:, None, :]
    return jnp.concatenate([first_half * cosine - second_half * sine_rows, second_half * cosine + first_half * sine_rows], axis=-1)

def attend(query_heads, key_heads, value_heads, seq_segments):
    seq_length = key_heads.shape[0]
    block_rows = min(512, seq_length)
    block_count = seq_length // block_rows
    score_scale = 1.0 / math.sqrt(HEAD)
    query_blocks = query_heads.reshape((block_count, block_rows) + query_heads.shape[1:])
    starts = jnp.arange(block_count, dtype=jnp.int32) * block_rows
    key_index = jnp.arange(seq_length, dtype=jnp.int32)

    def block_attend(block_item):
        query_block, start_row = block_item
        raw_scores = jnp.einsum('qhgd,khd->hgqk', query_block, key_heads, precision=HIGHEST)
        scores = low_back(raw_scores * score_scale)
        query_index = start_row + jnp.arange(block_rows, dtype=jnp.int32)
        query_segment = lax.dynamic_slice_in_dim(seq_segments, start_row, block_rows)
        allowed = (key_index[None, :] <= query_index[:, None]) & (seq_segments[None, :] == query_segment[:, None])
        scores = jnp.where(allowed, scores, MASKED)
        weights = jax.nn.softmax(scores, axis=-1)
        return jnp.einsum('hgqk,khd->qhgd', low(weights), value_heads, precision=HIGHEST)
    results = lax.map(jax.checkpoint(block_attend), (query_blocks, starts))
    return results.reshape(query_heads.shape)

def layer_forward(hidden, w_qkv, w_proj, w_gate_up, w_down, gain_values, seq_segments, cosine_table, sine_table):
    seq_length = hidden.shape[0]
    query_width = HEADS * HEAD
    key_width = KV_HEADS * HEAD
    gain_low = low(gain_values)
    gain_query = gain_low[:query_width]
    gain_key = gain_low[query_width:query_width + key_width]
    gain_attn = gain_low[query_width + key_width:query_width + key_width + D]
    gain_ffn = gain_low[query_width + key_width + D:]
    projected = low_back(jnp.dot(hidden, low(w_qkv), precision=HIGHEST))
    query_raw = projected[:, :query_width]
    key_raw = projected[:, query_width:query_width + key_width]
    value_raw = projected[:, query_width + key_width:]
    query_norm = query_raw * rms_scale(query_raw) * gain_query
    key_norm = key_raw * rms_scale(key_raw) * gain_key
    query_rot = low(rotate(query_norm.reshape(seq_length, HEADS, HEAD), cosine_table, sine_table))
    key_rot = low(rotate(key_norm.reshape(seq_length, KV_HEADS, HEAD), cosine_table, sine_table))
    value_low = low(value_raw).reshape(seq_length, KV_HEADS, HEAD)
    mixed = attend(query_rot.reshape(seq_length, KV_HEADS, HEADS // KV_HEADS, HEAD), key_rot, value_low, seq_segments)
    mixed_low = low(low_back(mixed.reshape(seq_length, query_width)))
    branch = low_back(jnp.dot(mixed_low, low(w_proj), precision=HIGHEST))
    residual = hidden + branch * rms_scale(branch) * gain_attn
    gate_up = low_back(jnp.dot(low(residual), low(w_gate_up), precision=HIGHEST))
    act_low = low(jax.nn.silu(gate_up[:, :FF]) * gate_up[:, FF:])
    ffn_out = low_back(jnp.dot(act_low, low(w_down), precision=HIGHEST))
    return residual + ffn_out * rms_scale(ffn_out) * gain_ffn

def adam_step(weight, moment, square, grad_sum, rate, decay):
    moment_new = BETA_ONE * moment + (1.0 - BETA_ONE) * grad_sum
    square_new = BETA_TWO * square + (1.0 - BETA_TWO) * grad_sum * grad_sum
    moment_hat = moment_new / (1.0 - BETA_ONE ** STEP)
    square_hat = square_new / (1.0 - BETA_TWO ** STEP)
    weight_new = weight - rate * (moment_hat / (jnp.sqrt(square_hat) + ADAM_EPS) + decay * weight)
    return (weight_new, moment_new, square_new)

def reference(hidden_in, segment_ids, out_cotangent, qkv_weight, qkv_moment, qkv_square, proj_weight, proj_moment, proj_square, gate_up_weight, gate_up_moment, gate_up_square, down_weight, down_moment, down_square, gains, gain_moment, gain_square):
    weights = (qkv_weight, proj_weight, gate_up_weight, down_weight, gains)
    hidden_all = hidden_in.astype(jnp.float32).reshape(SEQS, LEN, D)
    cotangent_all = out_cotangent.astype(jnp.float32).reshape(SEQS, LEN, D)

    def per_sequence(running, seq_item):
        hidden, cotangent, seq_segments = seq_item
        cosine_table, sine_table = rotary_tables(doc_positions(seq_segments), HEAD // 2)

        def forward(hidden_rows, w_qkv, w_proj, w_gate_up, w_down, gain_values):
            return layer_forward(hidden_rows, w_qkv, w_proj, w_gate_up, w_down, gain_values, seq_segments, cosine_table, sine_table)
        layer_out, pull_back = jax.vjp(forward, hidden, weights[0], weights[1], weights[2], weights[3], weights[4])
        gradients = pull_back(cotangent)
        running = tuple((before + increment for before, increment in zip(running, gradients[1:])))
        return (running, (layer_out.astype(jnp.bfloat16), gradients[0]))
    zero_grads = tuple((jnp.zeros_like(weight) for weight in weights))
    grad_sums, (layer_outs, input_grads) = lax.scan(per_sequence, zero_grads, (hidden_all, cotangent_all, segment_ids))
    block_out = layer_outs.reshape(TOKENS, D)
    input_grad = input_grads.reshape(TOKENS, D)
    new_qkv = adam_step(qkv_weight, qkv_moment, qkv_square, grad_sums[0], RATE_MATRIX, DECAY)
    new_proj = adam_step(proj_weight, proj_moment, proj_square, grad_sums[1], RATE_MATRIX, DECAY)
    new_gate_up = adam_step(gate_up_weight, gate_up_moment, gate_up_square, grad_sums[2], RATE_MATRIX, DECAY)
    new_down = adam_step(down_weight, down_moment, down_square, grad_sums[3], RATE_MATRIX, DECAY)
    new_gains = adam_step(gains, gain_moment, gain_square, grad_sums[4], RATE_GAIN, 0.0)
    return (block_out, input_grad, new_qkv[0], new_qkv[1], new_qkv[2], new_proj[0], new_proj[1], new_proj[2], new_gate_up[0], new_gate_up[1], new_gate_up[2], new_down[0], new_down[1], new_down[2], new_gains[0], new_gains[1], new_gains[2])
```

```python
import functools
import math

import jax
import jax.numpy as jnp
from jax import lax
from jax.experimental import pallas as pl
from jax.experimental.pallas import tpu as pltpu
from jax.sharding import PartitionSpec as P

D = 1024
FF = 3072
HEADS = 16
KV_HEADS = 8
HEAD = 128
STEP = 10

NORM_EPS = 1e-06
THETA = 500000.0
MASKED = -1e30
BETA_ONE = 0.9
BETA_TWO = 0.95
ADAM_EPS = 1e-08
RATE_MATRIX = 0.06
RATE_GAIN = 1.0
DECAY = 0.1

TOK = 128
HALF = 1024
RANKS = 8
QW = HEADS * HEAD
KW = KV_HEADS * HEAD
RQ = 256
RK = 128
RC = RQ + 2 * RK
RF = FF // RANKS
BLK = 256
SCORE_SCALE = 1.0 / math.sqrt(HEAD)
SCALE_TWO = SCORE_SCALE * math.log2(math.e)

MESH = pl.DeviceIdType.MESH
BF = jnp.bfloat16
F32 = jnp.float32
VMEM = pl.BlockSpec(memory_space=pltpu.VMEM)
DMA = pltpu.SemaphoreType.DMA


def coords():
    return lax.axis_index("dp"), lax.axis_index("ctx"), lax.axis_index("opt")


def sibling(c):
    return c + 1 - 2 * lax.rem(c, 2)


def rank_peer(d, c, o, t):
    flip = t // 4
    return (d, c + (1 - 2 * lax.rem(c, 2)) * flip, lax.rem(o + t % 4, 4))


def cross_peer(d, c, o, t):
    return rank_peer(d + 1 - 2 * lax.rem(d, 2), lax.rem(c + 2, 4), o, t)


def plane_peer(d, c, o, t):
    x_lo, y = lax.rem(d, 2), lax.div(d, 2)
    y = lax.rem(y + t // 4, 4)
    x_lo = x_lo + (1 - 2 * x_lo) * (t % 2)
    return (2 * y + x_lo, lax.rem(c + 2 * ((t % 4) // 2), 4), o)


def group_peer(d, c, o, t):
    return (d, lax.rem(c + t // 4, 4), lax.rem(o + t % 4, 4))


def dp_peer(d, c, o, t):
    return (lax.rem(d + t, 8), c, o)


def greet(peers):
    barrier = pltpu.get_barrier_semaphore()
    for to in peers:
        pl.semaphore_signal(barrier, inc=1, device_id=to, device_id_type=MESH)
    pl.semaphore_wait(barrier, len(peers))


def remote(src, dst, send, recv, to):
    return pltpu.make_async_remote_copy(
        src_ref=src, dst_ref=dst, send_sem=send, recv_sem=recv, device_id=to, device_id_type=MESH
    )


def rows(index, count):
    return pl.ds(pl.multiple_of(index * count, count), count)


def nn(a, b):
    return lax.dot_general(a, b, (((1,), (0,)), ((), ())), preferred_element_type=F32)


def nt(a, b):
    return lax.dot_general(a, b, (((1,), (1,)), ((), ())), preferred_element_type=F32)


def tn(a, b):
    return lax.dot_general(a, b, (((0,), (0,)), ((), ())), preferred_element_type=F32)


def row_sums(values):
    ones = jnp.ones((8, values.shape[1]), F32)
    return lax.dot_general(
        ones,
        values,
        (((1,), (1,)), ((), ())),
        precision=lax.Precision.HIGHEST,
        preferred_element_type=F32,
    )


def column(row):
    return jnp.transpose(jnp.broadcast_to(row, (128, 128)))


def rms_scale(values):
    return lax.rsqrt(jnp.mean(values * values, axis=-1, keepdims=True) + NORM_EPS)


def norm_back(grad_rows, unit_rows, scale_rows, gain_row):
    weighted = grad_rows * gain_row
    return scale_rows * (
        weighted - unit_rows * jnp.mean(weighted * unit_rows, axis=-1, keepdims=True)
    )


def rope(u, cos, sin):
    return u * cos + pltpu.roll(u, HEAD // 2, 1) * sin


def unrope(g, cos, sin):
    return g * cos - pltpu.roll(g, HEAD // 2, 1) * sin


def gather_start(full, send, recv):
    d, c, o = coords()
    rank = lax.rem(c, 2) * 4 + o
    own = full.at[rows(rank, TOK)]
    for t in (1, 3, 2):
        remote(own, own, send.at[t], recv.at[rank], (d, c, lax.rem(o + t, 4))).start()
    remote(own, own, send.at[0], recv.at[rank], (d, sibling(c), o)).start()


def gather_arrive(full, send, recv, off):
    d, c, o = coords()
    core = lax.rem(c, 2)
    at = lax.rem(o + off, 4)
    mine, other = core * 4 + at, (1 - core) * 4 + at
    to = (d, sibling(c), o)
    block = full.at[rows(mine, TOK)]

    @pl.when(off > 0)
    def _():
        remote(block, block, send.at[0], recv.at[mine], to).wait_recv()
        remote(block, block, send.at[3 + off], recv.at[mine], to).start()

    block = full.at[rows(other, TOK)]
    remote(block, block, send.at[0], recv.at[other], to).wait_recv()
    return mine, other


def gather_finish(full, send, recv):
    d, c, o = coords()
    own = full.at[rows(0, TOK)]
    for i in range(7):
        remote(own, own, send.at[i], recv.at[0], (d, sibling(c), o)).wait_send()


def scatter_sibling(off, part, s):
    d, c, o = coords()
    s["stage_s"][off] = part.astype(BF)
    remote(
        s["stage_s"].at[off], s["land_s"].at[off], s["send_s"].at[off], s["recv_s"].at[off], (d, sibling(c), o)
    ).start()


def scatter_along(off, s):
    d, c, o = coords()
    to = (d, sibling(c), o)
    remote(s["stage_s"].at[off], s["land_s"].at[off], s["send_s"].at[off], s["recv_s"].at[off], to).wait_recv()
    total = s["own"][off] + s["land_s"][off].astype(F32)

    @pl.when(off > 0)
    def _():
        s["stage_z"][off] = total.astype(BF)
        remote(
            s["stage_z"].at[off],
            s["land_z"].at[off],
            s["send_z"].at[off],
            s["recv_z"].at[off],
            (d, c, lax.rem(o + off, 4)),
        ).start()

    @pl.when(off == 0)
    def _():
        s["own"][0] = total


def scatter_result(s):
    d, c, o = coords()
    total = s["own"][0]
    for off in (1, 3, 2):
        remote(
            s["stage_z"].at[off], s["land_z"].at[off], s["send_z"].at[off], s["recv_z"].at[off], (d, sibling(c), o)
        ).wait_recv()
        total = total + s["land_z"][off].astype(F32)
    return total


def scatter_finish(s):
    d, c, o = coords()
    to = (d, sibling(c), o)
    for off in range(4):
        remote(s["stage_s"].at[off], s["land_s"].at[off], s["send_s"].at[off], s["recv_s"].at[off], to).wait_send()
    for off in range(1, 4):
        remote(s["stage_z"].at[off], s["land_z"].at[off], s["send_z"].at[off], s["recv_z"].at[off], to).wait_send()


SCATTER_NAMES = ("stage_s", "land_s", "stage_z", "land_z", "own", "send_s", "recv_s", "send_z", "recv_z")


def scatter_scratch():
    return [
        pltpu.VMEM((4, TOK, D), BF),
        pltpu.VMEM((4, TOK, D), BF),
        pltpu.VMEM((4, TOK, D), BF),
        pltpu.VMEM((4, TOK, D), BF),
        pltpu.VMEM((4, TOK, D), F32),
        DMA((4,)),
        DMA((4,)),
        DMA((4,)),
        DMA((4,)),
    ]


def order(step):
    return step + lax.div(step, 2) - 2 * lax.div(step, 3)


def sum_exchange(sums, land, send, recv):
    d, c, o = coords()
    rank = lax.rem(c, 2) * 4 + o
    land[rank] = sums[...]
    copies = []
    for t in range(1, 8):
        copies.append(
            remote(sums, land.at[rank], send.at[t], recv.at[rank], rank_peer(d, c, o, t))
        )
        copies[-1].start()
    for t in range(1, 8):
        _, c1, o1 = rank_peer(d, c, o, t)
        from_rank = lax.rem(c1, 2) * 4 + o1
        remote(sums, land.at[from_rank], send.at[t], recv.at[from_rank], (d, sibling(c), o)).wait_recv()
    for copy in copies:
        copy.wait_send()
    total = land[0]
    for i in range(1, 8):
        total = total + land[i]
    return total


def first_kernel(
    hid, w_rows, gain_parts, cos, sin,
    hid_all, w_all, gain_out, q_rot, k_rot, v_low, unit, scales,
    pieces, gain_land, qkv, sums, sums_land,
    h_send, h_recv, w_send, w_recv, g_send, g_recv, s_send, s_recv,
):
    d, c, o = coords()
    rank = lax.rem(c, 2) * 4 + o
    place = c * 4 + o
    peers = [rank_peer(d, c, o, t) for t in range(1, 8)] + [cross_peer(d, c, o, t) for t in range(8)]
    hid_all[rows(rank, TOK), :] = hid[...]
    for g in range(RANKS):
        pieces[g, :, 0:RQ] = w_rows[:, g * RQ : (g + 1) * RQ].astype(BF)
        pieces[g, :, RQ : RQ + RK] = w_rows[:, QW + g * RK : QW + (g + 1) * RK].astype(BF)
        pieces[g, :, RQ + RK : RC] = w_rows[:, QW + KW + g * RK : QW + KW + (g + 1) * RK].astype(BF)
    greet(peers)
    gather_start(hid_all, h_send, h_recv)
    mine = w_all.at[rows(place, 64)]
    copies = []
    for i, to in enumerate(peers):
        to_rank = lax.rem(to[1], 2) * 4 + to[2]
        copies.append(remote(pieces.at[to_rank], mine, w_send.at[i], w_recv.at[place], to))
        copies[-1].start()
    for i, to in enumerate(peers):
        to_rank = lax.rem(to[1], 2) * 4 + to[2]
        copies.append(
            remote(gain_parts.at[to_rank], gain_land.at[place], g_send.at[i], g_recv.at[place], to)
        )
        copies[-1].start()
    w_all[rows(place, 64), :] = pieces[rank]
    gain_land[place] = gain_parts[rank]
    for i, to in enumerate(peers):
        source = to[1] * 4 + to[2]
        remote(pieces.at[0], w_all.at[rows(source, 64)], w_send.at[i], w_recv.at[source], to).wait_recv()

    def project(step, _):
        off = order(step)
        mine, other = gather_arrive(hid_all, h_send, h_recv, off)
        both = jnp.concatenate([hid_all[rows(mine, TOK), :], hid_all[rows(other, TOK), :]], axis=0)
        out = nn(both, w_all[...])
        squares = out * out
        q_sum, k_sum = row_sums(squares[:, 0:RQ]), row_sums(squares[:, RQ : RQ + RK])
        upper = lax.broadcasted_iota(jnp.int32, (8, 2 * TOK), 0) < 4
        both_sums = jnp.where(upper, q_sum, k_sum)
        qkv[rows(mine, TOK), :] = out[0:TOK]
        qkv[rows(other, TOK), :] = out[TOK:]
        sums[mine] = both_sums[:, 0:TOK]
        sums[other] = both_sums[:, TOK:]
        return 0

    lax.fori_loop(0, 4, project, 0)
    for i, to in enumerate(peers):
        source = to[1] * 4 + to[2]
        remote(gain_parts.at[0], gain_land.at[source], g_send.at[i], g_recv.at[source], to).wait_recv()
    gains = gain_land[0]
    for i in range(1, 16):
        gains = gains + gain_land[i]
    gain_out[...] = gains
    total = sum_exchange(sums, sums_land, s_send, s_recv)
    upper = lax.broadcasted_iota(jnp.int32, (8, 8, TOK), 1) < 4
    mean = jnp.where(upper, total * (1.0 / QW), total * (1.0 / KW))
    scales[...] = lax.rsqrt(mean + NORM_EPS)

    def finish(b, _):
        at = rows(b, TOK)
        both = scales[b]
        q_scale, k_scale = column(both[0:1]), column(both[4:5])
        cosine, sine = cos[at, :], sin[at, :]
        for head in range(2):
            cols = slice(head * HEAD, (head + 1) * HEAD)
            q_unit = qkv[at, cols] * q_scale
            unit[at, cols] = q_unit
            q_rot[head, at, :] = rope(q_unit * gain_out[0:1, cols], cosine, sine).astype(BF)
        cols = slice(RQ, RQ + RK)
        k_unit = qkv[at, cols] * k_scale
        unit[at, cols] = k_unit
        k_rot[at, :] = rope(k_unit * gain_out[0:1, cols], cosine, sine).astype(BF)
        v_low[at, :] = qkv[at, RQ + RK : RC].astype(BF)
        return 0

    lax.fori_loop(0, RANKS, finish, 0)
    gather_finish(hid_all, h_send, h_recv)
    for copy in copies:
        copy.wait_send()


def call_first(hid, w_rows, gain_parts, cos, sin):
    return pl.pallas_call(
        first_kernel,
        name="gather_qkv",
        out_shape=(
            jax.ShapeDtypeStruct((HALF, D), BF),
            jax.ShapeDtypeStruct((D, RC), BF),
            jax.ShapeDtypeStruct((8, 512), F32),
            jax.ShapeDtypeStruct((2, HALF, HEAD), BF),
            jax.ShapeDtypeStruct((HALF, HEAD), BF),
            jax.ShapeDtypeStruct((HALF, HEAD), BF),
            jax.ShapeDtypeStruct((HALF, RQ + RK), F32),
            jax.ShapeDtypeStruct((8, 8, TOK), F32),
        ),
        in_specs=[VMEM] * 5,
        out_specs=[VMEM] * 8,
        scratch_shapes=[
            pltpu.VMEM((RANKS, 64, RC), BF),
            pltpu.VMEM((16, 8, 512), F32),
            pltpu.VMEM((HALF, RC), F32),
            pltpu.VMEM((8, 8, TOK), F32),
            pltpu.VMEM((8, 8, 8, TOK), F32),
            DMA((7,)),
            DMA((8,)),
            DMA((15,)),
            DMA((16,)),
            DMA((15,)),
            DMA((16,)),
            DMA((8,)),
            DMA((8,)),
        ],
        compiler_params=pltpu.CompilerParams(
            collective_id=1, has_side_effects=True, vmem_limit_bytes=40 * 2**20
        ),
    )(hid, w_rows, gain_parts, cos, sin)


def tile_mask(key_base, query_base, start_row):
    key_index = key_base + lax.broadcasted_iota(jnp.int32, (BLK, BLK), 0)
    query_index = query_base + lax.broadcasted_iota(jnp.int32, (BLK, BLK), 1)
    return (key_index >= start_row) & (key_index <= query_index)


def attend_kernel(
    q_rot, k_rot, v_low, start, gu_rows, pj_rows, dn_rows,
    kv_other, mixed, mixed_low, lse, gu_all, pj_all, dn_all,
    kv_own, gu_pieces, pj_own, dn_own, v_t, top, running, accum,
    kv_send, kv_recv, g_send, g_recv, p_send, p_recv, d_send, d_recv,
):
    d, c, o = coords()
    half = lax.div(c, 2)
    rank = lax.rem(c, 2) * 4 + o
    place = c * 4 + o
    partner = (d, lax.rem(c + 2, 4), o)
    peers = [rank_peer(d, c, o, t) for t in range(1, 8)] + [cross_peer(d, c, o, t) for t in range(8)]
    kv_own[0] = k_rot[...]
    kv_own[1] = v_low[...]
    for g in range(RANKS):
        gu_pieces[g, :, 0:RF] = gu_rows[:, g * RF : (g + 1) * RF].astype(BF)
        gu_pieces[g, :, RF:] = gu_rows[:, FF + g * RF : FF + (g + 1) * RF].astype(BF)
    pj_own[...] = pj_rows[...].astype(BF)
    dn_own[...] = dn_rows[...].astype(BF)
    greet(peers + [partner])

    kv_copy = remote(kv_own, kv_other, kv_send, kv_recv, partner)

    @pl.when(half == 0)
    def _():
        kv_copy.start()

    to_rank = lax.div(place, 2)
    slot = lax.rem(place, 2)
    near = (d, half * 2 + lax.div(to_rank, 4), lax.rem(to_rank, 4))
    far = (d + 1 - 2 * lax.rem(d, 2), (1 - half) * 2 + lax.div(to_rank, 4), lax.rem(to_rank, 4))
    pj_slot, dn_slot = pj_all.at[rows(slot, 128)], dn_all.at[rows(slot, 192)]
    keep = to_rank == rank
    pj_near = remote(pj_own, pj_slot, p_send.at[0], p_recv.at[slot], near)
    dn_near = remote(dn_own, dn_slot, d_send.at[0], d_recv.at[slot], near)
    pj_far = remote(pj_own, pj_slot, p_send.at[1], p_recv.at[slot], far)
    dn_far = remote(dn_own, dn_slot, d_send.at[1], d_recv.at[slot], far)

    @pl.when(jnp.logical_not(keep))
    def _():
        pj_near.start()
        dn_near.start()

    @pl.when(keep)
    def _():
        pj_all[rows(slot, 128), :] = pj_own[...]
        dn_all[rows(slot, 192), :] = dn_own[...]

    pj_far.start()
    dn_far.start()
    mine = gu_all.at[rows(place, 64)]
    copies = []
    for i, to in enumerate(peers):
        piece = lax.rem(to[1], 2) * 4 + to[2]
        copies.append(remote(gu_pieces.at[piece], mine, g_send.at[i], g_recv.at[place], to))
        copies[-1].start()
    gu_all[rows(place, 64), :] = gu_pieces[rank]

    v_t[0] = jnp.transpose(v_low[...].astype(F32)).astype(BF)

    def tile(strip, keys, values_t, base, key_base, carry):
        head, block = lax.div(strip, 4), lax.rem(strip, 4)
        at = rows(block, BLK)
        scores = nt(keys, q_rot[head, at, :]) * SCALE_TWO
        start_row = start[0:1, at]
        allowed = tile_mask(key_base, half * HALF + block * BLK, start_row)
        scores = jnp.where(allowed, scores, MASKED)
        top_now = jnp.max(scores, axis=0, keepdims=True)
        if carry is None:
            probs = jnp.exp2(scores - top_now)
            return top_now, jnp.sum(probs, axis=0, keepdims=True), nn(values_t, probs.astype(BF))
        top_old, run_old, acc_old = carry
        top_new = jnp.maximum(top_old, top_now)
        fade = jnp.exp2(top_old - top_new)
        probs = jnp.exp2(scores - top_new)
        return (
            top_new,
            run_old * fade + jnp.sum(probs, axis=0, keepdims=True),
            acc_old * fade + nn(values_t, probs.astype(BF)),
        )

    def keep_state(strip, state):
        top[strip] = jnp.broadcast_to(state[0], (8, BLK))
        running[strip] = jnp.broadcast_to(state[1], (8, BLK))
        accum[strip] = state[2]

    def local_strip(strip, _):
        block = lax.rem(strip, 4)
        base = half * HALF

        def local_tile(j, carry):
            return tile(
                strip, k_rot[rows(j, BLK), :], v_t[0, :, rows(j, BLK)], base, base + j * BLK, carry
            )

        state = local_tile(block, None)
        state = lax.fori_loop(0, block, local_tile, state)
        keep_state(strip, state)
        return 0

    lax.fori_loop(0, 8, local_strip, 0)

    @pl.when(half == 1)
    def _():
        kv_copy.wait_recv()
        v_t[1] = jnp.transpose(kv_other[1].astype(F32)).astype(BF)

        def other_strip(strip, _):
            state = (top[strip][0:1], running[strip][0:1], accum[strip])

            def other_tile(j, carry):
                return tile(
                    strip, kv_other[0, rows(j, BLK), :], v_t[1, :, rows(j, BLK)], 0, j * BLK, carry
                )

            keep_state(strip, lax.fori_loop(0, 4, other_tile, state))
            return 0

        lax.fori_loop(0, 8, other_strip, 0)

    @pl.when(half == 0)
    def _():
        kv_copy.wait_send()

    for strip in range(8):
        head, block = strip // 4, strip % 4
        run = running[strip]
        lse[head, :, block * BLK : (block + 1) * BLK] = top[strip] + jnp.log2(run)
        out = jnp.transpose(accum[strip] * (1.0 / run[0:1]))
        mixed[head, block * BLK : (block + 1) * BLK, :] = out
        mixed_low[block * BLK : (block + 1) * BLK, head * HEAD : (head + 1) * HEAD] = out.astype(BF)

    for i, to in enumerate(peers):
        source = to[1] * 4 + to[2]
        remote(gu_pieces.at[0], gu_all.at[rows(source, 64)], g_send.at[i], g_recv.at[source], to).wait_recv()
    for i in range(2):
        from_self = 2 * rank + i == place

        @pl.when(jnp.logical_not(from_self))
        def _(i=i):
            remote(pj_own, pj_all.at[pl.ds(i * 128, 128)], p_send.at[0], p_recv.at[i], partner).wait_recv()
            remote(dn_own, dn_all.at[pl.ds(i * 192, 192)], d_send.at[0], d_recv.at[i], partner).wait_recv()

    for copy in copies + [pj_far, dn_far]:
        copy.wait_send()

    @pl.when(jnp.logical_not(keep))
    def _():
        pj_near.wait_send()
        dn_near.wait_send()


def call_attend(q_rot, k_rot, v_low, start, gu_rows, pj_rows, dn_rows):
    return pl.pallas_call(
        attend_kernel,
        name="attend",
        out_shape=(
            jax.ShapeDtypeStruct((2, HALF, HEAD), BF),
            jax.ShapeDtypeStruct((2, HALF, HEAD), F32),
            jax.ShapeDtypeStruct((HALF, RQ), BF),
            jax.ShapeDtypeStruct((2, 8, HALF), F32),
            jax.ShapeDtypeStruct((D, 2 * RF), BF),
            jax.ShapeDtypeStruct((RQ, D), BF),
            jax.ShapeDtypeStruct((RF, D), BF),
        ),
        in_specs=[VMEM] * 7,
        out_specs=[VMEM] * 7,
        scratch_shapes=[
            pltpu.VMEM((2, HALF, HEAD), BF),
            pltpu.VMEM((RANKS, 64, 2 * RF), BF),
            pltpu.VMEM((128, D), BF),
            pltpu.VMEM((192, D), BF),
            pltpu.VMEM((2, HEAD, HALF), BF),
            pltpu.VMEM((8, 8, BLK), F32),
            pltpu.VMEM((8, 8, BLK), F32),
            pltpu.VMEM((8, HEAD, BLK), F32),
            DMA,
            DMA,
            DMA((15,)),
            DMA((16,)),
            DMA((2,)),
            DMA((2,)),
            DMA((2,)),
            DMA((2,)),
        ],
        compiler_params=pltpu.CompilerParams(
            collective_id=2, has_side_effects=True, vmem_limit_bytes=40 * 2**20
        ),
    )(q_rot, k_rot, v_low, start, gu_rows, pj_rows, dn_rows)


def middle_kernel(
    mixed_low, mixed, pj_all, gu_all, dn_all, hid, cot, gains,
    layer_out, back_resid, back_mixed, delta, gain_grads, pj_grad, gu_grad, dn_grad,
    full_res, full_ffn, full_branch, gate_up, act, back_gu,
    *scratch,
):
    d, c, o = coords()
    core = lax.rem(c, 2)
    rank = core * 4 + o
    scatters = [dict(zip(SCATTER_NAMES, scratch[9 * i : 9 * i + 9])) for i in range(3)]
    a_send, a_recv, b_send, b_recv, e_send, e_recv = scratch[27:33]
    peers = [(d, sibling(c), o)] + [(d, c, lax.rem(o + t, 4)) for t in (1, 2, 3)]
    gain_attn = jnp.concatenate([gains[1:2], gains[2:3]], axis=1)
    gain_ffn = jnp.concatenate([gains[3:4], gains[4:5]], axis=1)
    greet(peers)

    def both_rows(ref, mine, other):
        return jnp.concatenate([ref[rows(mine, TOK), :], ref[rows(other, TOK), :]], axis=0)

    def give(off, part, s):
        scatter_sibling(off, part[TOK:], s)
        s["own"][off] = part[0:TOK]

    s = scatters[0]

    def proj_step(step, _):
        off = lax.rem(step + 1, 4)
        at = lax.rem(o + off, 4)
        part = nn(both_rows(mixed_low, core * 4 + at, (1 - core) * 4 + at), pj_all[...])
        give(off, part, s)

        @pl.when(step > 0)
        def _():
            scatter_along(step, s)

        return 0

    lax.fori_loop(0, 4, proj_step, 0)
    scatter_along(0, s)
    branch = scatter_result(s)
    branch_scale = rms_scale(branch)
    branch_unit = branch * branch_scale
    residual = hid[...].astype(F32) + branch_unit * gain_attn
    full_res[rows(rank, TOK), :] = residual.astype(BF)
    gather_start(full_res, a_send, a_recv)
    scatter_finish(s)

    s1 = scatters[1]

    def ffn_step(step, _):
        off = order(step)
        mine, other = gather_arrive(full_res, a_send, a_recv, off)
        both = nn(both_rows(full_res, mine, other), gu_all[...])
        gate_up[rows(mine, TOK), :] = both[0:TOK]
        gate_up[rows(other, TOK), :] = both[TOK:]
        gate, up = both[:, 0:RF], both[:, RF:]
        act_low = (gate * jax.nn.sigmoid(gate) * up).astype(BF)
        act[rows(mine, TOK), :] = act_low[0:TOK]
        act[rows(other, TOK), :] = act_low[TOK:]
        give(off, nn(act_low, dn_all[...]), s1)

        @pl.when(step > 0)
        def _():
            scatter_along(order(step - 1), s1)

        return 0

    lax.fori_loop(0, 4, ffn_step, 0)
    scatter_along(2, s1)
    ffn = scatter_result(s1)
    ffn_scale = rms_scale(ffn)
    ffn_unit = ffn * ffn_scale
    layer_out[...] = residual + ffn_unit * gain_ffn
    cotangent = cot[...].astype(F32)
    back_ffn = norm_back(cotangent, ffn_unit, ffn_scale, gain_ffn)
    full_ffn[rows(rank, TOK), :] = back_ffn.astype(BF)
    gather_start(full_ffn, b_send, b_recv)
    gain_grads[...] = jnp.zeros_like(gain_grads)
    gain_grads[1:2, :] = jnp.sum(cotangent * ffn_unit, axis=0, keepdims=True)
    gather_finish(full_res, a_send, a_recv)
    scatter_finish(s1)

    s2 = scatters[2]

    def back_step(step, _):
        off = order(step)
        mine, other = gather_arrive(full_ffn, b_send, b_recv, off)
        back_act = nt(both_rows(full_ffn, mine, other), dn_all[...])
        both = both_rows(gate_up, mine, other)
        gate, up = both[:, 0:RF], both[:, RF:]
        sig = jax.nn.sigmoid(gate)
        back_gate = back_act * up * sig * (1.0 + gate * (1.0 - sig))
        back_up = back_act * (gate * sig)
        back_both = jnp.concatenate([back_gate, back_up], axis=1).astype(BF)
        back_gu[rows(mine, TOK), :] = back_both[0:TOK]
        back_gu[rows(other, TOK), :] = back_both[TOK:]
        give(off, nt(back_both, gu_all[...]), s2)

        @pl.when(step > 0)
        def _():
            scatter_along(order(step - 1), s2)

        return 0

    lax.fori_loop(0, 4, back_step, 0)
    scatter_along(2, s2)
    dn_grad[...] = tn(act[...], full_ffn[...]).astype(BF)
    resid_grad = cotangent + scatter_result(s2)
    back_resid[...] = resid_grad
    gain_grads[0:1, :] = jnp.sum(resid_grad * branch_unit, axis=0, keepdims=True)
    back_branch = norm_back(resid_grad, branch_unit, branch_scale, gain_attn)
    full_branch[rows(rank, TOK), :] = back_branch.astype(BF)
    gather_start(full_branch, e_send, e_recv)
    gather_finish(full_ffn, b_send, b_recv)
    scatter_finish(s2)
    gu_grad[...] = tn(full_res[...], back_gu[...]).astype(BF)

    def mixed_step(step, _):
        off = order(step)
        mine, other = gather_arrive(full_branch, e_send, e_recv, off)
        out = nt(both_rows(full_branch, mine, other), pj_all[...]).astype(BF)
        for head in range(2):
            cols = slice(head * HEAD, (head + 1) * HEAD)
            for i, b in enumerate((mine, other)):
                part = out[i * TOK : (i + 1) * TOK, cols]
                back_mixed[head, rows(b, TOK), :] = part
                delta[head, b] = row_sums(part.astype(F32) * mixed[head, rows(b, TOK), :])
        return 0

    lax.fori_loop(0, 4, mixed_step, 0)
    pj_grad[...] = tn(mixed_low[...], full_branch[...]).astype(BF)
    gather_finish(full_branch, e_send, e_recv)


def call_middle(mixed_low, mixed, pj_all, gu_all, dn_all, hid, cot, gains):
    return pl.pallas_call(
        middle_kernel,
        name="middle",
        out_shape=(
            jax.ShapeDtypeStruct((TOK, D), F32),
            jax.ShapeDtypeStruct((TOK, D), F32),
            jax.ShapeDtypeStruct((2, HALF, HEAD), BF),
            jax.ShapeDtypeStruct((2, 8, 8, TOK), F32),
            jax.ShapeDtypeStruct((8, D), F32),
            jax.ShapeDtypeStruct((RQ, D), BF),
            jax.ShapeDtypeStruct((D, 2 * RF), BF),
            jax.ShapeDtypeStruct((RF, D), BF),
        ),
        in_specs=[VMEM] * 8,
        out_specs=[VMEM] * 8,
        scratch_shapes=[
            pltpu.VMEM((HALF, D), BF),
            pltpu.VMEM((HALF, D), BF),
            pltpu.VMEM((HALF, D), BF),
            pltpu.VMEM((HALF, 2 * RF), F32),
            pltpu.VMEM((HALF, RF), BF),
            pltpu.VMEM((HALF, 2 * RF), BF),
        ]
        + scatter_scratch() * 3
        + [DMA((7,)), DMA((8,))] * 3,
        compiler_params=pltpu.CompilerParams(
            collective_id=3, has_side_effects=True, vmem_limit_bytes=56 * 2**20
        ),
    )(mixed_low, mixed, pj_all, gu_all, dn_all, hid, cot, gains)


def plane_slot(d, c):
    return lax.div(c, 2) * 8 + d


def attend_back_kernel(
    q_rot, k_rot, v_low, kv_other, back_mixed, lse, delta, start, pj_grad, gu_grad, dn_grad,
    back_q, back_k, back_v, pj_red, gu_red, dn_red,
    other_grad, land, back_other, pj_land, gu_land, dn_land,
    kv_send, kv_recv, p_send, p_recv, g_send, g_recv, d_send, d_recv,
):
    d, c, o = coords()
    half = lax.div(c, 2)
    partner = (d, lax.rem(c + 2, 4), o)
    peers = [plane_peer(d, c, o, t) for t in range(1, 16)]
    greet(peers)

    def cuts(to_d, to_c):
        to_half = lax.div(to_c, 2)
        part, side = lax.div(to_d, 2), lax.rem(to_d, 2)
        pj = pj_grad.at[rows(to_half * 8 + to_d, 16), :]
        dn = dn_grad.at[rows(to_half * 4 + part, 48), rows(side, 512)]
        gu = gu_grad.at[to_half, :, rows(part, 16), rows(side, RF)]
        return pj, gu, dn

    slot = plane_slot(d, c)
    copies = []
    for i, to in enumerate(peers):
        pj, gu, dn = cuts(to[0], to[1])
        for src, dst, send, recv in (
            (pj, pj_land, p_send, p_recv),
            (gu, gu_land, g_send, g_recv),
            (dn, dn_land, d_send, d_recv),
        ):
            copies.append(remote(src, dst.at[slot], send.at[i], recv.at[slot], to))
            copies[-1].start()
    part, side = lax.div(d, 2), lax.rem(d, 2)
    pj_land[slot] = pj_grad[rows(half * 8 + d, 16), :]
    dn_land[slot] = dn_grad[rows(half * 4 + part, 48), rows(side, 512)]
    gu_land[slot] = gu_grad[half, :, rows(part, 16), rows(side, RF)]

    back_q[...] = jnp.zeros_like(back_q)

    def tile(strip, keys, values, key_base, carry):
        grad_k, grad_v = carry
        head, block = lax.div(strip, 4), lax.rem(strip, 4)
        at = rows(block, BLK)
        query, grad_out = q_rot[head, at, :], back_mixed[head, at, :]
        scores = nt(keys, query) * SCALE_TWO
        allowed = tile_mask(key_base, half * HALF + block * BLK, start[0:1, at])
        probs = jnp.where(allowed, jnp.exp2(scores - lse[head, 0:1, at]), 0.0)
        back_prob = nt(values, grad_out)
        back_score = (probs * (back_prob - delta[head, 0:1, at])).astype(BF)
        grad_k = grad_k + nn(back_score, query)
        grad_v = grad_v + nn(probs.astype(BF), grad_out)
        back_q[head, at, :] += tn(back_score, keys)
        return grad_k, grad_v

    zero = (jnp.zeros((BLK, HEAD), F32), jnp.zeros((BLK, HEAD), F32))
    send_back = remote(other_grad, land, kv_send, kv_recv, partner)

    @pl.when(half == 1)
    def _():
        def other_block(j, _):
            at = rows(j, BLK)
            keys, values = kv_other[0, at, :], kv_other[1, at, :]
            grad_k, grad_v = lax.fori_loop(
                0, 8, lambda strip, carry: tile(strip, keys, values, j * BLK, carry), zero
            )
            other_grad[0, at, :] = (grad_k * SCORE_SCALE).astype(BF)
            other_grad[1, at, :] = grad_v.astype(BF)
            return 0

        lax.fori_loop(0, 4, other_block, 0)
        send_back.start()

    def local_block(j, _):
        at = rows(j, BLK)
        keys, values = k_rot[at, :], v_low[at, :]

        def step(i, carry):
            count = 4 - j
            strip = lax.div(i, count) * 4 + j + lax.rem(i, count)
            return tile(strip, keys, values, half * HALF + j * BLK, carry)

        grad_k, grad_v = lax.fori_loop(0, 2 * (4 - j), step, zero)
        back_k[at, :] = grad_k * SCORE_SCALE
        back_v[at, :] = grad_v
        return 0

    lax.fori_loop(0, 4, local_block, 0)
    back_q[...] = back_q[...] * SCORE_SCALE

    @pl.when(half == 1)
    def _():
        send_back.wait_send()

    @pl.when(half == 0)
    def _():
        send_back.wait_recv()
        back_k[...] += land[0].astype(F32)
        back_v[...] += land[1].astype(F32)

    for i, to in enumerate(peers):
        source = plane_slot(to[0], to[1])
        remote(pj_land.at[source], pj_land.at[source], p_send.at[i], p_recv.at[source], to).wait_recv()
        remote(gu_land.at[source], gu_land.at[source], g_send.at[i], g_recv.at[source], to).wait_recv()
        remote(dn_land.at[source], dn_land.at[source], d_send.at[i], d_recv.at[source], to).wait_recv()
    for landed, out in ((pj_land, pj_red), (gu_land, gu_red), (dn_land, dn_red)):
        total = landed[0].astype(F32)
        for i in range(1, 16):
            total = total + landed[i].astype(F32)
        out[...] = total.astype(BF)
    for copy in copies:
        copy.wait_send()


def call_attend_back(q_rot, k_rot, v_low, kv_other, back_mixed, lse, delta, start, pj_grad, gu_grad, dn_grad):
    return pl.pallas_call(
        attend_back_kernel,
        name="attend_back",
        out_shape=(
            jax.ShapeDtypeStruct((2, HALF, HEAD), F32),
            jax.ShapeDtypeStruct((HALF, HEAD), F32),
            jax.ShapeDtypeStruct((HALF, HEAD), F32),
            jax.ShapeDtypeStruct((16, D), BF),
            jax.ShapeDtypeStruct((8, 16, RF), BF),
            jax.ShapeDtypeStruct((48, 512), BF),
        ),
        in_specs=[VMEM] * 11,
        out_specs=[VMEM] * 6,
        scratch_shapes=[
            pltpu.VMEM((2, HALF, HEAD), BF),
            pltpu.VMEM((2, HALF, HEAD), BF),
            pltpu.VMEM((8, 128), F32),
            pltpu.VMEM((16, 16, D), BF),
            pltpu.VMEM((16, 8, 16, RF), BF),
            pltpu.VMEM((16, 48, 512), BF),
            DMA,
            DMA,
        ]
        + [DMA((15,)), DMA((16,))] * 3,
        compiler_params=pltpu.CompilerParams(
            collective_id=4, has_side_effects=True, vmem_limit_bytes=56 * 2**20
        ),
    )(q_rot, k_rot, v_low, kv_other, back_mixed, lse, delta, start, pj_grad, gu_grad, dn_grad)


def last_kernel(
    back_q, back_k, back_v, unit, scales, gains, gain_rest, cos, sin, w_all, hid_all, pj_red, gu_red, dn_red,
    input_part, qkv_sum, gu_sum, pj_sum, dn_sum, gain_sum,
    raw, back_qkv, sums, sums_land, qkv_grad, qkv_land, qkv_red, gain_vec, gain_land, gain_mid, gain_last,
    qkv_own, gu_own, pj_own, dn_own,
    *scratch,
):
    d, c, o = coords()
    half, core = lax.div(c, 2), lax.rem(c, 2)
    rank = core * 4 + o
    place = c * 4 + o
    part, side = lax.div(d, 2), lax.rem(d, 2)
    sib = (d, sibling(c), o)
    s = dict(zip(SCATTER_NAMES, scratch[0:9]))
    (
        s_send, s_recv, q_send, q_recv, v_send, v_recv, w_send, w_recv,
        a_send, a_recv, b_send, b_recv, m_send, m_recv, y_send, y_recv,
    ) = scratch[9:25]
    ranks = [rank_peer(d, c, o, t) for t in range(1, 8)]
    planes = [plane_peer(d, c, o, t) for t in range(1, 16)]
    owners = [dp_peer(d, c, o, t) for t in range(1, 8)]
    greet([group_peer(d, c, o, t) for t in range(1, 16)] + planes)
    done = []

    def launch(copy):
        copy.start()
        done.append(copy)

    target = 2 * rank + half
    to_owner = (d, lax.div(target, 4), lax.rem(target, 4))
    stay = target == place
    pj_move = remote(pj_red, pj_own, m_send.at[0], m_recv.at[0], to_owner)
    dn_move = remote(dn_red, dn_own, m_send.at[1], m_recv.at[1], to_owner)

    @pl.when(stay)
    def _():
        pj_own[...] = pj_red[...]
        dn_own[...] = dn_red[...]

    @pl.when(jnp.logical_not(stay))
    def _():
        pj_move.start()
        dn_move.start()

    gu_cols = rows(rank, RF)
    for i, to in enumerate(ranks):
        to_rank = lax.rem(to[1], 2) * 4 + to[2]
        launch(remote(gu_red.at[to_rank], gu_own.at[:, gu_cols], a_send.at[i], a_recv.at[rank], to))
    gu_own[:, gu_cols] = gu_red[rank]

    def weigh(b, _):
        at = rows(b, TOK)
        cosine, sine = cos[at, :], sin[at, :]
        totals = []
        for head in range(2):
            cols = slice(head * HEAD, (head + 1) * HEAD)
            grad = unrope(back_q[head, at, :], cosine, sine)
            raw[at, cols] = grad
            totals.append(grad * gains[0:1, cols] * unit[at, cols])
        cols = slice(RQ, RQ + RK)
        grad = unrope(back_k[at, :], cosine, sine)
        raw[at, cols] = grad
        q_sum = row_sums(totals[0] + totals[1])
        k_sum = row_sums(grad * gains[0:1, cols] * unit[at, cols])
        upper = lax.broadcasted_iota(jnp.int32, (8, TOK), 0) < 4
        sums[b] = jnp.where(upper, q_sum, k_sum)
        return 0

    lax.fori_loop(0, RANKS, weigh, 0)
    gain_vec[...] = jnp.zeros_like(gain_vec)
    gain_own = jnp.sum(raw[...] * unit[...], axis=0, keepdims=True)
    gain_vec[0:1, rows(rank, RQ)] = gain_own[:, 0:RQ]
    gain_vec[1:2, rows(rank, RK)] = gain_own[:, RQ:]
    gain_vec[2:4, 0:D] = gain_rest[0:2, :]
    vec_slot = plane_slot(d, c)
    for i, to in enumerate(planes):
        launch(remote(gain_vec, gain_land.at[vec_slot], v_send.at[i], v_recv.at[vec_slot], to))
    gain_land[vec_slot] = gain_vec[...]

    total = sum_exchange(sums, sums_land, s_send, s_recv)
    upper = lax.broadcasted_iota(jnp.int32, (8, 8, TOK), 1) < 4
    sums[...] = jnp.where(upper, total * (1.0 / QW), total * (1.0 / KW))

    def back_norm(b, _):
        at = rows(b, TOK)
        scale, mean = scales[b], sums[b]
        q_scale, k_scale = column(scale[0:1]), column(scale[4:5])
        q_mean, k_mean = column(mean[0:1]), column(mean[4:5])
        for head in range(2):
            cols = slice(head * HEAD, (head + 1) * HEAD)
            weighted = raw[at, cols] * gains[0:1, cols]
            back_qkv[at, cols] = (q_scale * (weighted - unit[at, cols] * q_mean)).astype(BF)
        cols = slice(RQ, RQ + RK)
        weighted = raw[at, cols] * gains[0:1, cols]
        back_qkv[at, cols] = (k_scale * (weighted - unit[at, cols] * k_mean)).astype(BF)
        back_qkv[at, RQ + RK : RC] = back_v[at, :].astype(BF)
        return 0

    lax.fori_loop(0, RANKS, back_norm, 0)

    def grad_step(b, _):
        q_block = lax.dot_general(
            hid_all[:, rows(b, 128)], back_qkv[...], (((0,), (0,)), ((), ())), preferred_element_type=F32
        )
        qkv_grad[lax.div(b, 4), rows(lax.rem(b, 4), 2)] = q_block.astype(BF).reshape(2, 64, RC)
        return 0

    lax.fori_loop(0, 8, grad_step, 0)
    slot = plane_slot(d, c)
    for i, to in enumerate(planes):
        src = qkv_grad.at[lax.div(to[1], 2), :, rows(lax.div(to[0], 2), 16), rows(lax.rem(to[0], 2), RQ)]
        launch(remote(src, qkv_land.at[slot], q_send.at[i], q_recv.at[slot], to))
    qkv_land[slot] = qkv_grad[half, :, rows(part, 16), rows(side, RQ)]

    def input_step(step, _):
        off = lax.rem(step + 1, 4)
        at = lax.rem(o + off, 4)
        mine, other = core * 4 + at, (1 - core) * 4 + at
        both = jnp.concatenate([back_qkv[rows(mine, TOK), :], back_qkv[rows(other, TOK), :]], axis=0)
        both = nt(both, w_all[...])
        scatter_sibling(off, both[TOK:], s)
        s["own"][off] = both[0:TOK]

        @pl.when(step > 0)
        def _():
            scatter_along(step, s)

        return 0

    lax.fori_loop(0, 4, input_step, 0)
    scatter_along(0, s)

    @pl.when(jnp.logical_not(stay))
    def _():
        pj_move.wait_send()
        dn_move.wait_send()
        pj_move.wait_recv()
        dn_move.wait_recv()

    for i, to in enumerate(ranks):
        from_rank = lax.rem(to[1], 2) * 4 + to[2]
        remote(gu_red.at[0], gu_own.at[:, rows(from_rank, RF)], a_send.at[i], a_recv.at[from_rank], sib).wait_recv()
    pj_at = pj_sum.at[rows(d, 16), :]
    dn_at = dn_sum.at[rows(part, 48), rows(side, 512)]
    gu_at = gu_sum.at[rows(part, 16), rows(side, FF)]
    for i, to in enumerate(owners):
        launch(remote(pj_own, pj_at, y_send.at[0, i], y_recv.at[0, d], to))
        launch(remote(dn_own, dn_at, y_send.at[1, i], y_recv.at[1, d], to))
        launch(remote(gu_own, gu_at, y_send.at[2, i], y_recv.at[2, d], to))
    pj_sum[rows(d, 16), :] = pj_own[...]
    dn_sum[rows(part, 48), rows(side, 512)] = dn_own[...]
    gu_sum[rows(part, 16), rows(side, FF)] = gu_own[...]

    for i, to in enumerate(planes):
        source = plane_slot(to[0], to[1])
        remote(gain_vec, gain_land.at[source], v_send.at[i], v_recv.at[source], sib).wait_recv()
    total = gain_land[0]
    for i in range(1, 16):
        total = total + gain_land[i]
    gain_mid[...] = total
    for i, to in enumerate(ranks):
        launch(remote(gain_mid, gain_last.at[rank], w_send.at[i], w_recv.at[rank], to))
    gain_last[rank] = total

    for i, to in enumerate(planes):
        source = plane_slot(to[0], to[1])
        remote(qkv_land.at[source], qkv_land.at[source], q_send.at[i], q_recv.at[source], sib).wait_recv()
    total = qkv_land[0].astype(F32)
    for i in range(1, 16):
        total = total + qkv_land[i].astype(F32)
    qkv_red[...] = total.astype(BF)

    def qkv_cols(of_rank, i):
        col = (1 - side) * (of_rank * 2 + i) + side * (of_rank + i * 8)
        return rows(col, RK)

    for i, to in enumerate(ranks):
        to_rank = lax.rem(to[1], 2) * 4 + to[2]
        for j in range(2):
            launch(
                remote(
                    qkv_red.at[to_rank, :, pl.ds(j * RK, RK)],
                    qkv_own.at[:, qkv_cols(rank, j)],
                    b_send.at[j, i],
                    b_recv.at[j, rank],
                    to,
                )
            )
    for j in range(2):
        qkv_own[:, qkv_cols(rank, j)] = qkv_red[rank][:, j * RK : (j + 1) * RK]

    input_part[...] = scatter_result(s)
    for i, to in enumerate(ranks):
        from_rank = lax.rem(to[1], 2) * 4 + to[2]
        remote(gain_mid, gain_last.at[from_rank], w_send.at[i], w_recv.at[from_rank], sib).wait_recv()
    total = gain_last[0]
    for i in range(1, 8):
        total = total + gain_last[i]
    gain_sum[...] = total

    for i, to in enumerate(ranks):
        from_rank = lax.rem(to[1], 2) * 4 + to[2]
        for j in range(2):
            remote(
                qkv_red.at[0, :, pl.ds(j * RK, RK)],
                qkv_own.at[:, qkv_cols(from_rank, j)],
                b_send.at[j, i],
                b_recv.at[j, from_rank],
                sib,
            ).wait_recv()
    qkv_at = qkv_sum.at[rows(part, 16), rows(side, QW)]
    for i, to in enumerate(owners):
        launch(remote(qkv_own, qkv_at, y_send.at[3, i], y_recv.at[3, d], to))
    qkv_sum[rows(part, 16), rows(side, QW)] = qkv_own[...]
    for i, to in enumerate(owners):
        e = to[0]
        e_part, e_side = lax.div(e, 2), lax.rem(e, 2)
        for n, (own, dst) in enumerate((
            (pj_own, pj_sum.at[rows(e, 16), :]),
            (dn_own, dn_sum.at[rows(e_part, 48), rows(e_side, 512)]),
            (gu_own, gu_sum.at[rows(e_part, 16), rows(e_side, FF)]),
            (qkv_own, qkv_sum.at[rows(e_part, 16), rows(e_side, QW)]),
        )):
            remote(own, dst, y_send.at[n, i], y_recv.at[n, e], sib).wait_recv()
    scatter_finish(s)
    for copy in done:
        copy.wait_send()


def call_last(back_q, back_k, back_v, unit, scales, gains, gain_rest, cos, sin, w_all, hid_all, pj_red, gu_red, dn_red):
    return pl.pallas_call(
        last_kernel,
        name="last",
        out_shape=(
            jax.ShapeDtypeStruct((TOK, D), F32),
            jax.ShapeDtypeStruct((64, QW + 2 * KW), BF),
            jax.ShapeDtypeStruct((64, 2 * FF), BF),
            jax.ShapeDtypeStruct((128, D), BF),
            jax.ShapeDtypeStruct((192, D), BF),
            jax.ShapeDtypeStruct((8, QW), F32),
        ),
        in_specs=[VMEM] * 14,
        out_specs=[VMEM] * 6,
        scratch_shapes=[
            pltpu.VMEM((HALF, RQ + RK), F32),
            pltpu.VMEM((HALF, RC), BF),
            pltpu.VMEM((8, 8, TOK), F32),
            pltpu.VMEM((8, 8, 8, TOK), F32),
            pltpu.VMEM((2, 8, 64, RC), BF),
            pltpu.VMEM((16, 8, 16, RQ), BF),
            pltpu.VMEM((8, 16, RQ), BF),
            pltpu.VMEM((8, QW), F32),
            pltpu.VMEM((16, 8, QW), F32),
            pltpu.VMEM((8, QW), F32),
            pltpu.VMEM((8, 8, QW), F32),
            pltpu.VMEM((16, QW), BF),
            pltpu.VMEM((16, FF), BF),
            pltpu.VMEM((16, D), BF),
            pltpu.VMEM((48, 512), BF),
        ]
        + scatter_scratch()
        + [
            DMA((8,)), DMA((8,)),
            DMA((15,)), DMA((16,)),
            DMA((15,)), DMA((16,)),
            DMA((7,)), DMA((8,)),
            DMA((7,)), DMA((8,)),
            DMA((2, 7)), DMA((2, 8)),
            DMA((2,)), DMA((2,)),
            DMA((4, 7)), DMA((4, 8)),
        ],
        compiler_params=pltpu.CompilerParams(
            collective_id=5, has_side_effects=True, vmem_limit_bytes=56 * 2**20
        ),
    )(back_q, back_k, back_v, unit, scales, gains, gain_rest, cos, sin, w_all, hid_all, pj_red, gu_red, dn_red)


def doc_positions(seq_segments):
    row_index = jnp.arange(seq_segments.shape[0], dtype=jnp.int32)
    new_doc = jnp.concatenate([jnp.ones((1,), dtype=bool), seq_segments[1:] != seq_segments[:-1]])
    starts = lax.cummax(jnp.where(new_doc, row_index, 0), axis=0)
    return row_index - starts


def adam_step(weight, moment, square, grad_sum, rate, decay):
    moment_new = BETA_ONE * moment + (1.0 - BETA_ONE) * grad_sum
    square_new = BETA_TWO * square + (1.0 - BETA_TWO) * grad_sum * grad_sum
    moment_hat = moment_new / (1.0 - BETA_ONE**STEP)
    square_hat = square_new / (1.0 - BETA_TWO**STEP)
    weight_new = weight - rate * (moment_hat / (jnp.sqrt(square_hat) + ADAM_EPS) + decay * weight)
    return (weight_new, moment_new, square_new)


def per_device(
    hidden_in,
    segment_ids,
    out_cotangent,
    qkv_weight,
    qkv_moment,
    qkv_square,
    proj_weight,
    proj_moment,
    proj_square,
    gate_up_weight,
    gate_up_moment,
    gate_up_square,
    down_weight,
    down_moment,
    down_square,
    gains,
    gain_moment,
    gain_square,
):
    _, c, o = coords()
    half = c // 2
    place = c * 4 + o
    positions = lax.dynamic_slice_in_dim(doc_positions(segment_ids[0]), half * HALF, HALF)
    start = half * HALF + jnp.arange(HALF, dtype=jnp.int32) - positions
    start = jnp.broadcast_to(start[None, :], (8, HALF))
    frequency = jnp.exp(jnp.arange(HEAD // 2, dtype=F32) * (-math.log(THETA) / (HEAD // 2)))
    angles = positions.astype(F32)[:, None] * frequency[None, :]
    cosine, sine = jnp.cos(angles), jnp.sin(angles)
    cos = jnp.concatenate([cosine, cosine], axis=1)
    sin = jnp.concatenate([-sine, sine], axis=1)

    placed = lax.dynamic_update_slice_in_dim(
        jnp.zeros((QW + KW + 2 * D,), F32), gains.astype(BF).astype(F32), place * gains.shape[0], axis=0
    )
    query_part = placed[:QW].reshape(RANKS, 1, RQ)
    key_part = placed[QW : QW + KW].reshape(RANKS, 1, RK)
    rest = jnp.broadcast_to(placed[QW + KW :].reshape(1, 4, 512), (RANKS, 4, 512))
    gain_parts = jnp.concatenate(
        [
            jnp.concatenate([query_part, key_part, jnp.zeros((RANKS, 1, 128), F32)], axis=2),
            rest,
            jnp.zeros((RANKS, 3, 512), F32),
        ],
        axis=1,
    )

    hid_all, w_all, gain_all, q_rot, k_rot, v_low, unit, scales = call_first(
        hidden_in, qkv_weight, gain_parts, cos, sin
    )
    kv_other, mixed, mixed_low, lse, gu_all, pj_all, dn_all = call_attend(
        q_rot, k_rot, v_low, start, gate_up_weight, proj_weight, down_weight
    )
    layer_out, back_resid, back_mixed, delta, gain_rest, pj_grad, gu_grad, dn_grad = call_middle(
        mixed_low, mixed, pj_all, gu_all, dn_all, hidden_in, out_cotangent, gain_all
    )
    delta_rows = jnp.transpose(delta, (0, 2, 1, 3)).reshape(2, 8, HALF)
    back_q, back_k, back_v, pj_red, gu_red, dn_red = call_attend_back(
        q_rot, k_rot, v_low, kv_other, back_mixed, lse, delta_rows, start,
        pj_grad, gu_grad.reshape(2, 8, 64, 2 * RF), dn_grad,
    )
    input_part, qkv_sum, gu_sum, pj_sum, dn_sum, gain_sum = call_last(
        back_q, back_k, back_v, unit, scales, gain_all, gain_rest, cos, sin, w_all, hid_all,
        pj_red, gu_red, dn_red,
    )
    gain_grad = jnp.concatenate([gain_sum[0], gain_sum[1, :KW], gain_sum[2, :D], gain_sum[3, :D]])
    gain_grad = lax.dynamic_slice_in_dim(gain_grad, place * gains.shape[0], gains.shape[0])
    return (
        (layer_out.astype(BF), back_resid + input_part)
        + adam_step(qkv_weight, qkv_moment, qkv_square, qkv_sum.astype(F32), RATE_MATRIX, DECAY)
        + adam_step(proj_weight, proj_moment, proj_square, pj_sum.astype(F32), RATE_MATRIX, DECAY)
        + adam_step(gate_up_weight, gate_up_moment, gate_up_square, gu_sum.astype(F32), RATE_MATRIX, DECAY)
        + adam_step(down_weight, down_moment, down_square, dn_sum.astype(F32), RATE_MATRIX, DECAY)
        + adam_step(gains, gain_moment, gain_square, gain_grad, RATE_GAIN, 0.0)
    )


def solution(mesh):
    seq = P(("dp", "ctx", "opt"), None)
    mat = P(("ctx", "opt"), None)
    vec = P(("ctx", "opt"))
    return jax.shard_map(
        per_device,
        mesh=mesh,
        in_specs=(seq, P("dp", None), seq) + (mat,) * 12 + (vec,) * 3,
        out_specs=(seq, seq) + (mat,) * 12 + (vec,) * 3,
        check_vma=False,
    )
```

```python
import math
import types

import jax
import jax.numpy as jnp
from jax import lax
from jax.experimental import pallas as pl
from jax.experimental.pallas import tpu as pltpu
from jax.sharding import PartitionSpec as P

D = 1024
FF = 3072
HEADS = 16
KV_HEADS = 8
HEAD = 128
STEP = 10

NORM_EPS = 1e-06
THETA = 500000.0
MASKED = -1e30
BETA_ONE = 0.9
BETA_TWO = 0.95
ADAM_EPS = 1e-08
RATE_MATRIX = 0.06
RATE_GAIN = 1.0
DECAY = 0.1

TOK = 128
HALF = 1024
RANKS = 8
QW = HEADS * HEAD
KW = KV_HEADS * HEAD
RQ = 256
RK = 128
RC = RQ + 2 * RK
RF = FF // RANKS
BLK = 256
SCORE_SCALE = 1.0 / math.sqrt(HEAD)
SCALE_TWO = SCORE_SCALE * math.log2(math.e)

MESH = pl.DeviceIdType.MESH
BF = jnp.bfloat16
F32 = jnp.float32
VMEM = pl.BlockSpec(memory_space=pltpu.VMEM)
DMA = pltpu.SemaphoreType.DMA


def coords():
    return lax.axis_index("dp"), lax.axis_index("ctx"), lax.axis_index("opt")


def sibling(c):
    return c + 1 - 2 * lax.rem(c, 2)


def rank_peer(d, c, o, t):
    flip = t // 4
    return (d, c + (1 - 2 * lax.rem(c, 2)) * flip, lax.rem(o + t % 4, 4))


def cross_peer(d, c, o, t):
    return rank_peer(d + 1 - 2 * lax.rem(d, 2), lax.rem(c + 2, 4), o, t)


def plane_peer(d, c, o, t):
    x_lo, y = lax.rem(d, 2), lax.div(d, 2)
    y = lax.rem(y + t // 4, 4)
    x_lo = x_lo + (1 - 2 * x_lo) * (t % 2)
    return (2 * y + x_lo, lax.rem(c + 2 * ((t % 4) // 2), 4), o)


def group_peer(d, c, o, t):
    return (d, lax.rem(c + t // 4, 4), lax.rem(o + t % 4, 4))


def dp_peer(d, c, o, t):
    return (lax.rem(d + t, 8), c, o)


def greet(peers):
    barrier = pltpu.get_barrier_semaphore()
    for to in peers:
        pl.semaphore_signal(barrier, inc=1, device_id=to, device_id_type=MESH)
    pl.semaphore_wait(barrier, len(peers))


def remote(src, dst, send, recv, to):
    return pltpu.make_async_remote_copy(
        src_ref=src, dst_ref=dst, send_sem=send, recv_sem=recv, device_id=to, device_id_type=MESH
    )


def rows(index, count):
    return pl.ds(pl.multiple_of(index * count, count), count)


def nn(a, b):
    return lax.dot_general(a, b, (((1,), (0,)), ((), ())), preferred_element_type=F32)


def nt(a, b):
    return lax.dot_general(a, b, (((1,), (1,)), ((), ())), preferred_element_type=F32)


def tn(a, b):
    return lax.dot_general(a, b, (((0,), (0,)), ((), ())), preferred_element_type=F32)


def row_sums(values):
    ones = jnp.ones((8, values.shape[1]), F32)
    return lax.dot_general(
        ones,
        values,
        (((1,), (1,)), ((), ())),
        precision=lax.Precision.HIGHEST,
        preferred_element_type=F32,
    )


def column(row):
    return jnp.transpose(jnp.broadcast_to(row, (128, 128)))


def rms_scale(values):
    return lax.rsqrt(jnp.mean(values * values, axis=-1, keepdims=True) + NORM_EPS)


def norm_back(grad_rows, unit_rows, scale_rows, gain_row):
    weighted = grad_rows * gain_row
    return scale_rows * (
        weighted - unit_rows * jnp.mean(weighted * unit_rows, axis=-1, keepdims=True)
    )


def rope(u, cos, sin):
    return u * cos + pltpu.roll(u, HEAD // 2, 1) * sin


def unrope(g, cos, sin):
    return g * cos - pltpu.roll(g, HEAD // 2, 1) * sin


def gather_start(full, send, recv):
    d, c, o = coords()
    rank = lax.rem(c, 2) * 4 + o
    own = full.at[rows(rank, TOK)]
    for t in (1, 3, 2):
        remote(own, own, send.at[t], recv.at[rank], (d, c, lax.rem(o + t, 4))).start()
    remote(own, own, send.at[0], recv.at[rank], (d, sibling(c), o)).start()


def gather_arrive(full, send, recv, off):
    d, c, o = coords()
    core = lax.rem(c, 2)
    at = lax.rem(o + off, 4)
    mine, other = core * 4 + at, (1 - core) * 4 + at
    to = (d, sibling(c), o)
    block = full.at[rows(mine, TOK)]

    @pl.when(off > 0)
    def _():
        remote(block, block, send.at[0], recv.at[mine], to).wait_recv()
        remote(block, block, send.at[3 + off], recv.at[mine], to).start()

    block = full.at[rows(other, TOK)]
    remote(block, block, send.at[0], recv.at[other], to).wait_recv()
    return mine, other


def gather_finish(full, send, recv):
    d, c, o = coords()
    own = full.at[rows(0, TOK)]
    for i in range(7):
        remote(own, own, send.at[i], recv.at[0], (d, sibling(c), o)).wait_send()


class Scatter:
    def __init__(self, r, index):
        self.stage_s, self.stage_z, self.own = r.stage_s, r.stage_z, r.own
        self.land_s, self.land_z = r.land_s.at[index % 2], r.land_z.at[index % 2]
        self.send_s, self.recv_s = r.send_s.at[index], r.recv_s.at[index]
        self.send_z, self.recv_z = r.send_z.at[index], r.recv_z.at[index]

    def near(self, off):
        d, c, o = coords()
        return remote(
            self.stage_s.at[off], self.land_s.at[off], self.send_s.at[off], self.recv_s.at[off], (d, sibling(c), o)
        )

    def along(self, off):
        d, c, o = coords()
        return remote(
            self.stage_z.at[off - 1],
            self.land_z.at[off - 1],
            self.send_z.at[off],
            self.recv_z.at[off],
            (d, c, lax.rem(o + off, 4)),
        )

    def give(self, off, part):
        self.stage_s[off] = part[TOK:].astype(BF)
        self.near(off).start()
        self.own[off] = part[0:TOK]

    def send(self, off):
        self.near(off).wait_recv()
        total = self.own[off] + self.land_s[off].astype(F32)

        @pl.when(off > 0)
        def _():
            self.stage_z[off - 1] = total.astype(BF)
            self.along(off).start()

        @pl.when(off == 0)
        def _():
            self.own[0] = total

    def result(self):
        total = self.own[0]
        for off in (1, 3, 2):
            self.along(off).wait_recv()
            total = total + self.land_z[off - 1].astype(F32)
        return total

    def finish(self):
        for off in range(4):
            self.near(off).wait_send()
        for off in range(1, 4):
            self.along(off).wait_send()


def order(step):
    return step + lax.div(step, 2) - 2 * lax.div(step, 3)


class SumExchange:
    def __init__(self, sums, land, send, recv):
        self.sums, self.land, self.send, self.recv = sums, land, send, recv

    def start(self):
        d, c, o = coords()
        rank = lax.rem(c, 2) * 4 + o
        self.land[rank] = self.sums[...]
        self.copies = []
        for t in range(1, 8):
            copy = remote(
                self.sums, self.land.at[rank], self.send.at[t], self.recv.at[rank], rank_peer(d, c, o, t)
            )
            copy.start()
            self.copies.append(copy)

    def total(self):
        d, c, o = coords()
        for t in range(1, 8):
            _, c1, o1 = rank_peer(d, c, o, t)
            source = lax.rem(c1, 2) * 4 + o1
            remote(
                self.sums, self.land.at[source], self.send.at[t], self.recv.at[source], (d, sibling(c), o)
            ).wait_recv()
        for copy in self.copies:
            copy.wait_send()
        total = self.land[0]
        for i in range(1, 8):
            total = total + self.land[i]
        return total


def plane_slot(d, c):
    return lax.div(c, 2) * 8 + d


def token_block(ref, b, head):
    at = pl.multiple_of(head * BLK + lax.rem(b, 2) * TOK, TOK)
    return lax.div(b, 2), pl.ds(at, TOK)


SCRATCH = dict(
    pieces=pltpu.VMEM((RANKS, 64, RC), BF),
    w_all=pltpu.VMEM((D, RC), BF),
    gu_raw=pltpu.VMEM((64, 2 * FF), F32),
    pj_raw=pltpu.VMEM((128, D), F32),
    dn_raw=pltpu.VMEM((192, D), F32),
    gu_pieces=pltpu.VMEM((RANKS, 64, 2 * RF), BF),
    pj_mine=pltpu.VMEM((128, D), BF),
    dn_mine=pltpu.VMEM((192, D), BF),
    gu_all=pltpu.VMEM((D, 2 * RF), BF),
    pj_all=pltpu.VMEM((RQ, D), BF),
    dn_all=pltpu.VMEM((RF, D), BF),
    gain_parts_land=pltpu.VMEM((16, 8, 512), F32),
    gains=pltpu.VMEM((8, 512), F32),
    hid_all=pltpu.VMEM((HALF, D), BF),
    unit=pltpu.VMEM((HALF, RQ + RK), F32),
    sums=pltpu.VMEM((8, 8, TOK), F32),
    sums_land=pltpu.VMEM((8, 8, 8, TOK), F32),
    sums_back=pltpu.VMEM((8, 8, TOK), F32),
    sums_back_land=pltpu.VMEM((8, 8, 8, TOK), F32),
    scales=pltpu.VMEM((8, 8, TOK), F32),
    q_rot=pltpu.VMEM((4, 2 * BLK, HEAD), BF),
    kv_own=pltpu.VMEM((2, HALF, HEAD), BF),
    kv_other=pltpu.VMEM((2, HALF, HEAD), BF),
    v_t=pltpu.VMEM((2, HEAD, HALF), BF),
    top=pltpu.VMEM((4, 8, 2 * BLK), F32),
    running=pltpu.VMEM((4, 8, 2 * BLK), F32),
    accum=pltpu.VMEM((4, HEAD, 2 * BLK), F32),
    mixed=pltpu.VMEM((4, 2 * BLK, HEAD), F32),
    mixed_low=pltpu.VMEM((HALF, RQ), BF),
    lse=pltpu.VMEM((4, 8, 2 * BLK), F32),
    delta=pltpu.VMEM((4, 8, 2 * BLK), F32),
    full_res=pltpu.VMEM((HALF, D), BF),
    full_ffn=pltpu.VMEM((HALF, D), BF),
    full_branch=pltpu.VMEM((HALF, D), BF),
    wide=pltpu.VMEM((HALF, 2 * RF), F32),
    act=pltpu.VMEM((HALF, RF), BF),
    back_gu=pltpu.VMEM((HALF, 2 * RF), BF),
    stage_s=pltpu.VMEM((4, TOK, D), BF),
    stage_z=pltpu.VMEM((3, TOK, D), BF),
    own=pltpu.VMEM((4, TOK, D), F32),
    land_s=pltpu.VMEM((2, 4, TOK, D), BF),
    land_z=pltpu.VMEM((2, 3, TOK, D), BF),
    gain_rest=pltpu.VMEM((4, 512), F32),
    back_mixed=pltpu.VMEM((4, 2 * BLK, HEAD), BF),
    back_q=pltpu.VMEM((4, 2 * BLK, HEAD), F32),
    back_k=pltpu.VMEM((HALF, HEAD), F32),
    back_v=pltpu.VMEM((HALF, HEAD), F32),
    other_grad=pltpu.VMEM((2, HALF, HEAD), BF),
    other_land=pltpu.VMEM((2, HALF, HEAD), BF),
    back_qkv=pltpu.VMEM((HALF, RC), BF),
    pj_grad=pltpu.VMEM((RQ, D), BF),
    gu_grad=pltpu.VMEM((2, 8, 64, 2 * RF), BF),
    dn_grad=pltpu.VMEM((RF, D), BF),
    qkv_grad=pltpu.VMEM((2, 8, 64, RC), BF),
    pj_land=pltpu.VMEM((16, 16, D), BF),
    gu_land=pltpu.VMEM((16, 8, 16, RF), BF),
    dn_land=pltpu.VMEM((16, 48, 512), BF),
    qkv_land=pltpu.VMEM((16, 8, 16, RQ), BF),
    pj_red=pltpu.VMEM((16, D), BF),
    gu_red=pltpu.VMEM((8, 16, RF), BF),
    dn_red=pltpu.VMEM((48, 512), BF),
    qkv_red=pltpu.VMEM((8, 16, RQ), BF),
    pj_own=pltpu.VMEM((16, D), BF),
    gu_own=pltpu.VMEM((16, FF), BF),
    dn_own=pltpu.VMEM((48, 512), BF),
    qkv_own=pltpu.VMEM((16, QW), BF),
    gain_vec=pltpu.VMEM((16, 512), F32),
    gain_land=pltpu.VMEM((16, 16, 512), F32),
    gain_mid=pltpu.VMEM((16, 512), F32),
    gain_last=pltpu.VMEM((8, 16, 512), F32),
    raw_sem=DMA((3,)),
    h_send=DMA((7,)),
    h_recv=DMA((8,)),
    w_send=DMA((15,)),
    w_recv=DMA((16,)),
    gp_send=DMA((15,)),
    gp_recv=DMA((16,)),
    sum_send=DMA((8,)),
    sum_recv=DMA((8,)),
    sumb_send=DMA((8,)),
    sumb_recv=DMA((8,)),
    kv_send=DMA,
    kv_recv=DMA,
    gu_send=DMA((15,)),
    gu_recv=DMA((16,)),
    pj_send=DMA((2,)),
    pj_recv=DMA((2,)),
    dn_send=DMA((2,)),
    dn_recv=DMA((2,)),
    send_s=DMA((4, 4)),
    recv_s=DMA((4, 4)),
    send_z=DMA((4, 4)),
    recv_z=DMA((4, 4)),
    a_send=DMA((7,)),
    a_recv=DMA((8,)),
    b_send=DMA((7,)),
    b_recv=DMA((8,)),
    e_send=DMA((7,)),
    e_recv=DMA((8,)),
    kvb_send=DMA,
    kvb_recv=DMA,
    plane_send=DMA((5, 15)),
    plane_recv=DMA((5, 16)),
    move_send=DMA((2,)),
    move_recv=DMA((2,)),
    gur_send=DMA((7,)),
    gur_recv=DMA((8,)),
    qr_send=DMA((2, 7)),
    qr_recv=DMA((2, 8)),
    gl_send=DMA((7,)),
    gl_recv=DMA((8,)),
    y_send=DMA((4, 7)),
    y_recv=DMA((4, 8)),
)


def layer_kernel(hid, cot, w_rows, gu_rows, pj_rows, dn_rows, gain_parts, cos, sin, start, *refs):
    layer_out, back_resid, input_part, qkv_sum, gu_sum, pj_sum, dn_sum, gain_sum = refs[:8]
    r = types.SimpleNamespace(**dict(zip(SCRATCH, refs[8:])))
    d, c, o = coords()
    half, core = lax.div(c, 2), lax.rem(c, 2)
    rank = core * 4 + o
    place = c * 4 + o
    part, side = lax.div(d, 2), lax.rem(d, 2)
    sib = (d, sibling(c), o)
    partner = (d, lax.rem(c + 2, 4), o)
    ranks = [rank_peer(d, c, o, t) for t in range(1, 8)]
    sources = ranks + [cross_peer(d, c, o, t) for t in range(8)]
    planes = [plane_peer(d, c, o, t) for t in range(1, 16)]
    owners = [dp_peer(d, c, o, t) for t in range(1, 8)]
    group = [group_peer(d, c, o, t) for t in range(1, 16)]
    crosses = [cross_peer(d, c, o, t) for t in range(8)]
    done = []

    def launch(copy):
        copy.start()
        done.append(copy)

    def rank_of(to):
        return lax.rem(to[1], 2) * 4 + to[2]

    raws = [
        pltpu.make_async_copy(src, dst, r.raw_sem.at[i])
        for i, (src, dst) in enumerate(((gu_rows, r.gu_raw), (pj_rows, r.pj_raw), (dn_rows, r.dn_raw)))
    ]
    for copy in raws:
        copy.start()
    r.hid_all[rows(rank, TOK), :] = hid[...]
    for g in range(RANKS):
        r.pieces[g, :, 0:RQ] = w_rows[:, g * RQ : (g + 1) * RQ].astype(BF)
        r.pieces[g, :, RQ : RQ + RK] = w_rows[:, QW + g * RK : QW + (g + 1) * RK].astype(BF)
        r.pieces[g, :, RQ + RK : RC] = w_rows[:, QW + KW + g * RK : QW + KW + (g + 1) * RK].astype(BF)
    greet(group + planes + crosses)

    gather_start(r.hid_all, r.h_send, r.h_recv)
    mine = r.w_all.at[rows(place, 64)]
    for i, to in enumerate(sources):
        launch(remote(r.pieces.at[rank_of(to)], mine, r.w_send.at[i], r.w_recv.at[place], to))
    for i, to in enumerate(sources):
        launch(
            remote(
                gain_parts.at[rank_of(to)], r.gain_parts_land.at[place], r.gp_send.at[i], r.gp_recv.at[place], to
            )
        )
    r.w_all[rows(place, 64), :] = r.pieces[rank]
    r.gain_parts_land[place] = gain_parts[rank]

    for copy in raws:
        copy.wait()
    for g in range(RANKS):
        r.gu_pieces[g, :, 0:RF] = r.gu_raw[:, g * RF : (g + 1) * RF].astype(BF)
        r.gu_pieces[g, :, RF:] = r.gu_raw[:, FF + g * RF : FF + (g + 1) * RF].astype(BF)
    r.pj_mine[...] = r.pj_raw[...].astype(BF)
    r.dn_mine[...] = r.dn_raw[...].astype(BF)

    for i, to in enumerate(sources):
        source = to[1] * 4 + to[2]
        remote(r.pieces.at[0], r.w_all.at[rows(source, 64)], r.w_send.at[i], r.w_recv.at[source], to).wait_recv()

    def project(step, _):
        off = order(step)
        mine, other = gather_arrive(r.hid_all, r.h_send, r.h_recv, off)
        both = jnp.concatenate([r.hid_all[rows(mine, TOK), :], r.hid_all[rows(other, TOK), :]], axis=0)
        out = nn(both, r.w_all[...])
        squares = out * out
        q_sum, k_sum = row_sums(squares[:, 0:RQ]), row_sums(squares[:, RQ : RQ + RK])
        upper = lax.broadcasted_iota(jnp.int32, (8, 2 * TOK), 0) < 4
        both_sums = jnp.where(upper, q_sum, k_sum)
        r.wide[rows(mine, TOK), 0:RC] = out[0:TOK]
        r.wide[rows(other, TOK), 0:RC] = out[TOK:]
        r.sums[mine] = both_sums[:, 0:TOK]
        r.sums[other] = both_sums[:, TOK:]
        return 0

    lax.fori_loop(0, 4, project, 0)
    exchange = SumExchange(r.sums, r.sums_land, r.sum_send, r.sum_recv)
    exchange.start()
    for i, to in enumerate(sources):
        source = to[1] * 4 + to[2]
        remote(
            gain_parts.at[0], r.gain_parts_land.at[source], r.gp_send.at[i], r.gp_recv.at[source], to
        ).wait_recv()
    gains = r.gain_parts_land[0]
    for i in range(1, 16):
        gains = gains + r.gain_parts_land[i]
    r.gains[...] = gains
    total = exchange.total()
    upper3 = lax.broadcasted_iota(jnp.int32, (8, 8, TOK), 1) < 4
    r.scales[...] = lax.rsqrt(jnp.where(upper3, total * (1.0 / QW), total * (1.0 / KW)) + NORM_EPS)

    def finish(b, _):
        at = rows(b, TOK)
        both = r.scales[b]
        q_scale, k_scale = column(both[0:1]), column(both[4:5])
        cosine, sine = cos[at, :], sin[at, :]
        for head in range(2):
            cols = slice(head * HEAD, (head + 1) * HEAD)
            q_unit = r.wide[at, cols] * q_scale
            r.unit[at, cols] = q_unit
            block, spot = token_block(r.q_rot, b, head)
            r.q_rot[block, spot, :] = rope(q_unit * r.gains[0:1, cols], cosine, sine).astype(BF)
        cols = slice(RQ, RQ + RK)
        k_unit = r.wide[at, cols] * k_scale
        r.unit[at, cols] = k_unit
        r.kv_own[0, at, :] = rope(k_unit * r.gains[0:1, cols], cosine, sine).astype(BF)
        r.kv_own[1, at, :] = r.wide[at, RQ + RK : RC].astype(BF)
        return 0

    lax.fori_loop(0, RANKS, finish, 0)

    kv_copy = remote(r.kv_own, r.kv_other, r.kv_send, r.kv_recv, partner)

    @pl.when(half == 0)
    def _():
        kv_copy.start()

    to_rank = lax.div(place, 2)
    slot = lax.rem(place, 2)
    near = (d, half * 2 + lax.div(to_rank, 4), lax.rem(to_rank, 4))
    far = (d + 1 - 2 * lax.rem(d, 2), (1 - half) * 2 + lax.div(to_rank, 4), lax.rem(to_rank, 4))
    pj_slot, dn_slot = r.pj_all.at[rows(slot, 128)], r.dn_all.at[rows(slot, 192)]
    keep = to_rank == rank
    pj_near = remote(r.pj_mine, pj_slot, r.pj_send.at[0], r.pj_recv.at[slot], near)
    dn_near = remote(r.dn_mine, dn_slot, r.dn_send.at[0], r.dn_recv.at[slot], near)

    @pl.when(jnp.logical_not(keep))
    def _():
        pj_near.start()
        dn_near.start()

    @pl.when(keep)
    def _():
        r.pj_all[rows(slot, 128), :] = r.pj_mine[...]
        r.dn_all[rows(slot, 192), :] = r.dn_mine[...]

    launch(remote(r.pj_mine, pj_slot, r.pj_send.at[1], r.pj_recv.at[slot], far))
    mine = r.gu_all.at[rows(place, 64)]
    for i, to in enumerate(sources):
        launch(remote(r.gu_pieces.at[rank_of(to)], mine, r.gu_send.at[i], r.gu_recv.at[place], to))
    r.gu_all[rows(place, 64), :] = r.gu_pieces[rank]
    launch(remote(r.dn_mine, dn_slot, r.dn_send.at[1], r.dn_recv.at[slot], far))
    gather_finish(r.hid_all, r.h_send, r.h_recv)

    r.v_t[0] = jnp.transpose(r.kv_own[1].astype(F32)).astype(BF)

    def allowed_tile(block, key_base):
        key_index = key_base + lax.broadcasted_iota(jnp.int32, (BLK, 2 * BLK), 0)
        lane = lax.broadcasted_iota(jnp.int32, (1, 2 * BLK), 1)
        query_index = half * HALF + block * BLK + lax.rem(lane, BLK)
        return (key_index >= start[block, 0:1, :]) & (key_index <= query_index)

    def tile(block, keys, values_t, key_base, carry):
        scores = nt(keys, r.q_rot[block]) * SCALE_TWO
        scores = jnp.where(allowed_tile(block, key_base), scores, MASKED)
        top_now = jnp.max(scores, axis=0, keepdims=True)
        if carry is None:
            probs = jnp.exp2(scores - top_now)
            return top_now, jnp.sum(probs, axis=0, keepdims=True), nn(values_t, probs.astype(BF))
        top_old, run_old, acc_old = carry
        top_new = jnp.maximum(top_old, top_now)
        fade = jnp.exp2(top_old - top_new)
        probs = jnp.exp2(scores - top_new)
        return (
            top_new,
            run_old * fade + jnp.sum(probs, axis=0, keepdims=True),
            acc_old * fade + nn(values_t, probs.astype(BF)),
        )

    def keep_state(block, state):
        r.top[block] = jnp.broadcast_to(state[0], (8, 2 * BLK))
        r.running[block] = jnp.broadcast_to(state[1], (8, 2 * BLK))
        r.accum[block] = state[2]

    def local_block(block, _):
        def local_tile(j, carry):
            return tile(
                block, r.kv_own[0, rows(j, BLK), :], r.v_t[0, :, rows(j, BLK)], half * HALF + j * BLK, carry
            )

        keep_state(block, lax.fori_loop(0, block, local_tile, local_tile(block, None)))
        return 0

    lax.fori_loop(0, 4, local_block, 0)

    @pl.when(half == 1)
    def _():
        kv_copy.wait_recv()
        r.v_t[1] = jnp.transpose(r.kv_other[1].astype(F32)).astype(BF)

        def other_block(block, _):
            state = (r.top[block][0:1], r.running[block][0:1], r.accum[block])

            def other_tile(j, carry):
                return tile(block, r.kv_other[0, rows(j, BLK), :], r.v_t[1, :, rows(j, BLK)], j * BLK, carry)

            keep_state(block, lax.fori_loop(0, 4, other_tile, state))
            return 0

        lax.fori_loop(0, 4, other_block, 0)

    @pl.when(half == 0)
    def _():
        kv_copy.wait_send()

    def close_block(block, _):
        run = r.running[block]
        r.lse[block] = r.top[block] + jnp.log2(run)
        out = jnp.transpose(r.accum[block] * (1.0 / run[0:1]))
        r.mixed[block] = out
        for head in range(2):
            r.mixed_low[rows(block, BLK), head * HEAD : (head + 1) * HEAD] = out[
                head * BLK : (head + 1) * BLK
            ].astype(BF)
        return 0

    lax.fori_loop(0, 4, close_block, 0)

    for i in range(2):
        from_self = 2 * rank + i == place

        @pl.when(jnp.logical_not(from_self))
        def _(i=i):
            remote(r.pj_mine, r.pj_all.at[pl.ds(i * 128, 128)], r.pj_send.at[0], r.pj_recv.at[i], partner).wait_recv()

    gain_attn = jnp.concatenate([r.gains[1:2], r.gains[2:3]], axis=1)
    gain_ffn = jnp.concatenate([r.gains[3:4], r.gains[4:5]], axis=1)

    def both_rows(ref, mine, other):
        return jnp.concatenate([ref[rows(mine, TOK), :], ref[rows(other, TOK), :]], axis=0)

    s = Scatter(r, 0)

    def proj_step(step, _):
        off = lax.rem(step + 1, 4)
        at = lax.rem(o + off, 4)
        s.give(off, nn(both_rows(r.mixed_low, core * 4 + at, (1 - core) * 4 + at), r.pj_all[...]))

        @pl.when(step > 0)
        def _():
            s.send(step)

        return 0

    lax.fori_loop(0, 4, proj_step, 0)
    s.send(0)
    for i, to in enumerate(sources):
        source = to[1] * 4 + to[2]
        remote(
            r.gu_pieces.at[0], r.gu_all.at[rows(source, 64)], r.gu_send.at[i], r.gu_recv.at[source], to
        ).wait_recv()
    branch = s.result()
    branch_scale = rms_scale(branch)
    branch_unit = branch * branch_scale
    residual = hid[...].astype(F32) + branch_unit * gain_attn
    r.full_res[rows(rank, TOK), :] = residual.astype(BF)
    gather_start(r.full_res, r.a_send, r.a_recv)
    s.finish()
    for i in range(2):
        from_self = 2 * rank + i == place

        @pl.when(jnp.logical_not(from_self))
        def _(i=i):
            remote(r.dn_mine, r.dn_all.at[pl.ds(i * 192, 192)], r.dn_send.at[0], r.dn_recv.at[i], partner).wait_recv()

    s1 = Scatter(r, 1)

    def ffn_step(step, _):
        off = order(step)
        mine, other = gather_arrive(r.full_res, r.a_send, r.a_recv, off)
        both = nn(both_rows(r.full_res, mine, other), r.gu_all[...])
        r.wide[rows(mine, TOK), :] = both[0:TOK]
        r.wide[rows(other, TOK), :] = both[TOK:]
        gate, up = both[:, 0:RF], both[:, RF:]
        act_low = (gate * jax.nn.sigmoid(gate) * up).astype(BF)
        r.act[rows(mine, TOK), :] = act_low[0:TOK]
        r.act[rows(other, TOK), :] = act_low[TOK:]
        s1.give(off, nn(act_low, r.dn_all[...]))

        @pl.when(step > 0)
        def _():
            s1.send(order(step - 1))

        return 0

    lax.fori_loop(0, 4, ffn_step, 0)
    s1.send(2)
    ffn = s1.result()
    ffn_scale = rms_scale(ffn)
    ffn_unit = ffn * ffn_scale
    layer_out[...] = residual + ffn_unit * gain_ffn
    cotangent = cot[...].astype(F32)
    back_ffn = norm_back(cotangent, ffn_unit, ffn_scale, gain_ffn)
    r.full_ffn[rows(rank, TOK), :] = back_ffn.astype(BF)
    gather_start(r.full_ffn, r.b_send, r.b_recv)
    gain_row = jnp.sum(cotangent * ffn_unit, axis=0, keepdims=True)
    r.gain_rest[2:3, :] = gain_row[:, 0:512]
    r.gain_rest[3:4, :] = gain_row[:, 512:]
    gather_finish(r.full_res, r.a_send, r.a_recv)
    s1.finish()

    s2 = Scatter(r, 2)

    def back_step(step, _):
        off = order(step)
        mine, other = gather_arrive(r.full_ffn, r.b_send, r.b_recv, off)
        back_act = nt(both_rows(r.full_ffn, mine, other), r.dn_all[...])
        both = both_rows(r.wide, mine, other)
        gate, up = both[:, 0:RF], both[:, RF:]
        sig = jax.nn.sigmoid(gate)
        back_gate = back_act * up * sig * (1.0 + gate * (1.0 - sig))
        back_up = back_act * (gate * sig)
        back_both = jnp.concatenate([back_gate, back_up], axis=1).astype(BF)
        r.back_gu[rows(mine, TOK), :] = back_both[0:TOK]
        r.back_gu[rows(other, TOK), :] = back_both[TOK:]
        s2.give(off, nt(back_both, r.gu_all[...]))

        @pl.when(step > 0)
        def _():
            s2.send(order(step - 1))

        return 0

    lax.fori_loop(0, 4, back_step, 0)
    s2.send(2)

    def plane_sends(index, cut, land):
        slot = plane_slot(d, c)
        for i, to in enumerate(planes):
            launch(
                remote(
                    cut(to[0], lax.div(to[1], 2)),
                    land.at[slot],
                    r.plane_send.at[index, i],
                    r.plane_recv.at[index, slot],
                    to,
                )
            )

    def plane_waits(index, land):
        for i, to in enumerate(planes):
            source = plane_slot(to[0], to[1])
            remote(
                land.at[source], land.at[source], r.plane_send.at[index, i], r.plane_recv.at[index, source], to
            ).wait_recv()

    def plane_total(land):
        total = land[0].astype(F32)
        for i in range(1, 16):
            total = total + land[i].astype(F32)
        return total

    def dn_cut(e, h):
        return rows(h * 4 + lax.div(e, 2), 48), rows(lax.rem(e, 2), 512)

    r.dn_grad[...] = tn(r.act[...], r.full_ffn[...]).astype(BF)
    plane_sends(0, lambda e, h: r.dn_grad.at[dn_cut(e, h)], r.dn_land)
    r.dn_land[plane_slot(d, c)] = r.dn_grad[dn_cut(d, half)]
    resid_grad = cotangent + s2.result()
    back_resid[...] = resid_grad
    gain_row = jnp.sum(resid_grad * branch_unit, axis=0, keepdims=True)
    r.gain_rest[0:1, :] = gain_row[:, 0:512]
    r.gain_rest[1:2, :] = gain_row[:, 512:]
    back_branch = norm_back(resid_grad, branch_unit, branch_scale, gain_attn)
    r.full_branch[rows(rank, TOK), :] = back_branch.astype(BF)
    gather_start(r.full_branch, r.e_send, r.e_recv)
    gather_finish(r.full_ffn, r.b_send, r.b_recv)
    s2.finish()

    def gu_step(b, _):
        grad = tn(r.full_res[:, rows(b, 128)], r.back_gu[...])
        r.gu_grad[lax.div(b, 4), rows(lax.rem(b, 4), 2)] = grad.astype(BF).reshape(2, 64, 2 * RF)
        return 0

    lax.fori_loop(0, 8, gu_step, 0)

    def gu_cut(e, h):
        return h, slice(None), rows(lax.div(e, 2), 16), rows(lax.rem(e, 2), RF)

    plane_sends(1, lambda e, h: r.gu_grad.at[gu_cut(e, h)], r.gu_land)
    r.gu_land[plane_slot(d, c)] = r.gu_grad[gu_cut(d, half)]

    def mixed_step(step, _):
        off = order(step)
        mine, other = gather_arrive(r.full_branch, r.e_send, r.e_recv, off)
        out = nt(both_rows(r.full_branch, mine, other), r.pj_all[...]).astype(BF)
        for head in range(2):
            for i, b in enumerate((mine, other)):
                block, spot = token_block(r.back_mixed, b, head)
                r.back_mixed[block, spot, :] = out[i * TOK : (i + 1) * TOK, head * HEAD : (head + 1) * HEAD]
        return 0

    lax.fori_loop(0, 4, mixed_step, 0)
    r.pj_grad[...] = tn(r.mixed_low[...], r.full_branch[...]).astype(BF)
    pj_cut = lambda e, h: rows(h * 8 + e, 16)
    plane_sends(2, lambda e, h: r.pj_grad.at[pj_cut(e, h)], r.pj_land)
    r.pj_land[plane_slot(d, c)] = r.pj_grad[pj_cut(d, half), :]
    gather_finish(r.full_branch, r.e_send, r.e_recv)

    def delta_step(block, _):
        r.delta[block] = row_sums(r.back_mixed[block].astype(F32) * r.mixed[block])
        r.back_q[block] = jnp.zeros((2 * BLK, HEAD), F32)
        return 0

    lax.fori_loop(0, 4, delta_step, 0)

    def back_tile(block, keys, values, key_base, carry):
        grad_k, grad_v = carry
        query, grad_out = r.q_rot[block], r.back_mixed[block]
        scores = nt(keys, query) * SCALE_TWO
        probs = jnp.where(allowed_tile(block, key_base), jnp.exp2(scores - r.lse[block, 0:1, :]), 0.0)
        back_prob = nt(values, grad_out)
        back_score = (probs * (back_prob - r.delta[block, 0:1, :])).astype(BF)
        grad_k = grad_k + nn(back_score, query)
        grad_v = grad_v + nn(probs.astype(BF), grad_out)
        r.back_q[block] += tn(back_score, keys)
        return grad_k, grad_v

    zero = (jnp.zeros((BLK, HEAD), F32), jnp.zeros((BLK, HEAD), F32))
    send_back = remote(r.other_grad, r.other_land, r.kvb_send, r.kvb_recv, partner)

    @pl.when(half == 1)
    def _():
        def other_keys(j, _):
            at = rows(j, BLK)
            keys, values = r.kv_other[0, at, :], r.kv_other[1, at, :]
            grad_k, grad_v = lax.fori_loop(
                0, 4, lambda block, carry: back_tile(block, keys, values, j * BLK, carry), zero
            )
            r.other_grad[0, at, :] = (grad_k * SCORE_SCALE).astype(BF)
            r.other_grad[1, at, :] = grad_v.astype(BF)
            return 0

        lax.fori_loop(0, 4, other_keys, 0)
        send_back.start()

    def local_keys(j, _):
        at = rows(j, BLK)
        keys, values = r.kv_own[0, at, :], r.kv_own[1, at, :]
        grad_k, grad_v = lax.fori_loop(
            j, 4, lambda block, carry: back_tile(block, keys, values, half * HALF + j * BLK, carry), zero
        )
        r.back_k[at, :] = grad_k * SCORE_SCALE
        r.back_v[at, :] = grad_v
        return 0

    lax.fori_loop(0, 4, local_keys, 0)

    @pl.when(half == 1)
    def _():
        send_back.wait_send()

    @pl.when(half == 0)
    def _():
        send_back.wait_recv()
        r.back_k[...] += r.other_land[0].astype(F32)
        r.back_v[...] += r.other_land[1].astype(F32)

    def weigh(b, _):
        at = rows(b, TOK)
        cosine, sine = cos[at, :], sin[at, :]
        totals = []
        for head in range(2):
            cols = slice(head * HEAD, (head + 1) * HEAD)
            block, spot = token_block(r.back_q, b, head)
            grad = unrope(r.back_q[block, spot, :] * SCORE_SCALE, cosine, sine)
            r.wide[at, cols] = grad
            totals.append(grad * r.gains[0:1, cols] * r.unit[at, cols])
        cols = slice(RQ, RQ + RK)
        grad = unrope(r.back_k[at, :], cosine, sine)
        r.wide[at, cols] = grad
        q_sum = row_sums(totals[0] + totals[1])
        k_sum = row_sums(grad * r.gains[0:1, cols] * r.unit[at, cols])
        upper = lax.broadcasted_iota(jnp.int32, (8, TOK), 0) < 4
        r.sums_back[b] = jnp.where(upper, q_sum, k_sum)
        return 0

    lax.fori_loop(0, RANKS, weigh, 0)
    exchange = SumExchange(r.sums_back, r.sums_back_land, r.sumb_send, r.sumb_recv)
    exchange.start()

    gain_own = jnp.sum(r.wide[:, 0 : RQ + RK] * r.unit[...], axis=0, keepdims=True)
    row = lax.broadcasted_iota(jnp.int32, (16, 512), 0)
    col = lax.broadcasted_iota(jnp.int32, (16, 512), 1)
    own_q, own_k = gain_own[:, 0:RQ], gain_own[:, RQ:]
    at_q = (row == lax.div(rank, 2)) & (lax.div(col, RQ) == lax.rem(rank, 2))
    at_k = (row == 4 + lax.div(rank, 4)) & (lax.div(col, RK) == lax.rem(rank, 4))
    r.gain_vec[...] = jnp.where(at_q, jnp.concatenate([own_q] * 2, axis=1), 0.0) + jnp.where(
        at_k, jnp.concatenate([own_k] * 4, axis=1), 0.0
    )
    r.gain_vec[6:10, :] = r.gain_rest[...]
    plane_sends(3, lambda e, h: r.gain_vec, r.gain_land)
    r.gain_land[plane_slot(d, c)] = r.gain_vec[...]

    total = exchange.total()
    r.sums_back[...] = jnp.where(upper3, total * (1.0 / QW), total * (1.0 / KW))

    def back_norm(b, _):
        at = rows(b, TOK)
        scale, mean = r.scales[b], r.sums_back[b]
        q_scale, k_scale = column(scale[0:1]), column(scale[4:5])
        q_mean, k_mean = column(mean[0:1]), column(mean[4:5])
        for head in range(2):
            cols = slice(head * HEAD, (head + 1) * HEAD)
            weighted = r.wide[at, cols] * r.gains[0:1, cols]
            r.back_qkv[at, cols] = (q_scale * (weighted - r.unit[at, cols] * q_mean)).astype(BF)
        cols = slice(RQ, RQ + RK)
        weighted = r.wide[at, cols] * r.gains[0:1, cols]
        r.back_qkv[at, cols] = (k_scale * (weighted - r.unit[at, cols] * k_mean)).astype(BF)
        r.back_qkv[at, RQ + RK : RC] = r.back_v[at, :].astype(BF)
        return 0

    lax.fori_loop(0, RANKS, back_norm, 0)

    def grad_step(b, _):
        grad = tn(r.hid_all[:, rows(b, 128)], r.back_qkv[...])
        r.qkv_grad[lax.div(b, 4), rows(lax.rem(b, 4), 2)] = grad.astype(BF).reshape(2, 64, RC)
        return 0

    lax.fori_loop(0, 8, grad_step, 0)

    def qkv_cut(e, h):
        return h, slice(None), rows(lax.div(e, 2), 16), rows(lax.rem(e, 2), RQ)

    plane_sends(4, lambda e, h: r.qkv_grad.at[qkv_cut(e, h)], r.qkv_land)
    r.qkv_land[plane_slot(d, c)] = r.qkv_grad[qkv_cut(d, half)]

    s3 = Scatter(r, 3)

    def input_step(step, _):
        off = lax.rem(step + 1, 4)
        at = lax.rem(o + off, 4)
        s3.give(off, nt(both_rows(r.back_qkv, core * 4 + at, (1 - core) * 4 + at), r.w_all[...]))

        @pl.when(step > 0)
        def _():
            s3.send(step)

        return 0

    lax.fori_loop(0, 4, input_step, 0)
    s3.send(0)

    for index, land, red in ((0, r.dn_land, r.dn_red), (1, r.gu_land, r.gu_red), (2, r.pj_land, r.pj_red)):
        plane_waits(index, land)
        red[...] = plane_total(land).astype(BF)
    target = 2 * rank + half
    to_owner = (d, lax.div(target, 4), lax.rem(target, 4))
    stay = target == place
    pj_move = remote(r.pj_red, r.pj_own, r.move_send.at[0], r.move_recv.at[0], to_owner)
    dn_move = remote(r.dn_red, r.dn_own, r.move_send.at[1], r.move_recv.at[1], to_owner)

    @pl.when(stay)
    def _():
        r.pj_own[...] = r.pj_red[...]
        r.dn_own[...] = r.dn_red[...]

    @pl.when(jnp.logical_not(stay))
    def _():
        pj_move.start()
        dn_move.start()

    for i, to in enumerate(ranks):
        launch(
            remote(
                r.gu_red.at[rank_of(to)],
                r.gu_own.at[:, rows(rank, RF)],
                r.gur_send.at[i],
                r.gur_recv.at[rank],
                to,
            )
        )
    r.gu_own[:, rows(rank, RF)] = r.gu_red[rank]

    plane_waits(3, r.gain_land)
    total = plane_total(r.gain_land)
    r.gain_mid[...] = total
    for i, to in enumerate(ranks):
        launch(remote(r.gain_mid, r.gain_last.at[rank], r.gl_send.at[i], r.gl_recv.at[rank], to))
    r.gain_last[rank] = total

    plane_waits(4, r.qkv_land)
    r.qkv_red[...] = plane_total(r.qkv_land).astype(BF)

    def qkv_cols(of_rank, i):
        return rows((1 - side) * (of_rank * 2 + i) + side * (of_rank + i * 8), RK)

    for i, to in enumerate(ranks):
        for j in range(2):
            launch(
                remote(
                    r.qkv_red.at[rank_of(to), :, pl.ds(j * RK, RK)],
                    r.qkv_own.at[:, qkv_cols(rank, j)],
                    r.qr_send.at[j, i],
                    r.qr_recv.at[j, rank],
                    to,
                )
            )
    for j in range(2):
        r.qkv_own[:, qkv_cols(rank, j)] = r.qkv_red[rank][:, j * RK : (j + 1) * RK]

    @pl.when(jnp.logical_not(stay))
    def _():
        pj_move.wait_send()
        dn_move.wait_send()
        pj_move.wait_recv()
        dn_move.wait_recv()

    for i, to in enumerate(ranks):
        remote(
            r.gu_red.at[0], r.gu_own.at[:, rows(rank_of(to), RF)], r.gur_send.at[i], r.gur_recv.at[rank_of(to)], sib
        ).wait_recv()

    def owned(n, e):
        e_part, e_side = lax.div(e, 2), lax.rem(e, 2)
        return (
            pj_sum.at[rows(e, 16), :],
            dn_sum.at[rows(e_part, 48), rows(e_side, 512)],
            gu_sum.at[rows(e_part, 16), rows(e_side, FF)],
            qkv_sum.at[rows(e_part, 16), rows(e_side, QW)],
        )[n]

    own_refs = (r.pj_own, r.dn_own, r.gu_own, r.qkv_own)
    for i, to in enumerate(owners):
        for n in range(3):
            launch(remote(own_refs[n], owned(n, d), r.y_send.at[n, i], r.y_recv.at[n, d], to))
    pj_sum[rows(d, 16), :] = r.pj_own[...]
    dn_sum[rows(part, 48), rows(side, 512)] = r.dn_own[...]
    gu_sum[rows(part, 16), rows(side, FF)] = r.gu_own[...]

    input_part[...] = s3.result()
    for i, to in enumerate(ranks):
        remote(
            r.gain_mid, r.gain_last.at[rank_of(to)], r.gl_send.at[i], r.gl_recv.at[rank_of(to)], sib
        ).wait_recv()
    total = r.gain_last[0]
    for i in range(1, 8):
        total = total + r.gain_last[i]
    gain_sum[...] = total

    for i, to in enumerate(ranks):
        for j in range(2):
            remote(
                r.qkv_red.at[0, :, pl.ds(j * RK, RK)],
                r.qkv_own.at[:, qkv_cols(rank_of(to), j)],
                r.qr_send.at[j, i],
                r.qr_recv.at[j, rank_of(to)],
                sib,
            ).wait_recv()
    for i, to in enumerate(owners):
        launch(remote(r.qkv_own, owned(3, d), r.y_send.at[3, i], r.y_recv.at[3, d], to))
    qkv_sum[rows(part, 16), rows(side, QW)] = r.qkv_own[...]
    for i, to in enumerate(owners):
        for n in range(4):
            remote(own_refs[n], owned(n, to[0]), r.y_send.at[n, i], r.y_recv.at[n, to[0]], sib).wait_recv()
    s3.finish()
    for copy in done:
        copy.wait_send()

    @pl.when(jnp.logical_not(keep))
    def _():
        pj_near.wait_send()
        dn_near.wait_send()


def call_layer(*operands):
    any_space = pl.BlockSpec(memory_space=pl.ANY)
    return pl.pallas_call(
        layer_kernel,
        name="layer",
        out_shape=(
            jax.ShapeDtypeStruct((TOK, D), F32),
            jax.ShapeDtypeStruct((TOK, D), F32),
            jax.ShapeDtypeStruct((TOK, D), F32),
            jax.ShapeDtypeStruct((64, QW + 2 * KW), BF),
            jax.ShapeDtypeStruct((64, 2 * FF), BF),
            jax.ShapeDtypeStruct((128, D), BF),
            jax.ShapeDtypeStruct((192, D), BF),
            jax.ShapeDtypeStruct((16, 512), F32),
        ),
        in_specs=[VMEM] * 3 + [any_space] * 3 + [VMEM] * 4,
        out_specs=[VMEM] * 8,
        scratch_shapes=list(SCRATCH.values()),
        compiler_params=pltpu.CompilerParams(
            collective_id=1, has_side_effects=True, vmem_limit_bytes=63 * 2**20
        ),
    )(*operands)


def doc_positions(seq_segments):
    row_index = jnp.arange(seq_segments.shape[0], dtype=jnp.int32)
    new_doc = jnp.concatenate([jnp.ones((1,), dtype=bool), seq_segments[1:] != seq_segments[:-1]])
    starts = lax.cummax(jnp.where(new_doc, row_index, 0), axis=0)
    return row_index - starts


def adam_step(weight, moment, square, grad_sum, rate, decay):
    moment_new = BETA_ONE * moment + (1.0 - BETA_ONE) * grad_sum
    square_new = BETA_TWO * square + (1.0 - BETA_TWO) * grad_sum * grad_sum
    moment_hat = moment_new / (1.0 - BETA_ONE**STEP)
    square_hat = square_new / (1.0 - BETA_TWO**STEP)
    weight_new = weight - rate * (moment_hat / (jnp.sqrt(square_hat) + ADAM_EPS) + decay * weight)
    return (weight_new, moment_new, square_new)


def per_device(
    hidden_in,
    segment_ids,
    out_cotangent,
    qkv_weight,
    qkv_moment,
    qkv_square,
    proj_weight,
    proj_moment,
    proj_square,
    gate_up_weight,
    gate_up_moment,
    gate_up_square,
    down_weight,
    down_moment,
    down_square,
    gains,
    gain_moment,
    gain_square,
):
    _, c, o = coords()
    half = c // 2
    place = c * 4 + o
    positions = lax.dynamic_slice_in_dim(doc_positions(segment_ids[0]), half * HALF, HALF)
    start = half * HALF + jnp.arange(HALF, dtype=jnp.int32) - positions
    start = jnp.broadcast_to(start.reshape(4, 1, 1, BLK), (4, 8, 2, BLK)).reshape(4, 8, 2 * BLK)
    frequency = jnp.exp(jnp.arange(HEAD // 2, dtype=F32) * (-math.log(THETA) / (HEAD // 2)))
    angles = positions.astype(F32)[:, None] * frequency[None, :]
    cosine, sine = jnp.cos(angles), jnp.sin(angles)
    cos = jnp.concatenate([cosine, cosine], axis=1)
    sin = jnp.concatenate([-sine, sine], axis=1)

    placed = lax.dynamic_update_slice_in_dim(
        jnp.zeros((QW + KW + 2 * D,), F32), gains.astype(BF).astype(F32), place * gains.shape[0], axis=0
    )
    query_part = placed[:QW].reshape(RANKS, 1, RQ)
    key_part = placed[QW : QW + KW].reshape(RANKS, 1, RK)
    rest = jnp.broadcast_to(placed[QW + KW :].reshape(1, 4, 512), (RANKS, 4, 512))
    gain_parts = jnp.concatenate(
        [
            jnp.concatenate([query_part, key_part, jnp.zeros((RANKS, 1, 128), F32)], axis=2),
            rest,
            jnp.zeros((RANKS, 3, 512), F32),
        ],
        axis=1,
    )

    layer_out, back_resid, input_part, qkv_sum, gu_sum, pj_sum, dn_sum, gain_sum = call_layer(
        hidden_in, out_cotangent, qkv_weight, gate_up_weight, proj_weight, down_weight, gain_parts, cos, sin, start
    )
    gain_grad = lax.dynamic_slice_in_dim(
        gain_sum[0:10].reshape(10 * 512), place * gains.shape[0], gains.shape[0]
    )
    return (
        (layer_out.astype(BF), back_resid + input_part)
        + adam_step(qkv_weight, qkv_moment, qkv_square, qkv_sum.astype(F32), RATE_MATRIX, DECAY)
        + adam_step(proj_weight, proj_moment, proj_square, pj_sum.astype(F32), RATE_MATRIX, DECAY)
        + adam_step(gate_up_weight, gate_up_moment, gate_up_square, gu_sum.astype(F32), RATE_MATRIX, DECAY)
        + adam_step(down_weight, down_moment, down_square, dn_sum.astype(F32), RATE_MATRIX, DECAY)
        + adam_step(gains, gain_moment, gain_square, gain_grad, RATE_GAIN, 0.0)
    )


def solution(mesh):
    seq = P(("dp", "ctx", "opt"), None)
    mat = P(("ctx", "opt"), None)
    vec = P(("ctx", "opt"))
    return jax.shard_map(
        per_device,
        mesh=mesh,
        in_specs=(seq, P("dp", None), seq) + (mat,) * 12 + (vec,) * 3,
        out_specs=(seq, seq) + (mat,) * 12 + (vec,) * 3,
        check_vma=False,
    )
```

```python
import math
import types

import jax
import jax.numpy as jnp
from jax import lax
from jax.experimental import pallas as pl
from jax.experimental.pallas import tpu as pltpu
from jax.sharding import PartitionSpec as P

D = 1024
FF = 3072
HEADS = 16
KV_HEADS = 8
HEAD = 128
STEP = 10

NORM_EPS = 1e-06
THETA = 500000.0
MASKED = -1e30
BETA_ONE = 0.9
BETA_TWO = 0.95
ADAM_EPS = 1e-08
RATE_MATRIX = 0.06
RATE_GAIN = 1.0
DECAY = 0.1

TOK = 128
HALF = 1024
RANKS = 8
QW = HEADS * HEAD
KW = KV_HEADS * HEAD
RQ = 256
RK = 128
RC = RQ + 2 * RK
RF = FF // RANKS
BLK = 256
SCORE_SCALE = 1.0 / math.sqrt(HEAD)
SCALE_TWO = SCORE_SCALE * math.log2(math.e)

MESH = pl.DeviceIdType.MESH
BF = jnp.bfloat16
F32 = jnp.float32
VMEM = pl.BlockSpec(memory_space=pltpu.VMEM)
DMA = pltpu.SemaphoreType.DMA


def coords():
    return lax.axis_index("dp"), lax.axis_index("ctx"), lax.axis_index("opt")


def sibling(c):
    return c + 1 - 2 * lax.rem(c, 2)


def rank_peer(d, c, o, t):
    flip = t // 4
    return (d, c + (1 - 2 * lax.rem(c, 2)) * flip, lax.rem(o + t % 4, 4))


def cross_peer(d, c, o, t):
    return rank_peer(d + 1 - 2 * lax.rem(d, 2), lax.rem(c + 2, 4), o, t)


def plane_peer(d, c, o, t):
    x_lo, y = lax.rem(d, 2), lax.div(d, 2)
    y = lax.rem(y + t // 4, 4)
    x_lo = x_lo + (1 - 2 * x_lo) * (t % 2)
    return (2 * y + x_lo, lax.rem(c + 2 * ((t % 4) // 2), 4), o)


def group_peer(d, c, o, t):
    return (d, lax.rem(c + t // 4, 4), lax.rem(o + t % 4, 4))


def dp_peer(d, c, o, t):
    return (lax.rem(d + t, 8), c, o)


def greet(peers):
    barrier = pltpu.get_barrier_semaphore()
    for to in peers:
        pl.semaphore_signal(barrier, inc=1, device_id=to, device_id_type=MESH)
    pl.semaphore_wait(barrier, len(peers))


def remote(src, dst, send, recv, to):
    return pltpu.make_async_remote_copy(
        src_ref=src, dst_ref=dst, send_sem=send, recv_sem=recv, device_id=to, device_id_type=MESH
    )


def rows(index, count):
    return pl.ds(pl.multiple_of(index * count, count), count)


def nn(a, b):
    return lax.dot_general(a, b, (((1,), (0,)), ((), ())), preferred_element_type=F32)


def nt(a, b):
    return lax.dot_general(a, b, (((1,), (1,)), ((), ())), preferred_element_type=F32)


def tn(a, b):
    return lax.dot_general(a, b, (((0,), (0,)), ((), ())), preferred_element_type=F32)


def row_sums(values):
    ones = jnp.ones((8, values.shape[1]), F32)
    return lax.dot_general(
        ones,
        values,
        (((1,), (1,)), ((), ())),
        precision=lax.Precision.HIGHEST,
        preferred_element_type=F32,
    )


def column(row):
    return jnp.transpose(jnp.broadcast_to(row, (128, 128)))


def rms_scale(values):
    return lax.rsqrt(jnp.mean(values * values, axis=-1, keepdims=True) + NORM_EPS)


def norm_back(grad_rows, unit_rows, scale_rows, gain_row):
    weighted = grad_rows * gain_row
    return scale_rows * (
        weighted - unit_rows * jnp.mean(weighted * unit_rows, axis=-1, keepdims=True)
    )


def rope(u, cos, sin):
    return u * cos + pltpu.roll(u, HEAD // 2, 1) * sin


def unrope(g, cos, sin):
    return g * cos - pltpu.roll(g, HEAD // 2, 1) * sin


def gather_start(full, send, recv):
    d, c, o = coords()
    rank = lax.rem(c, 2) * 4 + o
    own = full.at[rows(rank, TOK)]
    for t in (1, 3, 2):
        remote(own, own, send.at[t], recv.at[rank], (d, c, lax.rem(o + t, 4))).start()
    remote(own, own, send.at[0], recv.at[rank], (d, sibling(c), o)).start()


def gather_arrive(full, send, recv, off):
    d, c, o = coords()
    core = lax.rem(c, 2)
    at = lax.rem(o + off, 4)
    mine, other = core * 4 + at, (1 - core) * 4 + at
    to = (d, sibling(c), o)
    block = full.at[rows(mine, TOK)]

    @pl.when(off > 0)
    def _():
        remote(block, block, send.at[0], recv.at[mine], to).wait_recv()
        remote(block, block, send.at[3 + off], recv.at[mine], to).start()

    block = full.at[rows(other, TOK)]
    remote(block, block, send.at[0], recv.at[other], to).wait_recv()
    return mine, other


def gather_finish(full, send, recv):
    d, c, o = coords()
    own = full.at[rows(0, TOK)]
    for i in range(7):
        remote(own, own, send.at[i], recv.at[0], (d, sibling(c), o)).wait_send()


class Scatter:
    def __init__(self, r, index):
        self.stage_s, self.stage_z, self.own = r.stage_s, r.stage_z, r.own
        self.land_s, self.land_z = r.land_s.at[index % 2], r.land_z.at[index % 2]
        self.send_s, self.recv_s = r.send_s.at[index], r.recv_s.at[index]
        self.send_z, self.recv_z = r.send_z.at[index], r.recv_z.at[index]

    def near(self, off):
        d, c, o = coords()
        return remote(
            self.stage_s.at[off], self.land_s.at[off], self.send_s.at[off], self.recv_s.at[off], (d, sibling(c), o)
        )

    def along(self, off):
        d, c, o = coords()
        return remote(
            self.stage_z.at[off - 1],
            self.land_z.at[off - 1],
            self.send_z.at[off],
            self.recv_z.at[off],
            (d, c, lax.rem(o + off, 4)),
        )

    def give(self, off, part):
        self.stage_s[off] = part[TOK:].astype(BF)
        self.near(off).start()
        self.own[off] = part[0:TOK]

    def send(self, off):
        self.near(off).wait_recv()
        total = self.own[off] + self.land_s[off].astype(F32)

        @pl.when(off > 0)
        def _():
            self.stage_z[off - 1] = total.astype(BF)
            self.along(off).start()

        @pl.when(off == 0)
        def _():
            self.own[0] = total

    def result(self):
        total = self.own[0]
        for off in (1, 3, 2):
            self.along(off).wait_recv()
            total = total + self.land_z[off - 1].astype(F32)
        return total

    def finish(self):
        for off in range(4):
            self.near(off).wait_send()
        for off in range(1, 4):
            self.along(off).wait_send()


def order(step):
    return step + lax.div(step, 2) - 2 * lax.div(step, 3)


class SumExchange:
    def __init__(self, sums, land, send, recv):
        self.sums, self.land, self.send, self.recv = sums, land, send, recv

    def start(self):
        d, c, o = coords()
        rank = lax.rem(c, 2) * 4 + o
        self.land[rank] = self.sums[...]
        self.copies = []
        for t in range(1, 8):
            copy = remote(
                self.sums, self.land.at[rank], self.send.at[t], self.recv.at[rank], rank_peer(d, c, o, t)
            )
            copy.start()
            self.copies.append(copy)

    def total(self):
        d, c, o = coords()
        for t in range(1, 8):
            _, c1, o1 = rank_peer(d, c, o, t)
            source = lax.rem(c1, 2) * 4 + o1
            remote(
                self.sums, self.land.at[source], self.send.at[t], self.recv.at[source], (d, sibling(c), o)
            ).wait_recv()
        for copy in self.copies:
            copy.wait_send()
        total = self.land[0]
        for i in range(1, 8):
            total = total + self.land[i]
        return total


def plane_slot(d, c):
    return lax.div(c, 2) * 8 + d


def token_block(ref, b, head):
    at = pl.multiple_of(head * BLK + lax.rem(b, 2) * TOK, TOK)
    return lax.div(b, 2), pl.ds(at, TOK)


SCRATCH = dict(
    w_raw=pltpu.VMEM((16, QW + 2 * KW), F32),
    gu_raw=pltpu.VMEM((16, 2 * FF), F32),
    pj_raw=pltpu.VMEM((32, D), F32),
    dn_raw=pltpu.VMEM((48, D), F32),
    pieces=pltpu.VMEM((RANKS, 16, RC), BF),
    gu_pieces=pltpu.VMEM((RANKS, 16, 2 * RF), BF),
    pj_mine=pltpu.VMEM((32, D), BF),
    dn_mine=pltpu.VMEM((48, D), BF),
    w_all=pltpu.VMEM((16, 64, RC), BF),
    gu_all=pltpu.VMEM((16, 64, 2 * RF), BF),
    pj_all=pltpu.VMEM((2, 128, D), BF),
    dn_all=pltpu.VMEM((2, 192, D), BF),
    gain_parts_land=pltpu.VMEM((16, 32, 128), BF),
    gains=pltpu.VMEM((8, D), F32),
    cos=pltpu.VMEM((HALF, HEAD), F32),
    sin=pltpu.VMEM((HALF, HEAD), F32),
    start=pltpu.VMEM((4, 8, 2 * BLK), jnp.int32),
    hid_all=pltpu.VMEM((HALF, D), BF),
    unit=pltpu.VMEM((HALF, RQ + RK), F32),
    sums=pltpu.VMEM((8, 8, TOK), F32),
    sums_land=pltpu.VMEM((8, 8, 8, TOK), F32),
    sums_back=pltpu.VMEM((8, 8, TOK), F32),
    sums_back_land=pltpu.VMEM((8, 8, 8, TOK), F32),
    scales=pltpu.VMEM((8, 8, TOK), F32),
    q_rot=pltpu.VMEM((4, 2 * BLK, HEAD), BF),
    kv_own=pltpu.VMEM((2, HALF, HEAD), BF),
    kv_other=pltpu.VMEM((2, HALF, HEAD), BF),
    v_t=pltpu.VMEM((2, HEAD, HALF), BF),
    top=pltpu.VMEM((4, 8, 2 * BLK), F32),
    running=pltpu.VMEM((4, 8, 2 * BLK), F32),
    accum=pltpu.VMEM((4, HEAD, 2 * BLK), F32),
    mixed=pltpu.VMEM((4, 2 * BLK, HEAD), F32),
    mixed_low=pltpu.VMEM((HALF, RQ), BF),
    lse=pltpu.VMEM((4, 8, 2 * BLK), F32),
    delta=pltpu.VMEM((4, 8, 2 * BLK), F32),
    full_res=pltpu.VMEM((HALF, D), BF),
    full_ffn=pltpu.VMEM((HALF, D), BF),
    full_branch=pltpu.VMEM((HALF, D), BF),
    wide=pltpu.VMEM((HALF, 2 * RF), F32),
    act=pltpu.VMEM((HALF, RF), BF),
    back_gu=pltpu.VMEM((HALF, 2 * RF), BF),
    stage_s=pltpu.VMEM((4, TOK, D), BF),
    stage_z=pltpu.VMEM((3, TOK, D), BF),
    own=pltpu.VMEM((4, TOK, D), F32),
    land_s=pltpu.VMEM((2, 4, TOK, D), BF),
    land_z=pltpu.VMEM((2, 3, TOK, D), BF),
    gain_rest=pltpu.VMEM((4, 512), F32),
    back_mixed=pltpu.VMEM((4, 2 * BLK, HEAD), BF),
    back_q=pltpu.VMEM((4, 2 * BLK, HEAD), F32),
    back_k=pltpu.VMEM((HALF, HEAD), F32),
    back_v=pltpu.VMEM((HALF, HEAD), F32),
    other_grad=pltpu.VMEM((2, HALF, HEAD), BF),
    other_land=pltpu.VMEM((2, HALF, HEAD), BF),
    back_qkv=pltpu.VMEM((HALF, RC), BF),
    pj_grad=pltpu.VMEM((RQ, D), BF),
    gu_grad=pltpu.VMEM((2, 8, 64, 2 * RF), BF),
    dn_grad=pltpu.VMEM((RF, D), BF),
    qkv_grad=pltpu.VMEM((2, 8, 64, RC), BF),
    pj_land=pltpu.VMEM((16, 16, D), BF),
    gu_land=pltpu.VMEM((16, 8, 16, RF), BF),
    dn_land=pltpu.VMEM((16, 48, 512), BF),
    qkv_land=pltpu.VMEM((16, 8, 16, RQ), BF),
    pj_red=pltpu.VMEM((16, D), BF),
    gu_red=pltpu.VMEM((8, 16, RF), BF),
    dn_red=pltpu.VMEM((48, 512), BF),
    qkv_red=pltpu.VMEM((8, 16, RQ), BF),
    pj_own=pltpu.VMEM((16, D), BF),
    gu_own=pltpu.VMEM((16, FF), BF),
    dn_own=pltpu.VMEM((48, 512), BF),
    qkv_own=pltpu.VMEM((16, QW), BF),
    gain_vec=pltpu.VMEM((16, 512), F32),
    gain_land=pltpu.VMEM((16, 16, 512), F32),
    gain_mid=pltpu.VMEM((16, 512), F32),
    gain_last=pltpu.VMEM((8, 16, 512), F32),
    raw_sem=DMA((4,)),
    h_send=DMA((7,)),
    h_recv=DMA((8,)),
    w_send=DMA((15,)),
    w_recv=DMA((16,)),
    gp_send=DMA((15,)),
    gp_recv=DMA((16,)),
    sum_send=DMA((8,)),
    sum_recv=DMA((8,)),
    sumb_send=DMA((8,)),
    sumb_recv=DMA((8,)),
    kv_send=DMA,
    kv_recv=DMA,
    gu_send=DMA((15,)),
    gu_recv=DMA((16,)),
    yw_send=DMA((4, 3)),
    yw_recv=DMA((4, 4)),
    pj_send=DMA((2,)),
    pj_recv=DMA((2,)),
    dn_send=DMA((2,)),
    dn_recv=DMA((2,)),
    send_s=DMA((4, 4)),
    recv_s=DMA((4, 4)),
    send_z=DMA((4, 4)),
    recv_z=DMA((4, 4)),
    a_send=DMA((7,)),
    a_recv=DMA((8,)),
    b_send=DMA((7,)),
    b_recv=DMA((8,)),
    e_send=DMA((7,)),
    e_recv=DMA((8,)),
    kvb_send=DMA,
    kvb_recv=DMA,
    plane_send=DMA((5, 15)),
    plane_recv=DMA((5, 16)),
    move_send=DMA((2,)),
    move_recv=DMA((2,)),
    gur_send=DMA((7,)),
    gur_recv=DMA((8,)),
    qr_send=DMA((2, 7)),
    qr_recv=DMA((2, 8)),
    gl_send=DMA((7,)),
    gl_recv=DMA((8,)),
    y_send=DMA((4, 7)),
    y_recv=DMA((4, 8)),
)


def layer_kernel(hid, cot, segments, gain_parts, w_rows, gu_rows, pj_rows, dn_rows, *refs):
    layer_out, back_resid, input_part, qkv_sum, gu_sum, pj_sum, dn_sum, gain_sum = refs[:8]
    r = types.SimpleNamespace(**dict(zip(SCRATCH, refs[8:])))
    d, c, o = coords()
    half, core = lax.div(c, 2), lax.rem(c, 2)
    rank = core * 4 + o
    place = c * 4 + o
    part, side = lax.div(d, 2), lax.rem(d, 2)
    sib = (d, sibling(c), o)
    partner = (d, lax.rem(c + 2, 4), o)
    ranks = [rank_peer(d, c, o, t) for t in range(1, 8)]
    sources = ranks + [cross_peer(d, c, o, t) for t in range(8)]
    planes = [plane_peer(d, c, o, t) for t in range(1, 16)]
    owners = [dp_peer(d, c, o, t) for t in range(1, 8)]
    group = [group_peer(d, c, o, t) for t in range(1, 16)]
    crosses = [cross_peer(d, c, o, t) for t in range(8)]
    along_y = [(lax.rem(d + 2 * t, 8), c, o) for t in range(1, 4)]
    done = []

    def launch(copy):
        copy.start()
        done.append(copy)

    def rank_of(to):
        return lax.rem(to[1], 2) * 4 + to[2]

    raws = [
        pltpu.make_async_copy(src.at[rows(part, dst.shape[0])], dst, r.raw_sem.at[i])
        for i, (src, dst) in enumerate(
            ((w_rows, r.w_raw), (pj_rows, r.pj_raw), (gu_rows, r.gu_raw), (dn_rows, r.dn_raw))
        )
    ]
    for copy in raws:
        copy.start()
    r.hid_all[rows(rank, TOK), :] = hid[...]
    raws[0].wait()
    for g in range(RANKS):
        r.pieces[g, :, 0:RQ] = r.w_raw[:, g * RQ : (g + 1) * RQ].astype(BF)
        r.pieces[g, :, RQ : RQ + RK] = r.w_raw[:, QW + g * RK : QW + (g + 1) * RK].astype(BF)
        r.pieces[g, :, RQ + RK : RC] = r.w_raw[:, QW + KW + g * RK : QW + KW + (g + 1) * RK].astype(BF)
    greet(group + planes + crosses)

    def piece_rows(ref, source):
        return ref.at[source, rows(part, 16)]

    def send_pieces(pieces, ref, send, recv):
        for i, to in enumerate(sources):
            launch(remote(pieces.at[rank_of(to)], piece_rows(ref, place), send.at[i], recv.at[place], to))
        ref[place, rows(part, 16)] = pieces[rank]

    def wait_pieces(pieces, ref, send, recv):
        for i, to in enumerate(sources):
            source = to[1] * 4 + to[2]
            remote(pieces.at[0], piece_rows(ref, source), send.at[i], recv.at[source], to).wait_recv()

    def spread(index, cut):
        for i, to in enumerate(along_y):
            launch(remote(cut(part), cut(part), r.yw_send.at[index, i], r.yw_recv.at[index, part], to))

    def wait_spread(index, cut):
        for i, to in enumerate(along_y):
            y = lax.div(to[0], 2)
            remote(cut(y), cut(y), r.yw_send.at[index, i], r.yw_recv.at[index, y], to).wait_recv()

    def w_cut(y):
        return r.w_all.at[:, rows(y, 16)]

    def gu_all_cut(y):
        return r.gu_all.at[:, rows(y, 16)]

    def pj_all_cut(y):
        return r.pj_all.at[:, rows(y, 32)]

    def dn_all_cut(y):
        return r.dn_all.at[:, rows(y, 48)]

    to_rank = lax.div(place, 2)
    slot = lax.rem(place, 2)
    near = (d, half * 2 + lax.div(to_rank, 4), lax.rem(to_rank, 4))
    far = (d + 1 - 2 * lax.rem(d, 2), (1 - half) * 2 + lax.div(to_rank, 4), lax.rem(to_rank, 4))
    pj_slot, dn_slot = r.pj_all.at[slot, rows(part, 32)], r.dn_all.at[slot, rows(part, 48)]
    keep = to_rank == rank
    pj_near = remote(r.pj_mine, pj_slot, r.pj_send.at[0], r.pj_recv.at[slot], near)
    dn_near = remote(r.dn_mine, dn_slot, r.dn_send.at[0], r.dn_recv.at[slot], near)

    def send_rows():
        @pl.when(jnp.logical_not(keep))
        def _():
            pj_near.start()
            dn_near.start()

        @pl.when(keep)
        def _():
            r.pj_all[slot, rows(part, 32)] = r.pj_mine[...]
            r.dn_all[slot, rows(part, 48)] = r.dn_mine[...]

        launch(remote(r.pj_mine, pj_slot, r.pj_send.at[1], r.pj_recv.at[slot], far))
        launch(remote(r.dn_mine, dn_slot, r.dn_send.at[1], r.dn_recv.at[slot], far))

    def wait_rows():
        for i in range(2):
            from_self = 2 * rank + i == place

            @pl.when(jnp.logical_not(from_self))
            def _(i=i):
                pj_at, dn_at = r.pj_all.at[i, rows(part, 32)], r.dn_all.at[i, rows(part, 48)]
                remote(r.pj_mine, pj_at, r.pj_send.at[0], r.pj_recv.at[i], partner).wait_recv()
                remote(r.dn_mine, dn_at, r.dn_send.at[0], r.dn_recv.at[i], partner).wait_recv()

    send_pieces(r.pieces, r.w_all, r.w_send, r.w_recv)
    gather_start(r.hid_all, r.h_send, r.h_recv)
    for i, to in enumerate(sources):
        launch(
            remote(
                gain_parts.at[rank_of(to)], r.gain_parts_land.at[place], r.gp_send.at[i], r.gp_recv.at[place], to
            )
        )
    r.gain_parts_land[place] = gain_parts[rank]
    ids = segments[...]
    own_ids = segments[:, rows(half, HALF)]
    starts = jnp.zeros((1, HALF), jnp.int32)
    for i in range(1, 6):
        below = jnp.sum((ids < i).astype(F32), axis=1, keepdims=True).astype(jnp.int32)
        starts = jnp.where(own_ids == i, below, starts)
    for block in range(4):
        row = starts[:, block * BLK : (block + 1) * BLK]
        r.start[block] = jnp.broadcast_to(jnp.concatenate([row, row], axis=1), (8, 2 * BLK))
    lane = lax.broadcasted_iota(jnp.int32, (1, HEAD), 1)
    frequency = jnp.exp(lax.rem(lane, HEAD // 2).astype(F32) * (-math.log(THETA) / (HEAD // 2)))
    sign = jnp.where(lane < HEAD // 2, -1.0, 1.0)
    token = half * HALF + lax.broadcasted_iota(jnp.int32, (1, HALF), 1)
    position = (token - starts).astype(F32)
    for b in range(RANKS):
        angles = column(position[:, b * TOK : (b + 1) * TOK]) * frequency
        r.cos[b * TOK : (b + 1) * TOK, :] = jnp.cos(angles)
        r.sin[b * TOK : (b + 1) * TOK, :] = jnp.sin(angles) * sign
    wait_pieces(r.pieces, r.w_all, r.w_send, r.w_recv)
    spread(0, w_cut)
    for copy in raws[1:]:
        copy.wait()
    for g in range(RANKS):
        r.gu_pieces[g, :, 0:RF] = r.gu_raw[:, g * RF : (g + 1) * RF].astype(BF)
        r.gu_pieces[g, :, RF:] = r.gu_raw[:, FF + g * RF : FF + (g + 1) * RF].astype(BF)
    r.pj_mine[...] = r.pj_raw[...].astype(BF)
    r.dn_mine[...] = r.dn_raw[...].astype(BF)

    send_rows()
    send_pieces(r.gu_pieces, r.gu_all, r.gu_send, r.gu_recv)
    wait_spread(0, w_cut)
    wait_rows()
    spread(1, pj_all_cut)
    wait_pieces(r.gu_pieces, r.gu_all, r.gu_send, r.gu_recv)
    spread(2, gu_all_cut)
    spread(3, dn_all_cut)


    def project(step, _):
        off = order(step)
        mine, other = gather_arrive(r.hid_all, r.h_send, r.h_recv, off)
        both = jnp.concatenate([r.hid_all[rows(mine, TOK), :], r.hid_all[rows(other, TOK), :]], axis=0)
        out = nn(both, r.w_all[...].reshape(D, RC))
        squares = out * out
        q_sum, k_sum = row_sums(squares[:, 0:RQ]), row_sums(squares[:, RQ : RQ + RK])
        upper = lax.broadcasted_iota(jnp.int32, (8, 2 * TOK), 0) < 4
        both_sums = jnp.where(upper, q_sum, k_sum)
        r.wide[rows(mine, TOK), 0:RC] = out[0:TOK]
        r.wide[rows(other, TOK), 0:RC] = out[TOK:]
        r.sums[mine] = both_sums[:, 0:TOK]
        r.sums[other] = both_sums[:, TOK:]
        return 0

    lax.fori_loop(0, 4, project, 0)
    exchange = SumExchange(r.sums, r.sums_land, r.sum_send, r.sum_recv)
    exchange.start()
    for i, to in enumerate(sources):
        source = to[1] * 4 + to[2]
        remote(
            gain_parts.at[0], r.gain_parts_land.at[source], r.gp_send.at[i], r.gp_recv.at[source], to
        ).wait_recv()
    gains = r.gain_parts_land[0].astype(F32)
    for i in range(1, 16):
        gains = gains + r.gain_parts_land[i].astype(F32)
    for i in range(3):
        r.gains[0:1, i * 128 : (i + 1) * 128] = gains[i : i + 1]
    for i in range(8):
        r.gains[1:2, i * 128 : (i + 1) * 128] = gains[3 + i : 4 + i]
        r.gains[2:3, i * 128 : (i + 1) * 128] = gains[11 + i : 12 + i]
    total = exchange.total()
    upper3 = lax.broadcasted_iota(jnp.int32, (8, 8, TOK), 1) < 4
    r.scales[...] = lax.rsqrt(jnp.where(upper3, total * (1.0 / QW), total * (1.0 / KW)) + NORM_EPS)

    def finish(b, _):
        at = rows(b, TOK)
        both = r.scales[b]
        q_scale, k_scale = column(both[0:1]), column(both[4:5])
        cosine, sine = r.cos[at, :], r.sin[at, :]
        for head in range(2):
            cols = slice(head * HEAD, (head + 1) * HEAD)
            q_unit = r.wide[at, cols] * q_scale
            r.unit[at, cols] = q_unit
            block, spot = token_block(r.q_rot, b, head)
            r.q_rot[block, spot, :] = rope(q_unit * r.gains[0:1, cols], cosine, sine).astype(BF)
        cols = slice(RQ, RQ + RK)
        k_unit = r.wide[at, cols] * k_scale
        r.unit[at, cols] = k_unit
        r.kv_own[0, at, :] = rope(k_unit * r.gains[0:1, cols], cosine, sine).astype(BF)
        r.kv_own[1, at, :] = r.wide[at, RQ + RK : RC].astype(BF)
        return 0

    lax.fori_loop(0, RANKS, finish, 0)

    kv_copy = remote(r.kv_own, r.kv_other, r.kv_send, r.kv_recv, partner)

    @pl.when(half == 0)
    def _():
        kv_copy.start()

    gather_finish(r.hid_all, r.h_send, r.h_recv)

    r.v_t[0] = jnp.transpose(r.kv_own[1].astype(F32)).astype(BF)

    def allowed_tile(block, key_base):
        key_index = key_base + lax.broadcasted_iota(jnp.int32, (BLK, 2 * BLK), 0)
        lane = lax.broadcasted_iota(jnp.int32, (1, 2 * BLK), 1)
        query_index = half * HALF + block * BLK + lax.rem(lane, BLK)
        return (key_index >= r.start[block, 0:1, :]) & (key_index <= query_index)

    def tile(block, keys, values_t, key_base, carry):
        scores = nt(keys, r.q_rot[block]) * SCALE_TWO
        scores = jnp.where(allowed_tile(block, key_base), scores, MASKED)
        top_now = jnp.max(scores, axis=0, keepdims=True)
        if carry is None:
            probs = jnp.exp2(scores - top_now)
            return top_now, jnp.sum(probs, axis=0, keepdims=True), nn(values_t, probs.astype(BF))
        top_old, run_old, acc_old = carry
        top_new = jnp.maximum(top_old, top_now)
        fade = jnp.exp2(top_old - top_new)
        probs = jnp.exp2(scores - top_new)
        return (
            top_new,
            run_old * fade + jnp.sum(probs, axis=0, keepdims=True),
            acc_old * fade + nn(values_t, probs.astype(BF)),
        )

    def keep_state(block, state):
        r.top[block] = jnp.broadcast_to(state[0], (8, 2 * BLK))
        r.running[block] = jnp.broadcast_to(state[1], (8, 2 * BLK))
        r.accum[block] = state[2]

    def local_block(block, _):
        def local_tile(j, carry):
            return tile(
                block, r.kv_own[0, rows(j, BLK), :], r.v_t[0, :, rows(j, BLK)], half * HALF + j * BLK, carry
            )

        keep_state(block, lax.fori_loop(0, block, local_tile, local_tile(block, None)))
        return 0

    lax.fori_loop(0, 4, local_block, 0)

    @pl.when(half == 1)
    def _():
        kv_copy.wait_recv()
        r.v_t[1] = jnp.transpose(r.kv_other[1].astype(F32)).astype(BF)

        def other_block(block, _):
            state = (r.top[block][0:1], r.running[block][0:1], r.accum[block])

            def other_tile(j, carry):
                return tile(block, r.kv_other[0, rows(j, BLK), :], r.v_t[1, :, rows(j, BLK)], j * BLK, carry)

            keep_state(block, lax.fori_loop(0, 4, other_tile, state))
            return 0

        lax.fori_loop(0, 4, other_block, 0)

    @pl.when(half == 0)
    def _():
        kv_copy.wait_send()

    def close_block(block, _):
        run = r.running[block]
        r.lse[block] = r.top[block] + jnp.log2(run)
        out = jnp.transpose(r.accum[block] * (1.0 / run[0:1]))
        r.mixed[block] = out
        for head in range(2):
            r.mixed_low[rows(block, BLK), head * HEAD : (head + 1) * HEAD] = out[
                head * BLK : (head + 1) * BLK
            ].astype(BF)
        return 0

    lax.fori_loop(0, 4, close_block, 0)

    wait_spread(1, pj_all_cut)
    gain_attn, gain_ffn = r.gains[1:2, :], r.gains[2:3, :]

    def both_rows(ref, mine, other):
        return jnp.concatenate([ref[rows(mine, TOK), :], ref[rows(other, TOK), :]], axis=0)

    s = Scatter(r, 0)

    def proj_step(step, _):
        off = lax.rem(step + 1, 4)
        at = lax.rem(o + off, 4)
        s.give(off, nn(both_rows(r.mixed_low, core * 4 + at, (1 - core) * 4 + at), r.pj_all[...].reshape(RQ, D)))

        @pl.when(step > 0)
        def _():
            s.send(step)

        return 0

    lax.fori_loop(0, 4, proj_step, 0)
    s.send(0)
    branch = s.result()
    branch_scale = rms_scale(branch)
    branch_unit = branch * branch_scale
    residual = hid[...].astype(F32) + branch_unit * gain_attn
    r.full_res[rows(rank, TOK), :] = residual.astype(BF)
    gather_start(r.full_res, r.a_send, r.a_recv)
    s.finish()
    wait_spread(2, gu_all_cut)
    wait_spread(3, dn_all_cut)

    s1 = Scatter(r, 1)

    def ffn_step(step, _):
        off = order(step)
        mine, other = gather_arrive(r.full_res, r.a_send, r.a_recv, off)
        both = nn(both_rows(r.full_res, mine, other), r.gu_all[...].reshape(D, 2 * RF))
        r.wide[rows(mine, TOK), :] = both[0:TOK]
        r.wide[rows(other, TOK), :] = both[TOK:]
        gate, up = both[:, 0:RF], both[:, RF:]
        act_low = (gate * jax.nn.sigmoid(gate) * up).astype(BF)
        r.act[rows(mine, TOK), :] = act_low[0:TOK]
        r.act[rows(other, TOK), :] = act_low[TOK:]
        s1.give(off, nn(act_low, r.dn_all[...].reshape(RF, D)))

        @pl.when(step > 0)
        def _():
            s1.send(order(step - 1))

        return 0

    lax.fori_loop(0, 4, ffn_step, 0)
    s1.send(2)
    ffn = s1.result()
    ffn_scale = rms_scale(ffn)
    ffn_unit = ffn * ffn_scale
    layer_out[...] = residual + ffn_unit * gain_ffn
    cotangent = cot[...].astype(F32)
    back_ffn = norm_back(cotangent, ffn_unit, ffn_scale, gain_ffn)
    r.full_ffn[rows(rank, TOK), :] = back_ffn.astype(BF)
    gather_start(r.full_ffn, r.b_send, r.b_recv)
    gain_row = jnp.sum(cotangent * ffn_unit, axis=0, keepdims=True)
    r.gain_rest[2:3, :] = gain_row[:, 0:512]
    r.gain_rest[3:4, :] = gain_row[:, 512:]
    gather_finish(r.full_res, r.a_send, r.a_recv)
    s1.finish()

    s2 = Scatter(r, 2)

    def back_step(step, _):
        off = order(step)
        mine, other = gather_arrive(r.full_ffn, r.b_send, r.b_recv, off)
        back_act = nt(both_rows(r.full_ffn, mine, other), r.dn_all[...].reshape(RF, D))
        both = both_rows(r.wide, mine, other)
        gate, up = both[:, 0:RF], both[:, RF:]
        sig = jax.nn.sigmoid(gate)
        back_gate = back_act * up * sig * (1.0 + gate * (1.0 - sig))
        back_up = back_act * (gate * sig)
        back_both = jnp.concatenate([back_gate, back_up], axis=1).astype(BF)
        r.back_gu[rows(mine, TOK), :] = back_both[0:TOK]
        r.back_gu[rows(other, TOK), :] = back_both[TOK:]
        s2.give(off, nt(back_both, r.gu_all[...].reshape(D, 2 * RF)))

        @pl.when(step > 0)
        def _():
            s2.send(order(step - 1))

        return 0

    lax.fori_loop(0, 4, back_step, 0)
    s2.send(2)

    def plane_sends(index, cut, land):
        slot = plane_slot(d, c)
        for i, to in enumerate(planes):
            launch(
                remote(
                    cut(to[0], lax.div(to[1], 2)),
                    land.at[slot],
                    r.plane_send.at[index, i],
                    r.plane_recv.at[index, slot],
                    to,
                )
            )

    def plane_waits(index, land):
        for i, to in enumerate(planes):
            source = plane_slot(to[0], to[1])
            remote(
                land.at[source], land.at[source], r.plane_send.at[index, i], r.plane_recv.at[index, source], to
            ).wait_recv()

    def plane_total(land):
        total = land[0].astype(F32)
        for i in range(1, 16):
            total = total + land[i].astype(F32)
        return total

    def dn_cut(e, h):
        return rows(h * 4 + lax.div(e, 2), 48), rows(lax.rem(e, 2), 512)

    r.dn_grad[...] = tn(r.act[...], r.full_ffn[...]).astype(BF)
    plane_sends(0, lambda e, h: r.dn_grad.at[dn_cut(e, h)], r.dn_land)
    r.dn_land[plane_slot(d, c)] = r.dn_grad[dn_cut(d, half)]
    resid_grad = cotangent + s2.result()
    back_resid[...] = resid_grad
    gain_row = jnp.sum(resid_grad * branch_unit, axis=0, keepdims=True)
    r.gain_rest[0:1, :] = gain_row[:, 0:512]
    r.gain_rest[1:2, :] = gain_row[:, 512:]
    back_branch = norm_back(resid_grad, branch_unit, branch_scale, gain_attn)
    r.full_branch[rows(rank, TOK), :] = back_branch.astype(BF)
    gather_start(r.full_branch, r.e_send, r.e_recv)
    gather_finish(r.full_ffn, r.b_send, r.b_recv)
    s2.finish()

    def gu_step(b, _):
        grad = tn(r.full_res[:, rows(b, 128)], r.back_gu[...])
        r.gu_grad[lax.div(b, 4), rows(lax.rem(b, 4), 2)] = grad.astype(BF).reshape(2, 64, 2 * RF)
        return 0

    lax.fori_loop(0, 8, gu_step, 0)

    def gu_cut(e, h):
        return h, slice(None), rows(lax.div(e, 2), 16), rows(lax.rem(e, 2), RF)

    plane_sends(1, lambda e, h: r.gu_grad.at[gu_cut(e, h)], r.gu_land)
    r.gu_land[plane_slot(d, c)] = r.gu_grad[gu_cut(d, half)]

    def mixed_step(step, _):
        off = order(step)
        mine, other = gather_arrive(r.full_branch, r.e_send, r.e_recv, off)
        out = nt(both_rows(r.full_branch, mine, other), r.pj_all[...].reshape(RQ, D)).astype(BF)
        for head in range(2):
            for i, b in enumerate((mine, other)):
                block, spot = token_block(r.back_mixed, b, head)
                r.back_mixed[block, spot, :] = out[i * TOK : (i + 1) * TOK, head * HEAD : (head + 1) * HEAD]
        return 0

    lax.fori_loop(0, 4, mixed_step, 0)
    r.pj_grad[...] = tn(r.mixed_low[...], r.full_branch[...]).astype(BF)
    pj_cut = lambda e, h: rows(h * 8 + e, 16)
    plane_sends(2, lambda e, h: r.pj_grad.at[pj_cut(e, h)], r.pj_land)
    r.pj_land[plane_slot(d, c)] = r.pj_grad[pj_cut(d, half), :]
    gather_finish(r.full_branch, r.e_send, r.e_recv)

    def delta_step(block, _):
        r.delta[block] = row_sums(r.back_mixed[block].astype(F32) * r.mixed[block])
        r.back_q[block] = jnp.zeros((2 * BLK, HEAD), F32)
        return 0

    lax.fori_loop(0, 4, delta_step, 0)

    def back_tile(block, keys, values, key_base, carry):
        grad_k, grad_v = carry
        query, grad_out = r.q_rot[block], r.back_mixed[block]
        scores = nt(keys, query) * SCALE_TWO
        probs = jnp.where(allowed_tile(block, key_base), jnp.exp2(scores - r.lse[block, 0:1, :]), 0.0)
        back_prob = nt(values, grad_out)
        back_score = (probs * (back_prob - r.delta[block, 0:1, :])).astype(BF)
        grad_k = grad_k + nn(back_score, query)
        grad_v = grad_v + nn(probs.astype(BF), grad_out)
        r.back_q[block] += tn(back_score, keys)
        return grad_k, grad_v

    zero = (jnp.zeros((BLK, HEAD), F32), jnp.zeros((BLK, HEAD), F32))
    send_back = remote(r.other_grad, r.other_land, r.kvb_send, r.kvb_recv, partner)

    def local_keys(j, _):
        at = rows(j, BLK)
        keys, values = r.kv_own[0, at, :], r.kv_own[1, at, :]
        grad_k, grad_v = lax.fori_loop(
            j, 4, lambda block, carry: back_tile(block, keys, values, half * HALF + j * BLK, carry), zero
        )
        r.back_k[at, :] = grad_k * SCORE_SCALE
        r.back_v[at, :] = grad_v
        return 0

    lax.fori_loop(0, 4 * (1 - half), local_keys, 0)

    @pl.when(half == 1)
    def _():
        def other_keys(j, _):
            at = rows(j, BLK)
            keys, values = r.kv_other[0, at, :], r.kv_other[1, at, :]
            grad_k, grad_v = lax.fori_loop(
                0, 4, lambda block, carry: back_tile(block, keys, values, j * BLK, carry), zero
            )
            r.other_grad[0, at, :] = (grad_k * SCORE_SCALE).astype(BF)
            r.other_grad[1, at, :] = grad_v.astype(BF)
            return 0

        lax.fori_loop(0, 4, other_keys, 0)
        send_back.start()

    for index, land, red in ((0, r.dn_land, r.dn_red), (1, r.gu_land, r.gu_red), (2, r.pj_land, r.pj_red)):
        plane_waits(index, land)
        red[...] = plane_total(land).astype(BF)
    target = 2 * rank + half
    to_owner = (d, lax.div(target, 4), lax.rem(target, 4))
    stay = target == place
    pj_move = remote(r.pj_red, r.pj_own, r.move_send.at[0], r.move_recv.at[0], to_owner)
    dn_move = remote(r.dn_red, r.dn_own, r.move_send.at[1], r.move_recv.at[1], to_owner)

    @pl.when(stay)
    def _():
        r.pj_own[...] = r.pj_red[...]
        r.dn_own[...] = r.dn_red[...]

    @pl.when(jnp.logical_not(stay))
    def _():
        pj_move.start()
        dn_move.start()

    for i, to in enumerate(ranks):
        launch(
            remote(
                r.gu_red.at[rank_of(to)],
                r.gu_own.at[:, rows(rank, RF)],
                r.gur_send.at[i],
                r.gur_recv.at[rank],
                to,
            )
        )
    r.gu_own[:, rows(rank, RF)] = r.gu_red[rank]

    lax.fori_loop(0, 4 * half, local_keys, 0)

    @pl.when(jnp.logical_not(stay))
    def _():
        pj_move.wait_send()
        dn_move.wait_send()
        pj_move.wait_recv()
        dn_move.wait_recv()

    for i, to in enumerate(ranks):
        remote(
            r.gu_red.at[0], r.gu_own.at[:, rows(rank_of(to), RF)], r.gur_send.at[i], r.gur_recv.at[rank_of(to)], sib
        ).wait_recv()

    def owned(n, e):
        e_part, e_side = lax.div(e, 2), lax.rem(e, 2)
        return (
            pj_sum.at[rows(e, 16), :],
            dn_sum.at[rows(e_part, 48), rows(e_side, 512)],
            gu_sum.at[rows(e_part, 16), rows(e_side, FF)],
            qkv_sum.at[rows(e_part, 16), rows(e_side, QW)],
        )[n]

    own_refs = (r.pj_own, r.dn_own, r.gu_own, r.qkv_own)
    for i, to in enumerate(owners):
        for n in range(3):
            launch(remote(own_refs[n], owned(n, d), r.y_send.at[n, i], r.y_recv.at[n, d], to))
    pj_sum[rows(d, 16), :] = r.pj_own[...]
    dn_sum[rows(part, 48), rows(side, 512)] = r.dn_own[...]
    gu_sum[rows(part, 16), rows(side, FF)] = r.gu_own[...]

    @pl.when(half == 1)
    def _():
        send_back.wait_send()

    @pl.when(half == 0)
    def _():
        send_back.wait_recv()
        r.back_k[...] += r.other_land[0].astype(F32)
        r.back_v[...] += r.other_land[1].astype(F32)

    def weigh(b, _):
        at = rows(b, TOK)
        cosine, sine = r.cos[at, :], r.sin[at, :]
        totals = []
        for head in range(2):
            cols = slice(head * HEAD, (head + 1) * HEAD)
            block, spot = token_block(r.back_q, b, head)
            grad = unrope(r.back_q[block, spot, :] * SCORE_SCALE, cosine, sine)
            r.wide[at, cols] = grad
            totals.append(grad * r.gains[0:1, cols] * r.unit[at, cols])
        cols = slice(RQ, RQ + RK)
        grad = unrope(r.back_k[at, :], cosine, sine)
        r.wide[at, cols] = grad
        q_sum = row_sums(totals[0] + totals[1])
        k_sum = row_sums(grad * r.gains[0:1, cols] * r.unit[at, cols])
        upper = lax.broadcasted_iota(jnp.int32, (8, TOK), 0) < 4
        r.sums_back[b] = jnp.where(upper, q_sum, k_sum)
        return 0

    lax.fori_loop(0, RANKS, weigh, 0)
    exchange = SumExchange(r.sums_back, r.sums_back_land, r.sumb_send, r.sumb_recv)
    exchange.start()

    gain_own = jnp.sum(r.wide[:, 0 : RQ + RK] * r.unit[...], axis=0, keepdims=True)
    row = lax.broadcasted_iota(jnp.int32, (16, 512), 0)
    col = lax.broadcasted_iota(jnp.int32, (16, 512), 1)
    own_q, own_k = gain_own[:, 0:RQ], gain_own[:, RQ:]
    at_q = (row == lax.div(rank, 2)) & (lax.div(col, RQ) == lax.rem(rank, 2))
    at_k = (row == 4 + lax.div(rank, 4)) & (lax.div(col, RK) == lax.rem(rank, 4))
    r.gain_vec[...] = jnp.where(at_q, jnp.concatenate([own_q] * 2, axis=1), 0.0) + jnp.where(
        at_k, jnp.concatenate([own_k] * 4, axis=1), 0.0
    )
    r.gain_vec[6:10, :] = r.gain_rest[...]
    plane_sends(3, lambda e, h: r.gain_vec, r.gain_land)
    r.gain_land[plane_slot(d, c)] = r.gain_vec[...]

    total = exchange.total()
    r.sums_back[...] = jnp.where(upper3, total * (1.0 / QW), total * (1.0 / KW))

    def back_norm(b, _):
        at = rows(b, TOK)
        scale, mean = r.scales[b], r.sums_back[b]
        q_scale, k_scale = column(scale[0:1]), column(scale[4:5])
        q_mean, k_mean = column(mean[0:1]), column(mean[4:5])
        for head in range(2):
            cols = slice(head * HEAD, (head + 1) * HEAD)
            weighted = r.wide[at, cols] * r.gains[0:1, cols]
            r.back_qkv[at, cols] = (q_scale * (weighted - r.unit[at, cols] * q_mean)).astype(BF)
        cols = slice(RQ, RQ + RK)
        weighted = r.wide[at, cols] * r.gains[0:1, cols]
        r.back_qkv[at, cols] = (k_scale * (weighted - r.unit[at, cols] * k_mean)).astype(BF)
        r.back_qkv[at, RQ + RK : RC] = r.back_v[at, :].astype(BF)
        return 0

    lax.fori_loop(0, RANKS, back_norm, 0)

    def grad_step(b, _):
        grad = tn(r.hid_all[:, rows(b, 128)], r.back_qkv[...])
        r.qkv_grad[lax.div(b, 4), rows(lax.rem(b, 4), 2)] = grad.astype(BF).reshape(2, 64, RC)
        return 0

    lax.fori_loop(0, 8, grad_step, 0)

    def qkv_cut(e, h):
        return h, slice(None), rows(lax.div(e, 2), 16), rows(lax.rem(e, 2), RQ)

    plane_sends(4, lambda e, h: r.qkv_grad.at[qkv_cut(e, h)], r.qkv_land)
    r.qkv_land[plane_slot(d, c)] = r.qkv_grad[qkv_cut(d, half)]

    s3 = Scatter(r, 3)

    def input_step(step, _):
        off = lax.rem(step + 1, 4)
        at = lax.rem(o + off, 4)
        s3.give(off, nt(both_rows(r.back_qkv, core * 4 + at, (1 - core) * 4 + at), r.w_all[...].reshape(D, RC)))

        @pl.when(step > 0)
        def _():
            s3.send(step)

        return 0

    lax.fori_loop(0, 4, input_step, 0)
    s3.send(0)

    plane_waits(3, r.gain_land)
    total = plane_total(r.gain_land)
    r.gain_mid[...] = total
    for i, to in enumerate(ranks):
        launch(remote(r.gain_mid, r.gain_last.at[rank], r.gl_send.at[i], r.gl_recv.at[rank], to))
    r.gain_last[rank] = total

    plane_waits(4, r.qkv_land)
    r.qkv_red[...] = plane_total(r.qkv_land).astype(BF)

    def qkv_cols(of_rank, i):
        return rows((1 - side) * (of_rank * 2 + i) + side * (of_rank + i * 8), RK)

    for i, to in enumerate(ranks):
        for j in range(2):
            launch(
                remote(
                    r.qkv_red.at[rank_of(to), :, pl.ds(j * RK, RK)],
                    r.qkv_own.at[:, qkv_cols(rank, j)],
                    r.qr_send.at[j, i],
                    r.qr_recv.at[j, rank],
                    to,
                )
            )
    for j in range(2):
        r.qkv_own[:, qkv_cols(rank, j)] = r.qkv_red[rank][:, j * RK : (j + 1) * RK]

    input_part[...] = s3.result()
    for i, to in enumerate(ranks):
        remote(
            r.gain_mid, r.gain_last.at[rank_of(to)], r.gl_send.at[i], r.gl_recv.at[rank_of(to)], sib
        ).wait_recv()
    total = r.gain_last[0]
    for i in range(1, 8):
        total = total + r.gain_last[i]
    gain_sum[...] = total

    for i, to in enumerate(ranks):
        for j in range(2):
            remote(
                r.qkv_red.at[0, :, pl.ds(j * RK, RK)],
                r.qkv_own.at[:, qkv_cols(rank_of(to), j)],
                r.qr_send.at[j, i],
                r.qr_recv.at[j, rank_of(to)],
                sib,
            ).wait_recv()
    for i, to in enumerate(owners):
        launch(remote(r.qkv_own, owned(3, d), r.y_send.at[3, i], r.y_recv.at[3, d], to))
    qkv_sum[rows(part, 16), rows(side, QW)] = r.qkv_own[...]
    for i, to in enumerate(owners):
        for n in range(4):
            remote(own_refs[n], owned(n, to[0]), r.y_send.at[n, i], r.y_recv.at[n, to[0]], sib).wait_recv()
    s3.finish()
    for copy in done:
        copy.wait_send()

    @pl.when(jnp.logical_not(keep))
    def _():
        pj_near.wait_send()
        dn_near.wait_send()


def call_layer(*operands):
    any_space = pl.BlockSpec(memory_space=pl.ANY)
    return pl.pallas_call(
        layer_kernel,
        name="layer",
        out_shape=(
            jax.ShapeDtypeStruct((TOK, D), F32),
            jax.ShapeDtypeStruct((TOK, D), F32),
            jax.ShapeDtypeStruct((TOK, D), F32),
            jax.ShapeDtypeStruct((64, QW + 2 * KW), BF),
            jax.ShapeDtypeStruct((64, 2 * FF), BF),
            jax.ShapeDtypeStruct((128, D), BF),
            jax.ShapeDtypeStruct((192, D), BF),
            jax.ShapeDtypeStruct((16, 512), F32),
        ),
        in_specs=[VMEM] * 4 + [any_space] * 4,
        out_specs=[VMEM] * 8,
        scratch_shapes=list(SCRATCH.values()),
        compiler_params=pltpu.CompilerParams(
            collective_id=1, has_side_effects=True, vmem_limit_bytes=63 * 2**20
        ),
    )(*operands)


def adam_step(weight, moment, square, grad_sum, rate, decay):
    moment_new = BETA_ONE * moment + (1.0 - BETA_ONE) * grad_sum
    square_new = BETA_TWO * square + (1.0 - BETA_TWO) * grad_sum * grad_sum
    moment_hat = moment_new / (1.0 - BETA_ONE**STEP)
    square_hat = square_new / (1.0 - BETA_TWO**STEP)
    weight_new = weight - rate * (moment_hat / (jnp.sqrt(square_hat) + ADAM_EPS) + decay * weight)
    return (weight_new, moment_new, square_new)


def update_kernel(*refs):
    ins, outs = refs[:19], refs[19:]
    layer_out, back_resid, input_part = ins[:3]
    outs[0][...] = layer_out[...].astype(BF)
    outs[1][...] = back_resid[...] + input_part[...]
    for i in range(4):
        weight, moment, square, grad = (ref[...] for ref in ins[3 + 4 * i : 7 + 4 * i])
        new = adam_step(weight, moment, square, grad.astype(F32), RATE_MATRIX, DECAY)
        for ref, value in zip(outs[2 + 3 * i : 5 + 3 * i], new):
            ref[...] = value


def call_update(*operands):
    def half_rows(shape):
        return pl.BlockSpec((shape[0] // 2, shape[1]), lambda i: (i, 0))

    results = [operands[0], operands[1]] + [operands[3 + 4 * i + j] for i in range(4) for j in range(3)]
    types_out = [BF] + [F32] * 13
    return pl.pallas_call(
        update_kernel,
        name="update",
        grid=(2,),
        out_shape=[jax.ShapeDtypeStruct(a.shape, t) for a, t in zip(results, types_out)],
        in_specs=[half_rows(a.shape) for a in operands],
        out_specs=[half_rows(a.shape) for a in results],
        compiler_params=pltpu.CompilerParams(vmem_limit_bytes=62 * 2**20),
    )(*operands)


def per_device(
    hidden_in,
    segment_ids,
    out_cotangent,
    qkv_weight,
    qkv_moment,
    qkv_square,
    proj_weight,
    proj_moment,
    proj_square,
    gate_up_weight,
    gate_up_moment,
    gate_up_square,
    down_weight,
    down_moment,
    down_square,
    gains,
    gain_moment,
    gain_square,
):
    _, c, o = coords()
    place = c * 4 + o
    placed = lax.dynamic_update_slice_in_dim(
        jnp.zeros((QW + KW + 2 * D,), BF), gains.astype(BF), place * gains.shape[0], axis=0
    )
    gain_parts = jnp.concatenate(
        [
            placed[:QW].reshape(RANKS, 2, 128),
            placed[QW : QW + KW].reshape(RANKS, 1, 128),
            jnp.broadcast_to(placed[QW + KW :].reshape(1, 16, 128), (RANKS, 16, 128)),
            jnp.zeros((RANKS, 13, 128), BF),
        ],
        axis=1,
    )
    layer_out, back_resid, input_part, qkv_sum, gu_sum, pj_sum, dn_sum, gain_sum = call_layer(
        hidden_in, out_cotangent, segment_ids, gain_parts, qkv_weight, gate_up_weight, proj_weight, down_weight
    )
    gain_grad = lax.dynamic_slice_in_dim(
        gain_sum[0:10].reshape(10 * 512), place * gains.shape[0], gains.shape[0]
    )
    updated = call_update(
        layer_out, back_resid, input_part,
        qkv_weight, qkv_moment, qkv_square, qkv_sum,
        proj_weight, proj_moment, proj_square, pj_sum,
        gate_up_weight, gate_up_moment, gate_up_square, gu_sum,
        down_weight, down_moment, down_square, dn_sum,
    )
    return tuple(updated) + adam_step(gains, gain_moment, gain_square, gain_grad, RATE_GAIN, 0.0)


def solution(mesh):
    seq = P(("dp", "ctx", "opt"), None)
    mat = P(("ctx", "opt"), None)
    vec = P(("ctx", "opt"))
    return jax.shard_map(
        per_device,
        mesh=mesh,
        in_specs=(seq, P("dp", None), seq) + (mat,) * 12 + (vec,) * 3,
        out_specs=(seq, seq) + (mat,) * 12 + (vec,) * 3,
        check_vma=False,
    )
```

```python
import math
import types

import jax
import jax.numpy as jnp
from jax import lax
from jax.experimental import pallas as pl
from jax.experimental.pallas import tpu as pltpu
from jax.sharding import PartitionSpec as P

D = 1024
FF = 3072
HEADS = 16
KV_HEADS = 8
HEAD = 128
STEP = 10

NORM_EPS = 1e-06
THETA = 500000.0
MASKED = -1e30
BETA_ONE = 0.9
BETA_TWO = 0.95
ADAM_EPS = 1e-08
RATE_MATRIX = 0.06
RATE_GAIN = 1.0
DECAY = 0.1

TOK = 128
HALF = 1024
RANKS = 8
QW = HEADS * HEAD
KW = KV_HEADS * HEAD
RQ = 256
RK = 128
RC = RQ + 2 * RK
RF = FF // RANKS
BLK = 256
SCORE_SCALE = 1.0 / math.sqrt(HEAD)
SCALE_TWO = SCORE_SCALE * math.log2(math.e)

MESH = pl.DeviceIdType.MESH
BF = jnp.bfloat16
F32 = jnp.float32
VMEM = pl.BlockSpec(memory_space=pltpu.VMEM)
DMA = pltpu.SemaphoreType.DMA


def coords():
    return lax.axis_index("dp"), lax.axis_index("ctx"), lax.axis_index("opt")


def sibling(c):
    return c + 1 - 2 * lax.rem(c, 2)


def rank_peer(d, c, o, t):
    flip = t // 4
    return (d, c + (1 - 2 * lax.rem(c, 2)) * flip, lax.rem(o + t % 4, 4))


def cross_peer(d, c, o, t):
    return rank_peer(d + 1 - 2 * lax.rem(d, 2), lax.rem(c + 2, 4), o, t)


def plane_peer(d, c, o, t):
    x_lo, y = lax.rem(d, 2), lax.div(d, 2)
    y = lax.rem(y + t // 4, 4)
    x_lo = x_lo + (1 - 2 * x_lo) * (t % 2)
    return (2 * y + x_lo, lax.rem(c + 2 * ((t % 4) // 2), 4), o)


def group_peer(d, c, o, t):
    return (d, lax.rem(c + t // 4, 4), lax.rem(o + t % 4, 4))


def dp_peer(d, c, o, t):
    return (lax.rem(d + t, 8), c, o)


def greet(peers):
    barrier = pltpu.get_barrier_semaphore()
    for to in peers:
        pl.semaphore_signal(barrier, inc=1, device_id=to, device_id_type=MESH)
    return lambda: pl.semaphore_wait(barrier, len(peers))


def remote(src, dst, send, recv, to):
    return pltpu.make_async_remote_copy(
        src_ref=src, dst_ref=dst, send_sem=send, recv_sem=recv, device_id=to, device_id_type=MESH
    )


def rows(index, count):
    return pl.ds(pl.multiple_of(index * count, count), count)


def nn(a, b):
    return lax.dot_general(a, b, (((1,), (0,)), ((), ())), preferred_element_type=F32)


def nt(a, b):
    return lax.dot_general(a, b, (((1,), (1,)), ((), ())), preferred_element_type=F32)


def tn(a, b):
    return lax.dot_general(a, b, (((0,), (0,)), ((), ())), preferred_element_type=F32)


def row_sums(values):
    ones = jnp.ones((8, values.shape[1]), F32)
    return lax.dot_general(
        ones,
        values,
        (((1,), (1,)), ((), ())),
        precision=lax.Precision.HIGHEST,
        preferred_element_type=F32,
    )


def column(row):
    return jnp.transpose(jnp.broadcast_to(row, (128, 128)))


def rms_scale(values):
    return lax.rsqrt(jnp.mean(values * values, axis=-1, keepdims=True) + NORM_EPS)


def norm_back(grad_rows, unit_rows, scale_rows, gain_row):
    weighted = grad_rows * gain_row
    return scale_rows * (
        weighted - unit_rows * jnp.mean(weighted * unit_rows, axis=-1, keepdims=True)
    )


def rope(u, cos, sin):
    return u * cos + pltpu.roll(u, HEAD // 2, 1) * sin


def unrope(g, cos, sin):
    return g * cos - pltpu.roll(g, HEAD // 2, 1) * sin


def gather_start(full, send, recv):
    d, c, o = coords()
    rank = lax.rem(c, 2) * 4 + o
    own = full.at[rows(rank, TOK)]
    for t in (1, 3):
        remote(own, own, send.at[t], recv.at[rank], (d, c, lax.rem(o + t, 4))).start()
    remote(own, own, send.at[0], recv.at[rank], (d, sibling(c), o)).start()


def gather_relay(full, send, recv):
    d, c, o = coords()
    core = lax.rem(c, 2)
    to = (d, sibling(c), o)
    for off, part in ((1, 1), (3, 0)):
        mine = core * 4 + lax.rem(o + off, 4)
        block = full.at[rows(mine, TOK)]
        half = full.at[rows(mine * 2 + part, TOK // 2)]
        remote(block, block, send.at[off], recv.at[mine], to).wait_recv()
        landed = recv.at[8] if part else recv.at[mine]
        remote(half, half, send.at[2 + 5 * part], landed, (d, c, lax.rem(o + 4 - off, 4))).start()
        remote(block, block, send.at[3 + off], recv.at[mine], to).start()


def gather_arrive(full, send, recv, off):
    d, c, o = coords()
    core = lax.rem(c, 2)
    at = lax.rem(o + off, 4)
    mine, other = core * 4 + at, (1 - core) * 4 + at
    to = (d, sibling(c), o)
    block = full.at[rows(mine, TOK)]

    @pl.when(off == 2)
    def _():
        for part in range(2):
            half = full.at[rows(mine * 2 + part, TOK // 2)]
            landed = recv.at[8] if part else recv.at[mine]
            remote(half, half, send.at[2], landed, to).wait_recv()
        remote(block, block, send.at[5], recv.at[mine], to).start()

    block = full.at[rows(other, TOK)]
    remote(block, block, send.at[0], recv.at[other], to).wait_recv()
    return mine, other


def gather_step(full, send, recv, step):
    @pl.when(step == 1)
    def _():
        gather_relay(full, send, recv)

    return gather_arrive(full, send, recv, order(step))


def gather_finish(full, send, recv):
    d, c, o = coords()
    for i in range(8):
        part = full.at[rows(0, TOK // 2 if i in (2, 7) else TOK)]
        remote(part, part, send.at[i], recv.at[0], (d, sibling(c), o)).wait_send()


class Scatter:
    def __init__(self, r, index):
        self.stage_s, self.stage_z, self.own = r.stage_s, r.stage_z, r.own
        self.land_s, self.land_z = r.land_s.at[index % 2], r.land_z.at[index % 2]
        self.send_s, self.recv_s = r.send_s.at[index], r.recv_s.at[index]
        self.send_z, self.recv_z = r.send_z.at[index], r.recv_z.at[index]

    def near(self, off):
        d, c, o = coords()
        return remote(
            self.stage_s.at[off], self.land_s.at[off], self.send_s.at[off], self.recv_s.at[off], (d, sibling(c), o)
        )

    def along(self, off):
        d, c, o = coords()
        return remote(
            self.stage_z.at[off - 1],
            self.land_z.at[off - 1],
            self.send_z.at[off],
            self.recv_z.at[off],
            (d, c, lax.rem(o + off, 4)),
        )

    def give(self, off, part):
        self.stage_s[off] = part[TOK:].astype(BF)
        self.near(off).start()
        self.own[off] = part[0:TOK]

    def send(self, off):
        self.near(off).wait_recv()
        total = self.own[off] + self.land_s[off].astype(F32)

        @pl.when(off > 0)
        def _():
            self.stage_z[off - 1] = total.astype(BF)
            self.along(off).start()

        @pl.when(off == 0)
        def _():
            self.own[0] = total

    def result(self):
        total = self.own[0]
        for off in (1, 3, 2):
            self.along(off).wait_recv()
            total = total + self.land_z[off - 1].astype(F32)
        return total

    def finish(self):
        for off in range(4):
            self.near(off).wait_send()
        for off in range(1, 4):
            self.along(off).wait_send()


def order(step):
    return step + lax.div(step, 2) - 2 * lax.div(step, 3)


class SumExchange:
    def __init__(self, sums, land, send, recv):
        self.sums, self.land, self.send, self.recv = sums, land, send, recv

    def start(self):
        d, c, o = coords()
        rank = lax.rem(c, 2) * 4 + o
        self.land[rank] = self.sums[...]
        self.copies = []
        for t in range(1, 8):
            copy = remote(
                self.sums, self.land.at[rank], self.send.at[t], self.recv.at[rank], rank_peer(d, c, o, t)
            )
            copy.start()
            self.copies.append(copy)

    def total(self):
        d, c, o = coords()
        for t in range(1, 8):
            _, c1, o1 = rank_peer(d, c, o, t)
            source = lax.rem(c1, 2) * 4 + o1
            remote(
                self.sums, self.land.at[source], self.send.at[t], self.recv.at[source], (d, sibling(c), o)
            ).wait_recv()
        for copy in self.copies:
            copy.wait_send()
        total = self.land[0]
        for i in range(1, 8):
            total = total + self.land[i]
        return total


def plane_slot(d, c):
    return lax.div(c, 2) * 8 + d


def token_block(ref, b, head):
    at = pl.multiple_of(head * BLK + lax.rem(b, 2) * TOK, TOK)
    return lax.div(b, 2), pl.ds(at, TOK)


SCRATCH = dict(
    w_raw=pltpu.VMEM((16, QW + 2 * KW), F32),
    gu_raw=pltpu.VMEM((16, 2 * FF), F32),
    pj_raw=pltpu.VMEM((32, D), F32),
    dn_raw=pltpu.VMEM((48, D), F32),
    pieces=pltpu.VMEM((RANKS, 16, RC), BF),
    gu_pieces=pltpu.VMEM((RANKS, 16, 2 * RF), BF),
    pj_mine=pltpu.VMEM((32, D), BF),
    dn_mine=pltpu.VMEM((48, D), BF),
    w_all=pltpu.VMEM((16, 64, RC), BF),
    gu_all=pltpu.VMEM((16, 64, 2 * RF), BF),
    pj_all=pltpu.VMEM((2, 128, D), BF),
    dn_all=pltpu.VMEM((2, 192, D), BF),
    gain_parts_land=pltpu.VMEM((16, 32, 128), BF),
    gains=pltpu.VMEM((8, D), F32),
    cos=pltpu.VMEM((HALF, HEAD), F32),
    sin=pltpu.VMEM((HALF, HEAD), F32),
    start=pltpu.VMEM((4, 8, 2 * BLK), jnp.int32),
    hid_all=pltpu.VMEM((HALF, D), BF),
    unit=pltpu.VMEM((HALF, RQ + RK), F32),
    sums=pltpu.VMEM((8, 8, TOK), F32),
    sums_land=pltpu.VMEM((8, 8, 8, TOK), F32),
    sums_back=pltpu.VMEM((8, 8, TOK), F32),
    sums_back_land=pltpu.VMEM((8, 8, 8, TOK), F32),
    scales=pltpu.VMEM((8, 8, TOK), F32),
    q_rot=pltpu.VMEM((4, 2 * BLK, HEAD), BF),
    kv_own=pltpu.VMEM((2, HALF, HEAD), BF),
    kv_other=pltpu.VMEM((2, HALF, HEAD), BF),
    v_t=pltpu.VMEM((2, HEAD, HALF), BF),
    top=pltpu.VMEM((4, 8, 2 * BLK), F32),
    running=pltpu.VMEM((4, 8, 2 * BLK), F32),
    accum=pltpu.VMEM((4, HEAD, 2 * BLK), F32),
    mixed=pltpu.VMEM((4, 2 * BLK, HEAD), F32),
    mixed_low=pltpu.VMEM((HALF, RQ), BF),
    lse=pltpu.VMEM((4, 8, 2 * BLK), F32),
    delta=pltpu.VMEM((4, 8, 2 * BLK), F32),
    full_res=pltpu.VMEM((HALF, D), BF),
    full_ffn=pltpu.VMEM((HALF, D), BF),
    full_branch=pltpu.VMEM((HALF, D), BF),
    wide=pltpu.VMEM((HALF, 2 * RF), F32),
    act=pltpu.VMEM((HALF, RF), BF),
    back_gu=pltpu.VMEM((HALF, 2 * RF), BF),
    stage_s=pltpu.VMEM((4, TOK, D), BF),
    stage_z=pltpu.VMEM((3, TOK, D), BF),
    own=pltpu.VMEM((4, TOK, D), F32),
    land_s=pltpu.VMEM((2, 4, TOK, D), BF),
    land_z=pltpu.VMEM((2, 3, TOK, D), BF),
    gain_rest=pltpu.VMEM((4, 512), F32),
    back_mixed=pltpu.VMEM((4, 2 * BLK, HEAD), BF),
    back_q=pltpu.VMEM((4, 2 * BLK, HEAD), F32),
    back_k=pltpu.VMEM((HALF, HEAD), F32),
    back_v=pltpu.VMEM((HALF, HEAD), F32),
    other_grad=pltpu.VMEM((2, HALF, HEAD), BF),
    other_land=pltpu.VMEM((2, HALF, HEAD), BF),
    back_qkv=pltpu.VMEM((HALF, RC), BF),
    pj_grad=pltpu.VMEM((2, 4, 2, 16, D), BF),
    gu_grad=pltpu.VMEM((2, 8, 64, 2 * RF), BF),
    dn_grad=pltpu.VMEM((RF, D), BF),
    qkv_grad=pltpu.VMEM((2, 8, 64, RC), BF),
    pj_x=pltpu.VMEM((4, 4, 16, D), BF),
    pj_mid=pltpu.VMEM((4, 16, D), BF),
    pj_y=pltpu.VMEM((4, 16, D), BF),
    dn_x=pltpu.VMEM((4, 192, 512), BF),
    dn_mid=pltpu.VMEM((192, 512), BF),
    dn_y=pltpu.VMEM((4, 48, 512), BF),
    gu_y=pltpu.VMEM((4, 2, 8, 16, 2 * RF), BF),
    gu_mid=pltpu.VMEM((2, 8, 16, 2 * RF), BF),
    gu_x=pltpu.VMEM((4, 8, 16, RF), BF),
    qkv_land=pltpu.VMEM((16, 8, 16, RQ), BF),
    pj_red=pltpu.VMEM((16, D), BF),
    gu_red=pltpu.VMEM((8, 16, RF), BF),
    dn_red=pltpu.VMEM((48, 512), BF),
    qkv_red=pltpu.VMEM((8, 16, RQ), BF),
    pj_own=pltpu.VMEM((16, D), BF),
    gu_own=pltpu.VMEM((16, FF), BF),
    dn_own=pltpu.VMEM((48, 512), BF),
    qkv_own=pltpu.VMEM((16, QW), BF),
    gain_vec=pltpu.VMEM((16, 512), F32),
    gain_y=pltpu.VMEM((4, 16, 512), F32),
    gain_half=pltpu.VMEM((16, 512), F32),
    gain_x=pltpu.VMEM((4, 16, 512), F32),
    gain_mid=pltpu.VMEM((16, 512), F32),
    gain_last=pltpu.VMEM((8, 16, 512), F32),
    layer_out=pltpu.VMEM((TOK, D), F32),
    back_resid=pltpu.VMEM((TOK, D), F32),
    input_part=pltpu.VMEM((TOK, D), F32),
    write_sem=DMA((7,)),
    raw_sem=DMA((4,)),
    h_send=DMA((8,)),
    h_recv=DMA((9,)),
    w_send=DMA((15,)),
    w_recv=DMA((16,)),
    gp_send=DMA((15,)),
    gp_recv=DMA((16,)),
    sum_send=DMA((8,)),
    sum_recv=DMA((8,)),
    sumb_send=DMA((8,)),
    sumb_recv=DMA((8,)),
    kv_send=DMA,
    kv_recv=DMA,
    gu_send=DMA((15,)),
    gu_recv=DMA((16,)),
    yw_send=DMA((4, 3)),
    yw_recv=DMA((4, 4)),
    pj_send=DMA((2,)),
    pj_recv=DMA((2,)),
    dn_send=DMA((2,)),
    dn_recv=DMA((2,)),
    send_s=DMA((4, 4)),
    recv_s=DMA((4, 4)),
    send_z=DMA((4, 4)),
    recv_z=DMA((4, 4)),
    a_send=DMA((8,)),
    a_recv=DMA((9,)),
    b_send=DMA((8,)),
    b_recv=DMA((9,)),
    e_send=DMA((8,)),
    e_recv=DMA((9,)),
    kvb_send=DMA,
    kvb_recv=DMA,
    plane_send=DMA((15,)),
    plane_recv=DMA((16,)),
    fan_send=DMA((8, 3)),
    fan_recv=DMA((8, 4)),
    move_send=DMA((2,)),
    move_recv=DMA((2,)),
    gur_send=DMA((7,)),
    gur_recv=DMA((8,)),
    qr_send=DMA((2, 7)),
    qr_recv=DMA((2, 8)),
    gl_send=DMA((7,)),
    gl_recv=DMA((8,)),
    y_send=DMA((4, 7)),
    y_recv=DMA((4, 8)),
)


def layer_kernel(hid, cot, segments, gain_parts, w_rows, gu_rows, pj_rows, dn_rows, *refs):
    layer_out, back_resid, input_part, qkv_sum, gu_sum, pj_sum, dn_sum, gain_sum = refs[:8]
    writes = []
    r = types.SimpleNamespace(**dict(zip(SCRATCH, refs[8:])))
    d, c, o = coords()
    half, core = lax.div(c, 2), lax.rem(c, 2)
    rank = core * 4 + o
    place = c * 4 + o
    part, side = lax.div(d, 2), lax.rem(d, 2)
    sib = (d, sibling(c), o)
    partner = (d, lax.rem(c + 2, 4), o)
    ranks = [rank_peer(d, c, o, t) for t in range(1, 8)]
    sources = ranks + [cross_peer(d, c, o, t) for t in range(8)]
    planes = [plane_peer(d, c, o, t) for t in range(1, 16)]
    owners = [dp_peer(d, c, o, t) for t in range(1, 8)]
    group = [group_peer(d, c, o, t) for t in range(1, 16)]
    crosses = [cross_peer(d, c, o, t) for t in range(8)]
    along_y = [(lax.rem(d + 2 * t, 8), c, o) for t in range(1, 4)]
    along_x = [plane_peer(d, c, o, t) for t in range(1, 4)]
    done = []

    def launch(copy):
        copy.start()
        done.append(copy)

    def write(src, dst):
        copy = pltpu.make_async_copy(src, dst, r.write_sem.at[len(writes)])
        copy.start()
        writes.append(copy)

    def drain():
        for copy in done:
            copy.wait_send()
        done.clear()

    def rank_of(to):
        return lax.rem(to[1], 2) * 4 + to[2]

    raws = [
        pltpu.make_async_copy(src.at[rows(part, dst.shape[0])], dst, r.raw_sem.at[i])
        for i, (src, dst) in enumerate(
            ((w_rows, r.w_raw), (pj_rows, r.pj_raw), (gu_rows, r.gu_raw), (dn_rows, r.dn_raw))
        )
    ]
    for copy in raws:
        copy.start()
    all_here = greet(group + planes + crosses)
    r.hid_all[rows(rank, TOK), :] = hid[...]
    raws[0].wait()
    for g in range(RANKS):
        r.pieces[g, :, 0:RQ] = r.w_raw[:, g * RQ : (g + 1) * RQ].astype(BF)
        r.pieces[g, :, RQ : RQ + RK] = r.w_raw[:, QW + g * RK : QW + (g + 1) * RK].astype(BF)
        r.pieces[g, :, RQ + RK : RC] = r.w_raw[:, QW + KW + g * RK : QW + KW + (g + 1) * RK].astype(BF)
    all_here()

    def piece_rows(ref, source):
        return ref.at[source, rows(part, 16)]

    def send_pieces(pieces, ref, send, recv):
        for i, to in enumerate(sources):
            launch(remote(pieces.at[rank_of(to)], piece_rows(ref, place), send.at[i], recv.at[place], to))
        ref[place, rows(part, 16)] = pieces[rank]

    def wait_pieces(pieces, ref, send, recv):
        for i, to in enumerate(sources):
            source = to[1] * 4 + to[2]
            remote(pieces.at[0], piece_rows(ref, source), send.at[i], recv.at[source], to).wait_recv()

    def spread(index, cut):
        for i, to in enumerate(along_y):
            launch(remote(cut(part), cut(part), r.yw_send.at[index, i], r.yw_recv.at[index, part], to))

    def wait_spread(index, cut):
        for i, to in enumerate(along_y):
            y = lax.div(to[0], 2)
            remote(cut(y), cut(y), r.yw_send.at[index, i], r.yw_recv.at[index, y], to).wait_recv()

    def w_cut(y):
        return r.w_all.at[:, rows(y, 16)]

    def gu_all_cut(y):
        return r.gu_all.at[:, rows(y, 16)]

    def pj_all_cut(y):
        return r.pj_all.at[:, rows(y, 32)]

    def dn_all_cut(y):
        return r.dn_all.at[:, rows(y, 48)]

    to_rank = lax.div(place, 2)
    slot = lax.rem(place, 2)
    near = (d, half * 2 + lax.div(to_rank, 4), lax.rem(to_rank, 4))
    far = (d + 1 - 2 * lax.rem(d, 2), (1 - half) * 2 + lax.div(to_rank, 4), lax.rem(to_rank, 4))
    pj_slot, dn_slot = r.pj_all.at[slot, rows(part, 32)], r.dn_all.at[slot, rows(part, 48)]
    keep = to_rank == rank
    pj_near = remote(r.pj_mine, pj_slot, r.pj_send.at[0], r.pj_recv.at[slot], near)
    dn_near = remote(r.dn_mine, dn_slot, r.dn_send.at[0], r.dn_recv.at[slot], near)

    def send_rows():
        @pl.when(jnp.logical_not(keep))
        def _():
            pj_near.start()
            dn_near.start()

        @pl.when(keep)
        def _():
            r.pj_all[slot, rows(part, 32)] = r.pj_mine[...]
            r.dn_all[slot, rows(part, 48)] = r.dn_mine[...]

        launch(remote(r.pj_mine, pj_slot, r.pj_send.at[1], r.pj_recv.at[slot], far))
        launch(remote(r.dn_mine, dn_slot, r.dn_send.at[1], r.dn_recv.at[slot], far))

    def wait_rows():
        for i in range(2):
            from_self = 2 * rank + i == place

            @pl.when(jnp.logical_not(from_self))
            def _(i=i):
                pj_at, dn_at = r.pj_all.at[i, rows(part, 32)], r.dn_all.at[i, rows(part, 48)]
                remote(r.pj_mine, pj_at, r.pj_send.at[0], r.pj_recv.at[i], partner).wait_recv()
                remote(r.dn_mine, dn_at, r.dn_send.at[0], r.dn_recv.at[i], partner).wait_recv()

    send_pieces(r.pieces, r.w_all, r.w_send, r.w_recv)
    gather_start(r.hid_all, r.h_send, r.h_recv)
    for i, to in enumerate(sources):
        launch(
            remote(
                gain_parts.at[rank_of(to)], r.gain_parts_land.at[place], r.gp_send.at[i], r.gp_recv.at[place], to
            )
        )
    r.gain_parts_land[place] = gain_parts[rank]
    ids = segments[...]
    own_ids = segments[:, rows(half, HALF)]
    starts = jnp.zeros((1, HALF), jnp.int32)
    for i in range(1, 6):
        below = jnp.sum((ids < i).astype(F32), axis=1, keepdims=True).astype(jnp.int32)
        starts = jnp.where(own_ids == i, below, starts)
    for block in range(4):
        row = starts[:, block * BLK : (block + 1) * BLK]
        r.start[block] = jnp.broadcast_to(jnp.concatenate([row, row], axis=1), (8, 2 * BLK))
    lane = lax.broadcasted_iota(jnp.int32, (1, HEAD), 1)
    frequency = jnp.exp(lax.rem(lane, HEAD // 2).astype(F32) * (-math.log(THETA) / (HEAD // 2)))
    sign = jnp.where(lane < HEAD // 2, -1.0, 1.0)
    token = half * HALF + lax.broadcasted_iota(jnp.int32, (1, HALF), 1)
    position = (token - starts).astype(F32)
    for b in range(RANKS):
        angles = column(position[:, b * TOK : (b + 1) * TOK]) * frequency
        r.cos[b * TOK : (b + 1) * TOK, :] = jnp.cos(angles)
        r.sin[b * TOK : (b + 1) * TOK, :] = jnp.sin(angles) * sign
    wait_pieces(r.pieces, r.w_all, r.w_send, r.w_recv)
    spread(0, w_cut)
    for copy in raws[1:]:
        copy.wait()
    for g in range(RANKS):
        r.gu_pieces[g, :, 0:RF] = r.gu_raw[:, g * RF : (g + 1) * RF].astype(BF)
        r.gu_pieces[g, :, RF:] = r.gu_raw[:, FF + g * RF : FF + (g + 1) * RF].astype(BF)
    r.pj_mine[...] = r.pj_raw[...].astype(BF)
    r.dn_mine[...] = r.dn_raw[...].astype(BF)

    send_rows()
    send_pieces(r.gu_pieces, r.gu_all, r.gu_send, r.gu_recv)
    gather_relay(r.hid_all, r.h_send, r.h_recv)
    wait_spread(0, w_cut)
    wait_rows()
    spread(1, pj_all_cut)
    wait_pieces(r.gu_pieces, r.gu_all, r.gu_send, r.gu_recv)
    spread(2, gu_all_cut)
    spread(3, dn_all_cut)


    def project(step, _):
        mine, other = gather_arrive(r.hid_all, r.h_send, r.h_recv, order(step))
        both = jnp.concatenate([r.hid_all[rows(mine, TOK), :], r.hid_all[rows(other, TOK), :]], axis=0)
        out = nn(both, r.w_all[...].reshape(D, RC))
        squares = out * out
        q_sum, k_sum = row_sums(squares[:, 0:RQ]), row_sums(squares[:, RQ : RQ + RK])
        upper = lax.broadcasted_iota(jnp.int32, (8, 2 * TOK), 0) < 4
        both_sums = jnp.where(upper, q_sum, k_sum)
        r.wide[rows(mine, TOK), 0:RC] = out[0:TOK]
        r.wide[rows(other, TOK), 0:RC] = out[TOK:]
        r.sums[mine] = both_sums[:, 0:TOK]
        r.sums[other] = both_sums[:, TOK:]
        return 0

    lax.fori_loop(0, 4, project, 0)
    exchange = SumExchange(r.sums, r.sums_land, r.sum_send, r.sum_recv)
    exchange.start()
    for i, to in enumerate(sources):
        source = to[1] * 4 + to[2]
        remote(
            gain_parts.at[0], r.gain_parts_land.at[source], r.gp_send.at[i], r.gp_recv.at[source], to
        ).wait_recv()
    gains = r.gain_parts_land[0].astype(F32)
    for i in range(1, 16):
        gains = gains + r.gain_parts_land[i].astype(F32)
    for i in range(3):
        r.gains[0:1, i * 128 : (i + 1) * 128] = gains[i : i + 1]
    for i in range(8):
        r.gains[1:2, i * 128 : (i + 1) * 128] = gains[3 + i : 4 + i]
        r.gains[2:3, i * 128 : (i + 1) * 128] = gains[11 + i : 12 + i]
    total = exchange.total()
    upper3 = lax.broadcasted_iota(jnp.int32, (8, 8, TOK), 1) < 4
    r.scales[...] = lax.rsqrt(jnp.where(upper3, total * (1.0 / QW), total * (1.0 / KW)) + NORM_EPS)

    def finish(b, _):
        at = rows(b, TOK)
        both = r.scales[b]
        q_scale, k_scale = column(both[0:1]), column(both[4:5])
        cosine, sine = r.cos[at, :], r.sin[at, :]
        for head in range(2):
            cols = slice(head * HEAD, (head + 1) * HEAD)
            q_unit = r.wide[at, cols] * q_scale
            r.unit[at, cols] = q_unit
            block, spot = token_block(r.q_rot, b, head)
            r.q_rot[block, spot, :] = rope(q_unit * r.gains[0:1, cols], cosine, sine).astype(BF)
        cols = slice(RQ, RQ + RK)
        k_unit = r.wide[at, cols] * k_scale
        r.unit[at, cols] = k_unit
        r.kv_own[0, at, :] = rope(k_unit * r.gains[0:1, cols], cosine, sine).astype(BF)
        r.kv_own[1, at, :] = r.wide[at, RQ + RK : RC].astype(BF)
        return 0

    lax.fori_loop(0, RANKS, finish, 0)

    kv_copy = remote(r.kv_own, r.kv_other, r.kv_send, r.kv_recv, partner)

    @pl.when(half == 0)
    def _():
        kv_copy.start()

    gather_finish(r.hid_all, r.h_send, r.h_recv)

    r.v_t[0] = jnp.transpose(r.kv_own[1].astype(F32)).astype(BF)

    def allowed_tile(block, key_base, diagonal):
        key_index = lax.broadcasted_iota(jnp.int32, (BLK, 2 * BLK), 0)
        allowed = key_index >= r.start[block, 0:1, :] - key_base
        if diagonal:
            lane = lax.broadcasted_iota(jnp.int32, (1, 2 * BLK), 1)
            allowed = allowed & (key_index <= lax.rem(lane, BLK))
        return allowed

    def tile(block, keys, values_t, key_base, carry):
        scores = nt(keys, r.q_rot[block]) * SCALE_TWO
        scores = jnp.where(allowed_tile(block, key_base, carry is None), scores, MASKED)
        top_now = jnp.max(scores, axis=0, keepdims=True)
        if carry is None:
            probs = jnp.exp2(scores - top_now)
            return top_now, jnp.sum(probs, axis=0, keepdims=True), nn(values_t, probs.astype(BF))
        top_old, run_old, acc_old = carry
        top_new = jnp.maximum(top_old, top_now)
        fade = jnp.exp2(top_old - top_new)
        probs = jnp.exp2(scores - top_new)
        return (
            top_new,
            run_old * fade + jnp.sum(probs, axis=0, keepdims=True),
            acc_old * fade + nn(values_t, probs.astype(BF)),
        )

    def keep_state(block, state):
        r.top[block] = jnp.broadcast_to(state[0], (8, 2 * BLK))
        r.running[block] = jnp.broadcast_to(state[1], (8, 2 * BLK))
        r.accum[block] = state[2]

    def local_block(block, _):
        def local_tile(j, carry):
            return tile(
                block, r.kv_own[0, rows(j, BLK), :], r.v_t[0, :, rows(j, BLK)], half * HALF + j * BLK, carry
            )

        keep_state(block, lax.fori_loop(0, block, local_tile, local_tile(block, None)))
        return 0

    lax.fori_loop(0, 4, local_block, 0)

    @pl.when(half == 1)
    def _():
        kv_copy.wait_recv()
        r.v_t[1] = jnp.transpose(r.kv_other[1].astype(F32)).astype(BF)

        def other_block(block, _):
            state = (r.top[block][0:1], r.running[block][0:1], r.accum[block])

            def other_tile(j, carry):
                return tile(block, r.kv_other[0, rows(j, BLK), :], r.v_t[1, :, rows(j, BLK)], j * BLK, carry)

            keep_state(block, lax.fori_loop(0, 4, other_tile, state))
            return 0

        lax.fori_loop(0, 4, other_block, 0)

    @pl.when(half == 0)
    def _():
        kv_copy.wait_send()

    def close_block(block, _):
        run = r.running[block]
        r.lse[block] = r.top[block] + jnp.log2(run)
        out = jnp.transpose(r.accum[block] * (1.0 / run[0:1]))
        r.mixed[block] = out
        for head in range(2):
            r.mixed_low[rows(block, BLK), head * HEAD : (head + 1) * HEAD] = out[
                head * BLK : (head + 1) * BLK
            ].astype(BF)
        return 0

    lax.fori_loop(0, 4, close_block, 0)

    wait_spread(1, pj_all_cut)
    gain_attn, gain_ffn = r.gains[1:2, :], r.gains[2:3, :]

    def both_rows(ref, mine, other):
        return jnp.concatenate([ref[rows(mine, TOK), :], ref[rows(other, TOK), :]], axis=0)

    s = Scatter(r, 0)

    def proj_step(step, _):
        off = lax.rem(step + 1, 4)
        at = lax.rem(o + off, 4)
        s.give(off, nn(both_rows(r.mixed_low, core * 4 + at, (1 - core) * 4 + at), r.pj_all[...].reshape(RQ, D)))

        @pl.when(step > 0)
        def _():
            s.send(step)

        return 0

    lax.fori_loop(0, 4, proj_step, 0)
    s.send(0)
    branch = s.result()
    branch_scale = rms_scale(branch)
    branch_unit = branch * branch_scale
    residual = hid[...].astype(F32) + branch_unit * gain_attn
    r.full_res[rows(rank, TOK), :] = residual.astype(BF)
    gather_start(r.full_res, r.a_send, r.a_recv)
    s.finish()
    wait_spread(2, gu_all_cut)
    wait_spread(3, dn_all_cut)

    s1 = Scatter(r, 1)

    def ffn_step(step, _):
        off = order(step)
        mine, other = gather_step(r.full_res, r.a_send, r.a_recv, step)
        both = nn(both_rows(r.full_res, mine, other), r.gu_all[...].reshape(D, 2 * RF))
        r.wide[rows(mine, TOK), :] = both[0:TOK]
        r.wide[rows(other, TOK), :] = both[TOK:]
        gate, up = both[:, 0:RF], both[:, RF:]
        act_low = (gate * jax.nn.sigmoid(gate) * up).astype(BF)
        r.act[rows(mine, TOK), :] = act_low[0:TOK]
        r.act[rows(other, TOK), :] = act_low[TOK:]

        @pl.when(step > 0)
        def _():
            s1.send(order(step - 1))

        s1.give(off, nn(act_low, r.dn_all[...].reshape(RF, D)))
        return 0

    lax.fori_loop(0, 4, ffn_step, 0)
    s1.send(2)
    ffn = s1.result()
    ffn_scale = rms_scale(ffn)
    ffn_unit = ffn * ffn_scale
    r.layer_out[...] = residual + ffn_unit * gain_ffn
    write(r.layer_out, layer_out)
    cotangent = cot[...].astype(F32)
    back_ffn = norm_back(cotangent, ffn_unit, ffn_scale, gain_ffn)
    r.full_ffn[rows(rank, TOK), :] = back_ffn.astype(BF)
    gather_start(r.full_ffn, r.b_send, r.b_recv)
    gain_row = jnp.sum(cotangent * ffn_unit, axis=0, keepdims=True)
    r.gain_rest[2:3, :] = gain_row[:, 0:512]
    r.gain_rest[3:4, :] = gain_row[:, 512:]
    gather_finish(r.full_res, r.a_send, r.a_recv)
    s1.finish()

    s2 = Scatter(r, 2)

    def back_step(step, _):
        off = order(step)
        mine, other = gather_step(r.full_ffn, r.b_send, r.b_recv, step)
        back_act = nt(both_rows(r.full_ffn, mine, other), r.dn_all[...].reshape(RF, D))
        both = both_rows(r.wide, mine, other)
        gate, up = both[:, 0:RF], both[:, RF:]
        sig = jax.nn.sigmoid(gate)
        back_gate = back_act * up * sig * (1.0 + gate * (1.0 - sig))
        back_up = back_act * (gate * sig)
        back_both = jnp.concatenate([back_gate, back_up], axis=1).astype(BF)
        r.back_gu[rows(mine, TOK), :] = back_both[0:TOK]
        r.back_gu[rows(other, TOK), :] = back_both[TOK:]

        @pl.when(step > 0)
        def _():
            s2.send(order(step - 1))

        s2.give(off, nt(back_both, r.gu_all[...].reshape(D, 2 * RF)))
        return 0

    lax.fori_loop(0, 4, back_step, 0)
    s2.send(2)

    def y_of(to):
        return lax.div(to[0], 2)

    def x_of(to):
        return lax.div(to[1], 2) * 2 + lax.rem(to[0], 2)

    here = (d, c, o)

    def fan_out(index, peers, place_of, cut, land):
        slot = place_of(here)
        for i, to in enumerate(peers):
            launch(remote(cut(to), land.at[slot], r.fan_send.at[index, i], r.fan_recv.at[index, slot], to))
        land[slot] = cut(here)[...]

    def fan_in(index, peers, place_of, land):
        for i, to in enumerate(peers):
            slot = place_of(to)
            remote(
                land.at[slot], land.at[slot], r.fan_send.at[index, i], r.fan_recv.at[index, slot], to
            ).wait_recv()
        total = land[0].astype(F32)
        for i in range(1, 4):
            total = total + land[i].astype(F32)
        return total

    r.dn_grad[...] = tn(r.act[...], r.full_ffn[...]).astype(BF)
    fan_out(
        0,
        along_x,
        x_of,
        lambda to: r.dn_grad.at[rows(lax.div(to[1], 2), 192), rows(lax.rem(to[0], 2), 512)],
        r.dn_x,
    )
    resid_grad = cotangent + s2.result()
    r.back_resid[...] = resid_grad
    write(r.back_resid, back_resid)
    gain_row = jnp.sum(resid_grad * branch_unit, axis=0, keepdims=True)
    r.gain_rest[0:1, :] = gain_row[:, 0:512]
    r.gain_rest[1:2, :] = gain_row[:, 512:]
    back_branch = norm_back(resid_grad, branch_unit, branch_scale, gain_attn)
    r.full_branch[rows(rank, TOK), :] = back_branch.astype(BF)
    gather_start(r.full_branch, r.e_send, r.e_recv)
    gather_finish(r.full_ffn, r.b_send, r.b_recv)
    s2.finish()

    def gu_step(b, _):
        grad = tn(r.full_res[:, rows(b, 128)], r.back_gu[...])
        r.gu_grad[lax.div(b, 4), rows(lax.rem(b, 4), 2)] = grad.astype(BF).reshape(2, 64, 2 * RF)
        return 0

    lax.fori_loop(0, 8, gu_step, 0)

    fan_out(1, along_y, y_of, lambda to: r.gu_grad.at[:, :, rows(y_of(to), 16)], r.gu_y)

    def mixed_step(step, _):
        mine, other = gather_step(r.full_branch, r.e_send, r.e_recv, step)
        out = nt(both_rows(r.full_branch, mine, other), r.pj_all[...].reshape(RQ, D)).astype(BF)
        for head in range(2):
            for i, b in enumerate((mine, other)):
                block, spot = token_block(r.back_mixed, b, head)
                r.back_mixed[block, spot, :] = out[i * TOK : (i + 1) * TOK, head * HEAD : (head + 1) * HEAD]
        return 0

    lax.fori_loop(0, 4, mixed_step, 0)
    r.pj_grad[...] = tn(r.mixed_low[...], r.full_branch[...]).astype(BF).reshape(2, 4, 2, 16, D)
    fan_out(2, along_x, x_of, lambda to: r.pj_grad.at[lax.div(to[1], 2), :, lax.rem(to[0], 2)], r.pj_x)
    gather_finish(r.full_branch, r.e_send, r.e_recv)

    def delta_step(block, _):
        r.delta[block] = row_sums(r.back_mixed[block].astype(F32) * r.mixed[block])
        r.back_q[block] = jnp.zeros((2 * BLK, HEAD), F32)
        return 0

    lax.fori_loop(0, 4, delta_step, 0)

    def back_tile(block, keys, values, key_base, diagonal, carry):
        grad_k, grad_v = carry
        query, grad_out = r.q_rot[block], r.back_mixed[block]
        scores = nt(keys, query) * SCALE_TWO
        probs = jnp.where(allowed_tile(block, key_base, diagonal), jnp.exp2(scores - r.lse[block, 0:1, :]), 0.0)
        back_prob = nt(values, grad_out)
        back_score = (probs * (back_prob - r.delta[block, 0:1, :])).astype(BF)
        grad_k = grad_k + nn(back_score, query)
        grad_v = grad_v + nn(probs.astype(BF), grad_out)
        r.back_q[block] += tn(back_score, keys)
        return grad_k, grad_v

    zero = (jnp.zeros((BLK, HEAD), F32), jnp.zeros((BLK, HEAD), F32))
    send_back = remote(r.other_grad, r.other_land, r.kvb_send, r.kvb_recv, partner)

    def local_keys(j, _):
        at = rows(j, BLK)
        keys, values = r.kv_own[0, at, :], r.kv_own[1, at, :]
        base = half * HALF + j * BLK
        grad_k, grad_v = lax.fori_loop(
            j + 1,
            4,
            lambda block, carry: back_tile(block, keys, values, base, False, carry),
            back_tile(j, keys, values, base, True, zero),
        )
        r.back_k[at, :] = grad_k * SCORE_SCALE
        r.back_v[at, :] = grad_v
        return 0

    def other_keys(j, _):
        at = rows(j, BLK)
        keys, values = r.kv_other[0, at, :], r.kv_other[1, at, :]
        grad_k, grad_v = lax.fori_loop(
            0, 4, lambda block, carry: back_tile(block, keys, values, j * BLK, False, carry), zero
        )
        r.other_grad[0, at, :] = (grad_k * SCORE_SCALE).astype(BF)
        r.other_grad[1, at, :] = grad_v.astype(BF)
        return 0

    def first_part(low, high):
        lax.fori_loop(low, low + (high - low) * (1 - half), local_keys, 0)
        lax.fori_loop(low, low + (high - low) * half, other_keys, 0)

    first_part(0, 2)

    r.dn_mid[...] = fan_in(0, along_x, x_of, r.dn_x).astype(BF)
    fan_out(3, along_y, y_of, lambda to: r.dn_mid.at[rows(y_of(to), 48)], r.dn_y)
    r.gu_mid[...] = fan_in(1, along_y, y_of, r.gu_y).astype(BF)
    fan_out(
        4,
        along_x,
        x_of,
        lambda to: r.gu_mid.at[lax.div(to[1], 2), :, :, rows(lax.rem(to[0], 2), RF)],
        r.gu_x,
    )
    r.pj_mid[...] = fan_in(2, along_x, x_of, r.pj_x).astype(BF)
    fan_out(5, along_y, y_of, lambda to: r.pj_mid.at[y_of(to)], r.pj_y)

    first_part(2, 4)

    @pl.when(half == 1)
    def _():
        send_back.start()

    r.dn_red[...] = fan_in(3, along_y, y_of, r.dn_y).astype(BF)
    r.gu_red[...] = fan_in(4, along_x, x_of, r.gu_x).astype(BF)
    r.pj_red[...] = fan_in(5, along_y, y_of, r.pj_y).astype(BF)
    target = 2 * rank + half
    to_owner = (d, lax.div(target, 4), lax.rem(target, 4))
    stay = target == place
    pj_move = remote(r.pj_red, r.pj_own, r.move_send.at[0], r.move_recv.at[0], to_owner)
    dn_move = remote(r.dn_red, r.dn_own, r.move_send.at[1], r.move_recv.at[1], to_owner)

    @pl.when(stay)
    def _():
        r.pj_own[...] = r.pj_red[...]
        r.dn_own[...] = r.dn_red[...]

    @pl.when(jnp.logical_not(stay))
    def _():
        pj_move.start()
        dn_move.start()

    for i, to in enumerate(ranks):
        launch(
            remote(
                r.gu_red.at[rank_of(to)],
                r.gu_own.at[:, rows(rank, RF)],
                r.gur_send.at[i],
                r.gur_recv.at[rank],
                to,
            )
        )
    r.gu_own[:, rows(rank, RF)] = r.gu_red[rank]

    lax.fori_loop(0, 2 * half, local_keys, 0)

    @pl.when(jnp.logical_not(stay))
    def _():
        pj_move.wait_send()
        dn_move.wait_send()
        pj_move.wait_recv()
        dn_move.wait_recv()

    for i, to in enumerate(ranks):
        remote(
            r.gu_red.at[0], r.gu_own.at[:, rows(rank_of(to), RF)], r.gur_send.at[i], r.gur_recv.at[rank_of(to)], sib
        ).wait_recv()

    def owned(n, e):
        e_part, e_side = lax.div(e, 2), lax.rem(e, 2)
        return (
            pj_sum.at[rows(e, 16), :],
            dn_sum.at[rows(e_part, 48), rows(e_side, 512)],
            gu_sum.at[rows(e_part, 16), rows(e_side, FF)],
            qkv_sum.at[rows(e_part, 16), rows(e_side, QW)],
        )[n]

    own_refs = (r.pj_own, r.dn_own, r.gu_own, r.qkv_own)
    for i, to in enumerate(owners):
        for n in range(3):
            launch(remote(own_refs[n], owned(n, d), r.y_send.at[n, i], r.y_recv.at[n, d], to))
    for n in range(3):
        write(own_refs[n], owned(n, d))

    lax.fori_loop(2 * half, 4 * half, local_keys, 0)

    @pl.when(half == 1)
    def _():
        send_back.wait_send()

    @pl.when(half == 0)
    def _():
        send_back.wait_recv()
        r.back_k[...] += r.other_land[0].astype(F32)
        r.back_v[...] += r.other_land[1].astype(F32)

    def weigh(b, _):
        at = rows(b, TOK)
        cosine, sine = r.cos[at, :], r.sin[at, :]
        totals = []
        for head in range(2):
            cols = slice(head * HEAD, (head + 1) * HEAD)
            block, spot = token_block(r.back_q, b, head)
            grad = unrope(r.back_q[block, spot, :] * SCORE_SCALE, cosine, sine)
            r.wide[at, cols] = grad
            totals.append(grad * r.gains[0:1, cols] * r.unit[at, cols])
        cols = slice(RQ, RQ + RK)
        grad = unrope(r.back_k[at, :], cosine, sine)
        r.wide[at, cols] = grad
        q_sum = row_sums(totals[0] + totals[1])
        k_sum = row_sums(grad * r.gains[0:1, cols] * r.unit[at, cols])
        upper = lax.broadcasted_iota(jnp.int32, (8, TOK), 0) < 4
        r.sums_back[b] = jnp.where(upper, q_sum, k_sum)
        return 0

    lax.fori_loop(0, RANKS, weigh, 0)
    exchange = SumExchange(r.sums_back, r.sums_back_land, r.sumb_send, r.sumb_recv)
    exchange.start()

    gain_own = jnp.sum(r.wide[:, 0 : RQ + RK] * r.unit[...], axis=0, keepdims=True)
    row = lax.broadcasted_iota(jnp.int32, (16, 512), 0)
    col = lax.broadcasted_iota(jnp.int32, (16, 512), 1)
    own_q, own_k = gain_own[:, 0:RQ], gain_own[:, RQ:]
    at_q = (row == lax.div(rank, 2)) & (lax.div(col, RQ) == lax.rem(rank, 2))
    at_k = (row == 4 + lax.div(rank, 4)) & (lax.div(col, RK) == lax.rem(rank, 4))
    r.gain_vec[...] = jnp.where(at_q, jnp.concatenate([own_q] * 2, axis=1), 0.0) + jnp.where(
        at_k, jnp.concatenate([own_k] * 4, axis=1), 0.0
    )
    r.gain_vec[6:10, :] = r.gain_rest[...]
    fan_out(6, along_y, y_of, lambda to: r.gain_vec, r.gain_y)

    total = exchange.total()
    r.sums_back[...] = jnp.where(upper3, total * (1.0 / QW), total * (1.0 / KW))

    def back_norm(b, _):
        at = rows(b, TOK)
        scale, mean = r.scales[b], r.sums_back[b]
        q_scale, k_scale = column(scale[0:1]), column(scale[4:5])
        q_mean, k_mean = column(mean[0:1]), column(mean[4:5])
        for head in range(2):
            cols = slice(head * HEAD, (head + 1) * HEAD)
            weighted = r.wide[at, cols] * r.gains[0:1, cols]
            r.back_qkv[at, cols] = (q_scale * (weighted - r.unit[at, cols] * q_mean)).astype(BF)
        cols = slice(RQ, RQ + RK)
        weighted = r.wide[at, cols] * r.gains[0:1, cols]
        r.back_qkv[at, cols] = (k_scale * (weighted - r.unit[at, cols] * k_mean)).astype(BF)
        r.back_qkv[at, RQ + RK : RC] = r.back_v[at, :].astype(BF)
        return 0

    lax.fori_loop(0, RANKS, back_norm, 0)

    def grad_step(b, _):
        grad = tn(r.hid_all[:, rows(b, 128)], r.back_qkv[...])
        r.qkv_grad[lax.div(b, 4), rows(lax.rem(b, 4), 2)] = grad.astype(BF).reshape(2, 64, RC)
        return 0

    lax.fori_loop(0, 8, grad_step, 0)

    def qkv_cut(e, h):
        return h, slice(None), rows(lax.div(e, 2), 16), rows(lax.rem(e, 2), RQ)

    old = list(done)
    done.clear()

    def drain_old():
        for copy in old:
            copy.wait_send()

        @pl.when(jnp.logical_not(keep))
        def _():
            pj_near.wait_send()
            dn_near.wait_send()

    slot = plane_slot(d, c)
    for i, to in enumerate(planes):
        src = r.qkv_grad.at[qkv_cut(to[0], lax.div(to[1], 2))]
        launch(remote(src, r.qkv_land.at[slot], r.plane_send.at[i], r.plane_recv.at[slot], to))
    r.qkv_land[slot] = r.qkv_grad[qkv_cut(d, half)]
    r.gain_half[...] = fan_in(6, along_y, y_of, r.gain_y)
    fan_out(7, along_x, x_of, lambda to: r.gain_half, r.gain_x)

    s3 = Scatter(r, 3)

    def input_step(step, _):
        off = lax.rem(step + 1, 4)
        at = lax.rem(o + off, 4)
        s3.give(off, nt(both_rows(r.back_qkv, core * 4 + at, (1 - core) * 4 + at), r.w_all[...].reshape(D, RC)))

        @pl.when(step > 0)
        def _():
            s3.send(step)

        return 0

    lax.fori_loop(0, 4, input_step, 0)
    s3.send(0)
    drain_old()

    total = fan_in(7, along_x, x_of, r.gain_x)
    r.gain_mid[...] = total
    for i, to in enumerate(ranks):
        launch(remote(r.gain_mid, r.gain_last.at[rank], r.gl_send.at[i], r.gl_recv.at[rank], to))
    r.gain_last[rank] = total

    for i, to in enumerate(planes):
        source = plane_slot(to[0], to[1])
        land = r.qkv_land.at[source]
        remote(land, land, r.plane_send.at[i], r.plane_recv.at[source], to).wait_recv()
    total = r.qkv_land[0].astype(F32)
    for i in range(1, 16):
        total = total + r.qkv_land[i].astype(F32)
    r.qkv_red[...] = total.astype(BF)

    def qkv_cols(of_rank, i):
        return rows((1 - side) * (of_rank * 2 + i) + side * (of_rank + i * 8), RK)

    for i, to in enumerate(ranks):
        for j in range(2):
            launch(
                remote(
                    r.qkv_red.at[rank_of(to), :, pl.ds(j * RK, RK)],
                    r.qkv_own.at[:, qkv_cols(rank, j)],
                    r.qr_send.at[j, i],
                    r.qr_recv.at[j, rank],
                    to,
                )
            )
    for j in range(2):
        r.qkv_own[:, qkv_cols(rank, j)] = r.qkv_red[rank][:, j * RK : (j + 1) * RK]

    r.input_part[...] = s3.result()
    write(r.input_part, input_part)
    for i, to in enumerate(ranks):
        remote(
            r.gain_mid, r.gain_last.at[rank_of(to)], r.gl_send.at[i], r.gl_recv.at[rank_of(to)], sib
        ).wait_recv()
    total = r.gain_last[0]
    for i in range(1, 8):
        total = total + r.gain_last[i]
    for i in range(40):
        gain_sum[i : i + 1, :] = total[i // 4 : i // 4 + 1, (i % 4) * 128 : (i % 4 + 1) * 128]

    for i, to in enumerate(ranks):
        for j in range(2):
            remote(
                r.qkv_red.at[0, :, pl.ds(j * RK, RK)],
                r.qkv_own.at[:, qkv_cols(rank_of(to), j)],
                r.qr_send.at[j, i],
                r.qr_recv.at[j, rank_of(to)],
                sib,
            ).wait_recv()
    for i, to in enumerate(owners):
        launch(remote(r.qkv_own, owned(3, d), r.y_send.at[3, i], r.y_recv.at[3, d], to))
    write(r.qkv_own, owned(3, d))
    for i, to in enumerate(owners):
        for n in range(4):
            remote(own_refs[n], owned(n, to[0]), r.y_send.at[n, i], r.y_recv.at[n, to[0]], sib).wait_recv()
    s3.finish()
    drain()
    for copy in writes:
        copy.wait()


def call_layer(*operands):
    any_space = pl.BlockSpec(memory_space=pl.ANY)
    return pl.pallas_call(
        layer_kernel,
        name="layer",
        out_shape=(
            jax.ShapeDtypeStruct((TOK, D), F32),
            jax.ShapeDtypeStruct((TOK, D), F32),
            jax.ShapeDtypeStruct((TOK, D), F32),
            jax.ShapeDtypeStruct((64, QW + 2 * KW), BF),
            jax.ShapeDtypeStruct((64, 2 * FF), BF),
            jax.ShapeDtypeStruct((128, D), BF),
            jax.ShapeDtypeStruct((192, D), BF),
            jax.ShapeDtypeStruct((40, 128), F32),
        ),
        in_specs=[VMEM] * 4 + [any_space] * 4,
        out_specs=[any_space] * 7 + [VMEM],
        scratch_shapes=list(SCRATCH.values()),
        compiler_params=pltpu.CompilerParams(
            collective_id=1, has_side_effects=True, vmem_limit_bytes=63 * 2**20
        ),
    )(*operands)


def adam_step(weight, moment, square, grad_sum, rate, decay):
    moment_new = BETA_ONE * moment + (1.0 - BETA_ONE) * grad_sum
    square_new = BETA_TWO * square + (1.0 - BETA_TWO) * grad_sum * grad_sum
    moment_hat = moment_new / (1.0 - BETA_ONE**STEP)
    square_hat = square_new / (1.0 - BETA_TWO**STEP)
    weight_new = weight - rate * (moment_hat / (jnp.sqrt(square_hat) + ADAM_EPS) + decay * weight)
    return (weight_new, moment_new, square_new)


def update_kernel(*refs):
    ins, outs = refs[:19], refs[19:]
    layer_out, back_resid, input_part = ins[:3]
    outs[0][...] = layer_out[...].astype(BF)
    outs[1][...] = back_resid[...] + input_part[...]
    for i in range(4):
        weight, moment, square, grad = (ref[...] for ref in ins[3 + 4 * i : 7 + 4 * i])
        new = adam_step(weight, moment, square, grad.astype(F32), RATE_MATRIX, DECAY)
        for ref, value in zip(outs[2 + 3 * i : 5 + 3 * i], new):
            ref[...] = value


def call_update(*operands):
    def half_rows(shape):
        return pl.BlockSpec((shape[0] // 2, shape[1]), lambda i: (i, 0))

    results = [operands[0], operands[1]] + [operands[3 + 4 * i + j] for i in range(4) for j in range(3)]
    types_out = [BF] + [F32] * 13
    return pl.pallas_call(
        update_kernel,
        name="update",
        grid=(2,),
        out_shape=[jax.ShapeDtypeStruct(a.shape, t) for a, t in zip(results, types_out)],
        in_specs=[half_rows(a.shape) for a in operands],
        out_specs=[half_rows(a.shape) for a in results],
        compiler_params=pltpu.CompilerParams(vmem_limit_bytes=62 * 2**20),
    )(*operands)


def per_device(
    hidden_in,
    segment_ids,
    out_cotangent,
    qkv_weight,
    qkv_moment,
    qkv_square,
    proj_weight,
    proj_moment,
    proj_square,
    gate_up_weight,
    gate_up_moment,
    gate_up_square,
    down_weight,
    down_moment,
    down_square,
    gains,
    gain_moment,
    gain_square,
):
    _, c, o = coords()
    place = c * 4 + o
    placed = lax.dynamic_update_slice_in_dim(
        jnp.zeros((QW + KW + 2 * D,), BF), gains.astype(BF), place * gains.shape[0], axis=0
    )
    gain_parts = jnp.concatenate(
        [
            placed[:QW].reshape(RANKS, 2, 128),
            placed[QW : QW + KW].reshape(RANKS, 1, 128),
            jnp.broadcast_to(placed[QW + KW :].reshape(1, 16, 128), (RANKS, 16, 128)),
            jnp.zeros((RANKS, 13, 128), BF),
        ],
        axis=1,
    )
    layer_out, back_resid, input_part, qkv_sum, gu_sum, pj_sum, dn_sum, gain_sum = call_layer(
        hidden_in, out_cotangent, segment_ids, gain_parts, qkv_weight, gate_up_weight, proj_weight, down_weight
    )
    gain_grad = lax.dynamic_slice_in_dim(
        gain_sum.reshape(40 * 128), place * gains.shape[0], gains.shape[0]
    )
    updated = call_update(
        layer_out, back_resid, input_part,
        qkv_weight, qkv_moment, qkv_square, qkv_sum,
        proj_weight, proj_moment, proj_square, pj_sum,
        gate_up_weight, gate_up_moment, gate_up_square, gu_sum,
        down_weight, down_moment, down_square, dn_sum,
    )
    return tuple(updated) + adam_step(gains, gain_moment, gain_square, gain_grad, RATE_GAIN, 0.0)


def solution(mesh):
    seq = P(("dp", "ctx", "opt"), None)
    mat = P(("ctx", "opt"), None)
    vec = P(("ctx", "opt"))
    return jax.shard_map(
        per_device,
        mesh=mesh,
        in_specs=(seq, P("dp", None), seq) + (mat,) * 12 + (vec,) * 3,
        out_specs=(seq, seq) + (mat,) * 12 + (vec,) * 3,
        check_vma=False,
    )
```

```python
import math
import types

import jax
import jax.numpy as jnp
from jax import lax
from jax.experimental import pallas as pl
from jax.experimental.pallas import tpu as pltpu
from jax.sharding import PartitionSpec as P

D = 1024
FF = 3072
HEADS = 16
KV_HEADS = 8
HEAD = 128
STEP = 10

NORM_EPS = 1e-06
THETA = 500000.0
MASKED = -1e30
BETA_ONE = 0.9
BETA_TWO = 0.95
ADAM_EPS = 1e-08
RATE_MATRIX = 0.06
RATE_GAIN = 1.0
DECAY = 0.1

TOK = 128
HALF = 1024
RANKS = 8
QW = HEADS * HEAD
KW = KV_HEADS * HEAD
RQ = 256
RK = 128
RC = RQ + 2 * RK
RF = FF // RANKS
BLK = 256
SCORE_SCALE = 1.0 / math.sqrt(HEAD)
SCALE_TWO = SCORE_SCALE * math.log2(math.e)

MESH = pl.DeviceIdType.MESH
BF = jnp.bfloat16
F32 = jnp.float32
VMEM = pl.BlockSpec(memory_space=pltpu.VMEM)
DMA = pltpu.SemaphoreType.DMA


def coords():
    return lax.axis_index("dp"), lax.axis_index("ctx"), lax.axis_index("opt")


def sibling(c):
    return c + 1 - 2 * lax.rem(c, 2)


def rank_peer(d, c, o, t):
    flip = t // 4
    return (d, c + (1 - 2 * lax.rem(c, 2)) * flip, lax.rem(o + t % 4, 4))


def cross_peer(d, c, o, t):
    return rank_peer(d + 1 - 2 * lax.rem(d, 2), lax.rem(c + 2, 4), o, t)


def plane_peer(d, c, o, t):
    x_lo, y = lax.rem(d, 2), lax.div(d, 2)
    y = lax.rem(y + t // 4, 4)
    x_lo = x_lo + (1 - 2 * x_lo) * (t % 2)
    return (2 * y + x_lo, lax.rem(c + 2 * ((t % 4) // 2), 4), o)


def group_peer(d, c, o, t):
    return (d, lax.rem(c + t // 4, 4), lax.rem(o + t % 4, 4))


def dp_peer(d, c, o, t):
    return (lax.rem(d + t, 8), c, o)


def greet(peers):
    barrier = pltpu.get_barrier_semaphore()
    for to in peers:
        pl.semaphore_signal(barrier, inc=1, device_id=to, device_id_type=MESH)
    return lambda: pl.semaphore_wait(barrier, len(peers))


def remote(src, dst, send, recv, to):
    return pltpu.make_async_remote_copy(
        src_ref=src, dst_ref=dst, send_sem=send, recv_sem=recv, device_id=to, device_id_type=MESH
    )


def rows(index, count):
    return pl.ds(pl.multiple_of(index * count, count), count)


def nn(a, b):
    return lax.dot_general(a, b, (((1,), (0,)), ((), ())), preferred_element_type=F32)


def nt(a, b):
    return lax.dot_general(a, b, (((1,), (1,)), ((), ())), preferred_element_type=F32)


def tn(a, b):
    return lax.dot_general(a, b, (((0,), (0,)), ((), ())), preferred_element_type=F32)


def row_sums(values):
    ones = jnp.ones((8, values.shape[1]), F32)
    return lax.dot_general(
        ones,
        values,
        (((1,), (1,)), ((), ())),
        precision=lax.Precision.HIGHEST,
        preferred_element_type=F32,
    )


def column(row):
    return jnp.transpose(jnp.broadcast_to(row, (128, 128)))


def rms_scale(values):
    return lax.rsqrt(jnp.mean(values * values, axis=-1, keepdims=True) + NORM_EPS)


def norm_back(grad_rows, unit_rows, scale_rows, gain_row):
    weighted = grad_rows * gain_row
    return scale_rows * (
        weighted - unit_rows * jnp.mean(weighted * unit_rows, axis=-1, keepdims=True)
    )


def rope(u, cos, sin):
    return u * cos + pltpu.roll(u, HEAD // 2, 1) * sin


def unrope(g, cos, sin):
    return g * cos - pltpu.roll(g, HEAD // 2, 1) * sin


def gather_start(full, send, recv):
    d, c, o = coords()
    rank = lax.rem(c, 2) * 4 + o
    own = full.at[rows(rank, TOK)]
    for t in (1, 3):
        remote(own, own, send.at[t], recv.at[rank], (d, c, lax.rem(o + t, 4))).start()
    remote(own, own, send.at[0], recv.at[rank], (d, sibling(c), o)).start()


def gather_relay(full, send, recv):
    d, c, o = coords()
    core = lax.rem(c, 2)
    to = (d, sibling(c), o)
    for off, part in ((1, 1), (3, 0)):
        mine = core * 4 + lax.rem(o + off, 4)
        block = full.at[rows(mine, TOK)]
        half = full.at[rows(mine * 2 + part, TOK // 2)]
        remote(block, block, send.at[off], recv.at[mine], to).wait_recv()
        landed = recv.at[8] if part else recv.at[mine]
        remote(half, half, send.at[2 + 5 * part], landed, (d, c, lax.rem(o + 4 - off, 4))).start()
        remote(block, block, send.at[3 + off], recv.at[mine], to).start()


def gather_arrive(full, send, recv, off):
    d, c, o = coords()
    core = lax.rem(c, 2)
    at = lax.rem(o + off, 4)
    mine, other = core * 4 + at, (1 - core) * 4 + at
    to = (d, sibling(c), o)
    block = full.at[rows(mine, TOK)]

    @pl.when(off == 2)
    def _():
        for part in range(2):
            half = full.at[rows(mine * 2 + part, TOK // 2)]
            landed = recv.at[8] if part else recv.at[mine]
            remote(half, half, send.at[2], landed, to).wait_recv()
        remote(block, block, send.at[5], recv.at[mine], to).start()

    block = full.at[rows(other, TOK)]
    remote(block, block, send.at[0], recv.at[other], to).wait_recv()
    return mine, other


def gather_step(full, send, recv, step):
    @pl.when(step == 1)
    def _():
        gather_relay(full, send, recv)

    return gather_arrive(full, send, recv, order(step))


def gather_finish(full, send, recv):
    d, c, o = coords()
    for i in range(8):
        part = full.at[rows(0, TOK // 2 if i in (2, 7) else TOK)]
        remote(part, part, send.at[i], recv.at[0], (d, sibling(c), o)).wait_send()


class Scatter:
    def __init__(self, r, index):
        self.stage_s, self.stage_z, self.own = r.stage_s, r.stage_z, r.own
        self.land_s, self.land_z = r.land_s.at[index % 2], r.land_z.at[index % 2]
        self.send_s, self.recv_s = r.send_s.at[index], r.recv_s.at[index]
        self.send_z, self.recv_z = r.send_z.at[index], r.recv_z.at[index]

    def near(self, off):
        d, c, o = coords()
        return remote(
            self.stage_s.at[off], self.land_s.at[off], self.send_s.at[off], self.recv_s.at[off], (d, sibling(c), o)
        )

    def along(self, off):
        d, c, o = coords()
        return remote(
            self.stage_z.at[off - 1],
            self.land_z.at[off - 1],
            self.send_z.at[off],
            self.recv_z.at[off],
            (d, c, lax.rem(o + off, 4)),
        )

    def give(self, off, part):
        self.stage_s[off] = part[TOK:].astype(BF)
        self.near(off).start()
        self.own[off] = part[0:TOK]

    def send(self, off):
        self.near(off).wait_recv()
        total = self.own[off] + self.land_s[off].astype(F32)

        @pl.when(off > 0)
        def _():
            self.stage_z[off - 1] = total.astype(BF)
            self.along(off).start()

        @pl.when(off == 0)
        def _():
            self.own[0] = total

    def result(self):
        total = self.own[0]
        for off in (1, 3, 2):
            self.along(off).wait_recv()
            total = total + self.land_z[off - 1].astype(F32)
        return total

    def finish(self):
        for off in range(4):
            self.near(off).wait_send()
        for off in range(1, 4):
            self.along(off).wait_send()


def order(step):
    return step + lax.div(step, 2) - 2 * lax.div(step, 3)


class SumExchange:
    def __init__(self, sums, land, send, recv):
        self.sums, self.land, self.send, self.recv = sums, land, send, recv

    def start(self):
        d, c, o = coords()
        rank = lax.rem(c, 2) * 4 + o
        self.land[rank] = self.sums[...]
        self.copies = []
        for t in range(1, 8):
            copy = remote(
                self.sums, self.land.at[rank], self.send.at[t], self.recv.at[rank], rank_peer(d, c, o, t)
            )
            copy.start()
            self.copies.append(copy)

    def total(self):
        d, c, o = coords()
        for t in range(1, 8):
            _, c1, o1 = rank_peer(d, c, o, t)
            source = lax.rem(c1, 2) * 4 + o1
            remote(
                self.sums, self.land.at[source], self.send.at[t], self.recv.at[source], (d, sibling(c), o)
            ).wait_recv()
        for copy in self.copies:
            copy.wait_send()
        total = self.land[0]
        for i in range(1, 8):
            total = total + self.land[i]
        return total


def plane_slot(d, c):
    return lax.div(c, 2) * 8 + d


def token_block(ref, b, head):
    at = pl.multiple_of(head * BLK + lax.rem(b, 2) * TOK, TOK)
    return lax.div(b, 2), pl.ds(at, TOK)


SCRATCH = dict(
    w_raw=pltpu.VMEM((16, QW + 2 * KW), F32),
    gu_raw=pltpu.VMEM((16, 2 * FF), F32),
    pj_raw=pltpu.VMEM((32, D), F32),
    dn_raw=pltpu.VMEM((48, D), F32),
    pieces=pltpu.VMEM((RANKS, 16, RC), BF),
    gu_pieces=pltpu.VMEM((RANKS, 16, 2 * RF), BF),
    pj_mine=pltpu.VMEM((32, D), BF),
    dn_mine=pltpu.VMEM((48, D), BF),
    w_all=pltpu.VMEM((16, 64, RC), BF),
    gu_all=pltpu.VMEM((16, 64, 2 * RF), BF),
    pj_all=pltpu.VMEM((2, 128, D), BF),
    dn_all=pltpu.VMEM((2, 192, D), BF),
    gain_parts_land=pltpu.VMEM((16, 32, 128), BF),
    gains=pltpu.VMEM((8, D), F32),
    cos=pltpu.VMEM((HALF, HEAD), F32),
    sin=pltpu.VMEM((HALF, HEAD), F32),
    start=pltpu.VMEM((4, 8, 2 * BLK), jnp.int32),
    hid_all=pltpu.VMEM((HALF, D), BF),
    unit=pltpu.VMEM((HALF, RQ + RK), F32),
    sums=pltpu.VMEM((8, 8, TOK), F32),
    sums_land=pltpu.VMEM((8, 8, 8, TOK), F32),
    sums_back=pltpu.VMEM((8, 8, TOK), F32),
    sums_back_land=pltpu.VMEM((8, 8, 8, TOK), F32),
    scales=pltpu.VMEM((8, 8, TOK), F32),
    q_rot=pltpu.VMEM((4, 2 * BLK, HEAD), BF),
    kv_own=pltpu.VMEM((2, HALF, HEAD), BF),
    kv_other=pltpu.VMEM((2, HALF, HEAD), BF),
    v_t=pltpu.VMEM((2, HEAD, HALF), BF),
    top=pltpu.VMEM((4, 8, 2 * BLK), F32),
    running=pltpu.VMEM((4, 8, 2 * BLK), F32),
    accum=pltpu.VMEM((4, HEAD, 2 * BLK), F32),
    mixed=pltpu.VMEM((4, 2 * BLK, HEAD), F32),
    mixed_low=pltpu.VMEM((HALF, RQ), BF),
    lse=pltpu.VMEM((4, 8, 2 * BLK), F32),
    delta=pltpu.VMEM((4, 8, 2 * BLK), F32),
    full_res=pltpu.VMEM((HALF, D), BF),
    full_ffn=pltpu.VMEM((HALF, D), BF),
    full_branch=pltpu.VMEM((HALF, D), BF),
    wide=pltpu.VMEM((HALF, 2 * RF), F32),
    act=pltpu.VMEM((HALF, RF), BF),
    back_gu=pltpu.VMEM((HALF, 2 * RF), BF),
    stage_s=pltpu.VMEM((4, TOK, D), BF),
    stage_z=pltpu.VMEM((3, TOK, D), BF),
    own=pltpu.VMEM((4, TOK, D), F32),
    land_s=pltpu.VMEM((2, 4, TOK, D), BF),
    land_z=pltpu.VMEM((2, 3, TOK, D), BF),
    gain_rest=pltpu.VMEM((4, 512), F32),
    back_mixed=pltpu.VMEM((4, 2 * BLK, HEAD), BF),
    back_q=pltpu.VMEM((4, 2 * BLK, HEAD), F32),
    back_k=pltpu.VMEM((HALF, HEAD), F32),
    back_v=pltpu.VMEM((HALF, HEAD), F32),
    other_grad=pltpu.VMEM((2, HALF, HEAD), BF),
    other_land=pltpu.VMEM((2, HALF, HEAD), BF),
    back_qkv=pltpu.VMEM((HALF, RC), BF),
    pj_grad=pltpu.VMEM((2, 4, 2, 16, D), BF),
    gu_grad=pltpu.VMEM((2, 8, 64, 2 * RF), BF),
    dn_grad=pltpu.VMEM((RF, D), BF),
    qkv_grad=pltpu.VMEM((2, 8, 64, RC), BF),
    pj_x=pltpu.VMEM((4, 4, 16, D), BF),
    pj_mid=pltpu.VMEM((4, 16, D), BF),
    pj_y=pltpu.VMEM((4, 16, D), BF),
    dn_x=pltpu.VMEM((4, 192, 512), BF),
    dn_mid=pltpu.VMEM((192, 512), BF),
    dn_y=pltpu.VMEM((4, 48, 512), BF),
    gu_y=pltpu.VMEM((4, 2, 8, 16, 2 * RF), BF),
    gu_mid=pltpu.VMEM((2, 8, 16, 2 * RF), BF),
    gu_x=pltpu.VMEM((4, 8, 16, RF), BF),
    qkv_land=pltpu.VMEM((16, 8, 16, RQ), BF),
    pj_red=pltpu.VMEM((16, D), BF),
    gu_red=pltpu.VMEM((8, 16, RF), BF),
    dn_red=pltpu.VMEM((48, 512), BF),
    qkv_red=pltpu.VMEM((8, 16, RQ), BF),
    pj_own=pltpu.VMEM((16, D), BF),
    gu_own=pltpu.VMEM((16, FF), BF),
    dn_own=pltpu.VMEM((48, 512), BF),
    qkv_own=pltpu.VMEM((16, QW), BF),
    gain_vec=pltpu.VMEM((16, 512), F32),
    gain_y=pltpu.VMEM((4, 16, 512), F32),
    gain_half=pltpu.VMEM((16, 512), F32),
    gain_x=pltpu.VMEM((4, 16, 512), F32),
    gain_mid=pltpu.VMEM((16, 512), F32),
    gain_last=pltpu.VMEM((8, 16, 512), F32),
    layer_out=pltpu.VMEM((TOK, D), F32),
    back_resid=pltpu.VMEM((TOK, D), F32),
    input_part=pltpu.VMEM((TOK, D), F32),
    write_sem=DMA((4,)),
    kept_sem=DMA((3,)),
    raw_sem=DMA((4,)),
    h_send=DMA((8,)),
    h_recv=DMA((9,)),
    w_send=DMA((15,)),
    w_recv=DMA((16,)),
    gp_send=DMA((15,)),
    gp_recv=DMA((16,)),
    sum_send=DMA((8,)),
    sum_recv=DMA((8,)),
    sumb_send=DMA((8,)),
    sumb_recv=DMA((8,)),
    kv_send=DMA,
    kv_recv=DMA,
    gu_send=DMA((15,)),
    gu_recv=DMA((16,)),
    yw_send=DMA((4, 3)),
    yw_recv=DMA((4, 4)),
    pj_send=DMA((2,)),
    pj_recv=DMA((2,)),
    dn_send=DMA((2,)),
    dn_recv=DMA((2,)),
    send_s=DMA((4, 4)),
    recv_s=DMA((4, 4)),
    send_z=DMA((4, 4)),
    recv_z=DMA((4, 4)),
    a_send=DMA((8,)),
    a_recv=DMA((9,)),
    b_send=DMA((8,)),
    b_recv=DMA((9,)),
    e_send=DMA((8,)),
    e_recv=DMA((9,)),
    kvb_send=DMA((2,)),
    kvb_recv=DMA((2,)),
    plane_send=DMA((15,)),
    plane_recv=DMA((16,)),
    fan_send=DMA((8, 3)),
    fan_recv=DMA((8, 4)),
    move_send=DMA((2,)),
    move_recv=DMA((2,)),
    gur_send=DMA((7,)),
    gur_recv=DMA((8,)),
    qr_send=DMA((2, 7)),
    qr_recv=DMA((2, 8)),
    gl_send=DMA((7,)),
    gl_recv=DMA((8,)),
    y_send=DMA((4, 7)),
    y_recv=DMA((4, 8)),
)


def layer_kernel(hid, cot, segments, gain_parts, w_rows, gu_rows, pj_rows, dn_rows, *refs):
    layer_out, back_resid, input_part, qkv_sum, gu_sum, pj_sum, dn_sum, gain_sum = refs[:8]
    writes = []
    r = types.SimpleNamespace(**dict(zip(SCRATCH, refs[8:])))
    d, c, o = coords()
    half, core = lax.div(c, 2), lax.rem(c, 2)
    rank = core * 4 + o
    place = c * 4 + o
    part, side = lax.div(d, 2), lax.rem(d, 2)
    sib = (d, sibling(c), o)
    partner = (d, lax.rem(c + 2, 4), o)
    ranks = [rank_peer(d, c, o, t) for t in range(1, 8)]
    sources = ranks + [cross_peer(d, c, o, t) for t in range(8)]
    planes = [plane_peer(d, c, o, t) for t in range(1, 16)]
    owners = [dp_peer(d, c, o, t) for t in range(1, 8)]
    group = [group_peer(d, c, o, t) for t in range(1, 16)]
    crosses = [cross_peer(d, c, o, t) for t in range(8)]
    along_y = [(lax.rem(d + 2 * t, 8), c, o) for t in range(1, 4)]
    along_x = [plane_peer(d, c, o, t) for t in range(1, 4)]
    done = []

    def launch(copy):
        copy.start()
        done.append(copy)

    def write(src, dst):
        copy = pltpu.make_async_copy(src, dst, r.write_sem.at[len(writes)])
        copy.start()
        writes.append(copy)

    def drain():
        for copy in done:
            copy.wait_send()
        done.clear()

    def rank_of(to):
        return lax.rem(to[1], 2) * 4 + to[2]

    raws = [
        pltpu.make_async_copy(src.at[rows(part, dst.shape[0])], dst, r.raw_sem.at[i])
        for i, (src, dst) in enumerate(
            ((w_rows, r.w_raw), (pj_rows, r.pj_raw), (gu_rows, r.gu_raw), (dn_rows, r.dn_raw))
        )
    ]
    for copy in raws:
        copy.start()
    all_here = greet(group + planes + crosses)
    r.hid_all[rows(rank, TOK), :] = hid[...]
    raws[0].wait()
    for g in range(RANKS):
        r.pieces[g, :, 0:RQ] = r.w_raw[:, g * RQ : (g + 1) * RQ].astype(BF)
        r.pieces[g, :, RQ : RQ + RK] = r.w_raw[:, QW + g * RK : QW + (g + 1) * RK].astype(BF)
        r.pieces[g, :, RQ + RK : RC] = r.w_raw[:, QW + KW + g * RK : QW + KW + (g + 1) * RK].astype(BF)
    all_here()

    def piece_rows(ref, source):
        return ref.at[source, rows(part, 16)]

    def send_pieces(pieces, ref, send, recv):
        for i, to in enumerate(sources):
            launch(remote(pieces.at[rank_of(to)], piece_rows(ref, place), send.at[i], recv.at[place], to))
        ref[place, rows(part, 16)] = pieces[rank]

    def wait_pieces(pieces, ref, send, recv):
        for i, to in enumerate(sources):
            source = to[1] * 4 + to[2]
            remote(pieces.at[0], piece_rows(ref, source), send.at[i], recv.at[source], to).wait_recv()

    def spread(index, cut):
        for i, to in enumerate(along_y):
            launch(remote(cut(part), cut(part), r.yw_send.at[index, i], r.yw_recv.at[index, part], to))

    def wait_spread(index, cut):
        for i, to in enumerate(along_y):
            y = lax.div(to[0], 2)
            remote(cut(y), cut(y), r.yw_send.at[index, i], r.yw_recv.at[index, y], to).wait_recv()

    def w_cut(y):
        return r.w_all.at[:, rows(y, 16)]

    def gu_all_cut(y):
        return r.gu_all.at[:, rows(y, 16)]

    def pj_all_cut(y):
        return r.pj_all.at[:, rows(y, 32)]

    def dn_all_cut(y):
        return r.dn_all.at[:, rows(y, 48)]

    to_rank = lax.div(place, 2)
    slot = lax.rem(place, 2)
    near = (d, half * 2 + lax.div(to_rank, 4), lax.rem(to_rank, 4))
    far = (d + 1 - 2 * lax.rem(d, 2), (1 - half) * 2 + lax.div(to_rank, 4), lax.rem(to_rank, 4))
    pj_slot, dn_slot = r.pj_all.at[slot, rows(part, 32)], r.dn_all.at[slot, rows(part, 48)]
    keep = to_rank == rank
    pj_near = remote(r.pj_mine, pj_slot, r.pj_send.at[0], r.pj_recv.at[slot], near)
    dn_near = remote(r.dn_mine, dn_slot, r.dn_send.at[0], r.dn_recv.at[slot], near)

    def send_rows():
        @pl.when(jnp.logical_not(keep))
        def _():
            pj_near.start()
            dn_near.start()

        @pl.when(keep)
        def _():
            r.pj_all[slot, rows(part, 32)] = r.pj_mine[...]
            r.dn_all[slot, rows(part, 48)] = r.dn_mine[...]

        launch(remote(r.pj_mine, pj_slot, r.pj_send.at[1], r.pj_recv.at[slot], far))
        launch(remote(r.dn_mine, dn_slot, r.dn_send.at[1], r.dn_recv.at[slot], far))

    def wait_rows():
        for i in range(2):
            from_self = 2 * rank + i == place

            @pl.when(jnp.logical_not(from_self))
            def _(i=i):
                pj_at, dn_at = r.pj_all.at[i, rows(part, 32)], r.dn_all.at[i, rows(part, 48)]
                remote(r.pj_mine, pj_at, r.pj_send.at[0], r.pj_recv.at[i], partner).wait_recv()
                remote(r.dn_mine, dn_at, r.dn_send.at[0], r.dn_recv.at[i], partner).wait_recv()

    send_pieces(r.pieces, r.w_all, r.w_send, r.w_recv)
    gather_start(r.hid_all, r.h_send, r.h_recv)
    for i, to in enumerate(sources):
        launch(
            remote(
                gain_parts.at[rank_of(to)], r.gain_parts_land.at[place], r.gp_send.at[i], r.gp_recv.at[place], to
            )
        )
    r.gain_parts_land[place] = gain_parts[rank]
    ids = segments[...]
    own_ids = segments[:, rows(half, HALF)]
    starts = jnp.zeros((1, HALF), jnp.int32)
    for i in range(1, 6):
        below = jnp.sum((ids < i).astype(F32), axis=1, keepdims=True).astype(jnp.int32)
        starts = jnp.where(own_ids == i, below, starts)
    for block in range(4):
        row = starts[:, block * BLK : (block + 1) * BLK]
        r.start[block] = jnp.broadcast_to(jnp.concatenate([row, row], axis=1), (8, 2 * BLK))
    lane = lax.broadcasted_iota(jnp.int32, (1, HEAD), 1)
    frequency = jnp.exp(lax.rem(lane, HEAD // 2).astype(F32) * (-math.log(THETA) / (HEAD // 2)))
    sign = jnp.where(lane < HEAD // 2, -1.0, 1.0)
    token = half * HALF + lax.broadcasted_iota(jnp.int32, (1, HALF), 1)
    position = (token - starts).astype(F32)
    for b in range(RANKS):
        angles = column(position[:, b * TOK : (b + 1) * TOK]) * frequency
        r.cos[b * TOK : (b + 1) * TOK, :] = jnp.cos(angles)
        r.sin[b * TOK : (b + 1) * TOK, :] = jnp.sin(angles) * sign
    wait_pieces(r.pieces, r.w_all, r.w_send, r.w_recv)
    spread(0, w_cut)
    for copy in raws[1:]:
        copy.wait()
    for g in range(RANKS):
        r.gu_pieces[g, :, 0:RF] = r.gu_raw[:, g * RF : (g + 1) * RF].astype(BF)
        r.gu_pieces[g, :, RF:] = r.gu_raw[:, FF + g * RF : FF + (g + 1) * RF].astype(BF)
    r.pj_mine[...] = r.pj_raw[...].astype(BF)
    r.dn_mine[...] = r.dn_raw[...].astype(BF)

    send_rows()
    send_pieces(r.gu_pieces, r.gu_all, r.gu_send, r.gu_recv)
    gather_relay(r.hid_all, r.h_send, r.h_recv)
    wait_spread(0, w_cut)
    wait_rows()
    spread(1, pj_all_cut)
    wait_pieces(r.gu_pieces, r.gu_all, r.gu_send, r.gu_recv)
    spread(2, gu_all_cut)
    spread(3, dn_all_cut)


    def project(step, _):
        mine, other = gather_arrive(r.hid_all, r.h_send, r.h_recv, order(step))
        both = jnp.concatenate([r.hid_all[rows(mine, TOK), :], r.hid_all[rows(other, TOK), :]], axis=0)
        out = nn(both, r.w_all[...].reshape(D, RC))
        squares = out * out
        q_sum, k_sum = row_sums(squares[:, 0:RQ]), row_sums(squares[:, RQ : RQ + RK])
        upper = lax.broadcasted_iota(jnp.int32, (8, 2 * TOK), 0) < 4
        both_sums = jnp.where(upper, q_sum, k_sum)
        r.wide[rows(mine, TOK), 0:RC] = out[0:TOK]
        r.wide[rows(other, TOK), 0:RC] = out[TOK:]
        r.sums[mine] = both_sums[:, 0:TOK]
        r.sums[other] = both_sums[:, TOK:]
        return 0

    lax.fori_loop(0, 4, project, 0)
    exchange = SumExchange(r.sums, r.sums_land, r.sum_send, r.sum_recv)
    exchange.start()
    for i, to in enumerate(sources):
        source = to[1] * 4 + to[2]
        remote(
            gain_parts.at[0], r.gain_parts_land.at[source], r.gp_send.at[i], r.gp_recv.at[source], to
        ).wait_recv()
    gains = r.gain_parts_land[0].astype(F32)
    for i in range(1, 16):
        gains = gains + r.gain_parts_land[i].astype(F32)
    for i in range(3):
        r.gains[0:1, i * 128 : (i + 1) * 128] = gains[i : i + 1]
    for i in range(8):
        r.gains[1:2, i * 128 : (i + 1) * 128] = gains[3 + i : 4 + i]
        r.gains[2:3, i * 128 : (i + 1) * 128] = gains[11 + i : 12 + i]
    total = exchange.total()
    upper3 = lax.broadcasted_iota(jnp.int32, (8, 8, TOK), 1) < 4
    r.scales[...] = lax.rsqrt(jnp.where(upper3, total * (1.0 / QW), total * (1.0 / KW)) + NORM_EPS)

    def finish(b, _):
        at = rows(b, TOK)
        both = r.scales[b]
        q_scale, k_scale = column(both[0:1]), column(both[4:5])
        cosine, sine = r.cos[at, :], r.sin[at, :]
        for head in range(2):
            cols = slice(head * HEAD, (head + 1) * HEAD)
            q_unit = r.wide[at, cols] * q_scale
            r.unit[at, cols] = q_unit
            block, spot = token_block(r.q_rot, b, head)
            r.q_rot[block, spot, :] = rope(q_unit * r.gains[0:1, cols], cosine, sine).astype(BF)
        cols = slice(RQ, RQ + RK)
        k_unit = r.wide[at, cols] * k_scale
        r.unit[at, cols] = k_unit
        r.kv_own[0, at, :] = rope(k_unit * r.gains[0:1, cols], cosine, sine).astype(BF)
        r.kv_own[1, at, :] = r.wide[at, RQ + RK : RC].astype(BF)
        return 0

    lax.fori_loop(0, RANKS, finish, 0)

    kv_copy = remote(r.kv_own, r.kv_other, r.kv_send, r.kv_recv, partner)

    @pl.when(half == 0)
    def _():
        kv_copy.start()

    gather_finish(r.hid_all, r.h_send, r.h_recv)

    r.v_t[0] = jnp.transpose(r.kv_own[1].astype(F32)).astype(BF)

    def allowed_tile(block, key_base, diagonal):
        key_index = lax.broadcasted_iota(jnp.int32, (BLK, 2 * BLK), 0)
        allowed = key_index >= r.start[block, 0:1, :] - key_base
        if diagonal:
            lane = lax.broadcasted_iota(jnp.int32, (1, 2 * BLK), 1)
            allowed = allowed & (key_index <= lax.rem(lane, BLK))
        return allowed

    def tile(block, keys, values_t, key_base, carry):
        scores = nt(keys, r.q_rot[block]) * SCALE_TWO
        scores = jnp.where(allowed_tile(block, key_base, carry is None), scores, MASKED)
        top_now = jnp.max(scores, axis=0, keepdims=True)
        if carry is None:
            probs = jnp.exp2(scores - top_now)
            return top_now, jnp.sum(probs, axis=0, keepdims=True), nn(values_t, probs.astype(BF))
        top_old, run_old, acc_old = carry
        top_new = jnp.maximum(top_old, top_now)
        fade = jnp.exp2(top_old - top_new)
        probs = jnp.exp2(scores - top_new)
        return (
            top_new,
            run_old * fade + jnp.sum(probs, axis=0, keepdims=True),
            acc_old * fade + nn(values_t, probs.astype(BF)),
        )

    def keep_state(block, state):
        r.top[block] = jnp.broadcast_to(state[0], (8, 2 * BLK))
        r.running[block] = jnp.broadcast_to(state[1], (8, 2 * BLK))
        r.accum[block] = state[2]

    def local_block(block, _):
        def local_tile(j, carry):
            return tile(
                block, r.kv_own[0, rows(j, BLK), :], r.v_t[0, :, rows(j, BLK)], half * HALF + j * BLK, carry
            )

        keep_state(block, lax.fori_loop(0, block, local_tile, local_tile(block, None)))
        return 0

    lax.fori_loop(0, 4, local_block, 0)

    @pl.when(half == 1)
    def _():
        kv_copy.wait_recv()
        r.v_t[1] = jnp.transpose(r.kv_other[1].astype(F32)).astype(BF)

        def other_block(block, _):
            state = (r.top[block][0:1], r.running[block][0:1], r.accum[block])

            def other_tile(j, carry):
                return tile(block, r.kv_other[0, rows(j, BLK), :], r.v_t[1, :, rows(j, BLK)], j * BLK, carry)

            keep_state(block, lax.fori_loop(0, 4, other_tile, state, unroll=True))
            return 0

        lax.fori_loop(0, 4, other_block, 0)

    @pl.when(half == 0)
    def _():
        kv_copy.wait_send()

    def close_block(block, _):
        run = r.running[block]
        r.lse[block] = r.top[block] + jnp.log2(run)
        out = jnp.transpose(r.accum[block] * (1.0 / run[0:1]))
        r.mixed[block] = out
        for head in range(2):
            r.mixed_low[rows(block, BLK), head * HEAD : (head + 1) * HEAD] = out[
                head * BLK : (head + 1) * BLK
            ].astype(BF)
        return 0

    lax.fori_loop(0, 4, close_block, 0)

    wait_spread(1, pj_all_cut)
    gain_attn, gain_ffn = r.gains[1:2, :], r.gains[2:3, :]

    def both_rows(ref, mine, other):
        return jnp.concatenate([ref[rows(mine, TOK), :], ref[rows(other, TOK), :]], axis=0)

    s = Scatter(r, 0)

    def proj_step(step, _):
        off = lax.rem(step + 1, 4)
        at = lax.rem(o + off, 4)
        s.give(off, nn(both_rows(r.mixed_low, core * 4 + at, (1 - core) * 4 + at), r.pj_all[...].reshape(RQ, D)))

        @pl.when(step > 0)
        def _():
            s.send(step)

        return 0

    lax.fori_loop(0, 4, proj_step, 0)
    s.send(0)
    branch = s.result()
    branch_scale = rms_scale(branch)
    branch_unit = branch * branch_scale
    residual = hid[...].astype(F32) + branch_unit * gain_attn
    r.full_res[rows(rank, TOK), :] = residual.astype(BF)
    gather_start(r.full_res, r.a_send, r.a_recv)
    s.finish()
    wait_spread(2, gu_all_cut)
    wait_spread(3, dn_all_cut)

    s1 = Scatter(r, 1)

    def ffn_step(step, _):
        off = order(step)
        mine, other = gather_step(r.full_res, r.a_send, r.a_recv, step)
        both = nn(both_rows(r.full_res, mine, other), r.gu_all[...].reshape(D, 2 * RF))
        r.wide[rows(mine, TOK), :] = both[0:TOK]
        r.wide[rows(other, TOK), :] = both[TOK:]
        gate, up = both[:, 0:RF], both[:, RF:]
        act_low = (gate * jax.nn.sigmoid(gate) * up).astype(BF)
        r.act[rows(mine, TOK), :] = act_low[0:TOK]
        r.act[rows(other, TOK), :] = act_low[TOK:]

        @pl.when(step > 0)
        def _():
            s1.send(order(step - 1))

        s1.give(off, nn(act_low, r.dn_all[...].reshape(RF, D)))
        return 0

    lax.fori_loop(0, 4, ffn_step, 0)
    s1.send(2)
    ffn = s1.result()
    ffn_scale = rms_scale(ffn)
    ffn_unit = ffn * ffn_scale
    r.layer_out[...] = residual + ffn_unit * gain_ffn
    write(r.layer_out, layer_out)
    cotangent = cot[...].astype(F32)
    back_ffn = norm_back(cotangent, ffn_unit, ffn_scale, gain_ffn)
    r.full_ffn[rows(rank, TOK), :] = back_ffn.astype(BF)
    gather_start(r.full_ffn, r.b_send, r.b_recv)
    gain_row = jnp.sum(cotangent * ffn_unit, axis=0, keepdims=True)
    r.gain_rest[2:3, :] = gain_row[:, 0:512]
    r.gain_rest[3:4, :] = gain_row[:, 512:]
    gather_finish(r.full_res, r.a_send, r.a_recv)
    s1.finish()

    s2 = Scatter(r, 2)

    def back_step(step, _):
        off = order(step)
        mine, other = gather_step(r.full_ffn, r.b_send, r.b_recv, step)
        back_act = nt(both_rows(r.full_ffn, mine, other), r.dn_all[...].reshape(RF, D))
        both = both_rows(r.wide, mine, other)
        gate, up = both[:, 0:RF], both[:, RF:]
        sig = jax.nn.sigmoid(gate)
        back_gate = back_act * up * sig * (1.0 + gate * (1.0 - sig))
        back_up = back_act * (gate * sig)
        back_both = jnp.concatenate([back_gate, back_up], axis=1).astype(BF)
        r.back_gu[rows(mine, TOK), :] = back_both[0:TOK]
        r.back_gu[rows(other, TOK), :] = back_both[TOK:]

        @pl.when(step > 0)
        def _():
            s2.send(order(step - 1))

        s2.give(off, nt(back_both, r.gu_all[...].reshape(D, 2 * RF)))
        return 0

    lax.fori_loop(0, 4, back_step, 0)
    s2.send(2)

    def y_of(to):
        return lax.div(to[0], 2)

    def x_of(to):
        return lax.div(to[1], 2) * 2 + lax.rem(to[0], 2)

    here = (d, c, o)

    def fan_out(index, peers, place_of, cut, land):
        slot = place_of(here)
        for i, to in enumerate(peers):
            launch(remote(cut(to), land.at[slot], r.fan_send.at[index, i], r.fan_recv.at[index, slot], to))
        land[slot] = cut(here)[...]

    def fan_in(index, peers, place_of, land):
        for i, to in enumerate(peers):
            slot = place_of(to)
            remote(
                land.at[slot], land.at[slot], r.fan_send.at[index, i], r.fan_recv.at[index, slot], to
            ).wait_recv()
        total = land[0].astype(F32)
        for i in range(1, 4):
            total = total + land[i].astype(F32)
        return total

    def gu_step(b, _):
        grad = tn(r.full_res[:, rows(b, 128)], r.back_gu[...])
        r.gu_grad[lax.div(b, 4), rows(lax.rem(b, 4), 2)] = grad.astype(BF).reshape(2, 64, 2 * RF)
        return 0

    lax.fori_loop(0, 8, gu_step, 0)

    fan_out(1, along_y, y_of, lambda to: r.gu_grad.at[:, :, rows(y_of(to), 16)], r.gu_y)
    r.dn_grad[...] = tn(r.act[...], r.full_ffn[...]).astype(BF)
    fan_out(
        0,
        along_x,
        x_of,
        lambda to: r.dn_grad.at[rows(lax.div(to[1], 2), 192), rows(lax.rem(to[0], 2), 512)],
        r.dn_x,
    )
    resid_grad = cotangent + s2.result()
    r.back_resid[...] = resid_grad
    write(r.back_resid, back_resid)
    gain_row = jnp.sum(resid_grad * branch_unit, axis=0, keepdims=True)
    r.gain_rest[0:1, :] = gain_row[:, 0:512]
    r.gain_rest[1:2, :] = gain_row[:, 512:]
    back_branch = norm_back(resid_grad, branch_unit, branch_scale, gain_attn)
    r.full_branch[rows(rank, TOK), :] = back_branch.astype(BF)
    gather_start(r.full_branch, r.e_send, r.e_recv)
    gather_finish(r.full_ffn, r.b_send, r.b_recv)
    s2.finish()

    def mixed_step(step, _):
        mine, other = gather_step(r.full_branch, r.e_send, r.e_recv, step)
        out = nt(both_rows(r.full_branch, mine, other), r.pj_all[...].reshape(RQ, D)).astype(BF)
        for head in range(2):
            for i, b in enumerate((mine, other)):
                block, spot = token_block(r.back_mixed, b, head)
                r.back_mixed[block, spot, :] = out[i * TOK : (i + 1) * TOK, head * HEAD : (head + 1) * HEAD]
        return 0

    lax.fori_loop(0, 4, mixed_step, 0)
    r.pj_grad[...] = tn(r.mixed_low[...], r.full_branch[...]).astype(BF).reshape(2, 4, 2, 16, D)
    fan_out(2, along_x, x_of, lambda to: r.pj_grad.at[lax.div(to[1], 2), :, lax.rem(to[0], 2)], r.pj_x)
    gather_finish(r.full_branch, r.e_send, r.e_recv)

    def delta_step(block, _):
        r.delta[block] = row_sums(r.back_mixed[block].astype(F32) * r.mixed[block])
        r.back_q[block] = jnp.zeros((2 * BLK, HEAD), F32)
        return 0

    lax.fori_loop(0, 4, delta_step, 0)

    def back_tile(block, keys, values, key_base, diagonal, carry):
        grad_k, grad_v = carry
        query, grad_out = r.q_rot[block], r.back_mixed[block]
        scores = nt(keys, query) * SCALE_TWO
        probs = jnp.where(allowed_tile(block, key_base, diagonal), jnp.exp2(scores - r.lse[block, 0:1, :]), 0.0)
        back_prob = nt(values, grad_out)
        back_score = (probs * (back_prob - r.delta[block, 0:1, :])).astype(BF)
        grad_k = grad_k + nn(back_score, query)
        grad_v = grad_v + nn(probs.astype(BF), grad_out)
        r.back_q[block] += tn(back_score, keys)
        return grad_k, grad_v

    zero = (jnp.zeros((BLK, HEAD), F32), jnp.zeros((BLK, HEAD), F32))
    def send_back(i):
        at = rows(i, 2 * BLK)
        return remote(r.other_grad.at[:, at], r.other_land.at[:, at], r.kvb_send.at[i], r.kvb_recv.at[i], partner)


    def local_keys(j, _):
        at = rows(j, BLK)
        keys, values = r.kv_own[0, at, :], r.kv_own[1, at, :]
        base = half * HALF + j * BLK
        grad_k, grad_v = lax.fori_loop(
            j + 1,
            4,
            lambda block, carry: back_tile(block, keys, values, base, False, carry),
            back_tile(j, keys, values, base, True, zero),
        )
        r.back_k[at, :] = grad_k * SCORE_SCALE
        r.back_v[at, :] = grad_v
        return 0

    def other_keys(j, _):
        at = rows(j, BLK)
        keys, values = r.kv_other[0, at, :], r.kv_other[1, at, :]
        grad_k, grad_v = lax.fori_loop(
            0, 4, lambda block, carry: back_tile(block, keys, values, j * BLK, False, carry), zero
        )
        r.other_grad[0, at, :] = (grad_k * SCORE_SCALE).astype(BF)
        r.other_grad[1, at, :] = grad_v.astype(BF)
        return 0

    def first_part(low, high):
        lax.fori_loop(low, low + (high - low) * (1 - half), local_keys, 0)
        lax.fori_loop(low, low + (high - low) * half, other_keys, 0)

    first_part(0, 2)

    @pl.when(half == 1)
    def _():
        send_back(0).start()


    r.dn_mid[...] = fan_in(0, along_x, x_of, r.dn_x).astype(BF)
    fan_out(3, along_y, y_of, lambda to: r.dn_mid.at[rows(y_of(to), 48)], r.dn_y)
    r.gu_mid[...] = fan_in(1, along_y, y_of, r.gu_y).astype(BF)
    fan_out(
        4,
        along_x,
        x_of,
        lambda to: r.gu_mid.at[lax.div(to[1], 2), :, :, rows(lax.rem(to[0], 2), RF)],
        r.gu_x,
    )
    r.pj_mid[...] = fan_in(2, along_x, x_of, r.pj_x).astype(BF)
    fan_out(5, along_y, y_of, lambda to: r.pj_mid.at[y_of(to)], r.pj_y)

    first_part(2, 4)

    @pl.when(half == 1)
    def _():
        send_back(1).start()

    r.dn_red[...] = fan_in(3, along_y, y_of, r.dn_y).astype(BF)
    r.gu_red[...] = fan_in(4, along_x, x_of, r.gu_x).astype(BF)
    r.pj_red[...] = fan_in(5, along_y, y_of, r.pj_y).astype(BF)
    target = 2 * rank + half
    to_owner = (d, lax.div(target, 4), lax.rem(target, 4))
    stay = target == place
    pj_move = remote(r.pj_red, r.pj_own, r.move_send.at[0], r.move_recv.at[0], to_owner)
    dn_move = remote(r.dn_red, r.dn_own, r.move_send.at[1], r.move_recv.at[1], to_owner)

    @pl.when(stay)
    def _():
        r.pj_own[...] = r.pj_red[...]
        r.dn_own[...] = r.dn_red[...]

    @pl.when(jnp.logical_not(stay))
    def _():
        pj_move.start()
        dn_move.start()

    for i, to in enumerate(ranks):
        launch(
            remote(
                r.gu_red.at[rank_of(to)],
                r.gu_own.at[:, rows(rank, RF)],
                r.gur_send.at[i],
                r.gur_recv.at[rank],
                to,
            )
        )
    r.gu_own[:, rows(rank, RF)] = r.gu_red[rank]

    lax.fori_loop(0, 2 * half, local_keys, 0)

    @pl.when(half == 0)
    def _():
        for i in range(2):
            at = rows(i, 2 * BLK)
            send_back(i).wait_recv()
            r.back_k[at, :] += r.other_land[0, at, :].astype(F32)
            r.back_v[at, :] += r.other_land[1, at, :].astype(F32)

    @pl.when(jnp.logical_not(stay))
    def _():
        pj_move.wait_send()
        dn_move.wait_send()
        pj_move.wait_recv()
        dn_move.wait_recv()

    for i, to in enumerate(ranks):
        remote(
            r.gu_red.at[0], r.gu_own.at[:, rows(rank_of(to), RF)], r.gur_send.at[i], r.gur_recv.at[rank_of(to)], sib
        ).wait_recv()

    def owned(n, e):
        e_part, e_side = lax.div(e, 2), lax.rem(e, 2)
        return (
            pj_sum.at[rows(e, 16), :],
            dn_sum.at[rows(e_part, 48), rows(e_side, 512)],
            gu_sum.at[rows(e_part, 16), rows(e_side, FF)],
            qkv_sum.at[rows(e_part, 16), rows(e_side, QW)],
        )[n]

    own_refs = (r.pj_own, r.dn_own, r.gu_own, r.qkv_own)
    kept = [pltpu.make_async_copy(own_refs[n], owned(n, d), r.kept_sem.at[n]) for n in range(3)]
    for copy in kept:
        copy.start()
    across = (d + 1 - 2 * side, c, o)
    for n in range(2):
        launch(remote(own_refs[n], owned(n, d), r.y_send.at[n, 0], r.y_recv.at[n, 4], across))
    for i, to in enumerate(along_y):
        launch(remote(r.gu_own, owned(2, d), r.y_send.at[2, i], r.y_recv.at[2, part], to))

    def pair(n, y):
        return (pj_sum.at[rows(y, 32)], dn_sum.at[rows(y, 48)])[n]

    def column_half(of_side):
        return gu_sum.at[:, rows(of_side, FF)]

    def share_again():
        for copy in kept:
            copy.wait()
        for n in range(2):
            remote(own_refs[n], owned(n, across[0]), r.y_send.at[n, 0], r.y_recv.at[n, 4], across).wait_recv()
            for i, to in enumerate(along_y):
                launch(remote(pair(n, part), pair(n, part), r.y_send.at[n, 1 + i], r.y_recv.at[n, part], to))
        for i, to in enumerate(along_y):
            remote(r.gu_own, owned(2, to[0]), r.y_send.at[2, i], r.y_recv.at[2, y_of(to)], to).wait_recv()
        launch(remote(column_half(side), column_half(side), r.y_send.at[2, 3], r.y_recv.at[2, 4], across))

    def shared():
        for n in range(2):
            for i, to in enumerate(along_y):
                y = y_of(to)
                remote(pair(n, y), pair(n, y), r.y_send.at[n, 1 + i], r.y_recv.at[n, y], to).wait_recv()
        other_half = column_half(1 - side)
        remote(other_half, other_half, r.y_send.at[2, 3], r.y_recv.at[2, 4], across).wait_recv()

    lax.fori_loop(2 * half, 4 * half, local_keys, 0)

    @pl.when(half == 1)
    def _():
        for i in range(2):
            send_back(i).wait_send()

    def weigh(b, _):
        at = rows(b, TOK)
        cosine, sine = r.cos[at, :], r.sin[at, :]
        totals = []
        for head in range(2):
            cols = slice(head * HEAD, (head + 1) * HEAD)
            block, spot = token_block(r.back_q, b, head)
            grad = unrope(r.back_q[block, spot, :] * SCORE_SCALE, cosine, sine)
            r.wide[at, cols] = grad
            totals.append(grad * r.gains[0:1, cols] * r.unit[at, cols])
        cols = slice(RQ, RQ + RK)
        grad = unrope(r.back_k[at, :], cosine, sine)
        r.wide[at, cols] = grad
        q_sum = row_sums(totals[0] + totals[1])
        k_sum = row_sums(grad * r.gains[0:1, cols] * r.unit[at, cols])
        upper = lax.broadcasted_iota(jnp.int32, (8, TOK), 0) < 4
        r.sums_back[b] = jnp.where(upper, q_sum, k_sum)
        return 0

    lax.fori_loop(0, RANKS, weigh, 0)
    exchange = SumExchange(r.sums_back, r.sums_back_land, r.sumb_send, r.sumb_recv)
    exchange.start()

    gain_own = jnp.sum(r.wide[:, 0 : RQ + RK] * r.unit[...], axis=0, keepdims=True)
    row = lax.broadcasted_iota(jnp.int32, (16, 512), 0)
    col = lax.broadcasted_iota(jnp.int32, (16, 512), 1)
    own_q, own_k = gain_own[:, 0:RQ], gain_own[:, RQ:]
    at_q = (row == lax.div(rank, 2)) & (lax.div(col, RQ) == lax.rem(rank, 2))
    at_k = (row == 4 + lax.div(rank, 4)) & (lax.div(col, RK) == lax.rem(rank, 4))
    r.gain_vec[...] = jnp.where(at_q, jnp.concatenate([own_q] * 2, axis=1), 0.0) + jnp.where(
        at_k, jnp.concatenate([own_k] * 4, axis=1), 0.0
    )
    r.gain_vec[6:10, :] = r.gain_rest[...]
    fan_out(6, along_y, y_of, lambda to: r.gain_vec, r.gain_y)

    total = exchange.total()
    r.sums_back[...] = jnp.where(upper3, total * (1.0 / QW), total * (1.0 / KW))

    def back_norm(b, _):
        at = rows(b, TOK)
        scale, mean = r.scales[b], r.sums_back[b]
        q_scale, k_scale = column(scale[0:1]), column(scale[4:5])
        q_mean, k_mean = column(mean[0:1]), column(mean[4:5])
        for head in range(2):
            cols = slice(head * HEAD, (head + 1) * HEAD)
            weighted = r.wide[at, cols] * r.gains[0:1, cols]
            r.back_qkv[at, cols] = (q_scale * (weighted - r.unit[at, cols] * q_mean)).astype(BF)
        cols = slice(RQ, RQ + RK)
        weighted = r.wide[at, cols] * r.gains[0:1, cols]
        r.back_qkv[at, cols] = (k_scale * (weighted - r.unit[at, cols] * k_mean)).astype(BF)
        r.back_qkv[at, RQ + RK : RC] = r.back_v[at, :].astype(BF)
        return 0

    lax.fori_loop(0, RANKS, back_norm, 0)
    share_again()

    def grad_step(b, _):
        grad = tn(r.hid_all[:, rows(b, 128)], r.back_qkv[...])
        r.qkv_grad[lax.div(b, 4), rows(lax.rem(b, 4), 2)] = grad.astype(BF).reshape(2, 64, RC)
        return 0

    lax.fori_loop(0, 8, grad_step, 0)

    def qkv_cut(e, h):
        return h, slice(None), rows(lax.div(e, 2), 16), rows(lax.rem(e, 2), RQ)

    old = list(done)
    done.clear()

    def drain_old():
        for copy in old:
            copy.wait_send()

        @pl.when(jnp.logical_not(keep))
        def _():
            pj_near.wait_send()
            dn_near.wait_send()

    slot = plane_slot(d, c)
    for i, to in enumerate(planes):
        src = r.qkv_grad.at[qkv_cut(to[0], lax.div(to[1], 2))]
        launch(remote(src, r.qkv_land.at[slot], r.plane_send.at[i], r.plane_recv.at[slot], to))
    r.qkv_land[slot] = r.qkv_grad[qkv_cut(d, half)]
    r.gain_half[...] = fan_in(6, along_y, y_of, r.gain_y)
    fan_out(7, along_x, x_of, lambda to: r.gain_half, r.gain_x)

    s3 = Scatter(r, 3)

    def input_step(step, _):
        off = lax.rem(step + 1, 4)
        at = lax.rem(o + off, 4)
        s3.give(off, nt(both_rows(r.back_qkv, core * 4 + at, (1 - core) * 4 + at), r.w_all[...].reshape(D, RC)))

        @pl.when(step > 0)
        def _():
            s3.send(step)

        return 0

    lax.fori_loop(0, 4, input_step, 0)
    s3.send(0)
    drain_old()

    total = fan_in(7, along_x, x_of, r.gain_x)
    r.gain_mid[...] = total
    for i, to in enumerate(ranks):
        launch(remote(r.gain_mid, r.gain_last.at[rank], r.gl_send.at[i], r.gl_recv.at[rank], to))
    r.gain_last[rank] = total

    for i, to in enumerate(planes):
        source = plane_slot(to[0], to[1])
        land = r.qkv_land.at[source]
        remote(land, land, r.plane_send.at[i], r.plane_recv.at[source], to).wait_recv()
    total = r.qkv_land[0].astype(F32)
    for i in range(1, 16):
        total = total + r.qkv_land[i].astype(F32)
    r.qkv_red[...] = total.astype(BF)

    def qkv_cols(of_rank, i):
        return rows((1 - side) * (of_rank * 2 + i) + side * (of_rank + i * 8), RK)

    for i, to in enumerate(ranks):
        for j in range(2):
            launch(
                remote(
                    r.qkv_red.at[rank_of(to), :, pl.ds(j * RK, RK)],
                    r.qkv_own.at[:, qkv_cols(rank, j)],
                    r.qr_send.at[j, i],
                    r.qr_recv.at[j, rank],
                    to,
                )
            )
    for j in range(2):
        r.qkv_own[:, qkv_cols(rank, j)] = r.qkv_red[rank][:, j * RK : (j + 1) * RK]

    r.input_part[...] = s3.result()
    write(r.input_part, input_part)
    for i, to in enumerate(ranks):
        remote(
            r.gain_mid, r.gain_last.at[rank_of(to)], r.gl_send.at[i], r.gl_recv.at[rank_of(to)], sib
        ).wait_recv()
    total = r.gain_last[0]
    for i in range(1, 8):
        total = total + r.gain_last[i]
    for i in range(40):
        gain_sum[i : i + 1, :] = total[i // 4 : i // 4 + 1, (i % 4) * 128 : (i % 4 + 1) * 128]

    for i, to in enumerate(ranks):
        for j in range(2):
            remote(
                r.qkv_red.at[0, :, pl.ds(j * RK, RK)],
                r.qkv_own.at[:, qkv_cols(rank_of(to), j)],
                r.qr_send.at[j, i],
                r.qr_recv.at[j, rank_of(to)],
                sib,
            ).wait_recv()
    for i, to in enumerate(owners):
        launch(remote(r.qkv_own, owned(3, d), r.y_send.at[3, i], r.y_recv.at[3, d], to))
    write(r.qkv_own, owned(3, d))
    for i, to in enumerate(owners):
        remote(r.qkv_own, owned(3, to[0]), r.y_send.at[3, i], r.y_recv.at[3, to[0]], sib).wait_recv()
    shared()
    s3.finish()
    drain()
    for copy in writes:
        copy.wait()


def call_layer(*operands):
    any_space = pl.BlockSpec(memory_space=pl.ANY)
    return pl.pallas_call(
        layer_kernel,
        name="layer",
        out_shape=(
            jax.ShapeDtypeStruct((TOK, D), F32),
            jax.ShapeDtypeStruct((TOK, D), F32),
            jax.ShapeDtypeStruct((TOK, D), F32),
            jax.ShapeDtypeStruct((64, QW + 2 * KW), BF),
            jax.ShapeDtypeStruct((64, 2 * FF), BF),
            jax.ShapeDtypeStruct((128, D), BF),
            jax.ShapeDtypeStruct((192, D), BF),
            jax.ShapeDtypeStruct((40, 128), F32),
        ),
        in_specs=[VMEM] * 4 + [any_space] * 4,
        out_specs=[any_space] * 7 + [VMEM],
        scratch_shapes=list(SCRATCH.values()),
        compiler_params=pltpu.CompilerParams(
            collective_id=1, has_side_effects=True, vmem_limit_bytes=63 * 2**20
        ),
    )(*operands)


def adam_step(weight, moment, square, grad_sum, rate, decay):
    moment_new = BETA_ONE * moment + (1.0 - BETA_ONE) * grad_sum
    square_new = BETA_TWO * square + (1.0 - BETA_TWO) * grad_sum * grad_sum
    moment_hat = moment_new / (1.0 - BETA_ONE**STEP)
    square_hat = square_new / (1.0 - BETA_TWO**STEP)
    weight_new = weight - rate * (moment_hat / (jnp.sqrt(square_hat) + ADAM_EPS) + decay * weight)
    return (weight_new, moment_new, square_new)


def update_kernel(*refs):
    ins, outs = refs[:19], refs[19:]
    layer_out, back_resid, input_part = ins[:3]
    outs[0][...] = layer_out[...].astype(BF)
    outs[1][...] = back_resid[...] + input_part[...]
    for i in range(4):
        weight, moment, square, grad = (ref[...] for ref in ins[3 + 4 * i : 7 + 4 * i])
        new = adam_step(weight, moment, square, grad.astype(F32), RATE_MATRIX, DECAY)
        for ref, value in zip(outs[2 + 3 * i : 5 + 3 * i], new):
            ref[...] = value


def call_update(*operands):
    def half_rows(shape):
        return pl.BlockSpec((shape[0] // 2, shape[1]), lambda i: (i, 0))

    results = [operands[0], operands[1]] + [operands[3 + 4 * i + j] for i in range(4) for j in range(3)]
    types_out = [BF] + [F32] * 13
    return pl.pallas_call(
        update_kernel,
        name="update",
        grid=(2,),
        out_shape=[jax.ShapeDtypeStruct(a.shape, t) for a, t in zip(results, types_out)],
        in_specs=[half_rows(a.shape) for a in operands],
        out_specs=[half_rows(a.shape) for a in results],
        compiler_params=pltpu.CompilerParams(vmem_limit_bytes=62 * 2**20),
    )(*operands)


def per_device(
    hidden_in,
    segment_ids,
    out_cotangent,
    qkv_weight,
    qkv_moment,
    qkv_square,
    proj_weight,
    proj_moment,
    proj_square,
    gate_up_weight,
    gate_up_moment,
    gate_up_square,
    down_weight,
    down_moment,
    down_square,
    gains,
    gain_moment,
    gain_square,
):
    _, c, o = coords()
    place = c * 4 + o
    placed = lax.dynamic_update_slice_in_dim(
        jnp.zeros((QW + KW + 2 * D,), BF), gains.astype(BF), place * gains.shape[0], axis=0
    )
    gain_parts = jnp.concatenate(
        [
            placed[:QW].reshape(RANKS, 2, 128),
            placed[QW : QW + KW].reshape(RANKS, 1, 128),
            jnp.broadcast_to(placed[QW + KW :].reshape(1, 16, 128), (RANKS, 16, 128)),
            jnp.zeros((RANKS, 13, 128), BF),
        ],
        axis=1,
    )
    layer_out, back_resid, input_part, qkv_sum, gu_sum, pj_sum, dn_sum, gain_sum = call_layer(
        hidden_in, out_cotangent, segment_ids, gain_parts, qkv_weight, gate_up_weight, proj_weight, down_weight
    )
    gain_grad = lax.dynamic_slice_in_dim(
        gain_sum.reshape(40 * 128), place * gains.shape[0], gains.shape[0]
    )
    updated = call_update(
        layer_out, back_resid, input_part,
        qkv_weight, qkv_moment, qkv_square, qkv_sum,
        proj_weight, proj_moment, proj_square, pj_sum,
        gate_up_weight, gate_up_moment, gate_up_square, gu_sum,
        down_weight, down_moment, down_square, dn_sum,
    )
    return tuple(updated) + adam_step(gains, gain_moment, gain_square, gain_grad, RATE_GAIN, 0.0)


def solution(mesh):
    seq = P(("dp", "ctx", "opt"), None)
    mat = P(("ctx", "opt"), None)
    vec = P(("ctx", "opt"))
    return jax.shard_map(
        per_device,
        mesh=mesh,
        in_specs=(seq, P("dp", None), seq) + (mat,) * 12 + (vec,) * 3,
        out_specs=(seq, seq) + (mat,) * 12 + (vec,) * 3,
        check_vma=False,
    )
```

```python
import math
import types

import jax
import jax.numpy as jnp
from jax import lax
from jax.experimental import pallas as pl
from jax.experimental.pallas import tpu as pltpu
from jax.sharding import PartitionSpec as P

D = 1024
FF = 3072
HEADS = 16
KV_HEADS = 8
HEAD = 128
STEP = 10

NORM_EPS = 1e-06
THETA = 500000.0
MASKED = -1e30
BETA_ONE = 0.9
BETA_TWO = 0.95
ADAM_EPS = 1e-08
RATE_MATRIX = 0.06
RATE_GAIN = 1.0
DECAY = 0.1

TOK = 128
HALF = 1024
RANKS = 8
QW = HEADS * HEAD
KW = KV_HEADS * HEAD
RQ = 256
RK = 128
RC = RQ + 2 * RK
RF = FF // RANKS
BLK = 256
SCORE_SCALE = 1.0 / math.sqrt(HEAD)
SCALE_TWO = SCORE_SCALE * math.log2(math.e)

MESH = pl.DeviceIdType.MESH
BF = jnp.bfloat16
F32 = jnp.float32
VMEM = pl.BlockSpec(memory_space=pltpu.VMEM)
DMA = pltpu.SemaphoreType.DMA


def coords():
    return lax.axis_index("dp"), lax.axis_index("ctx"), lax.axis_index("opt")


def sibling(c):
    return c + 1 - 2 * lax.rem(c, 2)


def rank_peer(d, c, o, t):
    flip = t // 4
    return (d, c + (1 - 2 * lax.rem(c, 2)) * flip, lax.rem(o + t % 4, 4))


def cross_peer(d, c, o, t):
    return rank_peer(d + 1 - 2 * lax.rem(d, 2), lax.rem(c + 2, 4), o, t)


def plane_peer(d, c, o, t):
    x_lo, y = lax.rem(d, 2), lax.div(d, 2)
    y = lax.rem(y + t // 4, 4)
    x_lo = x_lo + (1 - 2 * x_lo) * (t % 2)
    return (2 * y + x_lo, lax.rem(c + 2 * ((t % 4) // 2), 4), o)


def group_peer(d, c, o, t):
    return (d, lax.rem(c + t // 4, 4), lax.rem(o + t % 4, 4))


def dp_peer(d, c, o, t):
    return (lax.rem(d + t, 8), c, o)


def greet(peers):
    barrier = pltpu.get_barrier_semaphore()
    for to in peers:
        pl.semaphore_signal(barrier, inc=1, device_id=to, device_id_type=MESH)
    return lambda: pl.semaphore_wait(barrier, len(peers))


def remote(src, dst, send, recv, to):
    return pltpu.make_async_remote_copy(
        src_ref=src, dst_ref=dst, send_sem=send, recv_sem=recv, device_id=to, device_id_type=MESH
    )


def rows(index, count):
    return pl.ds(pl.multiple_of(index * count, count), count)


def nn(a, b):
    return lax.dot_general(a, b, (((1,), (0,)), ((), ())), preferred_element_type=F32)


def nt(a, b):
    return lax.dot_general(a, b, (((1,), (1,)), ((), ())), preferred_element_type=F32)


def tn(a, b):
    return lax.dot_general(a, b, (((0,), (0,)), ((), ())), preferred_element_type=F32)


def row_sums(values):
    ones = jnp.ones((8, values.shape[1]), F32)
    return lax.dot_general(
        ones,
        values,
        (((1,), (1,)), ((), ())),
        precision=lax.Precision.HIGHEST,
        preferred_element_type=F32,
    )


def column(row):
    return jnp.transpose(jnp.broadcast_to(row, (128, 128)))


def rms_scale(values):
    return lax.rsqrt(jnp.mean(values * values, axis=-1, keepdims=True) + NORM_EPS)


def norm_back(grad_rows, unit_rows, scale_rows, gain_row):
    weighted = grad_rows * gain_row
    return scale_rows * (
        weighted - unit_rows * jnp.mean(weighted * unit_rows, axis=-1, keepdims=True)
    )


def rope(u, cos, sin):
    return u * cos + pltpu.roll(u, HEAD // 2, 1) * sin


def unrope(g, cos, sin):
    return g * cos - pltpu.roll(g, HEAD // 2, 1) * sin


def gather_start(full, send, recv):
    d, c, o = coords()
    rank = lax.rem(c, 2) * 4 + o
    own = full.at[rows(rank, TOK)]
    for t in (1, 3):
        remote(own, own, send.at[t], recv.at[rank], (d, c, lax.rem(o + t, 4))).start()
    remote(own, own, send.at[0], recv.at[rank], (d, sibling(c), o)).start()


def gather_relay(full, send, recv):
    d, c, o = coords()
    core = lax.rem(c, 2)
    to = (d, sibling(c), o)
    for off, part in ((1, 1), (3, 0)):
        mine = core * 4 + lax.rem(o + off, 4)
        block = full.at[rows(mine, TOK)]
        half = full.at[rows(mine * 2 + part, TOK // 2)]
        remote(block, block, send.at[off], recv.at[mine], to).wait_recv()
        landed = recv.at[8] if part else recv.at[mine]
        remote(half, half, send.at[2 + 5 * part], landed, (d, c, lax.rem(o + 4 - off, 4))).start()
        remote(block, block, send.at[3 + off], recv.at[mine], to).start()


def gather_arrive(full, send, recv, off):
    d, c, o = coords()
    core = lax.rem(c, 2)
    at = lax.rem(o + off, 4)
    mine, other = core * 4 + at, (1 - core) * 4 + at
    to = (d, sibling(c), o)
    block = full.at[rows(mine, TOK)]

    @pl.when(off == 2)
    def _():
        for part in range(2):
            half = full.at[rows(mine * 2 + part, TOK // 2)]
            landed = recv.at[8] if part else recv.at[mine]
            remote(half, half, send.at[2], landed, to).wait_recv()
        remote(block, block, send.at[5], recv.at[mine], to).start()

    block = full.at[rows(other, TOK)]
    remote(block, block, send.at[0], recv.at[other], to).wait_recv()
    return mine, other


def gather_step(full, send, recv, step):
    @pl.when(step == 1)
    def _():
        gather_relay(full, send, recv)

    return gather_arrive(full, send, recv, order(step))


def gather_finish(full, send, recv):
    d, c, o = coords()
    for i in range(8):
        part = full.at[rows(0, TOK // 2 if i in (2, 7) else TOK)]
        remote(part, part, send.at[i], recv.at[0], (d, sibling(c), o)).wait_send()


class Scatter:
    def __init__(self, r, index):
        self.stage_s, self.stage_z, self.own = r.stage_s, r.stage_z, r.own
        self.land_s, self.land_z = r.land_s.at[index % 2], r.land_z.at[index % 2]
        self.send_s, self.recv_s = r.send_s.at[index], r.recv_s.at[index]
        self.send_z, self.recv_z = r.send_z.at[index], r.recv_z.at[index]

    def near(self, off):
        d, c, o = coords()
        return remote(
            self.stage_s.at[off], self.land_s.at[off], self.send_s.at[off], self.recv_s.at[off], (d, sibling(c), o)
        )

    def along(self, off):
        d, c, o = coords()
        return remote(
            self.stage_z.at[off - 1],
            self.land_z.at[off - 1],
            self.send_z.at[off],
            self.recv_z.at[off],
            (d, c, lax.rem(o + off, 4)),
        )

    def give(self, off, part):
        self.stage_s[off] = part[TOK:].astype(BF)
        self.near(off).start()
        self.own[off] = part[0:TOK]

    def send(self, off):
        self.near(off).wait_recv()
        total = self.own[off] + self.land_s[off].astype(F32)

        @pl.when(off > 0)
        def _():
            self.stage_z[off - 1] = total.astype(BF)
            self.along(off).start()

        @pl.when(off == 0)
        def _():
            self.own[0] = total

    def result(self):
        total = self.own[0]
        for off in (1, 3, 2):
            self.along(off).wait_recv()
            total = total + self.land_z[off - 1].astype(F32)
        return total

    def finish(self):
        for off in range(4):
            self.near(off).wait_send()
        for off in range(1, 4):
            self.along(off).wait_send()


def far_first(step):
    return lax.rem(2 + 3 * step + 3 * lax.div(step, 2) + 2 * lax.div(step, 3), 4)


def order(step):
    return step + lax.div(step, 2) - 2 * lax.div(step, 3)


class SumExchange:
    def __init__(self, sums, land, send, recv):
        self.sums, self.land, self.send, self.recv = sums, land, send, recv

    def start(self):
        d, c, o = coords()
        rank = lax.rem(c, 2) * 4 + o
        self.land[rank] = self.sums[...]
        self.copies = []
        for t in range(1, 8):
            copy = remote(
                self.sums, self.land.at[rank], self.send.at[t], self.recv.at[rank], rank_peer(d, c, o, t)
            )
            copy.start()
            self.copies.append(copy)

    def total(self):
        d, c, o = coords()
        for t in range(1, 8):
            _, c1, o1 = rank_peer(d, c, o, t)
            source = lax.rem(c1, 2) * 4 + o1
            remote(
                self.sums, self.land.at[source], self.send.at[t], self.recv.at[source], (d, sibling(c), o)
            ).wait_recv()
        for copy in self.copies:
            copy.wait_send()
        total = self.land[0]
        for i in range(1, 8):
            total = total + self.land[i]
        return total


def plane_slot(d, c):
    return lax.div(c, 2) * 8 + d


def token_block(ref, b, head):
    at = pl.multiple_of(head * BLK + lax.rem(b, 2) * TOK, TOK)
    return lax.div(b, 2), pl.ds(at, TOK)


SCRATCH = dict(
    w_raw=pltpu.VMEM((16, QW + 2 * KW), F32),
    gu_raw=pltpu.VMEM((16, 2 * FF), F32),
    pj_raw=pltpu.VMEM((32, D), F32),
    dn_raw=pltpu.VMEM((48, D), F32),
    pieces=pltpu.VMEM((RANKS, 16, RC), BF),
    gu_pieces=pltpu.VMEM((RANKS, 16, 2 * RF), BF),
    pj_mine=pltpu.VMEM((32, D), BF),
    dn_mine=pltpu.VMEM((48, D), BF),
    w_all=pltpu.VMEM((16, 64, RC), BF),
    gu_all=pltpu.VMEM((16, 64, 2 * RF), BF),
    pj_all=pltpu.VMEM((2, 128, D), BF),
    dn_all=pltpu.VMEM((2, 192, D), BF),
    gain_parts_land=pltpu.VMEM((16, 32, 128), BF),
    gains=pltpu.VMEM((8, D), F32),
    cos=pltpu.VMEM((HALF, HEAD), F32),
    sin=pltpu.VMEM((HALF, HEAD), F32),
    start=pltpu.VMEM((4, 8, 2 * BLK), jnp.int32),
    hid_all=pltpu.VMEM((HALF, D), BF),
    unit=pltpu.VMEM((HALF, RQ + RK), F32),
    sums=pltpu.VMEM((2, 8, TOK), F32),
    sums_land=pltpu.VMEM((8, 2, 8, TOK), F32),
    sums_back=pltpu.VMEM((2, 8, TOK), F32),
    sums_back_land=pltpu.VMEM((8, 2, 8, TOK), F32),
    scales=pltpu.VMEM((2, 8, TOK), F32),
    q_rot=pltpu.VMEM((4, 2 * BLK, HEAD), BF),
    kv_own=pltpu.VMEM((2, HALF, HEAD), BF),
    kv_other=pltpu.VMEM((2, HALF, HEAD), BF),
    v_t=pltpu.VMEM((2, HEAD, HALF), BF),
    top=pltpu.VMEM((4, 8, 2 * BLK), F32),
    running=pltpu.VMEM((4, 8, 2 * BLK), F32),
    accum=pltpu.VMEM((4, HEAD, 2 * BLK), F32),
    mixed=pltpu.VMEM((4, 2 * BLK, HEAD), F32),
    mixed_low=pltpu.VMEM((HALF, RQ), BF),
    lse=pltpu.VMEM((4, 8, 2 * BLK), F32),
    delta=pltpu.VMEM((4, 8, 2 * BLK), F32),
    full_res=pltpu.VMEM((HALF, D), BF),
    full_ffn=pltpu.VMEM((HALF, D), BF),
    full_branch=pltpu.VMEM((HALF, D), BF),
    wide=pltpu.VMEM((HALF, 2 * RF), F32),
    act=pltpu.VMEM((HALF, RF), BF),
    back_gu=pltpu.VMEM((HALF, 2 * RF), BF),
    stage_s=pltpu.VMEM((4, TOK, D), BF),
    stage_z=pltpu.VMEM((3, TOK, D), BF),
    own=pltpu.VMEM((4, TOK, D), F32),
    land_s=pltpu.VMEM((2, 4, TOK, D), BF),
    land_z=pltpu.VMEM((2, 3, TOK, D), BF),
    gain_rest=pltpu.VMEM((4, 512), F32),
    back_mixed=pltpu.VMEM((4, 2 * BLK, HEAD), BF),
    back_q=pltpu.VMEM((4, 2 * BLK, HEAD), F32),
    back_k=pltpu.VMEM((HALF, HEAD), F32),
    back_v=pltpu.VMEM((HALF, HEAD), F32),
    other_grad=pltpu.VMEM((2, HALF, HEAD), BF),
    other_land=pltpu.VMEM((2, HALF, HEAD), BF),
    back_qkv=pltpu.VMEM((HALF, RC), BF),
    pj_grad=pltpu.VMEM((2, 4, 2, 16, D), BF),
    gu_grad=pltpu.VMEM((2, 8, 64, 2 * RF), BF),
    dn_grad=pltpu.VMEM((RF, D), BF),
    qkv_grad=pltpu.VMEM((2, 8, 64, RC), BF),
    pj_x=pltpu.VMEM((4, 4, 16, D), BF),
    pj_mid=pltpu.VMEM((4, 16, D), BF),
    pj_y=pltpu.VMEM((4, 16, D), BF),
    dn_x=pltpu.VMEM((4, 192, 512), BF),
    dn_mid=pltpu.VMEM((192, 512), BF),
    dn_y=pltpu.VMEM((4, 48, 512), BF),
    gu_y=pltpu.VMEM((4, 2, 8, 16, 2 * RF), BF),
    gu_mid=pltpu.VMEM((2, 8, 16, 2 * RF), BF),
    gu_x=pltpu.VMEM((4, 8, 16, RF), BF),
    qkv_land=pltpu.VMEM((16, 8, 16, RQ), BF),
    pj_red=pltpu.VMEM((16, D), BF),
    gu_red=pltpu.VMEM((8, 16, RF), BF),
    dn_red=pltpu.VMEM((48, 512), BF),
    qkv_red=pltpu.VMEM((8, 16, RQ), BF),
    pj_own=pltpu.VMEM((16, D), BF),
    gu_own=pltpu.VMEM((16, FF), BF),
    dn_own=pltpu.VMEM((48, 512), BF),
    qkv_own=pltpu.VMEM((16, QW), BF),
    gain_vec=pltpu.VMEM((16, 512), F32),
    gain_y=pltpu.VMEM((4, 16, 512), F32),
    gain_half=pltpu.VMEM((16, 512), F32),
    gain_x=pltpu.VMEM((4, 16, 512), F32),
    gain_mid=pltpu.VMEM((16, 512), F32),
    gain_last=pltpu.VMEM((8, 16, 512), F32),
    layer_out=pltpu.VMEM((TOK, D), F32),
    back_resid=pltpu.VMEM((TOK, D), F32),
    input_part=pltpu.VMEM((TOK, D), F32),
    write_sem=DMA((4,)),
    kept_sem=DMA((3,)),
    raw_sem=DMA((4,)),
    h_send=DMA((8,)),
    h_recv=DMA((9,)),
    w_send=DMA((15,)),
    w_recv=DMA((16,)),
    gp_send=DMA((15,)),
    gp_recv=DMA((16,)),
    sum_send=DMA((8,)),
    sum_recv=DMA((8,)),
    sumb_send=DMA((8,)),
    sumb_recv=DMA((8,)),
    kv_send=DMA,
    kv_recv=DMA,
    gu_send=DMA((15,)),
    gu_recv=DMA((16,)),
    yw_send=DMA((4, 3)),
    yw_recv=DMA((4, 4)),
    pj_send=DMA((2,)),
    pj_recv=DMA((2,)),
    dn_send=DMA((2,)),
    dn_recv=DMA((2,)),
    send_s=DMA((4, 4)),
    recv_s=DMA((4, 4)),
    send_z=DMA((4, 4)),
    recv_z=DMA((4, 4)),
    a_send=DMA((8,)),
    a_recv=DMA((9,)),
    b_send=DMA((8,)),
    b_recv=DMA((9,)),
    e_send=DMA((8,)),
    e_recv=DMA((9,)),
    kvb_send=DMA((2,)),
    kvb_recv=DMA((2,)),
    plane_send=DMA((15,)),
    plane_recv=DMA((16,)),
    fan_send=DMA((8, 3)),
    fan_recv=DMA((8, 4)),
    move_send=DMA((2,)),
    move_recv=DMA((2,)),
    gur_send=DMA((7,)),
    gur_recv=DMA((8,)),
    qr_send=DMA((2, 7)),
    qr_recv=DMA((2, 8)),
    gl_send=DMA((7,)),
    gl_recv=DMA((8,)),
    y_send=DMA((4, 7)),
    y_recv=DMA((4, 8)),
)


def layer_kernel(hid, cot, segments, gain_parts, w_rows, gu_rows, pj_rows, dn_rows, *refs):
    layer_out, back_resid, input_part, qkv_sum, gu_sum, pj_sum, dn_sum, gain_sum = refs[:8]
    writes = []
    r = types.SimpleNamespace(**dict(zip(SCRATCH, refs[8:])))
    d, c, o = coords()
    half, core = lax.div(c, 2), lax.rem(c, 2)
    rank = core * 4 + o
    place = c * 4 + o
    part, side = lax.div(d, 2), lax.rem(d, 2)
    sib = (d, sibling(c), o)
    partner = (d, lax.rem(c + 2, 4), o)
    ranks = [rank_peer(d, c, o, t) for t in range(1, 8)]
    sources = ranks + [cross_peer(d, c, o, t) for t in range(8)]
    planes = [plane_peer(d, c, o, t) for t in range(1, 16)]
    owners = [dp_peer(d, c, o, t) for t in range(1, 8)]
    group = [group_peer(d, c, o, t) for t in range(1, 16)]
    crosses = [cross_peer(d, c, o, t) for t in range(8)]
    along_y = [(lax.rem(d + 2 * t, 8), c, o) for t in range(1, 4)]
    along_x = [plane_peer(d, c, o, t) for t in range(1, 4)]
    done = []

    def launch(copy):
        copy.start()
        done.append(copy)

    def write(src, dst):
        copy = pltpu.make_async_copy(src, dst, r.write_sem.at[len(writes)])
        copy.start()
        writes.append(copy)

    def drain():
        for copy in done:
            copy.wait_send()
        done.clear()

    def rank_of(to):
        return lax.rem(to[1], 2) * 4 + to[2]

    raws = [
        pltpu.make_async_copy(src.at[rows(part, dst.shape[0])], dst, r.raw_sem.at[i])
        for i, (src, dst) in enumerate(
            ((w_rows, r.w_raw), (pj_rows, r.pj_raw), (gu_rows, r.gu_raw), (dn_rows, r.dn_raw))
        )
    ]
    for copy in raws:
        copy.start()
    all_here = greet(group + planes + crosses)
    r.hid_all[rows(rank, TOK), :] = hid[...]
    raws[0].wait()
    for g in range(RANKS):
        r.pieces[g, :, 0:RQ] = r.w_raw[:, g * RQ : (g + 1) * RQ].astype(BF)
        r.pieces[g, :, RQ : RQ + RK] = r.w_raw[:, QW + g * RK : QW + (g + 1) * RK].astype(BF)
        r.pieces[g, :, RQ + RK : RC] = r.w_raw[:, QW + KW + g * RK : QW + KW + (g + 1) * RK].astype(BF)
    all_here()

    def piece_rows(ref, source):
        return ref.at[source, rows(part, 16)]

    def send_pieces(pieces, ref, send, recv):
        for i, to in enumerate(sources):
            launch(remote(pieces.at[rank_of(to)], piece_rows(ref, place), send.at[i], recv.at[place], to))
        ref[place, rows(part, 16)] = pieces[rank]

    def wait_pieces(pieces, ref, send, recv):
        for i, to in enumerate(sources):
            source = to[1] * 4 + to[2]
            remote(pieces.at[0], piece_rows(ref, source), send.at[i], recv.at[source], to).wait_recv()

    def spread(index, cut):
        for i, to in enumerate(along_y):
            launch(remote(cut(part), cut(part), r.yw_send.at[index, i], r.yw_recv.at[index, part], to))

    def wait_spread(index, cut):
        for i, to in enumerate(along_y):
            y = lax.div(to[0], 2)
            remote(cut(y), cut(y), r.yw_send.at[index, i], r.yw_recv.at[index, y], to).wait_recv()

    def w_cut(y):
        return r.w_all.at[:, rows(y, 16)]

    def gu_all_cut(y):
        return r.gu_all.at[:, rows(y, 16)]

    def pj_all_cut(y):
        return r.pj_all.at[:, rows(y, 32)]

    def dn_all_cut(y):
        return r.dn_all.at[:, rows(y, 48)]

    to_rank = lax.div(place, 2)
    slot = lax.rem(place, 2)
    near = (d, half * 2 + lax.div(to_rank, 4), lax.rem(to_rank, 4))
    far = (d + 1 - 2 * lax.rem(d, 2), (1 - half) * 2 + lax.div(to_rank, 4), lax.rem(to_rank, 4))
    pj_slot, dn_slot = r.pj_all.at[slot, rows(part, 32)], r.dn_all.at[slot, rows(part, 48)]
    keep = to_rank == rank
    pj_near = remote(r.pj_mine, pj_slot, r.pj_send.at[0], r.pj_recv.at[slot], near)
    dn_near = remote(r.dn_mine, dn_slot, r.dn_send.at[0], r.dn_recv.at[slot], near)

    def send_rows():
        @pl.when(jnp.logical_not(keep))
        def _():
            pj_near.start()
            dn_near.start()

        @pl.when(keep)
        def _():
            r.pj_all[slot, rows(part, 32)] = r.pj_mine[...]
            r.dn_all[slot, rows(part, 48)] = r.dn_mine[...]

        launch(remote(r.pj_mine, pj_slot, r.pj_send.at[1], r.pj_recv.at[slot], far))
        launch(remote(r.dn_mine, dn_slot, r.dn_send.at[1], r.dn_recv.at[slot], far))

    def wait_rows():
        for i in range(2):
            from_self = 2 * rank + i == place

            @pl.when(jnp.logical_not(from_self))
            def _(i=i):
                pj_at, dn_at = r.pj_all.at[i, rows(part, 32)], r.dn_all.at[i, rows(part, 48)]
                remote(r.pj_mine, pj_at, r.pj_send.at[0], r.pj_recv.at[i], partner).wait_recv()
                remote(r.dn_mine, dn_at, r.dn_send.at[0], r.dn_recv.at[i], partner).wait_recv()

    send_pieces(r.pieces, r.w_all, r.w_send, r.w_recv)
    gather_start(r.hid_all, r.h_send, r.h_recv)
    for i, to in enumerate(sources):
        launch(
            remote(
                gain_parts.at[rank_of(to)], r.gain_parts_land.at[place], r.gp_send.at[i], r.gp_recv.at[place], to
            )
        )
    r.gain_parts_land[place] = gain_parts[rank]
    ids = segments[...]
    own_ids = segments[:, rows(half, HALF)]
    starts = jnp.zeros((1, HALF), jnp.int32)
    for i in range(1, 6):
        below = jnp.sum((ids < i).astype(F32), axis=1, keepdims=True).astype(jnp.int32)
        starts = jnp.where(own_ids == i, below, starts)
    for block in range(4):
        row = starts[:, block * BLK : (block + 1) * BLK]
        r.start[block] = jnp.broadcast_to(jnp.concatenate([row, row], axis=1), (8, 2 * BLK))
    lane = lax.broadcasted_iota(jnp.int32, (1, HEAD), 1)
    frequency = jnp.exp(lax.rem(lane, HEAD // 2).astype(F32) * (-math.log(THETA) / (HEAD // 2)))
    sign = jnp.where(lane < HEAD // 2, -1.0, 1.0)
    token = half * HALF + lax.broadcasted_iota(jnp.int32, (1, HALF), 1)
    position = (token - starts).astype(F32)
    for b in range(RANKS):
        angles = column(position[:, b * TOK : (b + 1) * TOK]) * frequency
        r.cos[b * TOK : (b + 1) * TOK, :] = jnp.cos(angles)
        r.sin[b * TOK : (b + 1) * TOK, :] = jnp.sin(angles) * sign
    wait_pieces(r.pieces, r.w_all, r.w_send, r.w_recv)
    spread(0, w_cut)
    for copy in raws[1:]:
        copy.wait()
    for g in range(RANKS):
        r.gu_pieces[g, :, 0:RF] = r.gu_raw[:, g * RF : (g + 1) * RF].astype(BF)
        r.gu_pieces[g, :, RF:] = r.gu_raw[:, FF + g * RF : FF + (g + 1) * RF].astype(BF)
    r.pj_mine[...] = r.pj_raw[...].astype(BF)
    r.dn_mine[...] = r.dn_raw[...].astype(BF)

    send_rows()
    send_pieces(r.gu_pieces, r.gu_all, r.gu_send, r.gu_recv)
    gather_relay(r.hid_all, r.h_send, r.h_recv)
    wait_spread(0, w_cut)
    wait_rows()
    spread(1, pj_all_cut)
    wait_pieces(r.gu_pieces, r.gu_all, r.gu_send, r.gu_recv)
    spread(2, gu_all_cut)
    spread(3, dn_all_cut)


    line = lax.broadcasted_iota(jnp.int32, (8, TOK), 0)

    def put_row(table, b, values):
        return jnp.where(line == b, values, table)

    def get_row(table, b):
        return jnp.sum(jnp.where(line == b, table, 0.0), axis=0, keepdims=True)

    r.sums[...] = jnp.zeros_like(r.sums)
    r.sums_back[...] = jnp.zeros_like(r.sums_back)

    def project(step, _):
        mine, other = gather_arrive(r.hid_all, r.h_send, r.h_recv, order(step))
        both = jnp.concatenate([r.hid_all[rows(mine, TOK), :], r.hid_all[rows(other, TOK), :]], axis=0)
        out = nn(both, r.w_all[...].reshape(D, RC))
        squares = out * out
        q_sum, k_sum = row_sums(squares[:, 0:RQ]), row_sums(squares[:, RQ : RQ + RK])
        r.wide[rows(mine, TOK), 0:RC] = out[0:TOK]
        r.wide[rows(other, TOK), 0:RC] = out[TOK:]
        for i, row_sum in enumerate((q_sum, k_sum)):
            with_mine = put_row(r.sums[i], mine, row_sum[:, 0:TOK])
            r.sums[i] = put_row(with_mine, other, row_sum[:, TOK:])
        return 0

    lax.fori_loop(0, 4, project, 0)
    exchange = SumExchange(r.sums, r.sums_land, r.sum_send, r.sum_recv)
    exchange.start()
    for i, to in enumerate(sources):
        source = to[1] * 4 + to[2]
        remote(
            gain_parts.at[0], r.gain_parts_land.at[source], r.gp_send.at[i], r.gp_recv.at[source], to
        ).wait_recv()
    gains = r.gain_parts_land[0].astype(F32)
    for i in range(1, 16):
        gains = gains + r.gain_parts_land[i].astype(F32)
    for i in range(3):
        r.gains[0:1, i * 128 : (i + 1) * 128] = gains[i : i + 1]
    for i in range(8):
        r.gains[1:2, i * 128 : (i + 1) * 128] = gains[3 + i : 4 + i]
        r.gains[2:3, i * 128 : (i + 1) * 128] = gains[11 + i : 12 + i]
    total = exchange.total()
    r.scales[0] = lax.rsqrt(total[0] * (1.0 / QW) + NORM_EPS)
    r.scales[1] = lax.rsqrt(total[1] * (1.0 / KW) + NORM_EPS)

    def finish(b, _):
        at = rows(b, TOK)
        q_scale, k_scale = column(get_row(r.scales[0], b)), column(get_row(r.scales[1], b))
        cosine, sine = r.cos[at, :], r.sin[at, :]
        for head in range(2):
            cols = slice(head * HEAD, (head + 1) * HEAD)
            q_unit = r.wide[at, cols] * q_scale
            r.unit[at, cols] = q_unit
            block, spot = token_block(r.q_rot, b, head)
            r.q_rot[block, spot, :] = rope(q_unit * r.gains[0:1, cols], cosine, sine).astype(BF)
        cols = slice(RQ, RQ + RK)
        k_unit = r.wide[at, cols] * k_scale
        r.unit[at, cols] = k_unit
        r.kv_own[0, at, :] = rope(k_unit * r.gains[0:1, cols], cosine, sine).astype(BF)
        r.kv_own[1, at, :] = r.wide[at, RQ + RK : RC].astype(BF)
        return 0

    lax.fori_loop(0, RANKS, finish, 0)

    kv_copy = remote(r.kv_own, r.kv_other, r.kv_send, r.kv_recv, partner)

    @pl.when(half == 0)
    def _():
        kv_copy.start()

    gather_finish(r.hid_all, r.h_send, r.h_recv)

    r.v_t[0] = jnp.transpose(r.kv_own[1].astype(F32)).astype(BF)

    def allowed_tile(block, key_base, diagonal):
        key_index = lax.broadcasted_iota(jnp.int32, (BLK, 2 * BLK), 0)
        allowed = key_index >= r.start[block, 0:1, :] - key_base
        if diagonal:
            lane = lax.broadcasted_iota(jnp.int32, (1, 2 * BLK), 1)
            allowed = allowed & (key_index <= lax.rem(lane, BLK))
        return allowed

    def tile(block, keys, values_t, key_base, carry):
        scores = nt(keys, r.q_rot[block]) * SCALE_TWO
        scores = jnp.where(allowed_tile(block, key_base, carry is None), scores, MASKED)
        top_now = jnp.max(scores, axis=0, keepdims=True)
        if carry is None:
            probs = jnp.exp2(scores - top_now)
            return top_now, jnp.sum(probs, axis=0, keepdims=True), nn(values_t, probs.astype(BF))
        top_old, run_old, acc_old = carry
        top_new = jnp.maximum(top_old, top_now)
        fade = jnp.exp2(top_old - top_new)
        probs = jnp.exp2(scores - top_new)
        return (
            top_new,
            run_old * fade + jnp.sum(probs, axis=0, keepdims=True),
            acc_old * fade + nn(values_t, probs.astype(BF)),
        )

    def keep_state(block, state):
        r.top[block] = jnp.broadcast_to(state[0], (8, 2 * BLK))
        r.running[block] = jnp.broadcast_to(state[1], (8, 2 * BLK))
        r.accum[block] = state[2]

    def local_block(block, _):
        def local_tile(j, carry):
            return tile(
                block, r.kv_own[0, rows(j, BLK), :], r.v_t[0, :, rows(j, BLK)], half * HALF + j * BLK, carry
            )

        keep_state(block, lax.fori_loop(0, block, local_tile, local_tile(block, None)))
        return 0

    lax.fori_loop(0, 4, local_block, 0)

    @pl.when(half == 1)
    def _():
        kv_copy.wait_recv()
        r.v_t[1] = jnp.transpose(r.kv_other[1].astype(F32)).astype(BF)

        def other_block(block, _):
            state = (r.top[block][0:1], r.running[block][0:1], r.accum[block])

            def other_tile(j, carry):
                return tile(block, r.kv_other[0, rows(j, BLK), :], r.v_t[1, :, rows(j, BLK)], j * BLK, carry)

            keep_state(block, lax.fori_loop(0, 4, other_tile, state, unroll=True))
            return 0

        lax.fori_loop(0, 4, other_block, 0)

    @pl.when(half == 0)
    def _():
        kv_copy.wait_send()

    def close_block(block, _):
        run = r.running[block]
        r.lse[block] = r.top[block] + jnp.log2(run)
        out = jnp.transpose(r.accum[block] * (1.0 / run[0:1]))
        r.mixed[block] = out
        for head in range(2):
            r.mixed_low[rows(block, BLK), head * HEAD : (head + 1) * HEAD] = out[
                head * BLK : (head + 1) * BLK
            ].astype(BF)
        return 0

    lax.fori_loop(0, 4, close_block, 0)

    wait_spread(1, pj_all_cut)
    gain_attn, gain_ffn = r.gains[1:2, :], r.gains[2:3, :]

    def both_rows(ref, mine, other):
        return jnp.concatenate([ref[rows(mine, TOK), :], ref[rows(other, TOK), :]], axis=0)

    s = Scatter(r, 0)

    def proj_step(step, _):
        off = far_first(step)
        at = lax.rem(o + off, 4)
        s.give(off, nn(both_rows(r.mixed_low, core * 4 + at, (1 - core) * 4 + at), r.pj_all[...].reshape(RQ, D)))

        @pl.when(step > 0)
        def _():
            s.send(far_first(step - 1))

        return 0

    lax.fori_loop(0, 4, proj_step, 0)
    s.send(0)
    branch = s.result()
    branch_scale = rms_scale(branch)
    branch_unit = branch * branch_scale
    residual = hid[...].astype(F32) + branch_unit * gain_attn
    r.full_res[rows(rank, TOK), :] = residual.astype(BF)
    gather_start(r.full_res, r.a_send, r.a_recv)
    s.finish()
    wait_spread(2, gu_all_cut)
    wait_spread(3, dn_all_cut)

    s1 = Scatter(r, 1)

    def ffn_step(step, _):
        off = order(step)
        mine, other = gather_step(r.full_res, r.a_send, r.a_recv, step)
        both = nn(both_rows(r.full_res, mine, other), r.gu_all[...].reshape(D, 2 * RF))
        r.wide[rows(mine, TOK), :] = both[0:TOK]
        r.wide[rows(other, TOK), :] = both[TOK:]
        gate, up = both[:, 0:RF], both[:, RF:]
        act_low = (gate * jax.nn.sigmoid(gate) * up).astype(BF)
        r.act[rows(mine, TOK), :] = act_low[0:TOK]
        r.act[rows(other, TOK), :] = act_low[TOK:]

        @pl.when(step > 0)
        def _():
            s1.send(order(step - 1))

        s1.give(off, nn(act_low, r.dn_all[...].reshape(RF, D)))
        return 0

    lax.fori_loop(0, 4, ffn_step, 0)
    s1.send(2)
    ffn = s1.result()
    ffn_scale = rms_scale(ffn)
    ffn_unit = ffn * ffn_scale
    r.layer_out[...] = residual + ffn_unit * gain_ffn
    write(r.layer_out, layer_out)
    cotangent = cot[...].astype(F32)
    back_ffn = norm_back(cotangent, ffn_unit, ffn_scale, gain_ffn)
    r.full_ffn[rows(rank, TOK), :] = back_ffn.astype(BF)
    gather_start(r.full_ffn, r.b_send, r.b_recv)
    gain_row = jnp.sum(cotangent * ffn_unit, axis=0, keepdims=True)
    r.gain_rest[2:3, :] = gain_row[:, 0:512]
    r.gain_rest[3:4, :] = gain_row[:, 512:]
    gather_finish(r.full_res, r.a_send, r.a_recv)
    s1.finish()

    s2 = Scatter(r, 2)

    def back_step(step, _):
        off = order(step)
        mine, other = gather_step(r.full_ffn, r.b_send, r.b_recv, step)
        back_act = nt(both_rows(r.full_ffn, mine, other), r.dn_all[...].reshape(RF, D))
        both = both_rows(r.wide, mine, other)
        gate, up = both[:, 0:RF], both[:, RF:]
        sig = jax.nn.sigmoid(gate)
        back_gate = back_act * up * sig * (1.0 + gate * (1.0 - sig))
        back_up = back_act * (gate * sig)
        back_both = jnp.concatenate([back_gate, back_up], axis=1).astype(BF)
        r.back_gu[rows(mine, TOK), :] = back_both[0:TOK]
        r.back_gu[rows(other, TOK), :] = back_both[TOK:]

        @pl.when(step > 0)
        def _():
            s2.send(order(step - 1))

        s2.give(off, nt(back_both, r.gu_all[...].reshape(D, 2 * RF)))
        return 0

    lax.fori_loop(0, 4, back_step, 0)
    s2.send(2)

    def y_of(to):
        return lax.div(to[0], 2)

    def x_of(to):
        return lax.div(to[1], 2) * 2 + lax.rem(to[0], 2)

    here = (d, c, o)

    def fan_out(index, peers, place_of, cut, land):
        slot = place_of(here)
        for i, to in enumerate(peers):
            launch(remote(cut(to), land.at[slot], r.fan_send.at[index, i], r.fan_recv.at[index, slot], to))
        land[slot] = cut(here)[...]

    def fan_in(index, peers, place_of, land):
        for i, to in enumerate(peers):
            slot = place_of(to)
            remote(
                land.at[slot], land.at[slot], r.fan_send.at[index, i], r.fan_recv.at[index, slot], to
            ).wait_recv()
        total = land[0].astype(F32)
        for i in range(1, 4):
            total = total + land[i].astype(F32)
        return total

    def gu_step(b, _):
        grad = tn(r.full_res[:, rows(b, 128)], r.back_gu[...])
        r.gu_grad[lax.div(b, 4), rows(lax.rem(b, 4), 2)] = grad.astype(BF).reshape(2, 64, 2 * RF)
        return 0

    lax.fori_loop(0, 8, gu_step, 0)

    fan_out(1, along_y, y_of, lambda to: r.gu_grad.at[:, :, rows(y_of(to), 16)], r.gu_y)
    r.dn_grad[...] = tn(r.act[...], r.full_ffn[...]).astype(BF)
    fan_out(
        0,
        along_x,
        x_of,
        lambda to: r.dn_grad.at[rows(lax.div(to[1], 2), 192), rows(lax.rem(to[0], 2), 512)],
        r.dn_x,
    )
    resid_grad = cotangent + s2.result()
    r.back_resid[...] = resid_grad
    write(r.back_resid, back_resid)
    gain_row = jnp.sum(resid_grad * branch_unit, axis=0, keepdims=True)
    r.gain_rest[0:1, :] = gain_row[:, 0:512]
    r.gain_rest[1:2, :] = gain_row[:, 512:]
    back_branch = norm_back(resid_grad, branch_unit, branch_scale, gain_attn)
    r.full_branch[rows(rank, TOK), :] = back_branch.astype(BF)
    gather_start(r.full_branch, r.e_send, r.e_recv)
    gather_finish(r.full_ffn, r.b_send, r.b_recv)
    s2.finish()

    def mixed_step(step, _):
        mine, other = gather_step(r.full_branch, r.e_send, r.e_recv, step)
        out = nt(both_rows(r.full_branch, mine, other), r.pj_all[...].reshape(RQ, D)).astype(BF)
        for head in range(2):
            for i, b in enumerate((mine, other)):
                block, spot = token_block(r.back_mixed, b, head)
                r.back_mixed[block, spot, :] = out[i * TOK : (i + 1) * TOK, head * HEAD : (head + 1) * HEAD]
        return 0

    lax.fori_loop(0, 4, mixed_step, 0)
    r.pj_grad[...] = tn(r.mixed_low[...], r.full_branch[...]).astype(BF).reshape(2, 4, 2, 16, D)
    fan_out(2, along_x, x_of, lambda to: r.pj_grad.at[lax.div(to[1], 2), :, lax.rem(to[0], 2)], r.pj_x)
    gather_finish(r.full_branch, r.e_send, r.e_recv)

    def delta_step(block, _):
        r.delta[block] = row_sums(r.back_mixed[block].astype(F32) * r.mixed[block])
        r.back_q[block] = jnp.zeros((2 * BLK, HEAD), F32)
        return 0

    lax.fori_loop(0, 4, delta_step, 0)

    def back_tile(block, keys, values, key_base, diagonal, carry):
        grad_k, grad_v = carry
        query, grad_out = r.q_rot[block], r.back_mixed[block]
        scores = nt(keys, query) * SCALE_TWO
        probs = jnp.where(allowed_tile(block, key_base, diagonal), jnp.exp2(scores - r.lse[block, 0:1, :]), 0.0)
        back_prob = nt(values, grad_out)
        back_score = (probs * (back_prob - r.delta[block, 0:1, :])).astype(BF)
        grad_k = grad_k + nn(back_score, query)
        grad_v = grad_v + nn(probs.astype(BF), grad_out)
        r.back_q[block] += tn(back_score, keys)
        return grad_k, grad_v

    zero = (jnp.zeros((BLK, HEAD), F32), jnp.zeros((BLK, HEAD), F32))
    def send_back(i):
        at = rows(i, 2 * BLK)
        return remote(r.other_grad.at[:, at], r.other_land.at[:, at], r.kvb_send.at[i], r.kvb_recv.at[i], partner)


    def local_keys(j, _):
        at = rows(j, BLK)
        keys, values = r.kv_own[0, at, :], r.kv_own[1, at, :]
        base = half * HALF + j * BLK
        grad_k, grad_v = lax.fori_loop(
            j + 1,
            4,
            lambda block, carry: back_tile(block, keys, values, base, False, carry),
            back_tile(j, keys, values, base, True, zero),
        )
        r.back_k[at, :] = grad_k * SCORE_SCALE
        r.back_v[at, :] = grad_v
        return 0

    def other_keys(j, _):
        at = rows(j, BLK)
        keys, values = r.kv_other[0, at, :], r.kv_other[1, at, :]
        grad_k, grad_v = lax.fori_loop(
            0, 4, lambda block, carry: back_tile(block, keys, values, j * BLK, False, carry), zero, unroll=2
        )
        r.other_grad[0, at, :] = (grad_k * SCORE_SCALE).astype(BF)
        r.other_grad[1, at, :] = grad_v.astype(BF)
        return 0

    def first_part(low, high):
        lax.fori_loop(low, low + (high - low) * (1 - half), local_keys, 0)
        lax.fori_loop(low, low + (high - low) * half, other_keys, 0)

    first_part(0, 2)

    @pl.when(half == 1)
    def _():
        send_back(0).start()


    r.dn_mid[...] = fan_in(0, along_x, x_of, r.dn_x).astype(BF)
    fan_out(3, along_y, y_of, lambda to: r.dn_mid.at[rows(y_of(to), 48)], r.dn_y)
    r.gu_mid[...] = fan_in(1, along_y, y_of, r.gu_y).astype(BF)
    fan_out(
        4,
        along_x,
        x_of,
        lambda to: r.gu_mid.at[lax.div(to[1], 2), :, :, rows(lax.rem(to[0], 2), RF)],
        r.gu_x,
    )
    r.pj_mid[...] = fan_in(2, along_x, x_of, r.pj_x).astype(BF)
    fan_out(5, along_y, y_of, lambda to: r.pj_mid.at[y_of(to)], r.pj_y)

    first_part(2, 4)

    @pl.when(half == 1)
    def _():
        send_back(1).start()

    r.dn_red[...] = fan_in(3, along_y, y_of, r.dn_y).astype(BF)
    r.gu_red[...] = fan_in(4, along_x, x_of, r.gu_x).astype(BF)
    r.pj_red[...] = fan_in(5, along_y, y_of, r.pj_y).astype(BF)
    target = 2 * rank + half
    to_owner = (d, lax.div(target, 4), lax.rem(target, 4))
    stay = target == place
    pj_move = remote(r.pj_red, r.pj_own, r.move_send.at[0], r.move_recv.at[0], to_owner)
    dn_move = remote(r.dn_red, r.dn_own, r.move_send.at[1], r.move_recv.at[1], to_owner)

    @pl.when(stay)
    def _():
        r.pj_own[...] = r.pj_red[...]
        r.dn_own[...] = r.dn_red[...]

    @pl.when(jnp.logical_not(stay))
    def _():
        pj_move.start()
        dn_move.start()

    for i, to in enumerate(ranks):
        launch(
            remote(
                r.gu_red.at[rank_of(to)],
                r.gu_own.at[:, rows(rank, RF)],
                r.gur_send.at[i],
                r.gur_recv.at[rank],
                to,
            )
        )
    r.gu_own[:, rows(rank, RF)] = r.gu_red[rank]

    lax.fori_loop(0, 2 * half, local_keys, 0)

    @pl.when(half == 0)
    def _():
        for i in range(2):
            at = rows(i, 2 * BLK)
            send_back(i).wait_recv()
            r.back_k[at, :] += r.other_land[0, at, :].astype(F32)
            r.back_v[at, :] += r.other_land[1, at, :].astype(F32)

    @pl.when(jnp.logical_not(stay))
    def _():
        pj_move.wait_send()
        dn_move.wait_send()
        pj_move.wait_recv()
        dn_move.wait_recv()

    for i, to in enumerate(ranks):
        remote(
            r.gu_red.at[0], r.gu_own.at[:, rows(rank_of(to), RF)], r.gur_send.at[i], r.gur_recv.at[rank_of(to)], sib
        ).wait_recv()

    def owned(n, e):
        e_part, e_side = lax.div(e, 2), lax.rem(e, 2)
        return (
            pj_sum.at[rows(e, 16), :],
            dn_sum.at[rows(e_part, 48), rows(e_side, 512)],
            gu_sum.at[rows(e_part, 16), rows(e_side, FF)],
            qkv_sum.at[rows(e_part, 16), rows(e_side, QW)],
        )[n]

    own_refs = (r.pj_own, r.dn_own, r.gu_own, r.qkv_own)
    kept = [pltpu.make_async_copy(own_refs[n], owned(n, d), r.kept_sem.at[n]) for n in range(3)]
    for copy in kept:
        copy.start()
    across = (d + 1 - 2 * side, c, o)
    for n in range(2):
        launch(remote(own_refs[n], owned(n, d), r.y_send.at[n, 0], r.y_recv.at[n, 4], across))
    for i, to in enumerate(along_y):
        launch(remote(r.gu_own, owned(2, d), r.y_send.at[2, i], r.y_recv.at[2, part], to))

    def pair(n, y):
        return (pj_sum.at[rows(y, 32)], dn_sum.at[rows(y, 48)])[n]

    def column_half(of_side):
        return gu_sum.at[:, rows(of_side, FF)]

    def share_again():
        for copy in kept:
            copy.wait()
        for n in range(2):
            remote(own_refs[n], owned(n, across[0]), r.y_send.at[n, 0], r.y_recv.at[n, 4], across).wait_recv()
            for i, to in enumerate(along_y):
                launch(remote(pair(n, part), pair(n, part), r.y_send.at[n, 1 + i], r.y_recv.at[n, part], to))
        for i, to in enumerate(along_y):
            remote(r.gu_own, owned(2, to[0]), r.y_send.at[2, i], r.y_recv.at[2, y_of(to)], to).wait_recv()
        launch(remote(column_half(side), column_half(side), r.y_send.at[2, 3], r.y_recv.at[2, 4], across))

    def shared():
        for n in range(2):
            for i, to in enumerate(along_y):
                y = y_of(to)
                remote(pair(n, y), pair(n, y), r.y_send.at[n, 1 + i], r.y_recv.at[n, y], to).wait_recv()
        other_half = column_half(1 - side)
        remote(other_half, other_half, r.y_send.at[2, 3], r.y_recv.at[2, 4], across).wait_recv()

    lax.fori_loop(2 * half, 4 * half, local_keys, 0)

    @pl.when(half == 1)
    def _():
        for i in range(2):
            send_back(i).wait_send()

    def weigh(b, _):
        at = rows(b, TOK)
        cosine, sine = r.cos[at, :], r.sin[at, :]
        totals = []
        for head in range(2):
            cols = slice(head * HEAD, (head + 1) * HEAD)
            block, spot = token_block(r.back_q, b, head)
            grad = unrope(r.back_q[block, spot, :] * SCORE_SCALE, cosine, sine)
            r.wide[at, cols] = grad
            totals.append(grad * r.gains[0:1, cols] * r.unit[at, cols])
        cols = slice(RQ, RQ + RK)
        grad = unrope(r.back_k[at, :], cosine, sine)
        r.wide[at, cols] = grad
        q_sum = row_sums(totals[0] + totals[1])
        k_sum = row_sums(grad * r.gains[0:1, cols] * r.unit[at, cols])
        r.sums_back[0] = put_row(r.sums_back[0], b, q_sum)
        r.sums_back[1] = put_row(r.sums_back[1], b, k_sum)
        return 0

    lax.fori_loop(0, RANKS, weigh, 0)
    exchange = SumExchange(r.sums_back, r.sums_back_land, r.sumb_send, r.sumb_recv)
    exchange.start()

    gain_own = jnp.sum(r.wide[:, 0 : RQ + RK] * r.unit[...], axis=0, keepdims=True)
    row = lax.broadcasted_iota(jnp.int32, (16, 512), 0)
    col = lax.broadcasted_iota(jnp.int32, (16, 512), 1)
    own_q, own_k = gain_own[:, 0:RQ], gain_own[:, RQ:]
    at_q = (row == lax.div(rank, 2)) & (lax.div(col, RQ) == lax.rem(rank, 2))
    at_k = (row == 4 + lax.div(rank, 4)) & (lax.div(col, RK) == lax.rem(rank, 4))
    r.gain_vec[...] = jnp.where(at_q, jnp.concatenate([own_q] * 2, axis=1), 0.0) + jnp.where(
        at_k, jnp.concatenate([own_k] * 4, axis=1), 0.0
    )
    r.gain_vec[6:10, :] = r.gain_rest[...]
    fan_out(6, along_y, y_of, lambda to: r.gain_vec, r.gain_y)

    total = exchange.total()
    r.sums_back[0] = total[0] * (1.0 / QW)
    r.sums_back[1] = total[1] * (1.0 / KW)

    def back_norm(b, _):
        at = rows(b, TOK)
        q_scale, k_scale = column(get_row(r.scales[0], b)), column(get_row(r.scales[1], b))
        q_mean, k_mean = column(get_row(r.sums_back[0], b)), column(get_row(r.sums_back[1], b))
        for head in range(2):
            cols = slice(head * HEAD, (head + 1) * HEAD)
            weighted = r.wide[at, cols] * r.gains[0:1, cols]
            r.back_qkv[at, cols] = (q_scale * (weighted - r.unit[at, cols] * q_mean)).astype(BF)
        cols = slice(RQ, RQ + RK)
        weighted = r.wide[at, cols] * r.gains[0:1, cols]
        r.back_qkv[at, cols] = (k_scale * (weighted - r.unit[at, cols] * k_mean)).astype(BF)
        r.back_qkv[at, RQ + RK : RC] = r.back_v[at, :].astype(BF)
        return 0

    lax.fori_loop(0, RANKS, back_norm, 0)
    share_again()

    def grad_step(b, _):
        grad = tn(r.hid_all[:, rows(b, 128)], r.back_qkv[...])
        r.qkv_grad[lax.div(b, 4), rows(lax.rem(b, 4), 2)] = grad.astype(BF).reshape(2, 64, RC)
        return 0

    def qkv_cut(e, h):
        return h, slice(None), rows(lax.div(e, 2), 16), rows(lax.rem(e, 2), RQ)

    old = list(done)
    done.clear()

    def drain_old():
        for copy in old:
            copy.wait_send()

        @pl.when(jnp.logical_not(keep))
        def _():
            pj_near.wait_send()
            dn_near.wait_send()

    slot = plane_slot(d, c)
    for which in range(2):
        rows_half = half + which - 2 * half * which
        lax.fori_loop(4 * rows_half, 4 * rows_half + 4, grad_step, 0)
        for i, to in enumerate(planes):
            if ((i + 1) % 4) // 2 == which:
                src = r.qkv_grad.at[qkv_cut(to[0], lax.div(to[1], 2))]
                launch(remote(src, r.qkv_land.at[slot], r.plane_send.at[i], r.plane_recv.at[slot], to))
    r.qkv_land[slot] = r.qkv_grad[qkv_cut(d, half)]
    r.gain_half[...] = fan_in(6, along_y, y_of, r.gain_y)
    fan_out(7, along_x, x_of, lambda to: r.gain_half, r.gain_x)

    s3 = Scatter(r, 3)

    def input_step(step, _):
        off = far_first(step)
        at = lax.rem(o + off, 4)
        s3.give(off, nt(both_rows(r.back_qkv, core * 4 + at, (1 - core) * 4 + at), r.w_all[...].reshape(D, RC)))

        @pl.when(step > 0)
        def _():
            s3.send(far_first(step - 1))

        return 0

    lax.fori_loop(0, 4, input_step, 0)
    s3.send(0)
    drain_old()

    total = fan_in(7, along_x, x_of, r.gain_x)
    r.gain_mid[...] = total
    for i, to in enumerate(ranks):
        launch(remote(r.gain_mid, r.gain_last.at[rank], r.gl_send.at[i], r.gl_recv.at[rank], to))
    r.gain_last[rank] = total

    for i, to in enumerate(planes):
        source = plane_slot(to[0], to[1])
        land = r.qkv_land.at[source]
        remote(land, land, r.plane_send.at[i], r.plane_recv.at[source], to).wait_recv()
    total = r.qkv_land[0].astype(F32)
    for i in range(1, 16):
        total = total + r.qkv_land[i].astype(F32)
    r.qkv_red[...] = total.astype(BF)

    def qkv_cols(of_rank, i):
        return rows((1 - side) * (of_rank * 2 + i) + side * (of_rank + i * 8), RK)

    for i, to in enumerate(ranks):
        for j in range(2):
            launch(
                remote(
                    r.qkv_red.at[rank_of(to), :, pl.ds(j * RK, RK)],
                    r.qkv_own.at[:, qkv_cols(rank, j)],
                    r.qr_send.at[j, i],
                    r.qr_recv.at[j, rank],
                    to,
                )
            )
    for j in range(2):
        r.qkv_own[:, qkv_cols(rank, j)] = r.qkv_red[rank][:, j * RK : (j + 1) * RK]

    r.input_part[...] = s3.result()
    write(r.input_part, input_part)
    for i, to in enumerate(ranks):
        remote(
            r.gain_mid, r.gain_last.at[rank_of(to)], r.gl_send.at[i], r.gl_recv.at[rank_of(to)], sib
        ).wait_recv()
    total = r.gain_last[0]
    for i in range(1, 8):
        total = total + r.gain_last[i]
    for i in range(40):
        gain_sum[i : i + 1, :] = total[i // 4 : i // 4 + 1, (i % 4) * 128 : (i % 4 + 1) * 128]

    for i, to in enumerate(ranks):
        for j in range(2):
            remote(
                r.qkv_red.at[0, :, pl.ds(j * RK, RK)],
                r.qkv_own.at[:, qkv_cols(rank_of(to), j)],
                r.qr_send.at[j, i],
                r.qr_recv.at[j, rank_of(to)],
                sib,
            ).wait_recv()
    for i, to in enumerate(owners):
        launch(remote(r.qkv_own, owned(3, d), r.y_send.at[3, i], r.y_recv.at[3, d], to))
    write(r.qkv_own, owned(3, d))
    for i, to in enumerate(owners):
        remote(r.qkv_own, owned(3, to[0]), r.y_send.at[3, i], r.y_recv.at[3, to[0]], sib).wait_recv()
    shared()
    s3.finish()
    drain()
    for copy in writes:
        copy.wait()


def call_layer(*operands):
    any_space = pl.BlockSpec(memory_space=pl.ANY)
    return pl.pallas_call(
        layer_kernel,
        name="layer",
        out_shape=(
            jax.ShapeDtypeStruct((TOK, D), F32),
            jax.ShapeDtypeStruct((TOK, D), F32),
            jax.ShapeDtypeStruct((TOK, D), F32),
            jax.ShapeDtypeStruct((64, QW + 2 * KW), BF),
            jax.ShapeDtypeStruct((64, 2 * FF), BF),
            jax.ShapeDtypeStruct((128, D), BF),
            jax.ShapeDtypeStruct((192, D), BF),
            jax.ShapeDtypeStruct((40, 128), F32),
        ),
        in_specs=[VMEM] * 4 + [any_space] * 4,
        out_specs=[any_space] * 7 + [VMEM],
        scratch_shapes=list(SCRATCH.values()),
        compiler_params=pltpu.CompilerParams(
            collective_id=1, has_side_effects=True, vmem_limit_bytes=63 * 2**20
        ),
    )(*operands)


def adam_step(weight, moment, square, grad_sum, rate, decay):
    moment_new = BETA_ONE * moment + (1.0 - BETA_ONE) * grad_sum
    square_new = BETA_TWO * square + (1.0 - BETA_TWO) * grad_sum * grad_sum
    moment_hat = moment_new / (1.0 - BETA_ONE**STEP)
    square_hat = square_new / (1.0 - BETA_TWO**STEP)
    weight_new = weight - rate * (moment_hat / (jnp.sqrt(square_hat) + ADAM_EPS) + decay * weight)
    return (weight_new, moment_new, square_new)


def update_kernel(*refs):
    ins, outs = refs[:19], refs[19:]
    layer_out, back_resid, input_part = ins[:3]
    outs[0][...] = layer_out[...].astype(BF)
    outs[1][...] = back_resid[...] + input_part[...]
    for i in range(4):
        weight, moment, square, grad = (ref[...] for ref in ins[3 + 4 * i : 7 + 4 * i])
        new = adam_step(weight, moment, square, grad.astype(F32), RATE_MATRIX, DECAY)
        for ref, value in zip(outs[2 + 3 * i : 5 + 3 * i], new):
            ref[...] = value


def call_update(*operands):
    def half_rows(shape):
        return pl.BlockSpec((shape[0] // 2, shape[1]), lambda i: (i, 0))

    results = [operands[0], operands[1]] + [operands[3 + 4 * i + j] for i in range(4) for j in range(3)]
    types_out = [BF] + [F32] * 13
    return pl.pallas_call(
        update_kernel,
        name="update",
        grid=(2,),
        out_shape=[jax.ShapeDtypeStruct(a.shape, t) for a, t in zip(results, types_out)],
        in_specs=[half_rows(a.shape) for a in operands],
        out_specs=[half_rows(a.shape) for a in results],
        compiler_params=pltpu.CompilerParams(vmem_limit_bytes=62 * 2**20),
    )(*operands)


def per_device(
    hidden_in,
    segment_ids,
    out_cotangent,
    qkv_weight,
    qkv_moment,
    qkv_square,
    proj_weight,
    proj_moment,
    proj_square,
    gate_up_weight,
    gate_up_moment,
    gate_up_square,
    down_weight,
    down_moment,
    down_square,
    gains,
    gain_moment,
    gain_square,
):
    _, c, o = coords()
    place = c * 4 + o
    placed = lax.dynamic_update_slice_in_dim(
        jnp.zeros((QW + KW + 2 * D,), BF), gains.astype(BF), place * gains.shape[0], axis=0
    )
    gain_parts = jnp.concatenate(
        [
            placed[:QW].reshape(RANKS, 2, 128),
            placed[QW : QW + KW].reshape(RANKS, 1, 128),
            jnp.broadcast_to(placed[QW + KW :].reshape(1, 16, 128), (RANKS, 16, 128)),
            jnp.zeros((RANKS, 13, 128), BF),
        ],
        axis=1,
    )
    layer_out, back_resid, input_part, qkv_sum, gu_sum, pj_sum, dn_sum, gain_sum = call_layer(
        hidden_in, out_cotangent, segment_ids, gain_parts, qkv_weight, gate_up_weight, proj_weight, down_weight
    )
    gain_grad = lax.dynamic_slice_in_dim(
        gain_sum.reshape(40 * 128), place * gains.shape[0], gains.shape[0]
    )
    updated = call_update(
        layer_out, back_resid, input_part,
        qkv_weight, qkv_moment, qkv_square, qkv_sum,
        proj_weight, proj_moment, proj_square, pj_sum,
        gate_up_weight, gate_up_moment, gate_up_square, gu_sum,
        down_weight, down_moment, down_square, dn_sum,
    )
    return tuple(updated) + adam_step(gains, gain_moment, gain_square, gain_grad, RATE_GAIN, 0.0)


def solution(mesh):
    seq = P(("dp", "ctx", "opt"), None)
    mat = P(("ctx", "opt"), None)
    vec = P(("ctx", "opt"))
    return jax.shard_map(
        per_device,
        mesh=mesh,
        in_specs=(seq, P("dp", None), seq) + (mat,) * 12 + (vec,) * 3,
        out_specs=(seq, seq) + (mat,) * 12 + (vec,) * 3,
        check_vma=False,
    )
```

```python
import math
import types

import jax
import jax.numpy as jnp
from jax import lax
from jax.experimental import pallas as pl
from jax.experimental.pallas import tpu as pltpu
from jax.sharding import PartitionSpec as P

D = 1024
FF = 3072
HEADS = 16
KV_HEADS = 8
HEAD = 128
STEP = 10

NORM_EPS = 1e-06
THETA = 500000.0
MASKED = -1e30
BETA_ONE = 0.9
BETA_TWO = 0.95
ADAM_EPS = 1e-08
RATE_MATRIX = 0.06
RATE_GAIN = 1.0
DECAY = 0.1

TOK = 128
HALF = 1024
RANKS = 8
QW = HEADS * HEAD
KW = KV_HEADS * HEAD
RQ = 256
RK = 128
RC = RQ + 2 * RK
RF = FF // RANKS
BLK = 256
SCORE_SCALE = 1.0 / math.sqrt(HEAD)
SCALE_TWO = SCORE_SCALE * math.log2(math.e)

MESH = pl.DeviceIdType.MESH
BF = jnp.bfloat16
F32 = jnp.float32
VMEM = pl.BlockSpec(memory_space=pltpu.VMEM)
DMA = pltpu.SemaphoreType.DMA


def coords():
    return lax.axis_index("dp"), lax.axis_index("ctx"), lax.axis_index("opt")


def sibling(c):
    return c + 1 - 2 * lax.rem(c, 2)


def rank_peer(d, c, o, t):
    flip = t // 4
    return (d, c + (1 - 2 * lax.rem(c, 2)) * flip, lax.rem(o + t % 4, 4))


def cross_peer(d, c, o, t):
    return rank_peer(d + 1 - 2 * lax.rem(d, 2), lax.rem(c + 2, 4), o, t)


def plane_peer(d, c, o, t):
    x_lo, y = lax.rem(d, 2), lax.div(d, 2)
    y = lax.rem(y + t // 4, 4)
    x_lo = x_lo + (1 - 2 * x_lo) * (t % 2)
    return (2 * y + x_lo, lax.rem(c + 2 * ((t % 4) // 2), 4), o)


def group_peer(d, c, o, t):
    return (d, lax.rem(c + t // 4, 4), lax.rem(o + t % 4, 4))


def dp_peer(d, c, o, t):
    return (lax.rem(d + t, 8), c, o)


def greet(peers):
    barrier = pltpu.get_barrier_semaphore()
    for to in peers:
        pl.semaphore_signal(barrier, inc=1, device_id=to, device_id_type=MESH)
    return lambda: pl.semaphore_wait(barrier, len(peers))


def remote(src, dst, send, recv, to):
    return pltpu.make_async_remote_copy(
        src_ref=src, dst_ref=dst, send_sem=send, recv_sem=recv, device_id=to, device_id_type=MESH
    )


def rows(index, count):
    return pl.ds(pl.multiple_of(index * count, count), count)


def nn(a, b):
    return lax.dot_general(a, b, (((1,), (0,)), ((), ())), preferred_element_type=F32)


def nt(a, b):
    return lax.dot_general(a, b, (((1,), (1,)), ((), ())), preferred_element_type=F32)


def tn(a, b):
    return lax.dot_general(a, b, (((0,), (0,)), ((), ())), preferred_element_type=F32)


def row_sums(values):
    ones = jnp.ones((8, values.shape[1]), F32)
    return lax.dot_general(
        ones,
        values,
        (((1,), (1,)), ((), ())),
        precision=lax.Precision.HIGHEST,
        preferred_element_type=F32,
    )


def column(row):
    return jnp.transpose(jnp.broadcast_to(row, (128, 128)))


def rms_scale(values):
    return lax.rsqrt(jnp.mean(values * values, axis=-1, keepdims=True) + NORM_EPS)


def norm_back(grad_rows, unit_rows, scale_rows, gain_row):
    weighted = grad_rows * gain_row
    return scale_rows * (
        weighted - unit_rows * jnp.mean(weighted * unit_rows, axis=-1, keepdims=True)
    )


def rope(u, cos, sin):
    return u * cos + pltpu.roll(u, HEAD // 2, 1) * sin


def unrope(g, cos, sin):
    return g * cos - pltpu.roll(g, HEAD // 2, 1) * sin


def gather_start(full, send, recv):
    d, c, o = coords()
    rank = lax.rem(c, 2) * 4 + o
    own = full.at[rows(rank, TOK)]
    for t in (1, 3):
        remote(own, own, send.at[t], recv.at[rank], (d, c, lax.rem(o + t, 4))).start()
    remote(own, own, send.at[0], recv.at[rank], (d, sibling(c), o)).start()


def gather_relay(full, send, recv):
    d, c, o = coords()
    core = lax.rem(c, 2)
    to = (d, sibling(c), o)
    for off, part in ((1, 1), (3, 0)):
        mine = core * 4 + lax.rem(o + off, 4)
        block = full.at[rows(mine, TOK)]
        half = full.at[rows(mine * 2 + part, TOK // 2)]
        remote(block, block, send.at[off], recv.at[mine], to).wait_recv()
        landed = recv.at[8] if part else recv.at[mine]
        remote(half, half, send.at[2 + 5 * part], landed, (d, c, lax.rem(o + 4 - off, 4))).start()
        remote(block, block, send.at[3 + off], recv.at[mine], to).start()


def gather_arrive(full, send, recv, off):
    d, c, o = coords()
    core = lax.rem(c, 2)
    at = lax.rem(o + off, 4)
    mine, other = core * 4 + at, (1 - core) * 4 + at
    to = (d, sibling(c), o)
    block = full.at[rows(mine, TOK)]

    @pl.when(off == 2)
    def _():
        for part in range(2):
            half = full.at[rows(mine * 2 + part, TOK // 2)]
            landed = recv.at[8] if part else recv.at[mine]
            remote(half, half, send.at[2], landed, to).wait_recv()
        remote(block, block, send.at[5], recv.at[mine], to).start()

    block = full.at[rows(other, TOK)]
    remote(block, block, send.at[0], recv.at[other], to).wait_recv()
    return mine, other


def gather_step(full, send, recv, step):
    @pl.when(step == 1)
    def _():
        gather_relay(full, send, recv)

    return gather_arrive(full, send, recv, order(step))


def gather_finish(full, send, recv):
    d, c, o = coords()
    for i in range(8):
        part = full.at[rows(0, TOK // 2 if i in (2, 7) else TOK)]
        remote(part, part, send.at[i], recv.at[0], (d, sibling(c), o)).wait_send()


class Scatter:
    def __init__(self, r, index):
        self.stage_s, self.stage_z, self.own = r.stage_s, r.stage_z, r.own
        self.land_s, self.land_z = r.land_s.at[index % 2], r.land_z.at[index % 2]
        self.send_s, self.recv_s = r.send_s.at[index], r.recv_s.at[index]
        self.send_z, self.recv_z = r.send_z.at[index], r.recv_z.at[index]

    def near(self, off):
        d, c, o = coords()
        return remote(
            self.stage_s.at[off], self.land_s.at[off], self.send_s.at[off], self.recv_s.at[off], (d, sibling(c), o)
        )

    def along(self, off):
        d, c, o = coords()
        return remote(
            self.stage_z.at[off - 1],
            self.land_z.at[off - 1],
            self.send_z.at[off],
            self.recv_z.at[off],
            (d, c, lax.rem(o + off, 4)),
        )

    def give(self, off, part):
        self.stage_s[off] = part[TOK:].astype(BF)
        self.near(off).start()
        self.own[off] = part[0:TOK]

    def send(self, off):
        self.near(off).wait_recv()
        total = self.own[off] + self.land_s[off].astype(F32)

        @pl.when(off > 0)
        def _():
            self.stage_z[off - 1] = total.astype(BF)
            self.along(off).start()

        @pl.when(off == 0)
        def _():
            self.own[0] = total

    def result(self):
        total = self.own[0]
        for off in (1, 3, 2):
            self.along(off).wait_recv()
            total = total + self.land_z[off - 1].astype(F32)
        return total

    def finish(self):
        for off in range(4):
            self.near(off).wait_send()
        for off in range(1, 4):
            self.along(off).wait_send()


def far_first(step):
    return lax.rem(2 + 3 * step + 3 * lax.div(step, 2) + 2 * lax.div(step, 3), 4)


def order(step):
    return step + lax.div(step, 2) - 2 * lax.div(step, 3)


class SumExchange:
    def __init__(self, sums, land, send, recv):
        self.sums, self.land, self.send, self.recv = sums, land, send, recv

    def start(self):
        d, c, o = coords()
        rank = lax.rem(c, 2) * 4 + o
        self.land[rank] = self.sums[...]
        self.copies = []
        for t in range(1, 8):
            copy = remote(
                self.sums, self.land.at[rank], self.send.at[t], self.recv.at[rank], rank_peer(d, c, o, t)
            )
            copy.start()
            self.copies.append(copy)

    def total(self):
        d, c, o = coords()
        for t in range(1, 8):
            _, c1, o1 = rank_peer(d, c, o, t)
            source = lax.rem(c1, 2) * 4 + o1
            remote(
                self.sums, self.land.at[source], self.send.at[t], self.recv.at[source], (d, sibling(c), o)
            ).wait_recv()
        for copy in self.copies:
            copy.wait_send()
        total = self.land[0]
        for i in range(1, 8):
            total = total + self.land[i]
        return total


def plane_slot(d, c):
    return lax.div(c, 2) * 8 + d


def token_block(ref, b, head):
    at = pl.multiple_of(head * BLK + lax.rem(b, 2) * TOK, TOK)
    return lax.div(b, 2), pl.ds(at, TOK)


SCRATCH = dict(
    w_raw=pltpu.VMEM((16, QW + 2 * KW), F32),
    gu_raw=pltpu.VMEM((16, 2 * FF), F32),
    pj_raw=pltpu.VMEM((32, D), F32),
    dn_raw=pltpu.VMEM((48, D), F32),
    pieces=pltpu.VMEM((RANKS, 16, RC), BF),
    gu_pieces=pltpu.VMEM((RANKS, 16, 2 * RF), BF),
    pj_mine=pltpu.VMEM((32, D), BF),
    dn_mine=pltpu.VMEM((48, D), BF),
    w_all=pltpu.VMEM((16, 64, RC), BF),
    gu_all=pltpu.VMEM((16, 64, 2 * RF), BF),
    pj_all=pltpu.VMEM((2, 128, D), BF),
    dn_all=pltpu.VMEM((2, 192, D), BF),
    gain_parts_land=pltpu.VMEM((16, 32, 128), BF),
    gains=pltpu.VMEM((8, D), F32),
    cos=pltpu.VMEM((HALF, HEAD), F32),
    sin=pltpu.VMEM((HALF, HEAD), F32),
    start=pltpu.VMEM((4, 8, 2 * BLK), jnp.int32),
    hid_all=pltpu.VMEM((HALF, D), BF),
    unit=pltpu.VMEM((HALF, RQ + RK), F32),
    sums=pltpu.VMEM((2, 8, TOK), F32),
    sums_land=pltpu.VMEM((8, 2, 8, TOK), F32),
    sums_back=pltpu.VMEM((2, 8, TOK), F32),
    sums_back_land=pltpu.VMEM((8, 2, 8, TOK), F32),
    scales=pltpu.VMEM((2, 8, TOK), F32),
    q_rot=pltpu.VMEM((4, 2 * BLK, HEAD), BF),
    kv_own=pltpu.VMEM((2, HALF, HEAD), BF),
    kv_other=pltpu.VMEM((2, HALF, HEAD), BF),
    v_t=pltpu.VMEM((2, HEAD, HALF), BF),
    top=pltpu.VMEM((4, 8, 2 * BLK), F32),
    running=pltpu.VMEM((4, 8, 2 * BLK), F32),
    accum=pltpu.VMEM((4, HEAD, 2 * BLK), F32),
    mixed=pltpu.VMEM((4, 2 * BLK, HEAD), F32),
    mixed_low=pltpu.VMEM((HALF, RQ), BF),
    lse=pltpu.VMEM((4, 8, 2 * BLK), F32),
    delta=pltpu.VMEM((4, 8, 2 * BLK), F32),
    full_res=pltpu.VMEM((HALF, D), BF),
    full_ffn=pltpu.VMEM((HALF, D), BF),
    full_branch=pltpu.VMEM((HALF, D), BF),
    wide=pltpu.VMEM((HALF, 2 * RF), F32),
    act=pltpu.VMEM((HALF, RF), BF),
    back_gu=pltpu.VMEM((HALF, 2 * RF), BF),
    stage_s=pltpu.VMEM((4, TOK, D), BF),
    stage_z=pltpu.VMEM((3, TOK, D), BF),
    own=pltpu.VMEM((4, TOK, D), F32),
    land_s=pltpu.VMEM((2, 4, TOK, D), BF),
    land_z=pltpu.VMEM((2, 3, TOK, D), BF),
    gain_rest=pltpu.VMEM((4, 512), F32),
    back_mixed=pltpu.VMEM((4, 2 * BLK, HEAD), BF),
    back_q=pltpu.VMEM((4, 2 * BLK, HEAD), F32),
    back_k=pltpu.VMEM((HALF, HEAD), F32),
    back_v=pltpu.VMEM((HALF, HEAD), F32),
    other_grad=pltpu.VMEM((2, HALF, HEAD), BF),
    other_land=pltpu.VMEM((2, HALF, HEAD), BF),
    back_qkv=pltpu.VMEM((HALF, RC), BF),
    pj_grad=pltpu.VMEM((2, 4, 2, 16, D), BF),
    gu_grad=pltpu.VMEM((2, 8, 64, 2 * RF), BF),
    dn_grad=pltpu.VMEM((RF, D), BF),
    qkv_grad=pltpu.VMEM((2, 8, 64, RC), BF),
    pj_x=pltpu.VMEM((4, 4, 16, D), BF),
    pj_mid=pltpu.VMEM((4, 16, D), BF),
    pj_y=pltpu.VMEM((4, 16, D), BF),
    dn_x=pltpu.VMEM((4, 192, 512), BF),
    dn_mid=pltpu.VMEM((192, 512), BF),
    dn_y=pltpu.VMEM((4, 48, 512), BF),
    gu_y=pltpu.VMEM((4, 2, 8, 16, 2 * RF), BF),
    gu_mid=pltpu.VMEM((2, 8, 16, 2 * RF), BF),
    gu_x=pltpu.VMEM((4, 8, 16, RF), BF),
    qkv_land=pltpu.VMEM((16, 8, 16, RQ), BF),
    pj_red=pltpu.VMEM((16, D), BF),
    gu_red=pltpu.VMEM((8, 16, RF), BF),
    dn_red=pltpu.VMEM((48, 512), BF),
    qkv_red=pltpu.VMEM((8, 16, RQ), BF),
    pj_own=pltpu.VMEM((16, D), BF),
    gu_own=pltpu.VMEM((16, FF), BF),
    dn_own=pltpu.VMEM((48, 512), BF),
    qkv_own=pltpu.VMEM((16, QW), BF),
    gain_vec=pltpu.VMEM((16, 512), F32),
    gain_y=pltpu.VMEM((4, 16, 512), F32),
    gain_half=pltpu.VMEM((16, 512), F32),
    gain_x=pltpu.VMEM((4, 16, 512), F32),
    gain_mid=pltpu.VMEM((16, 512), F32),
    gain_last=pltpu.VMEM((8, 16, 512), F32),
    layer_out=pltpu.VMEM((TOK, D), F32),
    back_resid=pltpu.VMEM((TOK, D), F32),
    input_part=pltpu.VMEM((TOK, D), F32),
    write_sem=DMA((4,)),
    kept_sem=DMA((3,)),
    raw_sem=DMA((4,)),
    h_send=DMA((8,)),
    h_recv=DMA((9,)),
    w_send=DMA((15,)),
    w_recv=DMA((16,)),
    gp_send=DMA((15,)),
    gp_recv=DMA((16,)),
    sum_send=DMA((8,)),
    sum_recv=DMA((8,)),
    sumb_send=DMA((8,)),
    sumb_recv=DMA((8,)),
    kv_send=DMA,
    kv_recv=DMA,
    gu_send=DMA((15,)),
    gu_recv=DMA((16,)),
    yw_send=DMA((4, 3)),
    yw_recv=DMA((4, 4)),
    pj_send=DMA((2,)),
    pj_recv=DMA((2,)),
    dn_send=DMA((2,)),
    dn_recv=DMA((2,)),
    send_s=DMA((4, 4)),
    recv_s=DMA((4, 4)),
    send_z=DMA((4, 4)),
    recv_z=DMA((4, 4)),
    a_send=DMA((8,)),
    a_recv=DMA((9,)),
    b_send=DMA((8,)),
    b_recv=DMA((9,)),
    e_send=DMA((8,)),
    e_recv=DMA((9,)),
    kvb_send=DMA((2,)),
    kvb_recv=DMA((2,)),
    plane_send=DMA((15,)),
    plane_recv=DMA((16,)),
    fan_send=DMA((8, 3)),
    fan_recv=DMA((8, 4)),
    move_send=DMA((2,)),
    move_recv=DMA((2,)),
    gur_send=DMA((7,)),
    gur_recv=DMA((8,)),
    qr_send=DMA((2, 7)),
    qr_recv=DMA((2, 8)),
    gl_send=DMA((7,)),
    gl_recv=DMA((8,)),
    y_send=DMA((4, 7)),
    y_recv=DMA((4, 8)),
)


def layer_kernel(hid, cot, segments, gain_parts, w_rows, gu_rows, pj_rows, dn_rows, *refs):
    layer_out, back_resid, input_part, qkv_sum, gu_sum, pj_sum, dn_sum, gain_sum = refs[:8]
    writes = []
    r = types.SimpleNamespace(**dict(zip(SCRATCH, refs[8:])))
    d, c, o = coords()
    half, core = lax.div(c, 2), lax.rem(c, 2)
    rank = core * 4 + o
    place = c * 4 + o
    part, side = lax.div(d, 2), lax.rem(d, 2)
    sib = (d, sibling(c), o)
    partner = (d, lax.rem(c + 2, 4), o)
    ranks = [rank_peer(d, c, o, t) for t in range(1, 8)]
    sources = ranks + [cross_peer(d, c, o, t) for t in range(8)]
    planes = [plane_peer(d, c, o, t) for t in range(1, 16)]
    owners = [dp_peer(d, c, o, t) for t in range(1, 8)]
    group = [group_peer(d, c, o, t) for t in range(1, 16)]
    crosses = [cross_peer(d, c, o, t) for t in range(8)]
    along_y = [(lax.rem(d + 2 * t, 8), c, o) for t in range(1, 4)]
    along_x = [plane_peer(d, c, o, t) for t in range(1, 4)]
    done = []

    def launch(copy):
        copy.start()
        done.append(copy)

    def write(src, dst):
        copy = pltpu.make_async_copy(src, dst, r.write_sem.at[len(writes)])
        copy.start()
        writes.append(copy)

    def drain():
        for copy in done:
            copy.wait_send()
        done.clear()

    def rank_of(to):
        return lax.rem(to[1], 2) * 4 + to[2]

    raws = [
        pltpu.make_async_copy(src.at[rows(part, dst.shape[0])], dst, r.raw_sem.at[i])
        for i, (src, dst) in enumerate(
            ((w_rows, r.w_raw), (pj_rows, r.pj_raw), (gu_rows, r.gu_raw), (dn_rows, r.dn_raw))
        )
    ]
    for copy in raws:
        copy.start()
    all_here = greet(group + planes + crosses)
    r.hid_all[rows(rank, TOK), :] = hid[...]
    raws[0].wait()
    for g in range(RANKS):
        r.pieces[g, :, 0:RQ] = r.w_raw[:, g * RQ : (g + 1) * RQ].astype(BF)
        r.pieces[g, :, RQ : RQ + RK] = r.w_raw[:, QW + g * RK : QW + (g + 1) * RK].astype(BF)
        r.pieces[g, :, RQ + RK : RC] = r.w_raw[:, QW + KW + g * RK : QW + KW + (g + 1) * RK].astype(BF)
    all_here()

    def piece_rows(ref, source):
        return ref.at[source, rows(part, 16)]

    def send_pieces(pieces, ref, send, recv):
        for i, to in enumerate(sources):
            launch(remote(pieces.at[rank_of(to)], piece_rows(ref, place), send.at[i], recv.at[place], to))
        ref[place, rows(part, 16)] = pieces[rank]

    def wait_pieces(pieces, ref, send, recv):
        for i, to in enumerate(sources):
            source = to[1] * 4 + to[2]
            remote(pieces.at[0], piece_rows(ref, source), send.at[i], recv.at[source], to).wait_recv()

    def spread(index, cut):
        for i, to in enumerate(along_y):
            launch(remote(cut(part), cut(part), r.yw_send.at[index, i], r.yw_recv.at[index, part], to))

    def wait_spread(index, cut):
        for i, to in enumerate(along_y):
            y = lax.div(to[0], 2)
            remote(cut(y), cut(y), r.yw_send.at[index, i], r.yw_recv.at[index, y], to).wait_recv()

    def w_cut(y):
        return r.w_all.at[:, rows(y, 16)]

    def gu_all_cut(y):
        return r.gu_all.at[:, rows(y, 16)]

    def pj_all_cut(y):
        return r.pj_all.at[:, rows(y, 32)]

    def dn_all_cut(y):
        return r.dn_all.at[:, rows(y, 48)]

    to_rank = lax.div(place, 2)
    slot = lax.rem(place, 2)
    near = (d, half * 2 + lax.div(to_rank, 4), lax.rem(to_rank, 4))
    far = (d + 1 - 2 * lax.rem(d, 2), (1 - half) * 2 + lax.div(to_rank, 4), lax.rem(to_rank, 4))
    pj_slot, dn_slot = r.pj_all.at[slot, rows(part, 32)], r.dn_all.at[slot, rows(part, 48)]
    keep = to_rank == rank
    pj_near = remote(r.pj_mine, pj_slot, r.pj_send.at[0], r.pj_recv.at[slot], near)
    dn_near = remote(r.dn_mine, dn_slot, r.dn_send.at[0], r.dn_recv.at[slot], near)

    def send_rows():
        @pl.when(jnp.logical_not(keep))
        def _():
            pj_near.start()
            dn_near.start()

        @pl.when(keep)
        def _():
            r.pj_all[slot, rows(part, 32)] = r.pj_mine[...]
            r.dn_all[slot, rows(part, 48)] = r.dn_mine[...]

        launch(remote(r.pj_mine, pj_slot, r.pj_send.at[1], r.pj_recv.at[slot], far))
        launch(remote(r.dn_mine, dn_slot, r.dn_send.at[1], r.dn_recv.at[slot], far))

    def wait_rows():
        for i in range(2):
            from_self = 2 * rank + i == place

            @pl.when(jnp.logical_not(from_self))
            def _(i=i):
                pj_at, dn_at = r.pj_all.at[i, rows(part, 32)], r.dn_all.at[i, rows(part, 48)]
                remote(r.pj_mine, pj_at, r.pj_send.at[0], r.pj_recv.at[i], partner).wait_recv()
                remote(r.dn_mine, dn_at, r.dn_send.at[0], r.dn_recv.at[i], partner).wait_recv()

    send_pieces(r.pieces, r.w_all, r.w_send, r.w_recv)
    gather_start(r.hid_all, r.h_send, r.h_recv)
    for i, to in enumerate(sources):
        launch(
            remote(
                gain_parts.at[rank_of(to)], r.gain_parts_land.at[place], r.gp_send.at[i], r.gp_recv.at[place], to
            )
        )
    r.gain_parts_land[place] = gain_parts[rank]
    ids = segments[...]
    own_ids = segments[:, rows(half, HALF)]
    starts = jnp.zeros((1, HALF), jnp.int32)
    for i in range(1, 6):
        below = jnp.sum((ids < i).astype(F32), axis=1, keepdims=True).astype(jnp.int32)
        starts = jnp.where(own_ids == i, below, starts)
    for block in range(4):
        row = starts[:, block * BLK : (block + 1) * BLK]
        r.start[block] = jnp.broadcast_to(jnp.concatenate([row, row], axis=1), (8, 2 * BLK))
    lane = lax.broadcasted_iota(jnp.int32, (1, HEAD), 1)
    frequency = jnp.exp(lax.rem(lane, HEAD // 2).astype(F32) * (-math.log(THETA) / (HEAD // 2)))
    sign = jnp.where(lane < HEAD // 2, -1.0, 1.0)
    token = half * HALF + lax.broadcasted_iota(jnp.int32, (1, HALF), 1)
    position = (token - starts).astype(F32)
    for b in range(RANKS):
        angles = column(position[:, b * TOK : (b + 1) * TOK]) * frequency
        r.cos[b * TOK : (b + 1) * TOK, :] = jnp.cos(angles)
        r.sin[b * TOK : (b + 1) * TOK, :] = jnp.sin(angles) * sign
    wait_pieces(r.pieces, r.w_all, r.w_send, r.w_recv)
    spread(0, w_cut)
    for copy in raws[1:]:
        copy.wait()
    for g in range(RANKS):
        r.gu_pieces[g, :, 0:RF] = r.gu_raw[:, g * RF : (g + 1) * RF].astype(BF)
        r.gu_pieces[g, :, RF:] = r.gu_raw[:, FF + g * RF : FF + (g + 1) * RF].astype(BF)
    r.pj_mine[...] = r.pj_raw[...].astype(BF)
    r.dn_mine[...] = r.dn_raw[...].astype(BF)

    send_rows()
    send_pieces(r.gu_pieces, r.gu_all, r.gu_send, r.gu_recv)
    gather_relay(r.hid_all, r.h_send, r.h_recv)
    wait_spread(0, w_cut)
    wait_rows()
    spread(1, pj_all_cut)
    wait_pieces(r.gu_pieces, r.gu_all, r.gu_send, r.gu_recv)
    spread(2, gu_all_cut)
    spread(3, dn_all_cut)


    line = lax.broadcasted_iota(jnp.int32, (8, TOK), 0)

    def put_row(table, b, values):
        return jnp.where(line == b, values, table)

    def get_row(table, b):
        return jnp.sum(jnp.where(line == b, table, 0.0), axis=0, keepdims=True)

    r.sums[...] = jnp.zeros_like(r.sums)
    r.sums_back[...] = jnp.zeros_like(r.sums_back)

    def project(step, _):
        mine, other = gather_arrive(r.hid_all, r.h_send, r.h_recv, order(step))
        both = jnp.concatenate([r.hid_all[rows(mine, TOK), :], r.hid_all[rows(other, TOK), :]], axis=0)
        out = nn(both, r.w_all[...].reshape(D, RC))
        squares = out * out
        q_sum, k_sum = row_sums(squares[:, 0:RQ]), row_sums(squares[:, RQ : RQ + RK])
        r.wide[rows(mine, TOK), 0:RC] = out[0:TOK]
        r.wide[rows(other, TOK), 0:RC] = out[TOK:]
        for i, row_sum in enumerate((q_sum, k_sum)):
            with_mine = put_row(r.sums[i], mine, row_sum[:, 0:TOK])
            r.sums[i] = put_row(with_mine, other, row_sum[:, TOK:])
        return 0

    lax.fori_loop(0, 4, project, 0)
    exchange = SumExchange(r.sums, r.sums_land, r.sum_send, r.sum_recv)
    exchange.start()
    for i, to in enumerate(sources):
        source = to[1] * 4 + to[2]
        remote(
            gain_parts.at[0], r.gain_parts_land.at[source], r.gp_send.at[i], r.gp_recv.at[source], to
        ).wait_recv()
    gains = r.gain_parts_land[0].astype(F32)
    for i in range(1, 16):
        gains = gains + r.gain_parts_land[i].astype(F32)
    for i in range(3):
        r.gains[0:1, i * 128 : (i + 1) * 128] = gains[i : i + 1]
    for i in range(8):
        r.gains[1:2, i * 128 : (i + 1) * 128] = gains[3 + i : 4 + i]
        r.gains[2:3, i * 128 : (i + 1) * 128] = gains[11 + i : 12 + i]
    total = exchange.total()
    r.scales[0] = lax.rsqrt(total[0] * (1.0 / QW) + NORM_EPS)
    r.scales[1] = lax.rsqrt(total[1] * (1.0 / KW) + NORM_EPS)

    def finish(b, _):
        at = rows(b, TOK)
        q_scale, k_scale = column(get_row(r.scales[0], b)), column(get_row(r.scales[1], b))
        cosine, sine = r.cos[at, :], r.sin[at, :]
        for head in range(2):
            cols = slice(head * HEAD, (head + 1) * HEAD)
            q_unit = r.wide[at, cols] * q_scale
            r.unit[at, cols] = q_unit
            block, spot = token_block(r.q_rot, b, head)
            r.q_rot[block, spot, :] = rope(q_unit * r.gains[0:1, cols], cosine, sine).astype(BF)
        cols = slice(RQ, RQ + RK)
        k_unit = r.wide[at, cols] * k_scale
        r.unit[at, cols] = k_unit
        r.kv_own[0, at, :] = rope(k_unit * r.gains[0:1, cols], cosine, sine).astype(BF)
        r.kv_own[1, at, :] = r.wide[at, RQ + RK : RC].astype(BF)
        return 0

    lax.fori_loop(0, RANKS, finish, 0)

    kv_copy = remote(r.kv_own, r.kv_other, r.kv_send, r.kv_recv, partner)

    @pl.when(half == 0)
    def _():
        kv_copy.start()

    gather_finish(r.hid_all, r.h_send, r.h_recv)

    r.v_t[0] = jnp.transpose(r.kv_own[1].astype(F32)).astype(BF)

    def allowed_tile(block, key_base, diagonal):
        key_index = lax.broadcasted_iota(jnp.int32, (BLK, 2 * BLK), 0)
        allowed = key_index >= r.start[block, 0:1, :] - key_base
        if diagonal:
            lane = lax.broadcasted_iota(jnp.int32, (1, 2 * BLK), 1)
            allowed = allowed & (key_index <= lax.rem(lane, BLK))
        return allowed

    def tile(block, keys, values_t, key_base, carry):
        scores = nt(keys, r.q_rot[block]) * SCALE_TWO
        scores = jnp.where(allowed_tile(block, key_base, carry is None), scores, MASKED)
        top_now = jnp.max(scores, axis=0, keepdims=True)
        if carry is None:
            probs = jnp.exp2(scores - top_now)
            return top_now, jnp.sum(probs, axis=0, keepdims=True), nn(values_t, probs.astype(BF))
        top_old, run_old, acc_old = carry
        top_new = jnp.maximum(top_old, top_now)
        fade = jnp.exp2(top_old - top_new)
        probs = jnp.exp2(scores - top_new)
        return (
            top_new,
            run_old * fade + jnp.sum(probs, axis=0, keepdims=True),
            acc_old * fade + nn(values_t, probs.astype(BF)),
        )

    def keep_state(block, state):
        r.top[block] = jnp.broadcast_to(state[0], (8, 2 * BLK))
        r.running[block] = jnp.broadcast_to(state[1], (8, 2 * BLK))
        r.accum[block] = state[2]

    def local_block(block, _):
        def local_tile(j, carry):
            return tile(
                block, r.kv_own[0, rows(j, BLK), :], r.v_t[0, :, rows(j, BLK)], half * HALF + j * BLK, carry
            )

        keep_state(block, lax.fori_loop(0, block, local_tile, local_tile(block, None)))
        return 0

    lax.fori_loop(0, 4, local_block, 0)

    @pl.when(half == 1)
    def _():
        kv_copy.wait_recv()
        r.v_t[1] = jnp.transpose(r.kv_other[1].astype(F32)).astype(BF)

        def other_block(block, _):
            state = (r.top[block][0:1], r.running[block][0:1], r.accum[block])

            def other_tile(j, carry):
                return tile(block, r.kv_other[0, rows(j, BLK), :], r.v_t[1, :, rows(j, BLK)], j * BLK, carry)

            keep_state(block, lax.fori_loop(0, 4, other_tile, state, unroll=True))
            return 0

        lax.fori_loop(0, 4, other_block, 0)

    @pl.when(half == 0)
    def _():
        kv_copy.wait_send()

    def close_block(block, _):
        run = r.running[block]
        r.lse[block] = r.top[block] + jnp.log2(run)
        out = jnp.transpose(r.accum[block] * (1.0 / run[0:1]))
        r.mixed[block] = out
        for head in range(2):
            r.mixed_low[rows(block, BLK), head * HEAD : (head + 1) * HEAD] = out[
                head * BLK : (head + 1) * BLK
            ].astype(BF)
        return 0

    lax.fori_loop(0, 4, close_block, 0)

    wait_spread(1, pj_all_cut)
    gain_attn, gain_ffn = r.gains[1:2, :], r.gains[2:3, :]

    def both_rows(ref, mine, other):
        return jnp.concatenate([ref[rows(mine, TOK), :], ref[rows(other, TOK), :]], axis=0)

    s = Scatter(r, 0)

    def proj_step(step, _):
        off = far_first(step)
        at = lax.rem(o + off, 4)
        s.give(off, nn(both_rows(r.mixed_low, core * 4 + at, (1 - core) * 4 + at), r.pj_all[...].reshape(RQ, D)))

        @pl.when(step > 0)
        def _():
            s.send(far_first(step - 1))

        return 0

    lax.fori_loop(0, 4, proj_step, 0)
    s.send(0)
    branch = s.result()
    branch_scale = rms_scale(branch)
    branch_unit = branch * branch_scale
    residual = hid[...].astype(F32) + branch_unit * gain_attn
    r.full_res[rows(rank, TOK), :] = residual.astype(BF)
    gather_start(r.full_res, r.a_send, r.a_recv)
    s.finish()
    wait_spread(2, gu_all_cut)
    wait_spread(3, dn_all_cut)

    s1 = Scatter(r, 1)

    def ffn_step(step, _):
        off = order(step)
        mine, other = gather_step(r.full_res, r.a_send, r.a_recv, step)
        both = nn(both_rows(r.full_res, mine, other), r.gu_all[...].reshape(D, 2 * RF))
        r.wide[rows(mine, TOK), :] = both[0:TOK]
        r.wide[rows(other, TOK), :] = both[TOK:]
        gate, up = both[:, 0:RF], both[:, RF:]
        act_low = (gate * jax.nn.sigmoid(gate) * up).astype(BF)
        r.act[rows(mine, TOK), :] = act_low[0:TOK]
        r.act[rows(other, TOK), :] = act_low[TOK:]

        @pl.when(step > 0)
        def _():
            s1.send(order(step - 1))

        s1.give(off, nn(act_low, r.dn_all[...].reshape(RF, D)))
        return 0

    lax.fori_loop(0, 4, ffn_step, 0)
    s1.send(2)
    ffn = s1.result()
    ffn_scale = rms_scale(ffn)
    ffn_unit = ffn * ffn_scale
    r.layer_out[...] = residual + ffn_unit * gain_ffn
    write(r.layer_out, layer_out)
    cotangent = cot[...].astype(F32)
    back_ffn = norm_back(cotangent, ffn_unit, ffn_scale, gain_ffn)
    r.full_ffn[rows(rank, TOK), :] = back_ffn.astype(BF)
    gather_start(r.full_ffn, r.b_send, r.b_recv)
    gain_row = jnp.sum(cotangent * ffn_unit, axis=0, keepdims=True)
    r.gain_rest[2:3, :] = gain_row[:, 0:512]
    r.gain_rest[3:4, :] = gain_row[:, 512:]
    gather_finish(r.full_res, r.a_send, r.a_recv)
    s1.finish()

    s2 = Scatter(r, 2)

    def back_step(step, _):
        off = order(step)
        mine, other = gather_step(r.full_ffn, r.b_send, r.b_recv, step)
        back_act = nt(both_rows(r.full_ffn, mine, other), r.dn_all[...].reshape(RF, D))
        both = both_rows(r.wide, mine, other)
        gate, up = both[:, 0:RF], both[:, RF:]
        sig = jax.nn.sigmoid(gate)
        back_gate = back_act * up * sig * (1.0 + gate * (1.0 - sig))
        back_up = back_act * (gate * sig)
        back_both = jnp.concatenate([back_gate, back_up], axis=1).astype(BF)
        r.back_gu[rows(mine, TOK), :] = back_both[0:TOK]
        r.back_gu[rows(other, TOK), :] = back_both[TOK:]

        @pl.when(step > 0)
        def _():
            s2.send(order(step - 1))

        s2.give(off, nt(back_both, r.gu_all[...].reshape(D, 2 * RF)))
        return 0

    lax.fori_loop(0, 4, back_step, 0)
    s2.send(2)

    def y_of(to):
        return lax.div(to[0], 2)

    def x_of(to):
        return lax.div(to[1], 2) * 2 + lax.rem(to[0], 2)

    here = (d, c, o)

    def fan_out(index, peers, place_of, cut, land):
        slot = place_of(here)
        for i, to in enumerate(peers):
            launch(remote(cut(to), land.at[slot], r.fan_send.at[index, i], r.fan_recv.at[index, slot], to))
        land[slot] = cut(here)[...]

    def fan_in(index, peers, place_of, land):
        for i, to in enumerate(peers):
            slot = place_of(to)
            remote(
                land.at[slot], land.at[slot], r.fan_send.at[index, i], r.fan_recv.at[index, slot], to
            ).wait_recv()
        total = land[0].astype(F32)
        for i in range(1, 4):
            total = total + land[i].astype(F32)
        return total

    def gu_step(b, _):
        grad = tn(r.full_res[:, rows(b, 128)], r.back_gu[...])
        r.gu_grad[lax.div(b, 4), rows(lax.rem(b, 4), 2)] = grad.astype(BF).reshape(2, 64, 2 * RF)
        return 0

    lax.fori_loop(0, 8, gu_step, 0)

    fan_out(1, along_y, y_of, lambda to: r.gu_grad.at[:, :, rows(y_of(to), 16)], r.gu_y)
    r.dn_grad[...] = tn(r.act[...], r.full_ffn[...]).astype(BF)
    fan_out(
        0,
        along_x,
        x_of,
        lambda to: r.dn_grad.at[rows(lax.div(to[1], 2), 192), rows(lax.rem(to[0], 2), 512)],
        r.dn_x,
    )
    resid_grad = cotangent + s2.result()
    r.back_resid[...] = resid_grad
    write(r.back_resid, back_resid)
    gain_row = jnp.sum(resid_grad * branch_unit, axis=0, keepdims=True)
    r.gain_rest[0:1, :] = gain_row[:, 0:512]
    r.gain_rest[1:2, :] = gain_row[:, 512:]
    back_branch = norm_back(resid_grad, branch_unit, branch_scale, gain_attn)
    r.full_branch[rows(rank, TOK), :] = back_branch.astype(BF)
    gather_start(r.full_branch, r.e_send, r.e_recv)
    gather_finish(r.full_ffn, r.b_send, r.b_recv)
    s2.finish()

    def mixed_step(step, _):
        mine, other = gather_step(r.full_branch, r.e_send, r.e_recv, step)
        out = nt(both_rows(r.full_branch, mine, other), r.pj_all[...].reshape(RQ, D)).astype(BF)
        for head in range(2):
            for i, b in enumerate((mine, other)):
                block, spot = token_block(r.back_mixed, b, head)
                r.back_mixed[block, spot, :] = out[i * TOK : (i + 1) * TOK, head * HEAD : (head + 1) * HEAD]
        return 0

    lax.fori_loop(0, 4, mixed_step, 0)
    r.pj_grad[...] = tn(r.mixed_low[...], r.full_branch[...]).astype(BF).reshape(2, 4, 2, 16, D)
    fan_out(2, along_x, x_of, lambda to: r.pj_grad.at[lax.div(to[1], 2), :, lax.rem(to[0], 2)], r.pj_x)
    gather_finish(r.full_branch, r.e_send, r.e_recv)

    def delta_step(block, _):
        r.delta[block] = row_sums(r.back_mixed[block].astype(F32) * r.mixed[block])
        r.back_q[block] = jnp.zeros((2 * BLK, HEAD), F32)
        return 0

    lax.fori_loop(0, 4, delta_step, 0)

    def back_tile(block, keys, values, key_base, diagonal, carry):
        grad_k, grad_v = carry
        query, grad_out = r.q_rot[block], r.back_mixed[block]
        scores = nt(keys, query) * SCALE_TWO
        probs = jnp.where(allowed_tile(block, key_base, diagonal), jnp.exp2(scores - r.lse[block, 0:1, :]), 0.0)
        back_prob = nt(values, grad_out)
        back_score = (probs * (back_prob - r.delta[block, 0:1, :])).astype(BF)
        grad_k = grad_k + nn(back_score, query)
        grad_v = grad_v + nn(probs.astype(BF), grad_out)
        r.back_q[block] += tn(back_score, keys)
        return grad_k, grad_v

    zero = (jnp.zeros((BLK, HEAD), F32), jnp.zeros((BLK, HEAD), F32))
    def send_back(i):
        at = rows(i, 2 * BLK)
        return remote(r.other_grad.at[:, at], r.other_land.at[:, at], r.kvb_send.at[i], r.kvb_recv.at[i], partner)


    def local_keys(j, _):
        at = rows(j, BLK)
        keys, values = r.kv_own[0, at, :], r.kv_own[1, at, :]
        base = half * HALF + j * BLK
        grad_k, grad_v = lax.fori_loop(
            j + 1,
            4,
            lambda block, carry: back_tile(block, keys, values, base, False, carry),
            back_tile(j, keys, values, base, True, zero),
        )
        r.back_k[at, :] = grad_k * SCORE_SCALE
        r.back_v[at, :] = grad_v
        return 0

    def other_keys(j, _):
        at = rows(j, BLK)
        keys, values = r.kv_other[0, at, :], r.kv_other[1, at, :]
        grad_k, grad_v = lax.fori_loop(
            0, 4, lambda block, carry: back_tile(block, keys, values, j * BLK, False, carry), zero, unroll=2
        )
        r.other_grad[0, at, :] = (grad_k * SCORE_SCALE).astype(BF)
        r.other_grad[1, at, :] = grad_v.astype(BF)
        return 0

    def first_part(low, high):
        lax.fori_loop(low, low + (high - low) * (1 - half), local_keys, 0)
        lax.fori_loop(low, low + (high - low) * half, other_keys, 0)

    first_part(0, 2)

    @pl.when(half == 1)
    def _():
        send_back(0).start()


    r.dn_mid[...] = fan_in(0, along_x, x_of, r.dn_x).astype(BF)
    fan_out(3, along_y, y_of, lambda to: r.dn_mid.at[rows(y_of(to), 48)], r.dn_y)
    r.gu_mid[...] = fan_in(1, along_y, y_of, r.gu_y).astype(BF)
    fan_out(
        4,
        along_x,
        x_of,
        lambda to: r.gu_mid.at[lax.div(to[1], 2), :, :, rows(lax.rem(to[0], 2), RF)],
        r.gu_x,
    )
    r.pj_mid[...] = fan_in(2, along_x, x_of, r.pj_x).astype(BF)
    fan_out(5, along_y, y_of, lambda to: r.pj_mid.at[y_of(to)], r.pj_y)

    first_part(2, 4)

    @pl.when(half == 1)
    def _():
        send_back(1).start()

    r.dn_red[...] = fan_in(3, along_y, y_of, r.dn_y).astype(BF)
    r.gu_red[...] = fan_in(4, along_x, x_of, r.gu_x).astype(BF)
    r.pj_red[...] = fan_in(5, along_y, y_of, r.pj_y).astype(BF)
    target = 2 * rank + half
    to_owner = (d, lax.div(target, 4), lax.rem(target, 4))
    stay = target == place
    pj_move = remote(r.pj_red, r.pj_own, r.move_send.at[0], r.move_recv.at[0], to_owner)
    dn_move = remote(r.dn_red, r.dn_own, r.move_send.at[1], r.move_recv.at[1], to_owner)

    @pl.when(stay)
    def _():
        r.pj_own[...] = r.pj_red[...]
        r.dn_own[...] = r.dn_red[...]

    @pl.when(jnp.logical_not(stay))
    def _():
        pj_move.start()
        dn_move.start()

    for i, to in enumerate(ranks):
        launch(
            remote(
                r.gu_red.at[rank_of(to)],
                r.gu_own.at[:, rows(rank, RF)],
                r.gur_send.at[i],
                r.gur_recv.at[rank],
                to,
            )
        )
    r.gu_own[:, rows(rank, RF)] = r.gu_red[rank]

    lax.fori_loop(0, 2 * half, local_keys, 0)

    @pl.when(half == 0)
    def _():
        for i in range(2):
            at = rows(i, 2 * BLK)
            send_back(i).wait_recv()
            r.back_k[at, :] += r.other_land[0, at, :].astype(F32)
            r.back_v[at, :] += r.other_land[1, at, :].astype(F32)

    @pl.when(jnp.logical_not(stay))
    def _():
        pj_move.wait_send()
        dn_move.wait_send()
        pj_move.wait_recv()
        dn_move.wait_recv()

    for i, to in enumerate(ranks):
        remote(
            r.gu_red.at[0], r.gu_own.at[:, rows(rank_of(to), RF)], r.gur_send.at[i], r.gur_recv.at[rank_of(to)], sib
        ).wait_recv()

    def owned(n, e):
        e_part, e_side = lax.div(e, 2), lax.rem(e, 2)
        return (
            pj_sum.at[rows(e, 16), :],
            dn_sum.at[rows(e_part, 48), rows(e_side, 512)],
            gu_sum.at[rows(e_part, 16), rows(e_side, FF)],
            qkv_sum.at[rows(e_part, 16), rows(e_side, QW)],
        )[n]

    own_refs = (r.pj_own, r.dn_own, r.gu_own, r.qkv_own)
    kept = [pltpu.make_async_copy(own_refs[n], owned(n, d), r.kept_sem.at[n]) for n in range(3)]
    for copy in kept:
        copy.start()
    across = (d + 1 - 2 * side, c, o)
    for n in range(2):
        launch(remote(own_refs[n], owned(n, d), r.y_send.at[n, 0], r.y_recv.at[n, 4], across))
    for i, to in enumerate(along_y):
        launch(remote(r.gu_own, owned(2, d), r.y_send.at[2, i], r.y_recv.at[2, part], to))

    def pair(n, y):
        return (pj_sum.at[rows(y, 32)], dn_sum.at[rows(y, 48)])[n]

    def column_half(of_side):
        return gu_sum.at[:, rows(of_side, FF)]

    def share_again():
        for copy in kept:
            copy.wait()
        for n in range(2):
            remote(own_refs[n], owned(n, across[0]), r.y_send.at[n, 0], r.y_recv.at[n, 4], across).wait_recv()
            for i, to in enumerate(along_y):
                launch(remote(pair(n, part), pair(n, part), r.y_send.at[n, 1 + i], r.y_recv.at[n, part], to))
        for i, to in enumerate(along_y):
            remote(r.gu_own, owned(2, to[0]), r.y_send.at[2, i], r.y_recv.at[2, y_of(to)], to).wait_recv()
        launch(remote(column_half(side), column_half(side), r.y_send.at[2, 3], r.y_recv.at[2, 4], across))

    def shared():
        for n in range(2):
            for i, to in enumerate(along_y):
                y = y_of(to)
                remote(pair(n, y), pair(n, y), r.y_send.at[n, 1 + i], r.y_recv.at[n, y], to).wait_recv()
        other_half = column_half(1 - side)
        remote(other_half, other_half, r.y_send.at[2, 3], r.y_recv.at[2, 4], across).wait_recv()

    lax.fori_loop(2 * half, 4 * half, local_keys, 0)

    @pl.when(half == 1)
    def _():
        for i in range(2):
            send_back(i).wait_send()

    def weigh(b, _):
        at = rows(b, TOK)
        cosine, sine = r.cos[at, :], r.sin[at, :]
        totals = []
        for head in range(2):
            cols = slice(head * HEAD, (head + 1) * HEAD)
            block, spot = token_block(r.back_q, b, head)
            grad = unrope(r.back_q[block, spot, :] * SCORE_SCALE, cosine, sine)
            r.wide[at, cols] = grad
            totals.append(grad * r.gains[0:1, cols] * r.unit[at, cols])
        cols = slice(RQ, RQ + RK)
        grad = unrope(r.back_k[at, :], cosine, sine)
        r.wide[at, cols] = grad
        q_sum = row_sums(totals[0] + totals[1])
        k_sum = row_sums(grad * r.gains[0:1, cols] * r.unit[at, cols])
        r.sums_back[0] = put_row(r.sums_back[0], b, q_sum)
        r.sums_back[1] = put_row(r.sums_back[1], b, k_sum)
        return 0

    lax.fori_loop(0, RANKS, weigh, 0)
    exchange = SumExchange(r.sums_back, r.sums_back_land, r.sumb_send, r.sumb_recv)
    exchange.start()

    gain_own = jnp.sum(r.wide[:, 0 : RQ + RK] * r.unit[...], axis=0, keepdims=True)
    row = lax.broadcasted_iota(jnp.int32, (16, 512), 0)
    col = lax.broadcasted_iota(jnp.int32, (16, 512), 1)
    own_q, own_k = gain_own[:, 0:RQ], gain_own[:, RQ:]
    at_q = (row == lax.div(rank, 2)) & (lax.div(col, RQ) == lax.rem(rank, 2))
    at_k = (row == 4 + lax.div(rank, 4)) & (lax.div(col, RK) == lax.rem(rank, 4))
    r.gain_vec[...] = jnp.where(at_q, jnp.concatenate([own_q] * 2, axis=1), 0.0) + jnp.where(
        at_k, jnp.concatenate([own_k] * 4, axis=1), 0.0
    )
    r.gain_vec[6:10, :] = r.gain_rest[...]
    fan_out(6, along_y, y_of, lambda to: r.gain_vec, r.gain_y)

    total = exchange.total()
    r.sums_back[0] = total[0] * (1.0 / QW)
    r.sums_back[1] = total[1] * (1.0 / KW)

    def back_norm(b, _):
        at = rows(b, TOK)
        q_scale, k_scale = column(get_row(r.scales[0], b)), column(get_row(r.scales[1], b))
        q_mean, k_mean = column(get_row(r.sums_back[0], b)), column(get_row(r.sums_back[1], b))
        for head in range(2):
            cols = slice(head * HEAD, (head + 1) * HEAD)
            weighted = r.wide[at, cols] * r.gains[0:1, cols]
            r.back_qkv[at, cols] = (q_scale * (weighted - r.unit[at, cols] * q_mean)).astype(BF)
        cols = slice(RQ, RQ + RK)
        weighted = r.wide[at, cols] * r.gains[0:1, cols]
        r.back_qkv[at, cols] = (k_scale * (weighted - r.unit[at, cols] * k_mean)).astype(BF)
        r.back_qkv[at, RQ + RK : RC] = r.back_v[at, :].astype(BF)
        return 0

    lax.fori_loop(0, RANKS, back_norm, 0)

    def grad_step(b, _):
        grad = tn(r.hid_all[:, rows(b, 128)], r.back_qkv[...])
        r.qkv_grad[lax.div(b, 4), rows(lax.rem(b, 4), 2)] = grad.astype(BF).reshape(2, 64, RC)
        return 0

    def qkv_cut(e, h):
        return h, slice(None), rows(lax.div(e, 2), 16), rows(lax.rem(e, 2), RQ)

    old = list(done)
    done.clear()

    def drain_old():
        for copy in old:
            copy.wait_send()

        @pl.when(jnp.logical_not(keep))
        def _():
            pj_near.wait_send()
            dn_near.wait_send()

    slot = plane_slot(d, c)
    for which in range(2):
        rows_half = half + which - 2 * half * which
        lax.fori_loop(4 * rows_half, 4 * rows_half + 4, grad_step, 0)
        for i, to in enumerate(planes):
            if ((i + 1) % 4) // 2 == which:
                src = r.qkv_grad.at[qkv_cut(to[0], lax.div(to[1], 2))]
                launch(remote(src, r.qkv_land.at[slot], r.plane_send.at[i], r.plane_recv.at[slot], to))
    r.qkv_land[slot] = r.qkv_grad[qkv_cut(d, half)]
    r.gain_half[...] = fan_in(6, along_y, y_of, r.gain_y)
    fan_out(7, along_x, x_of, lambda to: r.gain_half, r.gain_x)

    s3 = Scatter(r, 3)

    def input_step(step, _):
        off = far_first(step)
        at = lax.rem(o + off, 4)
        s3.give(off, nt(both_rows(r.back_qkv, core * 4 + at, (1 - core) * 4 + at), r.w_all[...].reshape(D, RC)))

        @pl.when(step > 0)
        def _():
            s3.send(far_first(step - 1))

        return 0

    lax.fori_loop(0, 4, input_step, 0)
    s3.send(0)
    share_again()
    drain_old()

    total = fan_in(7, along_x, x_of, r.gain_x)
    r.gain_mid[...] = total
    for i, to in enumerate(ranks):
        launch(remote(r.gain_mid, r.gain_last.at[rank], r.gl_send.at[i], r.gl_recv.at[rank], to))
    r.gain_last[rank] = total

    for i, to in enumerate(planes):
        source = plane_slot(to[0], to[1])
        land = r.qkv_land.at[source]
        remote(land, land, r.plane_send.at[i], r.plane_recv.at[source], to).wait_recv()
    total = r.qkv_land[0].astype(F32)
    for i in range(1, 16):
        total = total + r.qkv_land[i].astype(F32)
    r.qkv_red[...] = total.astype(BF)

    def qkv_cols(of_rank, i):
        return rows((1 - side) * (of_rank * 2 + i) + side * (of_rank + i * 8), RK)

    for i, to in enumerate(ranks):
        for j in range(2):
            launch(
                remote(
                    r.qkv_red.at[rank_of(to), :, pl.ds(j * RK, RK)],
                    r.qkv_own.at[:, qkv_cols(rank, j)],
                    r.qr_send.at[j, i],
                    r.qr_recv.at[j, rank],
                    to,
                )
            )
    for j in range(2):
        r.qkv_own[:, qkv_cols(rank, j)] = r.qkv_red[rank][:, j * RK : (j + 1) * RK]

    r.input_part[...] = s3.result()
    write(r.input_part, input_part)
    for i, to in enumerate(ranks):
        remote(
            r.gain_mid, r.gain_last.at[rank_of(to)], r.gl_send.at[i], r.gl_recv.at[rank_of(to)], sib
        ).wait_recv()
    total = r.gain_last[0]
    for i in range(1, 8):
        total = total + r.gain_last[i]
    for i in range(40):
        gain_sum[i : i + 1, :] = total[i // 4 : i // 4 + 1, (i % 4) * 128 : (i % 4 + 1) * 128]

    for i, to in enumerate(ranks):
        for j in range(2):
            remote(
                r.qkv_red.at[0, :, pl.ds(j * RK, RK)],
                r.qkv_own.at[:, qkv_cols(rank_of(to), j)],
                r.qr_send.at[j, i],
                r.qr_recv.at[j, rank_of(to)],
                sib,
            ).wait_recv()
    for i, to in enumerate(owners):
        launch(remote(r.qkv_own, owned(3, d), r.y_send.at[3, i], r.y_recv.at[3, d], to))
    write(r.qkv_own, owned(3, d))
    for i, to in enumerate(owners):
        remote(r.qkv_own, owned(3, to[0]), r.y_send.at[3, i], r.y_recv.at[3, to[0]], sib).wait_recv()
    shared()
    s3.finish()
    drain()
    for copy in writes:
        copy.wait()


def call_layer(*operands):
    any_space = pl.BlockSpec(memory_space=pl.ANY)
    return pl.pallas_call(
        layer_kernel,
        name="layer",
        out_shape=(
            jax.ShapeDtypeStruct((TOK, D), F32),
            jax.ShapeDtypeStruct((TOK, D), F32),
            jax.ShapeDtypeStruct((TOK, D), F32),
            jax.ShapeDtypeStruct((64, QW + 2 * KW), BF),
            jax.ShapeDtypeStruct((64, 2 * FF), BF),
            jax.ShapeDtypeStruct((128, D), BF),
            jax.ShapeDtypeStruct((192, D), BF),
            jax.ShapeDtypeStruct((40, 128), F32),
        ),
        in_specs=[VMEM] * 4 + [any_space] * 4,
        out_specs=[any_space] * 7 + [VMEM],
        scratch_shapes=list(SCRATCH.values()),
        compiler_params=pltpu.CompilerParams(
            collective_id=1, has_side_effects=True, vmem_limit_bytes=63 * 2**20
        ),
    )(*operands)


def adam_step(weight, moment, square, grad_sum, rate, decay):
    moment_new = BETA_ONE * moment + (1.0 - BETA_ONE) * grad_sum
    square_new = BETA_TWO * square + (1.0 - BETA_TWO) * grad_sum * grad_sum
    moment_hat = moment_new / (1.0 - BETA_ONE**STEP)
    square_hat = square_new / (1.0 - BETA_TWO**STEP)
    weight_new = weight - rate * (moment_hat / (jnp.sqrt(square_hat) + ADAM_EPS) + decay * weight)
    return (weight_new, moment_new, square_new)


def update_kernel(*refs):
    ins, outs = refs[:19], refs[19:]
    layer_out, back_resid, input_part = ins[:3]
    outs[0][...] = layer_out[...].astype(BF)
    outs[1][...] = back_resid[...] + input_part[...]
    for i in range(4):
        weight, moment, square, grad = (ref[...] for ref in ins[3 + 4 * i : 7 + 4 * i])
        new = adam_step(weight, moment, square, grad.astype(F32), RATE_MATRIX, DECAY)
        for ref, value in zip(outs[2 + 3 * i : 5 + 3 * i], new):
            ref[...] = value


def call_update(*operands):
    def half_rows(shape):
        return pl.BlockSpec((shape[0] // 2, shape[1]), lambda i: (i, 0))

    results = [operands[0], operands[1]] + [operands[3 + 4 * i + j] for i in range(4) for j in range(3)]
    types_out = [BF] + [F32] * 13
    return pl.pallas_call(
        update_kernel,
        name="update",
        grid=(2,),
        out_shape=[jax.ShapeDtypeStruct(a.shape, t) for a, t in zip(results, types_out)],
        in_specs=[half_rows(a.shape) for a in operands],
        out_specs=[half_rows(a.shape) for a in results],
        compiler_params=pltpu.CompilerParams(vmem_limit_bytes=62 * 2**20),
    )(*operands)


def per_device(
    hidden_in,
    segment_ids,
    out_cotangent,
    qkv_weight,
    qkv_moment,
    qkv_square,
    proj_weight,
    proj_moment,
    proj_square,
    gate_up_weight,
    gate_up_moment,
    gate_up_square,
    down_weight,
    down_moment,
    down_square,
    gains,
    gain_moment,
    gain_square,
):
    _, c, o = coords()
    place = c * 4 + o
    placed = lax.dynamic_update_slice_in_dim(
        jnp.zeros((QW + KW + 2 * D,), BF), gains.astype(BF), place * gains.shape[0], axis=0
    )
    gain_parts = jnp.concatenate(
        [
            placed[:QW].reshape(RANKS, 2, 128),
            placed[QW : QW + KW].reshape(RANKS, 1, 128),
            jnp.broadcast_to(placed[QW + KW :].reshape(1, 16, 128), (RANKS, 16, 128)),
            jnp.zeros((RANKS, 13, 128), BF),
        ],
        axis=1,
    )
    layer_out, back_resid, input_part, qkv_sum, gu_sum, pj_sum, dn_sum, gain_sum = call_layer(
        hidden_in, out_cotangent, segment_ids, gain_parts, qkv_weight, gate_up_weight, proj_weight, down_weight
    )
    gain_grad = lax.dynamic_slice_in_dim(
        gain_sum.reshape(40 * 128), place * gains.shape[0], gains.shape[0]
    )
    updated = call_update(
        layer_out, back_resid, input_part,
        qkv_weight, qkv_moment, qkv_square, qkv_sum,
        proj_weight, proj_moment, proj_square, pj_sum,
        gate_up_weight, gate_up_moment, gate_up_square, gu_sum,
        down_weight, down_moment, down_square, dn_sum,
    )
    return tuple(updated) + adam_step(gains, gain_moment, gain_square, gain_grad, RATE_GAIN, 0.0)


def solution(mesh):
    seq = P(("dp", "ctx", "opt"), None)
    mat = P(("ctx", "opt"), None)
    vec = P(("ctx", "opt"))
    return jax.shard_map(
        per_device,
        mesh=mesh,
        in_specs=(seq, P("dp", None), seq) + (mat,) * 12 + (vec,) * 3,
        out_specs=(seq, seq) + (mat,) * 12 + (vec,) * 3,
        check_vma=False,
    )
```
